32 devices in a mesh: pp: 4 (over y, core), node: 2 (over x), local: 4 (over z).
Axes of the slice: x: 2, y: 2, z: 4, core: 2. Of those that a mesh axis runs over, the one named last changes fastest.
Arguments:
- act_fwd: bfloat16 [4, 1024, 4096], P('pp', ('node', 'local')), may hold values from -6 to 6
- routes_fwd: int32 [4, 1024, 1], P('pp', ('node', 'local')), may hold values from 0 to 1; in each aligned block of 128 rows (0 to 127, 128 to 255, ..., all dimensions but the last counted through in order) at most 80 rows name the same one
- weight_fwd: float32 [4, 1024], P('pp', ('node', 'local')), may hold values from 0.25 to 1
- grad_bwd: bfloat16 [4, 1024, 4096], P('pp', ('node', 'local')), may hold values from -6 to 6
- routes_bwd: int32 [4, 1024, 1], P('pp', ('node', 'local')), may hold values from 0 to 1; in each aligned block of 128 rows (0 to 127, 128 to 255, ..., all dimensions but the last counted through in order) at most 80 rows name the same one
- weight_bwd: float32 [4, 1024], P('pp', ('node', 'local')), may hold values from 0.25 to 1
- saved_bwd: bfloat16 [4, 1024, 2048], P('pp', ('node', 'local')), may hold values from -8 to 8
- w_gate_up: bfloat16 [4, 2, 4096, 2048], P('pp', 'node', 'local'), may hold values from -0.09375 to 0.09375
- w_down: bfloat16 [4, 2, 1024, 4096], P('pp', 'node', None, 'local'), may hold values from -0.1875 to 0.1875
Outputs:
- next_input: bfloat16 [4, 1024, 4096], P('pp', ('node', 'local'))
- prev_grad: bfloat16 [4, 1024, 4096], P('pp', ('node', 'local'))
The draws below stay inside these ranges and needn't reach their ends.
Inputs may be any that keep to these rules, and one draw needn't show every extreme that they name: `routes_fwd`: within each device's 128 tokens (aligned blocks of rows), no expert is named more than 80 times, a bound that some block reaches. `routes_bwd`: within each device's 128 tokens (aligned blocks of rows), no expert is named more than 80 times, a bound that some block reaches.
All inputs are finite; a program needn't handle non-finite values.
Results may differ from the reference program's by a relative error of at most 0.017.
Values may be sent and summed in bfloat16 or wider, within the bound.
No kernel may reach another device: no remote copies, remote signals or barrier semaphores. Data moves between devices by JAX's collectives and lax.ppermute only.
A program may use at most 128 MiB of HBM per device.

```python
import math
import jax
import jax.numpy as jnp
import numpy as np
from jax import lax

D = 4096
H = 1024
TOK_DEV = 128
TOPK = 1
EXPERTS = 2
CAP = 80
TOKENS = 1024
N_PP = 4
N_NODE = 2
N_LOCAL = 4


def levels(own_key, dims, shards, low, top_value):
    factor_of = 1.0
    for dim, parts in shards:
        draws = jax.random.uniform(jax.random.fold_in(jax.random.fold_in(own_key, 6), dim), (parts,), jnp.float32, low / len(shards), top_value / len(shards))
        factor_of = factor_of * jnp.repeat(jnp.exp(draws), dims[dim] // parts).reshape((-1,) + (1,) * (len(dims) - 1 - dim))
    return factor_of


def assign_block(stream_key, own, number, rows, count, top, reach, skew):
    order = jax.random.permutation(stream_key, count)
    packed, common = load_shares(count, rows * top, reach, skew, True), load_shares(count, rows * top, reach, skew, False)
    places = jnp.arange(count)

    def named(sizes, turn):
        used = int((sizes > 0).sum())
        fixed = max(1, used // 4)
        passed = fixed + (places - fixed + turn * (used - fixed)) % max(1, count - fixed)
        return jnp.zeros((count,), jnp.int32).at[order[jnp.where(places < fixed, places, passed)]].set(jnp.asarray(sizes, jnp.int32))

    sizes = jnp.where(number % 4 == 0, named(packed, number // 4), named(common, number - number // 4 - 1))
    mixed = jax.random.permutation(jax.random.fold_in(own, 3), count)
    source_of, sink = mixed[0:count // 2 * 2:2], mixed[1:count // 2 * 2:2]
    room = jnp.minimum(sizes[source_of] - 1, reach - sizes[sink]) // 2
    room = jnp.where((source_of == order[0]) | (sink == order[0]) | (sizes[sink] == 0), 0, jnp.maximum(room, 0))
    passed = jax.random.randint(jax.random.fold_in(own, 4), (count // 2,), 0, 1 << 20) % (room + 1)
    sizes = sizes.at[source_of].add(-passed).at[sink].add(passed)
    items = jnp.searchsorted(jnp.cumsum(sizes), jnp.arange(rows * top), side="right").astype(jnp.int32)
    listing = items.reshape(top, rows).T
    listing = listing[jax.random.permutation(jax.random.fold_in(own, 1), rows)]
    turn = jax.random.randint(jax.random.fold_in(own, 2), (rows, 1), 0, top)
    return jnp.take_along_axis(listing, (jnp.arange(top)[None, :] + turn) % top, axis=1)


def load_shares(amount, total, limit, lean, full):
    portions = [(1 << 20) // math.isqrt(standing ** lean) + 1 for standing in range(1, amount + 1)]
    largest = limit if full else min(limit, max(-(-total // amount), total * portions[0] // sum(portions)))
    least = 1 if total - largest >= amount - 1 else 0
    given, spare = [largest] + [least] * (amount - 1), total - largest - least * (amount - 1)
    while spare > 0:
        free = [i for i in range(1, amount) if given[i] < largest] or [i for i in range(1, amount) if given[i] < limit]
        pool, remaining = sum([portions[i] for i in free]), spare
        for i in free:
            extra = min(limit - given[i], max(1, remaining * portions[i] // pool), spare)
            given[i] = given[i] + extra
            spare = spare - extra
    return np.array(given)


def gaussian(rng, dims, spread, limit, pieces=(), held_as=jnp.bfloat16):
    gain = levels(rng, dims, pieces, -0.22, 0.18) if pieces else 1.0
    drawn = jax.random.normal(rng, dims, jnp.float32) * spread * gain
    return jnp.minimum(jnp.maximum(drawn, -limit), limit).astype(held_as)


def setup_inputs(seed: int = 0) -> dict:
    splits = jax.random.split(jax.random.key(seed), 10)
    act_fwd = gaussian(splits[0], (N_PP, TOKENS, D), 1.0, 6.0, ((0, 4), (1, 8)))
    routes_fwd_keys = jax.random.split(jax.random.fold_in(splits[1], 1), N_PP * TOKENS // TOK_DEV)
    routes_fwd_turns = jax.random.permutation(jax.random.fold_in(splits[1], 3), N_PP * TOKENS // TOK_DEV)
    routes_fwd = jax.vmap(lambda own, number: assign_block(jax.random.fold_in(splits[1], 2), own, number, TOK_DEV, EXPERTS, TOPK, CAP, 2))(routes_fwd_keys, routes_fwd_turns).reshape((N_PP, TOKENS, TOPK))
    weight_fwd = jnp.clip(jnp.exp(math.log(1.0) - 1.3862944 * jax.random.uniform(splits[2], (N_PP, TOKENS), jnp.float32) ** levels(splits[2], (N_PP, TOKENS), ((0, 4), (1, 8)), -0.2, 0.2)), 0.25, 1.0)
    grad_bwd = gaussian(splits[3], (N_PP, TOKENS, D), 1.0, 6.0, ((0, 4), (1, 8)))
    routes_bwd_keys = jax.random.split(jax.random.fold_in(splits[4], 1), N_PP * TOKENS // TOK_DEV)
    routes_bwd_turns = jax.random.permutation(jax.random.fold_in(splits[4], 3), N_PP * TOKENS // TOK_DEV)
    routes_bwd = jax.vmap(lambda own, number: assign_block(jax.random.fold_in(splits[4], 2), own, number, TOK_DEV, EXPERTS, TOPK, CAP, 2))(routes_bwd_keys, routes_bwd_turns).reshape((N_PP, TOKENS, TOPK))
    weight_bwd = jnp.clip(jnp.exp(math.log(1.0) - 1.3862944 * jax.random.uniform(splits[5], (N_PP, TOKENS), jnp.float32) ** levels(splits[5], (N_PP, TOKENS), ((0, 4), (1, 8)), -0.2, 0.2)), 0.25, 1.0)
    saved_bwd = gaussian(splits[6], (N_PP, TOKENS, 2 * H), 1.5, 8.0, ((0, 4), (1, 8)))
    w_gate_up = gaussian(splits[7], (N_PP, EXPERTS, D, 2 * H), D ** -0.5, 0.09375, ((0, 4), (1, 2), (2, 4)))
    w_down = gaussian(splits[8], (N_PP, EXPERTS, H, D), H ** -0.5, 0.1875, ((0, 4), (1, 2), (3, 4)))
    return {"act_fwd": act_fwd, "routes_fwd": routes_fwd, "weight_fwd": weight_fwd, "grad_bwd": grad_bwd, "routes_bwd": routes_bwd, "weight_bwd": weight_bwd, "saved_bwd": saved_bwd, "w_gate_up": w_gate_up, "w_down": w_down}


def route_slots(route):
    device_count = N_NODE * N_LOCAL
    blocked = route.reshape(device_count, TOK_DEV).astype(jnp.int32)
    onehot = (blocked[:, :, None] == jnp.arange(EXPERTS, dtype=jnp.int32)[None, None, :]).astype(jnp.int32)
    before = jnp.cumsum(onehot, axis=1) - onehot
    slot_of = jnp.sum(before * onehot, axis=2).astype(jnp.int32)
    device_of = jnp.broadcast_to(jnp.arange(device_count, dtype=jnp.int32)[:, None], (device_count, TOK_DEV))
    return blocked.reshape(-1), device_of.reshape(-1), slot_of.reshape(-1)


def pack_rows(values, where):
    expert_of, device_of, slot_of = where
    buffer = jnp.zeros((EXPERTS, N_NODE * N_LOCAL, CAP, values.shape[1]), values.dtype)
    buffer = buffer.at[expert_of, device_of, slot_of].set(values)
    return buffer.reshape(EXPERTS, N_NODE * N_LOCAL * CAP, values.shape[1])


def unpack_rows(rows_out, where):
    expert_of, device_of, slot_of = where
    blocked = rows_out.reshape(EXPERTS, N_NODE * N_LOCAL, CAP, rows_out.shape[-1])
    return blocked[expert_of, device_of, slot_of]


def block_sum(left, right):
    row_count = left.shape[0]
    column = left.shape[1] // N_LOCAL
    left_blocks = left.astype(jnp.float32).reshape(row_count, N_LOCAL, column)
    right_blocks = right.astype(jnp.float32).reshape(N_LOCAL, column, right.shape[1])
    partial_value = jnp.einsum("rjd,jdk->rjk", left_blocks, right_blocks)
    return jnp.sum(partial_value.astype(jnp.bfloat16).astype(jnp.float32), axis=1)


def expert_forward(operands):
    rows_in, w_gu, w_dn = operands
    preact = block_sum(rows_in, w_gu)
    hidden = (jax.nn.silu(preact[:, :H]) * preact[:, H:]).astype(jnp.bfloat16)
    return jnp.dot(hidden, w_dn, preferred_element_type=jnp.float32).astype(jnp.bfloat16)


def expert_backward(operands):
    rows_in, saved_rows, w_gu, w_dn = operands
    grad_hidden = block_sum(rows_in, jnp.transpose(w_dn))
    gate_pre = saved_rows[:, :H].astype(jnp.float32)
    up_pre = saved_rows[:, H:].astype(jnp.float32)
    sigmoid_g = 1.0 / (1.0 + jnp.exp(-gate_pre))
    grad_gate = grad_hidden * up_pre * sigmoid_g * (1.0 + gate_pre * (1.0 - sigmoid_g))
    grad_up = grad_hidden * gate_pre * sigmoid_g
    grad_gu = jnp.concatenate([grad_gate, grad_up], axis=1).astype(jnp.bfloat16)
    return jnp.dot(grad_gu, jnp.transpose(w_gu), preferred_element_type=jnp.float32).astype(jnp.bfloat16)


def reference(act_fwd, routes_fwd, weight_fwd, grad_bwd, routes_bwd, weight_bwd, saved_bwd, w_gate_up, w_down):
    outputs_fwd = []
    outputs_bwd = []
    for segment in range(N_PP):
        where_a = route_slots(routes_fwd[segment, :, 0])
        tokens_a = act_fwd[segment]
        rows_a = pack_rows(tokens_a, where_a)
        done_a = lax.map(expert_forward, (rows_a, w_gate_up[segment], w_down[segment]))
        moe_a = unpack_rows(done_a, where_a)
        result_a = tokens_a.astype(jnp.float32) + weight_fwd[segment][:, None] * moe_a.astype(jnp.float32)
        outputs_fwd.append(result_a.astype(jnp.bfloat16))

        where_b = route_slots(routes_bwd[segment, :, 0])
        cotangent = grad_bwd[segment]
        scaled = (weight_bwd[segment][:, None] * cotangent.astype(jnp.float32)).astype(jnp.bfloat16)
        rows_b = pack_rows(scaled, where_b)
        saved_b = pack_rows(saved_bwd[segment], where_b)
        done_b = lax.map(expert_backward, (rows_b, saved_b, w_gate_up[segment], w_down[segment]))
        moe_b = unpack_rows(done_b, where_b)
        result_b = cotangent.astype(jnp.float32) + moe_b.astype(jnp.float32)
        outputs_bwd.append(result_b.astype(jnp.bfloat16))
    next_input = jnp.roll(jnp.stack(outputs_fwd, axis=0), 1, axis=0)
    prev_grad = jnp.roll(jnp.stack(outputs_bwd, axis=0), -1, axis=0)
    return (next_input, prev_grad)
```

```python
import jax
import jax.numpy as jnp
from jax import lax
from jax.sharding import PartitionSpec as P

F32 = jnp.float32
BF16 = jnp.bfloat16
AXES = ("pp", "node", "local")


def move(value, by_pp=0, by_node=0, by_local=0):
    pps, nodes, locs = (lax.axis_size(a) for a in AXES)
    pairs = []
    for s in range(pps):
        for n in range(nodes):
            for l in range(locs):
                source = (s * nodes + n) * locs + l
                target = (((s + by_pp) % pps) * nodes + (n ^ by_node)) * locs + (l ^ by_local)
                pairs.append((source, target))
    return lax.ppermute(value, AXES, pairs)


def sorted_places(route):
    ones = route.astype(F32)
    count = route.shape[0]
    earlier = (jnp.arange(count)[None, :] < jnp.arange(count)[:, None]).astype(F32)
    ones_before = jnp.dot(earlier, ones[:, None], preferred_element_type=F32)[:, 0]
    zeros = count - jnp.sum(ones)
    index = jnp.arange(count, dtype=F32)
    place = jnp.where(route == 0, index - ones_before, zeros + ones_before)
    return place.astype(jnp.int32)


def sorter(route):
    place = sorted_places(route)
    rows = jnp.arange(route.shape[0], dtype=jnp.int32)
    return (rows[:, None] == place[None, :]).astype(BF16)


def window_placer(route, node, capacity):
    place = sorted_places(route)
    start = route.shape[0] - capacity
    in_window = place - jnp.where(route == 1, start, 0)
    row = jnp.where(route == node, in_window, in_window + capacity)
    rows = jnp.arange(2 * capacity, dtype=jnp.int32)
    return (rows[:, None] == row[None, :]).astype(BF16)


def dot_t(left, right):
    return lax.dot_general(left, right, (((1,), (1,)), ((), ())), preferred_element_type=F32)


def windows(blocks, node, capacity):
    tokens = blocks.shape[-2]
    start = tokens - capacity
    low = lax.slice_in_dim(blocks, 0, capacity, axis=-2 + blocks.ndim)
    high = lax.slice_in_dim(blocks, start, tokens, axis=-2 + blocks.ndim)
    own = jnp.where(node == 0, low, high)
    other = jnp.where(node == 0, high, low)
    return own, other


def scatter_in(tokens, placer, node, local, capacity):
    column = tokens.shape[1] // 4
    blocks = []
    for k in range(4):
        block = lax.dynamic_slice_in_dim(tokens, (local ^ k) * column, column, axis=1)
        block = jnp.dot(placer, block, preferred_element_type=F32).astype(BF16)
        blocks.append(block if k == 0 else move(block, by_local=k))
    rows = jnp.stack(blocks)
    own, other = windows(rows, node, capacity)
    got = move(other, by_node=1)
    return jnp.stack([own, got], axis=1)


def reduce_scatter(partial):
    out = jnp.stack([partial[1], partial[3]]).astype(BF16)
    got = move(out, by_local=1).astype(F32)
    own0 = partial[0] + got[0]
    own2 = (partial[2] + got[1]).astype(BF16)
    got2 = move(own2, by_local=2).astype(F32)
    return own0 + got2


def all_gather(rows):
    got2 = move(rows, by_local=2)
    got = move(jnp.stack([rows, got2]), by_local=1)
    return jnp.stack([rows, got[0], got2, got[1]])


def give_back(done, by_pp):
    result = []
    for k in range(4):
        own = move(done[k, 0], by_pp=by_pp, by_local=k)
        other = move(done[k, 1], by_pp=by_pp, by_node=1, by_local=k)
        result.append(jnp.concatenate([own, other], axis=0))
    return result


def unsort(blocks, placer, local):
    column = blocks[0].shape[1]
    full = jnp.zeros((placer.shape[1], 4 * column), F32)
    for k in range(4):
        moe = lax.dot_general(
            placer, blocks[k], (((0,), (0,)), ((), ())), preferred_element_type=F32
        )
        full = lax.dynamic_update_slice_in_dim(full, moe, (local ^ k) * column, axis=1)
    return full


def body_pair(
    act_fwd, routes_fwd, weight_fwd, grad_bwd, routes_bwd, weight_bwd, saved_bwd, w_gate_up, w_down
):
    node = lax.axis_index("node")
    local = lax.axis_index("local")
    tokens_here = act_fwd.shape[1]
    capacity = 5 * tokens_here // 8
    w_gu = w_gate_up[0, 0]
    w_dn = w_down[0, 0]
    hidden_units = w_dn.shape[0]

    act = act_fwd[0]
    grad = grad_bwd[0]
    sort_a = sorter(routes_fwd[0, :, 0])
    sort_b = sorter(routes_bwd[0, :, 0])
    rows_a = scatter_in(act, sort_a, node, local, capacity)
    dy = (weight_bwd[0][:, None] * grad.astype(F32)).astype(BF16)
    rows_b = scatter_in(dy, sort_b, node, local, capacity)
    saved = jnp.dot(sort_b, saved_bwd[0], preferred_element_type=F32).astype(BF16)
    saved_own, saved_other = windows(saved, node, capacity)
    saved_rows = jnp.stack([saved_own, move(saved_other, by_node=1)])

    act_next = move(act, by_pp=1)
    grad_next = move(grad, by_pp=-1)
    route_a_next = move(routes_fwd[0, :, 0], by_pp=1)
    route_b_next = move(routes_bwd[0, :, 0], by_pp=-1)
    weight_next = move(weight_fwd[0], by_pp=1)

    shape = (4, 2, capacity)
    column = rows_a.shape[-1]
    part_a = jnp.dot(rows_a.reshape(-1, column), w_gu, preferred_element_type=F32)
    preact = reduce_scatter(part_a.reshape(shape + (2 * hidden_units,)))
    part_b = dot_t(rows_b.reshape(-1, column), w_dn)
    dh = reduce_scatter(part_b.reshape(shape + (hidden_units,)))

    hidden = (jax.nn.silu(preact[..., :hidden_units]) * preact[..., hidden_units:]).astype(BF16)
    all_hidden = all_gather(hidden)
    done_a = jnp.dot(
        all_hidden.reshape(-1, hidden_units), w_dn, preferred_element_type=F32
    ).astype(BF16)

    g = saved_rows[..., :hidden_units].astype(F32)
    u = saved_rows[..., hidden_units:].astype(F32)
    q = 1.0 / (1.0 + jnp.exp(-g))
    grad_gu = jnp.concatenate([dh * u * q * (1.0 + g * (1.0 - q)), dh * g * q], axis=-1).astype(
        BF16
    )
    all_gu = all_gather(grad_gu)
    done_b = dot_t(all_gu.reshape(-1, 2 * hidden_units), w_gu).astype(BF16)

    back_a = give_back(done_a.reshape(shape + (column,)), 1)
    back_b = give_back(done_b.reshape(shape + (column,)), -1)

    moe_a = unsort(back_a, window_placer(route_a_next, node, capacity), local)
    next_input = (act_next.astype(F32) + weight_next[:, None] * moe_a).astype(BF16)
    moe_b = unsort(back_b, window_placer(route_b_next, node, capacity), local)
    prev_grad = (grad_next.astype(F32) + moe_b).astype(BF16)
    return next_input[None], prev_grad[None]


def from_behind(value, axis, by):
    length = lax.axis_size(axis)
    return lax.ppermute(value, axis, [(i, (i + by) % length) for i in range(length)])


def place_matrix(route, expert_count, capacity):
    onehot = (route[:, None] == jnp.arange(expert_count, dtype=jnp.int32)[None, :]).astype(
        jnp.int32
    )
    before = jnp.cumsum(onehot, axis=0) - onehot
    slot_index = jnp.sum(before * onehot, axis=1)
    target = route * capacity + slot_index
    positions = jnp.arange(expert_count * capacity, dtype=jnp.int32)
    return (positions[:, None] == target[None, :]).astype(jnp.bfloat16)


def pack_rows(placer, values, expert_count, capacity):
    packed = jnp.dot(placer, values, preferred_element_type=jnp.float32).astype(jnp.bfloat16)
    return packed.reshape(expert_count, capacity, values.shape[1])


def unpack_rows(placer, packed):
    flattened = packed.reshape(-1, packed.shape[-1])
    result = lax.dot_general(
        placer, flattened, (((0,), (0,)), ((), ())), preferred_element_type=jnp.float32
    )
    return result.astype(jnp.bfloat16)


def flat_outgoing(packed, local_count):
    expert_count, capacity, feature_count = packed.shape
    column = feature_count // local_count
    outgoing = packed.reshape(expert_count, capacity, local_count, column).transpose(0, 2, 1, 3)
    return outgoing.reshape(expert_count * local_count, capacity, column)


def flat_layout(received, expert_count, local_count):
    capacity = received.shape[1]
    column = received.shape[2]
    rows_in = received.reshape(expert_count, local_count, capacity, column).transpose(1, 0, 2, 3)
    return rows_in.reshape(-1, column)


def send_rows(packs, local_count):
    expert_count = packs[0].shape[0]
    outgoing = tuple((flat_outgoing(packed, local_count) for packed in packs))
    received = (
        lax.all_to_all(outgoing[0], ("node", "local"), split_axis=0, concat_axis=0, tiled=True),
        lax.all_to_all(outgoing[1], ("node", "local"), split_axis=0, concat_axis=0, tiled=True),
    )
    return tuple((flat_layout(item, expert_count, local_count) for item in received))


def return_rows(finished_pair, expert_count, capacity, local_count):
    column = finished_pair[0].shape[1]
    blocks = tuple(
        (item.reshape(local_count, expert_count, capacity, column) for item in finished_pair)
    )
    outgoing = tuple(
        (
            item.transpose(1, 0, 2, 3).reshape(expert_count * local_count, capacity, column)
            for item in blocks
        )
    )
    received = (
        lax.all_to_all(outgoing[0], ("node", "local"), split_axis=0, concat_axis=0, tiled=True),
        lax.all_to_all(outgoing[1], ("node", "local"), split_axis=0, concat_axis=0, tiled=True),
    )
    results = []
    for item in received:
        arranged = item.reshape(expert_count, local_count, capacity, column).transpose(0, 2, 1, 3)
        results.append(arranged.reshape(expert_count, capacity, local_count * column))
    return tuple(results)


def body(
    act_fwd, routes_fwd, weight_fwd, grad_bwd, routes_bwd, weight_bwd, saved_bwd, w_gate_up, w_down
):
    node_count = lax.axis_size("node")
    local_count = lax.axis_size("local")
    tokens_here = act_fwd.shape[1]
    capacity = 5 * tokens_here // (4 * node_count)
    rows_each = node_count * capacity
    w_gu = w_gate_up[0, 0]
    w_dn = w_down[0, 0]
    hidden_units = w_dn.shape[0]
    tokens_a = act_fwd[0]
    placer_a = place_matrix(routes_fwd[0, :, 0], node_count, capacity)
    cotangent = grad_bwd[0]
    placer_b = place_matrix(routes_bwd[0, :, 0], node_count, capacity)
    scaled = (weight_bwd[0][:, None] * cotangent.astype(jnp.float32)).astype(jnp.bfloat16)
    packed_a = pack_rows(placer_a, tokens_a, node_count, capacity)
    packed_b = pack_rows(placer_b, scaled, node_count, capacity)
    rows_a, rows_b = send_rows((packed_a, packed_b), local_count)
    saved_packed = pack_rows(placer_b, saved_bwd[0], node_count, capacity)
    saved_rows = lax.all_to_all(
        saved_packed, "node", split_axis=0, concat_axis=0, tiled=True
    ).reshape(rows_each, -1)
    row_block = rows_a
    preact = lax.psum_scatter(
        jnp.dot(row_block, w_gu, preferred_element_type=jnp.float32).astype(jnp.bfloat16),
        "local",
        scatter_dimension=0,
        tiled=True,
    ).astype(jnp.float32)
    row_block = rows_b
    grad_hidden = lax.psum_scatter(
        lax.dot_general(
            row_block, w_dn, (((1,), (1,)), ((), ())), preferred_element_type=jnp.float32
        ).astype(jnp.bfloat16),
        "local",
        scatter_dimension=0,
        tiled=True,
    ).astype(jnp.float32)
    hidden = (jax.nn.silu(preact[:, :hidden_units]) * preact[:, hidden_units:]).astype(jnp.bfloat16)
    done_a = jnp.dot(
        lax.all_gather(hidden, "local", axis=0, tiled=True),
        w_dn,
        preferred_element_type=jnp.float32,
    ).astype(jnp.bfloat16)
    gate_pre = saved_rows[:, :hidden_units].astype(jnp.float32)
    up_pre = saved_rows[:, hidden_units:].astype(jnp.float32)
    sigmoid_g = 1.0 / (1.0 + jnp.exp(-gate_pre))
    grad_gate = grad_hidden * up_pre * sigmoid_g * (1.0 + gate_pre * (1.0 - sigmoid_g))
    grad_up = grad_hidden * gate_pre * sigmoid_g
    grad_gu = jnp.concatenate([grad_gate, grad_up], axis=1).astype(jnp.bfloat16)
    product = lax.dot_general(
        lax.all_gather(grad_gu, "local", axis=0, tiled=True),
        w_gu,
        (((1,), (1,)), ((), ())),
        preferred_element_type=jnp.float32,
    )
    done_b = product.astype(jnp.bfloat16)
    back_a, back_b = return_rows((done_a, done_b), node_count, capacity, local_count)
    moe_a = unpack_rows(placer_a, back_a)
    result_a = tokens_a.astype(jnp.float32) + weight_fwd[0][:, None] * moe_a.astype(jnp.float32)
    result_a = result_a.astype(jnp.bfloat16)
    moe_b = unpack_rows(placer_b, back_b)
    result_b = (cotangent.astype(jnp.float32) + moe_b.astype(jnp.float32)).astype(jnp.bfloat16)
    next_input = from_behind(result_a[None], "pp", 1)
    prev_grad = from_behind(result_b[None], "pp", -1)
    return (next_input, prev_grad)


def solution(mesh):
    in_specs = (
        P("pp", ("node", "local"), None),
        P("pp", ("node", "local"), None),
        P("pp", ("node", "local")),
        P("pp", ("node", "local"), None),
        P("pp", ("node", "local"), None),
        P("pp", ("node", "local")),
        P("pp", ("node", "local"), None),
        P("pp", "node", "local", None),
        P("pp", "node", None, "local"),
    )
    out_specs = (P("pp", ("node", "local"), None), P("pp", ("node", "local"), None))
    paired = mesh.shape["node"] == 2 and mesh.shape["local"] == 4
    plan = body_pair if paired else body
    return jax.shard_map(plan, mesh=mesh, in_specs=in_specs, out_specs=out_specs, check_vma=False)
```

```python
import jax
import jax.numpy as jnp
from jax import lax
from jax.sharding import PartitionSpec as P

F32 = jnp.float32
BF16 = jnp.bfloat16
AXES = ("pp", "node", "local")


def move(value, by_pp=0, by_node=0, by_local=0, wrap=True, first=0, last=None):
    pps, nodes, locs = (lax.axis_size(a) for a in AXES)
    last = locs - 1 if last is None else last
    pairs = []
    for s in range(pps):
        for n in range(nodes):
            for l in range(locs):
                to = l + by_local
                if not wrap and not (first <= l <= last and 0 <= to < locs):
                    continue
                source = (s * nodes + n) * locs + l
                target = (((s + by_pp) % pps) * nodes + (n ^ by_node)) * locs + to % locs
                pairs.append((source, target))
    return lax.ppermute(value, AXES, pairs)


def sorted_places(route):
    ones = route.astype(F32)
    count = route.shape[0]
    earlier = (jnp.arange(count)[None, :] < jnp.arange(count)[:, None]).astype(F32)
    ones_before = jnp.dot(earlier, ones[:, None], preferred_element_type=F32)[:, 0]
    zeros = count - jnp.sum(ones)
    index = jnp.arange(count, dtype=F32)
    place = jnp.where(route == 0, index - ones_before, zeros + ones_before)
    return place.astype(jnp.int32)


def sorter(route):
    place = sorted_places(route)
    rows = jnp.arange(route.shape[0], dtype=jnp.int32)
    return (rows[:, None] == place[None, :]).astype(BF16)


def window_placer(route, node, capacity):
    place = sorted_places(route)
    start = route.shape[0] - capacity
    in_window = place - jnp.where(route == 1, start, 0)
    row = jnp.where(route == node, in_window, in_window + capacity)
    rows = jnp.arange(2 * capacity, dtype=jnp.int32)
    return (rows[:, None] == row[None, :]).astype(BF16)


def dot_t(left, right):
    return lax.dot_general(left, right, (((1,), (1,)), ((), ())), preferred_element_type=F32)


def windows(blocks, node, capacity):
    tokens = blocks.shape[-2]
    start = tokens - capacity
    low = lax.slice_in_dim(blocks, 0, capacity, axis=-2 + blocks.ndim)
    high = lax.slice_in_dim(blocks, start, tokens, axis=-2 + blocks.ndim)
    own = jnp.where(node == 0, low, high)
    other = jnp.where(node == 0, high, low)
    return own, other


def join(*values):
    return lax.optimization_barrier(values)


def to_owners(tokens, placer, local, after=()):
    column = tokens.shape[1] // 4
    blocks = []
    for m in range(4):
        block = lax.dynamic_slice_in_dim(tokens, ((local - m) % 4) * column, column, axis=1)
        blocks.append(jnp.dot(placer, block, preferred_element_type=F32).astype(BF16))
    if after:
        blocks = join(*blocks, *after)[:4]
    return join(blocks[0], *(move(blocks[m], by_local=-m) for m in (1, 2, 3)))


def to_expert(blocks, node, capacity):
    own, other = windows(jnp.stack(blocks), node, capacity)
    got = move(other, by_node=1)
    return jnp.stack([own, got], axis=1)


def reduce_scatter(partial):
    right, left = partial[3], partial[1]
    for step in (1, 2, 3):
        got_r = move(right.astype(BF16), by_local=1, wrap=False, last=step - 1)
        got_l = move(left.astype(BF16), by_local=-1, wrap=False, first=4 - step)
        right = partial[3 - step] + got_r.astype(F32)
        if step < 3:
            left = partial[step + 1] + got_l.astype(F32)
    return right + got_l.astype(F32)


def all_gather(rows, local):
    from_left, from_right = [rows], [rows]
    for step in (1, 2, 3):
        from_left.append(move(from_left[-1], by_local=1, wrap=False, first=step - 1))
        from_right.append(move(from_right[-1], by_local=-1, wrap=False, last=4 - step))
    slots = [rows]
    for m in (1, 2, 3):
        slots.append(jnp.where(local + m < 4, from_right[m], from_left[4 - m]))
    return jnp.stack(slots)


def give_back(done, by_pp):
    got = []
    for m in (2, 1, 3, 0):
        got.append(move(done[m, 0], by_pp=by_pp, by_local=m))
        got.append(move(done[m, 1], by_pp=by_pp, by_node=1, by_local=m))
    got = join(*got)
    rows = [None] * 4
    for i, m in enumerate((2, 1, 3, 0)):
        rows[m] = jnp.concatenate([got[2 * i], got[2 * i + 1]], axis=0)
    return rows


def unsort(blocks, placer, local):
    column = blocks[0].shape[1]
    full = jnp.zeros((placer.shape[1], 4 * column), F32)
    for m in range(4):
        moe = lax.dot_general(
            placer, blocks[m], (((0,), (0,)), ((), ())), preferred_element_type=F32
        )
        full = lax.dynamic_update_slice_in_dim(full, moe, ((local - m) % 4) * column, axis=1)
    return full


def body_pair(
    act_fwd, routes_fwd, weight_fwd, grad_bwd, routes_bwd, weight_bwd, saved_bwd, w_gate_up, w_down
):
    node = lax.axis_index("node")
    local = lax.axis_index("local")
    tokens_here = act_fwd.shape[1]
    capacity = 5 * tokens_here // 8
    w_gu = w_gate_up[0, 0]
    w_dn = w_down[0, 0]
    hidden_units = w_dn.shape[0]

    act = act_fwd[0]
    grad = grad_bwd[0]
    sort_a = sorter(routes_fwd[0, :, 0])
    sort_b = sorter(routes_bwd[0, :, 0])
    dy = (weight_bwd[0][:, None] * grad.astype(F32)).astype(BF16)
    blocks_b = to_owners(dy, sort_b, local)
    blocks_a = to_owners(act, sort_a, local, after=blocks_b[1:])
    rows_b = to_expert(blocks_b, node, capacity)
    rows_a = to_expert(blocks_a, node, capacity)
    saved = jnp.dot(sort_b, saved_bwd[0], preferred_element_type=F32).astype(BF16)
    saved_own, saved_other = windows(saved, node, capacity)
    saved_rows = jnp.stack([saved_own, move(saved_other, by_node=1)])

    act_next = move(act, by_pp=1)
    grad_next = move(grad, by_pp=-1)
    route_a_next = move(routes_fwd[0, :, 0], by_pp=1)
    route_b_next = move(routes_bwd[0, :, 0], by_pp=-1)
    weight_next = move(weight_fwd[0], by_pp=1)

    shape = (4, 2, capacity)
    column = rows_a.shape[-1]
    part_a = jnp.dot(rows_a.reshape(-1, column), w_gu, preferred_element_type=F32)
    preact = reduce_scatter(part_a.reshape(shape + (2 * hidden_units,)))
    part_b = dot_t(rows_b.reshape(-1, column), w_dn)
    dh = reduce_scatter(part_b.reshape(shape + (hidden_units,)))

    hidden = (jax.nn.silu(preact[..., :hidden_units]) * preact[..., hidden_units:]).astype(BF16)
    all_hidden = all_gather(hidden, local)
    done_a = jnp.dot(
        all_hidden.reshape(-1, hidden_units), w_dn, preferred_element_type=F32
    ).astype(BF16)

    g = saved_rows[..., :hidden_units].astype(F32)
    u = saved_rows[..., hidden_units:].astype(F32)
    q = 1.0 / (1.0 + jnp.exp(-g))
    grad_gu = jnp.concatenate([dh * u * q * (1.0 + g * (1.0 - q)), dh * g * q], axis=-1).astype(
        BF16
    )
    all_gu = all_gather(grad_gu, local)
    done_b = dot_t(all_gu.reshape(-1, 2 * hidden_units), w_gu).astype(BF16)

    back_a = give_back(done_a.reshape(shape + (column,)), 1)
    back_b = give_back(done_b.reshape(shape + (column,)), -1)

    moe_a = unsort(back_a, window_placer(route_a_next, node, capacity), local)
    next_input = (act_next.astype(F32) + weight_next[:, None] * moe_a).astype(BF16)
    moe_b = unsort(back_b, window_placer(route_b_next, node, capacity), local)
    prev_grad = (grad_next.astype(F32) + moe_b).astype(BF16)
    return next_input[None], prev_grad[None]


def from_behind(value, axis, by):
    length = lax.axis_size(axis)
    return lax.ppermute(value, axis, [(i, (i + by) % length) for i in range(length)])


def place_matrix(route, expert_count, capacity):
    onehot = (route[:, None] == jnp.arange(expert_count, dtype=jnp.int32)[None, :]).astype(
        jnp.int32
    )
    before = jnp.cumsum(onehot, axis=0) - onehot
    slot_index = jnp.sum(before * onehot, axis=1)
    target = route * capacity + slot_index
    positions = jnp.arange(expert_count * capacity, dtype=jnp.int32)
    return (positions[:, None] == target[None, :]).astype(jnp.bfloat16)


def pack_rows(placer, values, expert_count, capacity):
    packed = jnp.dot(placer, values, preferred_element_type=jnp.float32).astype(jnp.bfloat16)
    return packed.reshape(expert_count, capacity, values.shape[1])


def unpack_rows(placer, packed):
    flattened = packed.reshape(-1, packed.shape[-1])
    result = lax.dot_general(
        placer, flattened, (((0,), (0,)), ((), ())), preferred_element_type=jnp.float32
    )
    return result.astype(jnp.bfloat16)


def flat_outgoing(packed, local_count):
    expert_count, capacity, feature_count = packed.shape
    column = feature_count // local_count
    outgoing = packed.reshape(expert_count, capacity, local_count, column).transpose(0, 2, 1, 3)
    return outgoing.reshape(expert_count * local_count, capacity, column)


def flat_layout(received, expert_count, local_count):
    capacity = received.shape[1]
    column = received.shape[2]
    rows_in = received.reshape(expert_count, local_count, capacity, column).transpose(1, 0, 2, 3)
    return rows_in.reshape(-1, column)


def send_rows(packs, local_count):
    expert_count = packs[0].shape[0]
    outgoing = tuple((flat_outgoing(packed, local_count) for packed in packs))
    received = (
        lax.all_to_all(outgoing[0], ("node", "local"), split_axis=0, concat_axis=0, tiled=True),
        lax.all_to_all(outgoing[1], ("node", "local"), split_axis=0, concat_axis=0, tiled=True),
    )
    return tuple((flat_layout(item, expert_count, local_count) for item in received))


def return_rows(finished_pair, expert_count, capacity, local_count):
    column = finished_pair[0].shape[1]
    blocks = tuple(
        (item.reshape(local_count, expert_count, capacity, column) for item in finished_pair)
    )
    outgoing = tuple(
        (
            item.transpose(1, 0, 2, 3).reshape(expert_count * local_count, capacity, column)
            for item in blocks
        )
    )
    received = (
        lax.all_to_all(outgoing[0], ("node", "local"), split_axis=0, concat_axis=0, tiled=True),
        lax.all_to_all(outgoing[1], ("node", "local"), split_axis=0, concat_axis=0, tiled=True),
    )
    results = []
    for item in received:
        arranged = item.reshape(expert_count, local_count, capacity, column).transpose(0, 2, 1, 3)
        results.append(arranged.reshape(expert_count, capacity, local_count * column))
    return tuple(results)


def body(
    act_fwd, routes_fwd, weight_fwd, grad_bwd, routes_bwd, weight_bwd, saved_bwd, w_gate_up, w_down
):
    node_count = lax.axis_size("node")
    local_count = lax.axis_size("local")
    tokens_here = act_fwd.shape[1]
    capacity = 5 * tokens_here // (4 * node_count)
    rows_each = node_count * capacity
    w_gu = w_gate_up[0, 0]
    w_dn = w_down[0, 0]
    hidden_units = w_dn.shape[0]
    tokens_a = act_fwd[0]
    placer_a = place_matrix(routes_fwd[0, :, 0], node_count, capacity)
    cotangent = grad_bwd[0]
    placer_b = place_matrix(routes_bwd[0, :, 0], node_count, capacity)
    scaled = (weight_bwd[0][:, None] * cotangent.astype(jnp.float32)).astype(jnp.bfloat16)
    packed_a = pack_rows(placer_a, tokens_a, node_count, capacity)
    packed_b = pack_rows(placer_b, scaled, node_count, capacity)
    rows_a, rows_b = send_rows((packed_a, packed_b), local_count)
    saved_packed = pack_rows(placer_b, saved_bwd[0], node_count, capacity)
    saved_rows = lax.all_to_all(
        saved_packed, "node", split_axis=0, concat_axis=0, tiled=True
    ).reshape(rows_each, -1)
    row_block = rows_a
    preact = lax.psum_scatter(
        jnp.dot(row_block, w_gu, preferred_element_type=jnp.float32).astype(jnp.bfloat16),
        "local",
        scatter_dimension=0,
        tiled=True,
    ).astype(jnp.float32)
    row_block = rows_b
    grad_hidden = lax.psum_scatter(
        lax.dot_general(
            row_block, w_dn, (((1,), (1,)), ((), ())), preferred_element_type=jnp.float32
        ).astype(jnp.bfloat16),
        "local",
        scatter_dimension=0,
        tiled=True,
    ).astype(jnp.float32)
    hidden = (jax.nn.silu(preact[:, :hidden_units]) * preact[:, hidden_units:]).astype(jnp.bfloat16)
    done_a = jnp.dot(
        lax.all_gather(hidden, "local", axis=0, tiled=True),
        w_dn,
        preferred_element_type=jnp.float32,
    ).astype(jnp.bfloat16)
    gate_pre = saved_rows[:, :hidden_units].astype(jnp.float32)
    up_pre = saved_rows[:, hidden_units:].astype(jnp.float32)
    sigmoid_g = 1.0 / (1.0 + jnp.exp(-gate_pre))
    grad_gate = grad_hidden * up_pre * sigmoid_g * (1.0 + gate_pre * (1.0 - sigmoid_g))
    grad_up = grad_hidden * gate_pre * sigmoid_g
    grad_gu = jnp.concatenate([grad_gate, grad_up], axis=1).astype(jnp.bfloat16)
    product = lax.dot_general(
        lax.all_gather(grad_gu, "local", axis=0, tiled=True),
        w_gu,
        (((1,), (1,)), ((), ())),
        preferred_element_type=jnp.float32,
    )
    done_b = product.astype(jnp.bfloat16)
    back_a, back_b = return_rows((done_a, done_b), node_count, capacity, local_count)
    moe_a = unpack_rows(placer_a, back_a)
    result_a = tokens_a.astype(jnp.float32) + weight_fwd[0][:, None] * moe_a.astype(jnp.float32)
    result_a = result_a.astype(jnp.bfloat16)
    moe_b = unpack_rows(placer_b, back_b)
    result_b = (cotangent.astype(jnp.float32) + moe_b.astype(jnp.float32)).astype(jnp.bfloat16)
    next_input = from_behind(result_a[None], "pp", 1)
    prev_grad = from_behind(result_b[None], "pp", -1)
    return (next_input, prev_grad)


def solution(mesh):
    in_specs = (
        P("pp", ("node", "local"), None),
        P("pp", ("node", "local"), None),
        P("pp", ("node", "local")),
        P("pp", ("node", "local"), None),
        P("pp", ("node", "local"), None),
        P("pp", ("node", "local")),
        P("pp", ("node", "local"), None),
        P("pp", "node", "local", None),
        P("pp", "node", None, "local"),
    )
    out_specs = (P("pp", ("node", "local"), None), P("pp", ("node", "local"), None))
    paired = mesh.shape["node"] == 2 and mesh.shape["local"] == 4
    plan = body_pair if paired else body
    return jax.shard_map(plan, mesh=mesh, in_specs=in_specs, out_specs=out_specs, check_vma=False)
```

```python
import jax
import jax.numpy as jnp
from jax import lax
from jax.sharding import PartitionSpec as P

F32 = jnp.float32
BF16 = jnp.bfloat16
AXES = ("pp", "node", "local")


def move(value, by_pp=0, by_node=0, by_local=0, wrap=True, first=0, last=None):
    pps, nodes, locs = (lax.axis_size(a) for a in AXES)
    last = locs - 1 if last is None else last
    pairs = []
    for s in range(pps):
        for n in range(nodes):
            for l in range(locs):
                to = l + by_local
                if not wrap and not (first <= l <= last and 0 <= to < locs):
                    continue
                source = (s * nodes + n) * locs + l
                target = (((s + by_pp) % pps) * nodes + (n ^ by_node)) * locs + to % locs
                pairs.append((source, target))
    return lax.ppermute(value, AXES, pairs)


def sorted_places(route):
    ones = route.astype(F32)
    count = route.shape[0]
    earlier = (jnp.arange(count)[None, :] < jnp.arange(count)[:, None]).astype(F32)
    ones_before = jnp.dot(earlier, ones[:, None], preferred_element_type=F32)[:, 0]
    zeros = count - jnp.sum(ones)
    index = jnp.arange(count, dtype=F32)
    place = jnp.where(route == 0, index - ones_before, zeros + ones_before)
    return place.astype(jnp.int32)


def sorter(route):
    place = sorted_places(route)
    rows = jnp.arange(route.shape[0], dtype=jnp.int32)
    return (rows[:, None] == place[None, :]).astype(BF16)


def window_placer(route, node, capacity):
    place = sorted_places(route)
    start = route.shape[0] - capacity
    in_window = place - jnp.where(route == 1, start, 0)
    row = jnp.where(route == node, in_window, in_window + capacity)
    rows = jnp.arange(2 * capacity, dtype=jnp.int32)
    return (rows[:, None] == row[None, :]).astype(BF16)


def dot_t(left, right):
    return lax.dot_general(left, right, (((1,), (1,)), ((), ())), preferred_element_type=F32)


def windows(blocks, node, capacity):
    tokens = blocks.shape[-2]
    start = tokens - capacity
    low = lax.slice_in_dim(blocks, 0, capacity, axis=-2 + blocks.ndim)
    high = lax.slice_in_dim(blocks, start, tokens, axis=-2 + blocks.ndim)
    own = jnp.where(node == 0, low, high)
    other = jnp.where(node == 0, high, low)
    return own, other


def join(*values):
    return lax.optimization_barrier(values)


def after(values, *others):
    return list(join(*values, *others)[: len(values)])


def cut(tokens, placer, local):
    column = tokens.shape[1] // 4
    blocks = []
    for m in range(4):
        block = lax.dynamic_slice_in_dim(tokens, ((local - m) % 4) * column, column, axis=1)
        blocks.append(jnp.dot(placer, block, preferred_element_type=F32).astype(BF16))
    return blocks


def sums(partial):
    right, left = partial[3], partial[1]
    for step in (1, 2, 3):
        right, left = right.astype(BF16), left.astype(BF16)
        got_r, got_l = yield (
            (right, dict(by_local=1, wrap=False, last=step - 1)),
            (left, dict(by_local=-1, wrap=False, first=4 - step)),
        )
        right = partial[3 - step] + got_r.astype(F32)
        if step < 3:
            left = partial[step + 1] + got_l.astype(F32)
    yield right + got_l.astype(F32)


def gathers(rows, local):
    from_left, from_right = [rows], [rows]
    for step in (1, 2, 3):
        got_r, got_l = yield (
            (from_left[-1], dict(by_local=1, wrap=False, first=step - 1)),
            (from_right[-1], dict(by_local=-1, wrap=False, last=4 - step)),
        )
        from_left.append(got_r)
        from_right.append(got_l)
    slots = [rows]
    for m in (1, 2, 3):
        slots.append(jnp.where(local + m < 4, from_right[m], from_left[4 - m]))
    yield jnp.stack(slots)


def send(pieces):
    return [move(value, **how) for value, how in pieces]


def operands(pieces):
    return [value for value, _ in pieces]


def returns(done, by_pp):
    pieces = []
    for m in (2, 1, 3, 0):
        pieces.append((done[m, 0], dict(by_pp=by_pp, by_local=m)))
        pieces.append((done[m, 1], dict(by_pp=by_pp, by_node=1, by_local=m)))
    return pieces


def at_home(got):
    got = join(*got)
    rows = [None] * 4
    for i, m in enumerate((2, 1, 3, 0)):
        rows[m] = jnp.concatenate([got[2 * i], got[2 * i + 1]], axis=0)
    return rows


def later(pieces, *others):
    values = after(operands(pieces), *others)
    return [(value, how) for value, (_, how) in zip(values, pieces)]


def unsort(blocks, placer, local):
    column = blocks[0].shape[1]
    full = jnp.zeros((placer.shape[1], 4 * column), F32)
    for m in range(4):
        moe = lax.dot_general(
            placer, blocks[m], (((0,), (0,)), ((), ())), preferred_element_type=F32
        )
        full = lax.dynamic_update_slice_in_dim(full, moe, ((local - m) % 4) * column, axis=1)
    return full


def body_pair(
    act_fwd, routes_fwd, weight_fwd, grad_bwd, routes_bwd, weight_bwd, saved_bwd, w_gate_up, w_down
):
    node = lax.axis_index("node")
    local = lax.axis_index("local")
    tokens_here = act_fwd.shape[1]
    capacity = 5 * tokens_here // 8
    w_gu = w_gate_up[0, 0]
    w_dn = w_down[0, 0]
    hidden_units = w_dn.shape[0]
    shape = (4, 2, capacity)

    act, grad = act_fwd[0], grad_bwd[0]
    route_a, route_b = routes_fwd[0, :, 0], routes_bwd[0, :, 0]
    sort_b, sort_a = sorter(route_b), sorter(route_a)

    dy = (weight_bwd[0][:, None] * grad.astype(F32)).astype(BF16)
    cut_b = cut(dy, sort_b, local)
    cut_a = cut(act, sort_a, local)
    got_b = [move(cut_b[m], by_local=-m) for m in (2, 1, 3)]
    grad_next = move(grad, by_pp=-1)
    route_b_next = move(route_b, by_pp=-1)
    saved = jnp.dot(sort_b, saved_bwd[0], preferred_element_type=F32).astype(BF16)
    saved_own, saved_other = windows(saved, node, capacity)
    saved_got = move(saved_other, by_node=1)
    got_a2 = move(cut_a[2], by_local=-2)
    *got_b, grad_next, route_b_next, saved_got = join(*got_b, grad_next, route_b_next, saved_got)
    cut_a1, cut_a3 = after([cut_a[1], cut_a[3]], *got_b)
    got_a = [got_a2, move(cut_a1, by_local=-1), move(cut_a3, by_local=-3)]
    act_next = move(act, by_pp=1)
    small_next = move(jnp.stack([route_a.astype(F32), weight_fwd[0]]), by_pp=1)

    def to_expert(blocks):
        own, other = windows(jnp.stack(blocks), node, capacity)
        return own, other

    def expert_rows(own, got):
        rows = jnp.stack([own, got], axis=1)
        return rows.reshape(-1, rows.shape[-1])

    own_b, other_b = to_expert([cut_b[0], got_b[1], got_b[0], got_b[2]])
    got_bx = move(other_b, by_node=1)
    part_b = dot_t(expert_rows(own_b, got_bx), w_dn).reshape(shape + (hidden_units,))
    chain_b = sums(part_b)
    pieces_b = next(chain_b)
    back_b = send(pieces_b)

    *got_a, act_next, small_next = join(*got_a, act_next, small_next)
    own_a, other_a = to_expert([cut_a[0], got_a[1], got_a[0], got_a[2]])
    (got_ax,) = after([move(other_a, by_node=1)], *operands(pieces_b))
    back_b = after(back_b, other_a)
    pieces_b = chain_b.send(back_b)
    back_b = send(pieces_b)
    (got_ax,) = after([got_ax], *operands(pieces_b))
    part_a = jnp.dot(expert_rows(own_a, got_ax), w_gu, preferred_element_type=F32)
    chain_a = sums(part_a.reshape(shape + (2 * hidden_units,)))
    pieces_a = next(chain_a)
    back_a = send(pieces_a)
    back_b = after(back_b, *operands(pieces_a))
    pieces_b = chain_b.send(back_b)
    back_b = send(pieces_b)
    dh = chain_b.send(back_b)

    saved_rows = jnp.stack([saved_own, saved_got])
    g = saved_rows[..., :hidden_units].astype(F32)
    u = saved_rows[..., hidden_units:].astype(F32)
    q = 1.0 / (1.0 + jnp.exp(-g))
    grad_gu = jnp.concatenate([dh * u * q * (1.0 + g * (1.0 - q)), dh * g * q], axis=-1).astype(
        BF16
    )
    chain_b = gathers(grad_gu, local)
    pieces_b = next(chain_b)
    back_b = send(pieces_b)
    for _ in (2, 3):
        back_a = after(back_a, *operands(pieces_b))
        pieces_a = chain_a.send(back_a)
        back_a = send(pieces_a)
        back_b = after(back_b, *operands(pieces_a))
        pieces_b = chain_b.send(back_b)
        back_b = send(pieces_b)
    back_a = after(back_a, *operands(pieces_b))
    preact = chain_a.send(back_a)
    hidden = (jax.nn.silu(preact[..., :hidden_units]) * preact[..., hidden_units:]).astype(BF16)
    chain_a = gathers(hidden, local)
    pieces_a = next(chain_a)
    back_a = send(pieces_a)
    back_b = after(back_b, *operands(pieces_a))
    all_gu = chain_b.send(back_b)
    done_b = dot_t(all_gu.reshape(-1, 2 * hidden_units), w_gu).astype(BF16)
    done_b = done_b.reshape(shape + (done_b.shape[-1],))
    out_b = returns(done_b, -1)
    home_b = send(out_b[:3])
    for group in (out_b[3:6], out_b[6:]):
        pieces_a = chain_a.send(after(back_a, done_b))
        back_a = send(pieces_a)
        home_b += send(later(group, *operands(pieces_a)))
    all_hidden = chain_a.send(back_a)
    done_a = jnp.dot(
        all_hidden.reshape(-1, hidden_units), w_dn, preferred_element_type=F32
    ).astype(BF16)
    done_a = done_a.reshape(shape + (done_a.shape[-1],))

    home_a = send(returns(done_a, 1))

    moe_b = unsort(at_home(home_b), window_placer(route_b_next, node, capacity), local)
    prev_grad = (grad_next.astype(F32) + moe_b).astype(BF16)
    route_a_next = small_next[0].astype(jnp.int32)
    moe_a = unsort(at_home(home_a), window_placer(route_a_next, node, capacity), local)
    next_input = (act_next.astype(F32) + small_next[1][:, None] * moe_a).astype(BF16)
    return next_input[None], prev_grad[None]


def from_behind(value, axis, by):
    length = lax.axis_size(axis)
    return lax.ppermute(value, axis, [(i, (i + by) % length) for i in range(length)])


def place_matrix(route, expert_count, capacity):
    onehot = (route[:, None] == jnp.arange(expert_count, dtype=jnp.int32)[None, :]).astype(
        jnp.int32
    )
    before = jnp.cumsum(onehot, axis=0) - onehot
    slot_index = jnp.sum(before * onehot, axis=1)
    target = route * capacity + slot_index
    positions = jnp.arange(expert_count * capacity, dtype=jnp.int32)
    return (positions[:, None] == target[None, :]).astype(jnp.bfloat16)


def pack_rows(placer, values, expert_count, capacity):
    packed = jnp.dot(placer, values, preferred_element_type=jnp.float32).astype(jnp.bfloat16)
    return packed.reshape(expert_count, capacity, values.shape[1])


def unpack_rows(placer, packed):
    flattened = packed.reshape(-1, packed.shape[-1])
    result = lax.dot_general(
        placer, flattened, (((0,), (0,)), ((), ())), preferred_element_type=jnp.float32
    )
    return result.astype(jnp.bfloat16)


def flat_outgoing(packed, local_count):
    expert_count, capacity, feature_count = packed.shape
    column = feature_count // local_count
    outgoing = packed.reshape(expert_count, capacity, local_count, column).transpose(0, 2, 1, 3)
    return outgoing.reshape(expert_count * local_count, capacity, column)


def flat_layout(received, expert_count, local_count):
    capacity = received.shape[1]
    column = received.shape[2]
    rows_in = received.reshape(expert_count, local_count, capacity, column).transpose(1, 0, 2, 3)
    return rows_in.reshape(-1, column)


def send_rows(packs, local_count):
    expert_count = packs[0].shape[0]
    outgoing = tuple((flat_outgoing(packed, local_count) for packed in packs))
    received = (
        lax.all_to_all(outgoing[0], ("node", "local"), split_axis=0, concat_axis=0, tiled=True),
        lax.all_to_all(outgoing[1], ("node", "local"), split_axis=0, concat_axis=0, tiled=True),
    )
    return tuple((flat_layout(item, expert_count, local_count) for item in received))


def return_rows(finished_pair, expert_count, capacity, local_count):
    column = finished_pair[0].shape[1]
    blocks = tuple(
        (item.reshape(local_count, expert_count, capacity, column) for item in finished_pair)
    )
    outgoing = tuple(
        (
            item.transpose(1, 0, 2, 3).reshape(expert_count * local_count, capacity, column)
            for item in blocks
        )
    )
    received = (
        lax.all_to_all(outgoing[0], ("node", "local"), split_axis=0, concat_axis=0, tiled=True),
        lax.all_to_all(outgoing[1], ("node", "local"), split_axis=0, concat_axis=0, tiled=True),
    )
    results = []
    for item in received:
        arranged = item.reshape(expert_count, local_count, capacity, column).transpose(0, 2, 1, 3)
        results.append(arranged.reshape(expert_count, capacity, local_count * column))
    return tuple(results)


def body(
    act_fwd, routes_fwd, weight_fwd, grad_bwd, routes_bwd, weight_bwd, saved_bwd, w_gate_up, w_down
):
    node_count = lax.axis_size("node")
    local_count = lax.axis_size("local")
    tokens_here = act_fwd.shape[1]
    capacity = 5 * tokens_here // (4 * node_count)
    rows_each = node_count * capacity
    w_gu = w_gate_up[0, 0]
    w_dn = w_down[0, 0]
    hidden_units = w_dn.shape[0]
    tokens_a = act_fwd[0]
    placer_a = place_matrix(routes_fwd[0, :, 0], node_count, capacity)
    cotangent = grad_bwd[0]
    placer_b = place_matrix(routes_bwd[0, :, 0], node_count, capacity)
    scaled = (weight_bwd[0][:, None] * cotangent.astype(jnp.float32)).astype(jnp.bfloat16)
    packed_a = pack_rows(placer_a, tokens_a, node_count, capacity)
    packed_b = pack_rows(placer_b, scaled, node_count, capacity)
    rows_a, rows_b = send_rows((packed_a, packed_b), local_count)
    saved_packed = pack_rows(placer_b, saved_bwd[0], node_count, capacity)
    saved_rows = lax.all_to_all(
        saved_packed, "node", split_axis=0, concat_axis=0, tiled=True
    ).reshape(rows_each, -1)
    row_block = rows_a
    preact = lax.psum_scatter(
        jnp.dot(row_block, w_gu, preferred_element_type=jnp.float32).astype(jnp.bfloat16),
        "local",
        scatter_dimension=0,
        tiled=True,
    ).astype(jnp.float32)
    row_block = rows_b
    grad_hidden = lax.psum_scatter(
        lax.dot_general(
            row_block, w_dn, (((1,), (1,)), ((), ())), preferred_element_type=jnp.float32
        ).astype(jnp.bfloat16),
        "local",
        scatter_dimension=0,
        tiled=True,
    ).astype(jnp.float32)
    hidden = (jax.nn.silu(preact[:, :hidden_units]) * preact[:, hidden_units:]).astype(jnp.bfloat16)
    done_a = jnp.dot(
        lax.all_gather(hidden, "local", axis=0, tiled=True),
        w_dn,
        preferred_element_type=jnp.float32,
    ).astype(jnp.bfloat16)
    gate_pre = saved_rows[:, :hidden_units].astype(jnp.float32)
    up_pre = saved_rows[:, hidden_units:].astype(jnp.float32)
    sigmoid_g = 1.0 / (1.0 + jnp.exp(-gate_pre))
    grad_gate = grad_hidden * up_pre * sigmoid_g * (1.0 + gate_pre * (1.0 - sigmoid_g))
    grad_up = grad_hidden * gate_pre * sigmoid_g
    grad_gu = jnp.concatenate([grad_gate, grad_up], axis=1).astype(jnp.bfloat16)
    product = lax.dot_general(
        lax.all_gather(grad_gu, "local", axis=0, tiled=True),
        w_gu,
        (((1,), (1,)), ((), ())),
        preferred_element_type=jnp.float32,
    )
    done_b = product.astype(jnp.bfloat16)
    back_a, back_b = return_rows((done_a, done_b), node_count, capacity, local_count)
    moe_a = unpack_rows(placer_a, back_a)
    result_a = tokens_a.astype(jnp.float32) + weight_fwd[0][:, None] * moe_a.astype(jnp.float32)
    result_a = result_a.astype(jnp.bfloat16)
    moe_b = unpack_rows(placer_b, back_b)
    result_b = (cotangent.astype(jnp.float32) + moe_b.astype(jnp.float32)).astype(jnp.bfloat16)
    next_input = from_behind(result_a[None], "pp", 1)
    prev_grad = from_behind(result_b[None], "pp", -1)
    return (next_input, prev_grad)


def solution(mesh):
    in_specs = (
        P("pp", ("node", "local"), None),
        P("pp", ("node", "local"), None),
        P("pp", ("node", "local")),
        P("pp", ("node", "local"), None),
        P("pp", ("node", "local"), None),
        P("pp", ("node", "local")),
        P("pp", ("node", "local"), None),
        P("pp", "node", "local", None),
        P("pp", "node", None, "local"),
    )
    out_specs = (P("pp", ("node", "local"), None), P("pp", ("node", "local"), None))
    paired = mesh.shape["node"] == 2 and mesh.shape["local"] == 4
    plan = body_pair if paired else body
    return jax.shard_map(plan, mesh=mesh, in_specs=in_specs, out_specs=out_specs, check_vma=False)
```

```python
import jax
import jax.numpy as jnp
from jax import lax
from jax.sharding import PartitionSpec as P

F32 = jnp.float32
BF16 = jnp.bfloat16
AXES = ("pp", "node", "local")


def move(value, by_pp=0, by_node=0, by_local=0, wrap=True, first=0, last=None):
    pps, nodes, locs = (lax.axis_size(a) for a in AXES)
    last = locs - 1 if last is None else last
    pairs = []
    for s in range(pps):
        for n in range(nodes):
            for l in range(locs):
                to = l + by_local
                if not wrap and not (first <= l <= last and 0 <= to < locs):
                    continue
                source = (s * nodes + n) * locs + l
                target = (((s + by_pp) % pps) * nodes + (n ^ by_node)) * locs + to % locs
                pairs.append((source, target))
    return lax.ppermute(value, AXES, pairs)


def sorted_places(route):
    ones = route.astype(F32)
    count = route.shape[0]
    earlier = (jnp.arange(count)[None, :] < jnp.arange(count)[:, None]).astype(F32)
    ones_before = jnp.dot(earlier, ones[:, None], preferred_element_type=F32)[:, 0]
    zeros = count - jnp.sum(ones)
    index = jnp.arange(count, dtype=F32)
    place = jnp.where(route == 0, index - ones_before, zeros + ones_before)
    return place.astype(jnp.int32)


def sorter(route):
    place = sorted_places(route)
    rows = jnp.arange(route.shape[0], dtype=jnp.int32)
    return (rows[:, None] == place[None, :]).astype(BF16)


def window_placer(route, first, capacity):
    place = sorted_places(route)
    start = route.shape[0] - capacity
    in_window = place - jnp.where(route == 1, start, 0)
    row = jnp.where(route == first, in_window, in_window + capacity)
    rows = jnp.arange(2 * capacity, dtype=jnp.int32)
    return (rows[:, None] == row[None, :]).astype(BF16)


def dot_t(left, right):
    return lax.dot_general(left, right, (((1,), (1,)), ((), ())), preferred_element_type=F32)


def windows(blocks, node, capacity):
    tokens = blocks.shape[-2]
    start = tokens - capacity
    low = lax.slice_in_dim(blocks, 0, capacity, axis=-2 + blocks.ndim)
    high = lax.slice_in_dim(blocks, start, tokens, axis=-2 + blocks.ndim)
    own = jnp.where(node == 0, low, high)
    other = jnp.where(node == 0, high, low)
    return own, other


def join(*values):
    return lax.optimization_barrier(values)


def after(values, *others):
    return list(join(*values, *others)[: len(values)])


def cut(tokens, placer, local):
    column = tokens.shape[1] // 4
    blocks = []
    for m in range(4):
        block = lax.dynamic_slice_in_dim(tokens, ((local - m) % 4) * column, column, axis=1)
        blocks.append(jnp.dot(placer, block, preferred_element_type=F32).astype(BF16))
    return blocks


def sums(partial):
    right, left = partial(3), partial(1)
    for step in (1, 2, 3):
        right, left = right.astype(BF16), left.astype(BF16)
        got_r, got_l = yield (
            (right, dict(by_local=1, wrap=False, last=step - 1)),
            (left, dict(by_local=-1, wrap=False, first=4 - step)),
        )
        right = partial(3 - step) + got_r.astype(F32)
        if step < 3:
            left = partial(step + 1) + got_l.astype(F32)
    yield right + got_l.astype(F32)


def gathers(rows, local):
    from_left, from_right = [rows], [rows]
    for step in (1, 2, 3):
        got_r, got_l = yield (
            (from_left[-1], dict(by_local=1, wrap=False, first=step - 1)),
            (from_right[-1], dict(by_local=-1, wrap=False, last=4 - step)),
        )
        from_left.append(got_r)
        from_right.append(got_l)
    slots = [rows]
    for m in (1, 2, 3):
        slots.append(jnp.where(local + m < 4, from_right[m], from_left[4 - m]))
    yield jnp.stack(slots)


def send(pieces):
    return [move(value, **how) for value, how in pieces]


def operands(pieces):
    return [value for value, _ in pieces]


def returns(done, by_pp):
    pieces = []
    for m in (2, 1, 3, 0):
        pieces.append((done(m, 0), dict(by_pp=by_pp, by_local=m)))
        pieces.append((done(m, 1), dict(by_pp=by_pp, by_node=1, by_local=m)))
    return pieces


def at_home(got):
    got = join(*got)
    rows = [None] * 4
    for i, m in enumerate((2, 1, 3, 0)):
        rows[m] = jnp.concatenate([got[2 * i], got[2 * i + 1]], axis=0)
    return rows


def later(pieces, *others):
    values = after(operands(pieces), *others)
    return [(value, how) for value, (_, how) in zip(values, pieces)]


def unsort(blocks, placer, local):
    column = blocks[0].shape[1]
    full = jnp.zeros((placer.shape[1], 4 * column), F32)
    for m in range(4):
        moe = lax.dot_general(
            placer, blocks[m], (((0,), (0,)), ((), ())), preferred_element_type=F32
        )
        full = lax.dynamic_update_slice_in_dim(full, moe, ((local - m) % 4) * column, axis=1)
    return full


def body_pair(
    act_fwd, routes_fwd, weight_fwd, grad_bwd, routes_bwd, weight_bwd, saved_bwd, w_gate_up, w_down
):
    node = lax.axis_index("node")
    local = lax.axis_index("local")
    tokens_here = act_fwd.shape[1]
    capacity = 5 * tokens_here // 8
    w_gu = w_gate_up[0, 0]
    w_dn = w_down[0, 0]
    hidden_units = w_dn.shape[0]
    shape = (4, 2, capacity)

    act, grad = act_fwd[0], grad_bwd[0]
    route_a, route_b = routes_fwd[0, :, 0], routes_bwd[0, :, 0]
    sort_b = sorter(route_b)

    dy = (weight_bwd[0][:, None] * grad.astype(F32)).astype(BF16)
    cut_b = cut(dy, sort_b, local)
    got_b = [move(cut_b[m], by_local=-m) for m in (2, 1, 3)]
    placer_a = window_placer(route_a, 0, capacity)
    column = act.shape[1] // 4
    packed_a = jnp.stack(
        [
            jnp.dot(
                placer_a, act[:, j * column : (j + 1) * column], preferred_element_type=F32
            ).astype(BF16).reshape(2, capacity, column)
            for j in range(4)
        ],
        axis=1,
    )
    (packed_a,) = after([packed_a], cut_b[3])
    got_a = lax.all_to_all(
        packed_a.reshape(8, capacity, column), ("node", "local"), split_axis=0, concat_axis=0, tiled=True
    )
    saved = jnp.dot(sort_b, saved_bwd[0], preferred_element_type=F32).astype(BF16)
    saved_own, saved_other = windows(saved, node, capacity)
    (saved_other,) = after([saved_other], packed_a)
    saved_got = move(saved_other, by_node=1)
    *got_b, saved_got = join(*got_b, saved_got)

    own_b, other_b = windows(
        jnp.stack([cut_b[0], got_b[1], got_b[0], got_b[2]]), node, capacity
    )
    got_bx = move(other_b, by_node=1)
    act_wait, small = after(
        [act, jnp.stack([route_a.astype(F32), weight_fwd[0]])], other_b
    )
    act_next = move(act_wait, by_pp=1)
    small_next = move(small, by_pp=1)
    rows_b = jnp.stack([own_b, got_bx], axis=1).reshape(-1, column)
    part_b = dot_t(rows_b, w_dn).reshape(shape + (hidden_units,))
    chain_b = sums(lambda slot: part_b[slot])
    pieces_b = next(chain_b)
    back_b = send(pieces_b)

    def homes(array, axis):
        return lambda slot: lax.dynamic_index_in_dim(
            array, (local + slot) % 4, axis=axis, keepdims=False
        )

    got_a, act_next, small_next = after([got_a, act_next, small_next], *operands(pieces_b))
    grad_wait, route_wait = after([grad, route_b], act_next)
    grad_next = move(grad_wait, by_pp=-1)
    route_b_next = move(route_wait, by_pp=-1)
    part_a = jnp.dot(got_a.reshape(-1, column), w_gu, preferred_element_type=F32)
    chain_a = sums(homes(part_a.reshape(2, 4, capacity, 2 * hidden_units), 1))
    pieces_a = next(chain_a)
    back_a = send(pieces_a)
    back_b = after(back_b, *operands(pieces_a))
    for _ in (2, 3):
        pieces_b = chain_b.send(back_b)
        back_b = send(pieces_b)
    *back_b, grad_next, route_b_next = join(*back_b, grad_next, route_b_next)
    dh = chain_b.send(back_b)

    saved_rows = jnp.stack([saved_own, saved_got])
    g = saved_rows[..., :hidden_units].astype(F32)
    u = saved_rows[..., hidden_units:].astype(F32)
    q = 1.0 / (1.0 + jnp.exp(-g))
    grad_gu = jnp.concatenate([dh * u * q * (1.0 + g * (1.0 - q)), dh * g * q], axis=-1).astype(
        BF16
    )
    chain_b = gathers(grad_gu, local)
    pieces_b = next(chain_b)
    back_b = send(pieces_b)
    for _ in (2, 3):
        back_a = after(back_a, *operands(pieces_b))
        pieces_a = chain_a.send(back_a)
        back_a = send(pieces_a)
        back_b = after(back_b, *operands(pieces_a))
        pieces_b = chain_b.send(back_b)
        back_b = send(pieces_b)
    back_a = after(back_a, *operands(pieces_b))
    preact = chain_a.send(back_a)
    hidden = (jax.nn.silu(preact[..., :hidden_units]) * preact[..., hidden_units:]).astype(BF16)
    all_hidden = [hidden] + [move(hidden, by_local=-m) for m in (1, 2, 3)]
    back_b = after(back_b, hidden)
    all_gu = chain_b.send(back_b)
    done_b = dot_t(all_gu.reshape(-1, 2 * hidden_units), w_gu).astype(BF16)
    done_b = done_b.reshape(shape + (column,))
    out_b = returns(lambda slot, other: done_b[slot, other], -1)
    all_hidden = after(all_hidden, done_b)
    done_a = jnp.dot(
        jnp.stack(all_hidden).reshape(-1, hidden_units), w_dn, preferred_element_type=F32
    ).astype(BF16)
    done_a = done_a.reshape(4, 2, capacity, column)
    home_b = send(out_b)
    home_a = send(returns(
            lambda slot, other: lax.dynamic_index_in_dim(done_a[slot], node ^ other, keepdims=False), 1
        ))

    moe_b = unsort(at_home(home_b), window_placer(route_b_next, node, capacity), local)
    prev_grad = (grad_next.astype(F32) + moe_b).astype(BF16)
    route_a_next = small_next[0].astype(jnp.int32)
    moe_a = unsort(at_home(home_a), window_placer(route_a_next, node, capacity), local)
    next_input = (act_next.astype(F32) + small_next[1][:, None] * moe_a).astype(BF16)
    return next_input[None], prev_grad[None]


def from_behind(value, axis, by):
    length = lax.axis_size(axis)
    return lax.ppermute(value, axis, [(i, (i + by) % length) for i in range(length)])


def place_matrix(route, expert_count, capacity):
    onehot = (route[:, None] == jnp.arange(expert_count, dtype=jnp.int32)[None, :]).astype(
        jnp.int32
    )
    before = jnp.cumsum(onehot, axis=0) - onehot
    slot_index = jnp.sum(before * onehot, axis=1)
    target = route * capacity + slot_index
    positions = jnp.arange(expert_count * capacity, dtype=jnp.int32)
    return (positions[:, None] == target[None, :]).astype(jnp.bfloat16)


def pack_rows(placer, values, expert_count, capacity):
    packed = jnp.dot(placer, values, preferred_element_type=jnp.float32).astype(jnp.bfloat16)
    return packed.reshape(expert_count, capacity, values.shape[1])


def unpack_rows(placer, packed):
    flattened = packed.reshape(-1, packed.shape[-1])
    result = lax.dot_general(
        placer, flattened, (((0,), (0,)), ((), ())), preferred_element_type=jnp.float32
    )
    return result.astype(jnp.bfloat16)


def flat_outgoing(packed, local_count):
    expert_count, capacity, feature_count = packed.shape
    column = feature_count // local_count
    outgoing = packed.reshape(expert_count, capacity, local_count, column).transpose(0, 2, 1, 3)
    return outgoing.reshape(expert_count * local_count, capacity, column)


def flat_layout(received, expert_count, local_count):
    capacity = received.shape[1]
    column = received.shape[2]
    rows_in = received.reshape(expert_count, local_count, capacity, column).transpose(1, 0, 2, 3)
    return rows_in.reshape(-1, column)


def send_rows(packs, local_count):
    expert_count = packs[0].shape[0]
    outgoing = tuple((flat_outgoing(packed, local_count) for packed in packs))
    received = (
        lax.all_to_all(outgoing[0], ("node", "local"), split_axis=0, concat_axis=0, tiled=True),
        lax.all_to_all(outgoing[1], ("node", "local"), split_axis=0, concat_axis=0, tiled=True),
    )
    return tuple((flat_layout(item, expert_count, local_count) for item in received))


def return_rows(finished_pair, expert_count, capacity, local_count):
    column = finished_pair[0].shape[1]
    blocks = tuple(
        (item.reshape(local_count, expert_count, capacity, column) for item in finished_pair)
    )
    outgoing = tuple(
        (
            item.transpose(1, 0, 2, 3).reshape(expert_count * local_count, capacity, column)
            for item in blocks
        )
    )
    received = (
        lax.all_to_all(outgoing[0], ("node", "local"), split_axis=0, concat_axis=0, tiled=True),
        lax.all_to_all(outgoing[1], ("node", "local"), split_axis=0, concat_axis=0, tiled=True),
    )
    results = []
    for item in received:
        arranged = item.reshape(expert_count, local_count, capacity, column).transpose(0, 2, 1, 3)
        results.append(arranged.reshape(expert_count, capacity, local_count * column))
    return tuple(results)


def body(
    act_fwd, routes_fwd, weight_fwd, grad_bwd, routes_bwd, weight_bwd, saved_bwd, w_gate_up, w_down
):
    node_count = lax.axis_size("node")
    local_count = lax.axis_size("local")
    tokens_here = act_fwd.shape[1]
    capacity = 5 * tokens_here // (4 * node_count)
    rows_each = node_count * capacity
    w_gu = w_gate_up[0, 0]
    w_dn = w_down[0, 0]
    hidden_units = w_dn.shape[0]
    tokens_a = act_fwd[0]
    placer_a = place_matrix(routes_fwd[0, :, 0], node_count, capacity)
    cotangent = grad_bwd[0]
    placer_b = place_matrix(routes_bwd[0, :, 0], node_count, capacity)
    scaled = (weight_bwd[0][:, None] * cotangent.astype(jnp.float32)).astype(jnp.bfloat16)
    packed_a = pack_rows(placer_a, tokens_a, node_count, capacity)
    packed_b = pack_rows(placer_b, scaled, node_count, capacity)
    rows_a, rows_b = send_rows((packed_a, packed_b), local_count)
    saved_packed = pack_rows(placer_b, saved_bwd[0], node_count, capacity)
    saved_rows = lax.all_to_all(
        saved_packed, "node", split_axis=0, concat_axis=0, tiled=True
    ).reshape(rows_each, -1)
    row_block = rows_a
    preact = lax.psum_scatter(
        jnp.dot(row_block, w_gu, preferred_element_type=jnp.float32).astype(jnp.bfloat16),
        "local",
        scatter_dimension=0,
        tiled=True,
    ).astype(jnp.float32)
    row_block = rows_b
    grad_hidden = lax.psum_scatter(
        lax.dot_general(
            row_block, w_dn, (((1,), (1,)), ((), ())), preferred_element_type=jnp.float32
        ).astype(jnp.bfloat16),
        "local",
        scatter_dimension=0,
        tiled=True,
    ).astype(jnp.float32)
    hidden = (jax.nn.silu(preact[:, :hidden_units]) * preact[:, hidden_units:]).astype(jnp.bfloat16)
    done_a = jnp.dot(
        lax.all_gather(hidden, "local", axis=0, tiled=True),
        w_dn,
        preferred_element_type=jnp.float32,
    ).astype(jnp.bfloat16)
    gate_pre = saved_rows[:, :hidden_units].astype(jnp.float32)
    up_pre = saved_rows[:, hidden_units:].astype(jnp.float32)
    sigmoid_g = 1.0 / (1.0 + jnp.exp(-gate_pre))
    grad_gate = grad_hidden * up_pre * sigmoid_g * (1.0 + gate_pre * (1.0 - sigmoid_g))
    grad_up = grad_hidden * gate_pre * sigmoid_g
    grad_gu = jnp.concatenate([grad_gate, grad_up], axis=1).astype(jnp.bfloat16)
    product = lax.dot_general(
        lax.all_gather(grad_gu, "local", axis=0, tiled=True),
        w_gu,
        (((1,), (1,)), ((), ())),
        preferred_element_type=jnp.float32,
    )
    done_b = product.astype(jnp.bfloat16)
    back_a, back_b = return_rows((done_a, done_b), node_count, capacity, local_count)
    moe_a = unpack_rows(placer_a, back_a)
    result_a = tokens_a.astype(jnp.float32) + weight_fwd[0][:, None] * moe_a.astype(jnp.float32)
    result_a = result_a.astype(jnp.bfloat16)
    moe_b = unpack_rows(placer_b, back_b)
    result_b = (cotangent.astype(jnp.float32) + moe_b.astype(jnp.float32)).astype(jnp.bfloat16)
    next_input = from_behind(result_a[None], "pp", 1)
    prev_grad = from_behind(result_b[None], "pp", -1)
    return (next_input, prev_grad)


def solution(mesh):
    in_specs = (
        P("pp", ("node", "local"), None),
        P("pp", ("node", "local"), None),
        P("pp", ("node", "local")),
        P("pp", ("node", "local"), None),
        P("pp", ("node", "local"), None),
        P("pp", ("node", "local")),
        P("pp", ("node", "local"), None),
        P("pp", "node", "local", None),
        P("pp", "node", None, "local"),
    )
    out_specs = (P("pp", ("node", "local"), None), P("pp", ("node", "local"), None))
    paired = mesh.shape["node"] == 2 and mesh.shape["local"] == 4
    plan = body_pair if paired else body
    return jax.shard_map(plan, mesh=mesh, in_specs=in_specs, out_specs=out_specs, check_vma=False)
```

```python
import jax
import jax.numpy as jnp
from jax import lax
from jax.sharding import PartitionSpec as P

F32 = jnp.float32
BF16 = jnp.bfloat16
AXES = ("pp", "node", "local")


def move(value, by_pp=0, by_node=0, by_local=0, wrap=True, first=0, last=None):
    pps, nodes, locs = (lax.axis_size(a) for a in AXES)
    last = locs - 1 if last is None else last
    pairs = []
    for s in range(pps):
        for n in range(nodes):
            for l in range(locs):
                to = l + by_local
                if not wrap and not (first <= l <= last and 0 <= to < locs):
                    continue
                source = (s * nodes + n) * locs + l
                target = (((s + by_pp) % pps) * nodes + (n ^ by_node)) * locs + to % locs
                pairs.append((source, target))
    return lax.ppermute(value, AXES, pairs)


def sorted_places(route):
    ones = route.astype(F32)
    count = route.shape[0]
    earlier = (jnp.arange(count)[None, :] < jnp.arange(count)[:, None]).astype(F32)
    ones_before = jnp.dot(earlier, ones[:, None], preferred_element_type=F32)[:, 0]
    zeros = count - jnp.sum(ones)
    index = jnp.arange(count, dtype=F32)
    place = jnp.where(route == 0, index - ones_before, zeros + ones_before)
    return place.astype(jnp.int32)


def sorter(route):
    place = sorted_places(route)
    rows = jnp.arange(route.shape[0], dtype=jnp.int32)
    return (rows[:, None] == place[None, :]).astype(BF16)


def dot_t(left, right):
    return lax.dot_general(left, right, (((1,), (1,)), ((), ())), preferred_element_type=F32)


def windows(blocks, node, capacity):
    tokens = blocks.shape[-2]
    start = tokens - capacity
    low = lax.slice_in_dim(blocks, 0, capacity, axis=-2 + blocks.ndim)
    high = lax.slice_in_dim(blocks, start, tokens, axis=-2 + blocks.ndim)
    own = jnp.where(node == 0, low, high)
    other = jnp.where(node == 0, high, low)
    return own, other


def join(*values):
    return lax.optimization_barrier(values)


def after(values, *others):
    return list(join(*values, *others)[: len(values)])


def cut(tokens, placer, local):
    column = tokens.shape[1] // 4
    blocks = []
    for m in range(4):
        block = lax.dynamic_slice_in_dim(tokens, ((local - m) % 4) * column, column, axis=1)
        blocks.append(jnp.dot(placer, block, preferred_element_type=F32).astype(BF16))
    return blocks


def sums(partial):
    right, left = partial[3], partial[1]
    for step in (1, 2, 3):
        right, left = right.astype(BF16), left.astype(BF16)
        got_r, got_l = yield (
            (right, dict(by_local=1, wrap=False, last=step - 1)),
            (left, dict(by_local=-1, wrap=False, first=4 - step)),
        )
        right = partial[3 - step] + got_r.astype(F32)
        if step < 3:
            left = partial[step + 1] + got_l.astype(F32)
    yield right + got_l.astype(F32)


def gathers(rows, local):
    from_left, from_right = [rows], [rows]
    for step in (1, 2, 3):
        got_r, got_l = yield (
            (from_left[-1], dict(by_local=1, wrap=False, first=step - 1)),
            (from_right[-1], dict(by_local=-1, wrap=False, last=4 - step)),
        )
        from_left.append(got_r)
        from_right.append(got_l)
    slots = [rows]
    for m in (1, 2, 3):
        slots.append(jnp.where(local + m < 4, from_right[m], from_left[4 - m]))
    yield jnp.stack(slots)


def send(pieces):
    return [move(value, **how) for value, how in pieces]


def operands(pieces):
    return [value for value, _ in pieces]


def later(pieces, *others):
    values = after(operands(pieces), *others)
    return [(value, how) for value, (_, how) in zip(values, pieces)]


def valid(zeros, node, tokens, capacity):
    row = jnp.arange(capacity, dtype=F32)[None, :]
    return jnp.where(node == 0, row < zeros[:, None], row + (tokens - capacity) >= zeros[:, None])


def merge(own, other, node, tokens):
    slots, capacity, column = own.shape
    low = jnp.where(node == 0, own, other)
    high = jnp.where(node == 0, other, own)
    rest = jnp.zeros((slots, tokens - capacity, column), own.dtype)
    return jnp.concatenate([low, rest], axis=1) + jnp.concatenate([rest, high], axis=1)


def homeward(merged, by_pp):
    return [(merged[m], dict(by_pp=by_pp, by_local=m)) for m in (2, 1, 3, 0)]


def unsort(got, placer, local):
    blocks = dict(zip((2, 1, 3, 0), join(*got)))
    column = blocks[0].shape[1]
    full = jnp.zeros((placer.shape[1], 4 * column), F32)
    for m in range(4):
        moe = lax.dot_general(
            placer, blocks[m], (((0,), (0,)), ((), ())), preferred_element_type=F32
        )
        full = lax.dynamic_update_slice_in_dim(full, moe, ((local - m) % 4) * column, axis=1)
    return full


def body_pair(
    act_fwd, routes_fwd, weight_fwd, grad_bwd, routes_bwd, weight_bwd, saved_bwd, w_gate_up, w_down
):
    node = lax.axis_index("node")
    local = lax.axis_index("local")
    tokens_here = act_fwd.shape[1]
    capacity = 5 * tokens_here // 8
    w_gu = w_gate_up[0, 0]
    w_dn = w_down[0, 0]
    hidden_units = w_dn.shape[0]
    shape = (4, 2, capacity)

    act, grad = act_fwd[0], grad_bwd[0]
    route_a, route_b = routes_fwd[0, :, 0], routes_bwd[0, :, 0]
    sort_b, sort_a = sorter(route_b), sorter(route_a)

    counts = jnp.stack([tokens_here - jnp.sum(route_a), tokens_here - jnp.sum(route_b)])
    counts = counts.astype(F32)

    dy = (weight_bwd[0][:, None] * grad.astype(F32)).astype(BF16)
    cut_b = cut(dy, sort_b, local)
    got_b = [move(cut_b[m], by_local=-m) for m in (2, 1, 3)]
    saved = jnp.dot(sort_b, saved_bwd[0], preferred_element_type=F32).astype(BF16)
    (saved,) = after([saved], *cut_b[1:])
    saved_own, saved_other = windows(saved, node, capacity)
    saved_got = move(saved_other, by_node=1)
    counts_got = move(after([counts], *cut_b[1:])[0], by_node=1)
    cut_a = cut(act, sort_a, local)
    *got_b, saved_got, counts_got = join(*got_b, saved_got, counts_got, *cut_a)[:5]
    zeros = jnp.stack([counts, counts_got])
    cut_a = after(cut_a, *got_b)
    got_a = [move(cut_a[m], by_local=-m) for m in (2, 1, 3)]

    def to_expert(blocks):
        return windows(jnp.stack(blocks), node, capacity)

    def expert_rows(own, got):
        rows = jnp.stack([own, got], axis=1)
        return rows.reshape(-1, rows.shape[-1])

    own_b, other_b = to_expert([cut_b[0], got_b[1], got_b[0], got_b[2]])
    got_bx = move(other_b, by_node=1)
    part_b = dot_t(expert_rows(own_b, got_bx), w_dn).reshape(shape + (hidden_units,))
    chain_b = sums(part_b)
    pieces_b = next(chain_b)
    back_b = send(pieces_b)

    got_a = after(got_a, *back_b)
    own_a, other_a = to_expert([cut_a[0], got_a[1], got_a[0], got_a[2]])
    got_ax = move(other_a, by_node=1)
    act_wait, small_wait = after([act, jnp.stack([route_a.astype(F32), weight_fwd[0]])], other_a)
    act_next = move(act_wait, by_pp=1)
    small_next = move(small_wait, by_pp=1)
    back_b = after(back_b, other_a)
    pieces_b = chain_b.send(back_b)
    back_b = send(pieces_b)
    got_ax, act_next, small_next = after([got_ax, act_next, small_next], *operands(pieces_b))
    part_a = jnp.dot(expert_rows(own_a, got_ax), w_gu, preferred_element_type=F32)
    chain_a = sums(part_a.reshape(shape + (2 * hidden_units,)))
    pieces_a = next(chain_a)
    back_a = send(pieces_a)
    back_b = after(back_b, *operands(pieces_a))
    pieces_b = chain_b.send(back_b)
    back_b = send(pieces_b)
    grad_wait, route_wait = after([grad, route_b], act_next, small_next, *operands(pieces_b))
    grad_next = move(grad_wait, by_pp=-1)
    route_b_next = move(route_wait, by_pp=-1)
    dh = chain_b.send(back_b)

    saved_rows = jnp.stack([saved_own, saved_got])
    g = saved_rows[..., :hidden_units].astype(F32)
    u = saved_rows[..., hidden_units:].astype(F32)
    q = 1.0 / (1.0 + jnp.exp(-g))
    dh = jnp.where(valid(zeros[:, 1], node, tokens_here, capacity)[..., None], dh, 0.0)
    grad_gu = jnp.concatenate([dh * u * q * (1.0 + g * (1.0 - q)), dh * g * q], axis=-1).astype(
        BF16
    )
    chain_b = gathers(grad_gu, local)
    pieces_b = next(chain_b)
    back_b = send(pieces_b)
    back_a = list(join(*back_a, grad_next, route_b_next, *operands(pieces_b)))
    grad_next, route_b_next, back_a = back_a[2], back_a[3], back_a[:2]
    for _ in (2, 3):
        back_a = after(back_a, *operands(pieces_b))
        pieces_a = chain_a.send(back_a)
        back_a = send(pieces_a)
        back_b = after(back_b, *operands(pieces_a))
        pieces_b = chain_b.send(back_b)
        back_b = send(pieces_b)
    back_a = after(back_a, *operands(pieces_b))
    preact = chain_a.send(back_a)
    preact = jnp.where(valid(zeros[:, 0], node, tokens_here, capacity)[..., None], preact, 0.0)
    hidden = (jax.nn.silu(preact[..., :hidden_units]) * preact[..., hidden_units:]).astype(BF16)
    all_hidden = [hidden] + [move(hidden, by_local=-m) for m in (1, 2, 3)]
    back_b = after(back_b, hidden)
    all_gu = chain_b.send(back_b)
    done_b = dot_t(all_gu.reshape(-1, 2 * hidden_units), w_gu).astype(BF16)
    done_b = done_b.reshape(shape + (done_b.shape[-1],))
    other_b = move(done_b[:, 1], by_node=1)
    all_hidden = after(all_hidden, done_b)
    done_a = jnp.dot(
        jnp.stack(all_hidden).reshape(-1, hidden_units), w_dn, preferred_element_type=F32
    ).astype(BF16)
    done_a = done_a.reshape(shape + (done_a.shape[-1],))
    other_a = move(done_a[:, 1], by_node=1)
    (other_b,) = after([other_b], done_a)
    merged_b = merge(done_b[:, 0], other_b, node, tokens_here)
    home_b = send(homeward(merged_b, -1))
    (other_a,) = after([other_a], merged_b)
    merged_a = merge(done_a[:, 0], other_a, node, tokens_here)
    home_a = send(homeward(merged_a, 1))
    home_b = after(home_b, merged_a)

    moe_b = unsort(home_b, sorter(route_b_next), local)
    prev_grad = (grad_next.astype(F32) + moe_b).astype(BF16)
    route_a_next = small_next[0].astype(jnp.int32)
    moe_a = unsort(home_a, sorter(route_a_next), local)
    next_input = (act_next.astype(F32) + small_next[1][:, None] * moe_a).astype(BF16)
    return next_input[None], prev_grad[None]


def from_behind(value, axis, by):
    length = lax.axis_size(axis)
    return lax.ppermute(value, axis, [(i, (i + by) % length) for i in range(length)])


def place_matrix(route, expert_count, capacity):
    onehot = (route[:, None] == jnp.arange(expert_count, dtype=jnp.int32)[None, :]).astype(
        jnp.int32
    )
    before = jnp.cumsum(onehot, axis=0) - onehot
    slot_index = jnp.sum(before * onehot, axis=1)
    target = route * capacity + slot_index
    positions = jnp.arange(expert_count * capacity, dtype=jnp.int32)
    return (positions[:, None] == target[None, :]).astype(jnp.bfloat16)


def pack_rows(placer, values, expert_count, capacity):
    packed = jnp.dot(placer, values, preferred_element_type=jnp.float32).astype(jnp.bfloat16)
    return packed.reshape(expert_count, capacity, values.shape[1])


def unpack_rows(placer, packed):
    flattened = packed.reshape(-1, packed.shape[-1])
    result = lax.dot_general(
        placer, flattened, (((0,), (0,)), ((), ())), preferred_element_type=jnp.float32
    )
    return result.astype(jnp.bfloat16)


def flat_outgoing(packed, local_count):
    expert_count, capacity, feature_count = packed.shape
    column = feature_count // local_count
    outgoing = packed.reshape(expert_count, capacity, local_count, column).transpose(0, 2, 1, 3)
    return outgoing.reshape(expert_count * local_count, capacity, column)


def flat_layout(received, expert_count, local_count):
    capacity = received.shape[1]
    column = received.shape[2]
    rows_in = received.reshape(expert_count, local_count, capacity, column).transpose(1, 0, 2, 3)
    return rows_in.reshape(-1, column)


def send_rows(packs, local_count):
    expert_count = packs[0].shape[0]
    outgoing = tuple((flat_outgoing(packed, local_count) for packed in packs))
    received = (
        lax.all_to_all(outgoing[0], ("node", "local"), split_axis=0, concat_axis=0, tiled=True),
        lax.all_to_all(outgoing[1], ("node", "local"), split_axis=0, concat_axis=0, tiled=True),
    )
    return tuple((flat_layout(item, expert_count, local_count) for item in received))


def return_rows(finished_pair, expert_count, capacity, local_count):
    column = finished_pair[0].shape[1]
    blocks = tuple(
        (item.reshape(local_count, expert_count, capacity, column) for item in finished_pair)
    )
    outgoing = tuple(
        (
            item.transpose(1, 0, 2, 3).reshape(expert_count * local_count, capacity, column)
            for item in blocks
        )
    )
    received = (
        lax.all_to_all(outgoing[0], ("node", "local"), split_axis=0, concat_axis=0, tiled=True),
        lax.all_to_all(outgoing[1], ("node", "local"), split_axis=0, concat_axis=0, tiled=True),
    )
    results = []
    for item in received:
        arranged = item.reshape(expert_count, local_count, capacity, column).transpose(0, 2, 1, 3)
        results.append(arranged.reshape(expert_count, capacity, local_count * column))
    return tuple(results)


def body(
    act_fwd, routes_fwd, weight_fwd, grad_bwd, routes_bwd, weight_bwd, saved_bwd, w_gate_up, w_down
):
    node_count = lax.axis_size("node")
    local_count = lax.axis_size("local")
    tokens_here = act_fwd.shape[1]
    capacity = 5 * tokens_here // (4 * node_count)
    rows_each = node_count * capacity
    w_gu = w_gate_up[0, 0]
    w_dn = w_down[0, 0]
    hidden_units = w_dn.shape[0]
    tokens_a = act_fwd[0]
    placer_a = place_matrix(routes_fwd[0, :, 0], node_count, capacity)
    cotangent = grad_bwd[0]
    placer_b = place_matrix(routes_bwd[0, :, 0], node_count, capacity)
    scaled = (weight_bwd[0][:, None] * cotangent.astype(jnp.float32)).astype(jnp.bfloat16)
    packed_a = pack_rows(placer_a, tokens_a, node_count, capacity)
    packed_b = pack_rows(placer_b, scaled, node_count, capacity)
    rows_a, rows_b = send_rows((packed_a, packed_b), local_count)
    saved_packed = pack_rows(placer_b, saved_bwd[0], node_count, capacity)
    saved_rows = lax.all_to_all(
        saved_packed, "node", split_axis=0, concat_axis=0, tiled=True
    ).reshape(rows_each, -1)
    row_block = rows_a
    preact = lax.psum_scatter(
        jnp.dot(row_block, w_gu, preferred_element_type=jnp.float32).astype(jnp.bfloat16),
        "local",
        scatter_dimension=0,
        tiled=True,
    ).astype(jnp.float32)
    row_block = rows_b
    grad_hidden = lax.psum_scatter(
        lax.dot_general(
            row_block, w_dn, (((1,), (1,)), ((), ())), preferred_element_type=jnp.float32
        ).astype(jnp.bfloat16),
        "local",
        scatter_dimension=0,
        tiled=True,
    ).astype(jnp.float32)
    hidden = (jax.nn.silu(preact[:, :hidden_units]) * preact[:, hidden_units:]).astype(jnp.bfloat16)
    done_a = jnp.dot(
        lax.all_gather(hidden, "local", axis=0, tiled=True),
        w_dn,
        preferred_element_type=jnp.float32,
    ).astype(jnp.bfloat16)
    gate_pre = saved_rows[:, :hidden_units].astype(jnp.float32)
    up_pre = saved_rows[:, hidden_units:].astype(jnp.float32)
    sigmoid_g = 1.0 / (1.0 + jnp.exp(-gate_pre))
    grad_gate = grad_hidden * up_pre * sigmoid_g * (1.0 + gate_pre * (1.0 - sigmoid_g))
    grad_up = grad_hidden * gate_pre * sigmoid_g
    grad_gu = jnp.concatenate([grad_gate, grad_up], axis=1).astype(jnp.bfloat16)
    product = lax.dot_general(
        lax.all_gather(grad_gu, "local", axis=0, tiled=True),
        w_gu,
        (((1,), (1,)), ((), ())),
        preferred_element_type=jnp.float32,
    )
    done_b = product.astype(jnp.bfloat16)
    back_a, back_b = return_rows((done_a, done_b), node_count, capacity, local_count)
    moe_a = unpack_rows(placer_a, back_a)
    result_a = tokens_a.astype(jnp.float32) + weight_fwd[0][:, None] * moe_a.astype(jnp.float32)
    result_a = result_a.astype(jnp.bfloat16)
    moe_b = unpack_rows(placer_b, back_b)
    result_b = (cotangent.astype(jnp.float32) + moe_b.astype(jnp.float32)).astype(jnp.bfloat16)
    next_input = from_behind(result_a[None], "pp", 1)
    prev_grad = from_behind(result_b[None], "pp", -1)
    return (next_input, prev_grad)


def solution(mesh):
    in_specs = (
        P("pp", ("node", "local"), None),
        P("pp", ("node", "local"), None),
        P("pp", ("node", "local")),
        P("pp", ("node", "local"), None),
        P("pp", ("node", "local"), None),
        P("pp", ("node", "local")),
        P("pp", ("node", "local"), None),
        P("pp", "node", "local", None),
        P("pp", "node", None, "local"),
    )
    out_specs = (P("pp", ("node", "local"), None), P("pp", ("node", "local"), None))
    paired = mesh.shape["node"] == 2 and mesh.shape["local"] == 4
    plan = body_pair if paired else body
    return jax.shard_map(plan, mesh=mesh, in_specs=in_specs, out_specs=out_specs, check_vma=False)
```

```python
import jax
import jax.numpy as jnp
from jax import lax
from jax.sharding import PartitionSpec as P

F32 = jnp.float32
BF16 = jnp.bfloat16
AXES = ("pp", "node", "local")


def move(value, by_pp=0, by_node=0, by_local=0, wrap=True, first=0, last=None):
    pps, nodes, locs = (lax.axis_size(a) for a in AXES)
    last = locs - 1 if last is None else last
    pairs = []
    for s in range(pps):
        for n in range(nodes):
            for l in range(locs):
                to = l + by_local
                if not wrap and not (first <= l <= last and 0 <= to < locs):
                    continue
                source = (s * nodes + n) * locs + l
                target = (((s + by_pp) % pps) * nodes + (n ^ by_node)) * locs + to % locs
                pairs.append((source, target))
    return lax.ppermute(value, AXES, pairs)


def sorted_places(route):
    ones = route.astype(F32)
    count = route.shape[0]
    earlier = (jnp.arange(count)[None, :] < jnp.arange(count)[:, None]).astype(F32)
    ones_before = jnp.dot(earlier, ones[:, None], preferred_element_type=F32)[:, 0]
    zeros = count - jnp.sum(ones)
    index = jnp.arange(count, dtype=F32)
    place = jnp.where(route == 0, index - ones_before, zeros + ones_before)
    return place.astype(jnp.int32)


def sorter(route):
    place = sorted_places(route)
    rows = jnp.arange(route.shape[0], dtype=jnp.int32)
    return (rows[:, None] == place[None, :]).astype(BF16)


def window_placer(route, node, capacity):
    place = sorted_places(route)
    start = route.shape[0] - capacity
    in_window = place - jnp.where(route == 1, start, 0)
    row = jnp.where(route == node, in_window, in_window + capacity)
    rows = jnp.arange(2 * capacity, dtype=jnp.int32)
    return (rows[:, None] == row[None, :]).astype(BF16)


def dot_t(left, right):
    return lax.dot_general(left, right, (((1,), (1,)), ((), ())), preferred_element_type=F32)


def windows(blocks, node, capacity):
    tokens = blocks.shape[-2]
    start = tokens - capacity
    low = lax.slice_in_dim(blocks, 0, capacity, axis=-2 + blocks.ndim)
    high = lax.slice_in_dim(blocks, start, tokens, axis=-2 + blocks.ndim)
    own = jnp.where(node == 0, low, high)
    other = jnp.where(node == 0, high, low)
    return own, other


def join(*values):
    return lax.optimization_barrier(values)


def after(values, *others):
    return list(join(*values, *others)[: len(values)])


def cut(tokens, placer, local):
    column = tokens.shape[1] // 4
    blocks = []
    for m in range(4):
        block = lax.dynamic_slice_in_dim(tokens, ((local - m) % 4) * column, column, axis=1)
        blocks.append(jnp.dot(placer, block, preferred_element_type=F32).astype(BF16))
    return blocks


def sums(partial):
    right, left = partial[3], partial[1]
    for step in (1, 2, 3):
        right, left = right.astype(BF16), left.astype(BF16)
        got_r, got_l = yield (
            (right, dict(by_local=1, wrap=False, last=step - 1)),
            (left, dict(by_local=-1, wrap=False, first=4 - step)),
        )
        right = partial[3 - step] + got_r.astype(F32)
        if step < 3:
            left = partial[step + 1] + got_l.astype(F32)
    yield right + got_l.astype(F32)


def gathers(rows, local):
    from_left, from_right = [rows], [rows]
    for step in (1, 2, 3):
        got_r, got_l = yield (
            (from_left[-1], dict(by_local=1, wrap=False, first=step - 1)),
            (from_right[-1], dict(by_local=-1, wrap=False, last=4 - step)),
        )
        from_left.append(got_r)
        from_right.append(got_l)
    slots = [rows]
    for m in (1, 2, 3):
        slots.append(jnp.where(local + m < 4, from_right[m], from_left[4 - m]))
    yield jnp.stack(slots)


def send(pieces):
    return [move(value, **how) for value, how in pieces]


def operands(pieces):
    return [value for value, _ in pieces]


def returns(done, by_pp):
    pieces = []
    for m in (2, 1, 3, 0):
        pieces.append((done[m, 0], dict(by_pp=by_pp, by_local=m)))
        pieces.append((done[m, 1], dict(by_pp=by_pp, by_node=1, by_local=m)))
    return pieces


def at_home(got):
    got = join(*got)
    rows = [None] * 4
    for i, m in enumerate((2, 1, 3, 0)):
        rows[m] = jnp.concatenate([got[2 * i], got[2 * i + 1]], axis=0)
    return rows


def later(pieces, *others):
    values = after(operands(pieces), *others)
    return [(value, how) for value, (_, how) in zip(values, pieces)]


def unsort(blocks, placer, local):
    column = blocks[0].shape[1]
    full = jnp.zeros((placer.shape[1], 4 * column), F32)
    for m in range(4):
        moe = lax.dot_general(
            placer, blocks[m], (((0,), (0,)), ((), ())), preferred_element_type=F32
        )
        full = lax.dynamic_update_slice_in_dim(full, moe, ((local - m) % 4) * column, axis=1)
    return full


def body_pair(
    act_fwd, routes_fwd, weight_fwd, grad_bwd, routes_bwd, weight_bwd, saved_bwd, w_gate_up, w_down
):
    node = lax.axis_index("node")
    local = lax.axis_index("local")
    tokens_here = act_fwd.shape[1]
    capacity = 5 * tokens_here // 8
    w_gu = w_gate_up[0, 0]
    w_dn = w_down[0, 0]
    hidden_units = w_dn.shape[0]
    shape = (4, 2, capacity)

    act, grad = act_fwd[0], grad_bwd[0]
    route_a, route_b = routes_fwd[0, :, 0], routes_bwd[0, :, 0]
    sort_b, sort_a = sorter(route_b), sorter(route_a)

    dy = (weight_bwd[0][:, None] * grad.astype(F32)).astype(BF16)
    cut_b = cut(dy, sort_b, local)
    got_b = [move(cut_b[m], by_local=-m) for m in (2, 1, 3)]
    saved = jnp.dot(sort_b, saved_bwd[0], preferred_element_type=F32).astype(BF16)
    (saved,) = after([saved], *cut_b[1:])
    saved_own, saved_other = windows(saved, node, capacity)
    saved_got = move(saved_other, by_node=1)
    cut_a = cut(act, sort_a, local)
    *got_b, saved_got = join(*got_b, saved_got)
    cut_a = after(cut_a, *got_b)
    got_a = [move(cut_a[m], by_local=-m) for m in (2, 1, 3)]

    def to_expert(blocks):
        return windows(jnp.stack(blocks), node, capacity)

    def expert_rows(own, got):
        rows = jnp.stack([own, got], axis=1)
        return rows.reshape(-1, rows.shape[-1])

    own_b, other_b = to_expert([cut_b[0], got_b[1], got_b[0], got_b[2]])
    got_bx = move(other_b, by_node=1)
    act_next = move(after([act], other_b)[0], by_pp=1)
    *got_a, got_bx, act_next = join(*got_a, got_bx, act_next)

    own_a, other_a = to_expert([cut_a[0], got_a[1], got_a[0], got_a[2]])
    got_ax = move(other_a, by_node=1)
    part_b = dot_t(expert_rows(own_b, got_bx), w_dn).reshape(shape + (hidden_units,))
    chain_b = sums(part_b)
    pieces_b = next(chain_b)
    back_b = send(pieces_b)
    small_wait = after([jnp.stack([route_a.astype(F32), weight_fwd[0]])], other_a)[0]
    small_next = move(small_wait, by_pp=1)
    *back_b, got_ax, small_next = join(*back_b, got_ax, small_next)

    part_a = jnp.dot(expert_rows(own_a, got_ax), w_gu, preferred_element_type=F32)
    chain_a = sums(part_a.reshape(shape + (2 * hidden_units,)))
    pieces_a = next(chain_a)
    pieces_b = chain_b.send(back_b)
    back_a = send(pieces_a)
    back_b = send(pieces_b)
    grad_wait, route_wait = after([grad, route_b], small_next)
    grad_next = move(grad_wait, by_pp=-1)
    route_b_next = move(route_wait, by_pp=-1)
    *back_b, grad_next, route_b_next = join(*back_b, grad_next, route_b_next)
    pieces_b = chain_b.send(back_b)
    back_b = send(pieces_b)
    back_a = after(back_a, *operands(pieces_b))
    pieces_a = chain_a.send(back_a)
    back_a = send(pieces_a)
    back_b = after(back_b, *operands(pieces_a))
    dh = chain_b.send(back_b)

    saved_rows = jnp.stack([saved_own, saved_got])
    g = saved_rows[..., :hidden_units].astype(F32)
    u = saved_rows[..., hidden_units:].astype(F32)
    q = 1.0 / (1.0 + jnp.exp(-g))
    grad_gu = jnp.concatenate([dh * u * q * (1.0 + g * (1.0 - q)), dh * g * q], axis=-1).astype(
        BF16
    )
    chain_b = gathers(grad_gu, local)
    pieces_b = next(chain_b)
    back_b = send(pieces_b)
    back_a = after(back_a, *operands(pieces_b))
    pieces_a = chain_a.send(back_a)
    back_a = send(pieces_a)
    back_b = after(back_b, *operands(pieces_a))
    pieces_b = chain_b.send(back_b)
    back_b = send(pieces_b)
    back_a = after(back_a, *operands(pieces_b))
    preact = chain_a.send(back_a)
    hidden = (jax.nn.silu(preact[..., :hidden_units]) * preact[..., hidden_units:]).astype(BF16)
    all_hidden = [hidden] + [move(hidden, by_local=-m) for m in (1, 2, 3)]
    back_b = after(back_b, hidden)
    pieces_b = chain_b.send(back_b)
    back_b = send(pieces_b)
    all_hidden = after(all_hidden, *operands(pieces_b))
    done_a = jnp.dot(
        jnp.stack(all_hidden).reshape(-1, hidden_units), w_dn, preferred_element_type=F32
    ).astype(BF16)
    out_a = returns(done_a.reshape(shape + (done_a.shape[-1],)), 1)
    home_a = send(out_a[:3])
    back_b = after(back_b, *operands(out_a))
    home_a += send(later(out_a[3:], *back_b))
    all_gu = chain_b.send(back_b)
    done_b = dot_t(all_gu.reshape(-1, 2 * hidden_units), w_gu).astype(BF16)
    home_b = send(returns(done_b.reshape(shape + (done_b.shape[-1],)), -1))

    moe_b = unsort(at_home(home_b), window_placer(route_b_next, node, capacity), local)
    prev_grad = (grad_next.astype(F32) + moe_b).astype(BF16)
    route_a_next = small_next[0].astype(jnp.int32)
    moe_a = unsort(at_home(home_a), window_placer(route_a_next, node, capacity), local)
    next_input = (act_next.astype(F32) + small_next[1][:, None] * moe_a).astype(BF16)
    return next_input[None], prev_grad[None]


def from_behind(value, axis, by):
    length = lax.axis_size(axis)
    return lax.ppermute(value, axis, [(i, (i + by) % length) for i in range(length)])


def place_matrix(route, expert_count, capacity):
    onehot = (route[:, None] == jnp.arange(expert_count, dtype=jnp.int32)[None, :]).astype(
        jnp.int32
    )
    before = jnp.cumsum(onehot, axis=0) - onehot
    slot_index = jnp.sum(before * onehot, axis=1)
    target = route * capacity + slot_index
    positions = jnp.arange(expert_count * capacity, dtype=jnp.int32)
    return (positions[:, None] == target[None, :]).astype(jnp.bfloat16)


def pack_rows(placer, values, expert_count, capacity):
    packed = jnp.dot(placer, values, preferred_element_type=jnp.float32).astype(jnp.bfloat16)
    return packed.reshape(expert_count, capacity, values.shape[1])


def unpack_rows(placer, packed):
    flattened = packed.reshape(-1, packed.shape[-1])
    result = lax.dot_general(
        placer, flattened, (((0,), (0,)), ((), ())), preferred_element_type=jnp.float32
    )
    return result.astype(jnp.bfloat16)


def flat_outgoing(packed, local_count):
    expert_count, capacity, feature_count = packed.shape
    column = feature_count // local_count
    outgoing = packed.reshape(expert_count, capacity, local_count, column).transpose(0, 2, 1, 3)
    return outgoing.reshape(expert_count * local_count, capacity, column)


def flat_layout(received, expert_count, local_count):
    capacity = received.shape[1]
    column = received.shape[2]
    rows_in = received.reshape(expert_count, local_count, capacity, column).transpose(1, 0, 2, 3)
    return rows_in.reshape(-1, column)


def send_rows(packs, local_count):
    expert_count = packs[0].shape[0]
    outgoing = tuple((flat_outgoing(packed, local_count) for packed in packs))
    received = (
        lax.all_to_all(outgoing[0], ("node", "local"), split_axis=0, concat_axis=0, tiled=True),
        lax.all_to_all(outgoing[1], ("node", "local"), split_axis=0, concat_axis=0, tiled=True),
    )
    return tuple((flat_layout(item, expert_count, local_count) for item in received))


def return_rows(finished_pair, expert_count, capacity, local_count):
    column = finished_pair[0].shape[1]
    blocks = tuple(
        (item.reshape(local_count, expert_count, capacity, column) for item in finished_pair)
    )
    outgoing = tuple(
        (
            item.transpose(1, 0, 2, 3).reshape(expert_count * local_count, capacity, column)
            for item in blocks
        )
    )
    received = (
        lax.all_to_all(outgoing[0], ("node", "local"), split_axis=0, concat_axis=0, tiled=True),
        lax.all_to_all(outgoing[1], ("node", "local"), split_axis=0, concat_axis=0, tiled=True),
    )
    results = []
    for item in received:
        arranged = item.reshape(expert_count, local_count, capacity, column).transpose(0, 2, 1, 3)
        results.append(arranged.reshape(expert_count, capacity, local_count * column))
    return tuple(results)


def body(
    act_fwd, routes_fwd, weight_fwd, grad_bwd, routes_bwd, weight_bwd, saved_bwd, w_gate_up, w_down
):
    node_count = lax.axis_size("node")
    local_count = lax.axis_size("local")
    tokens_here = act_fwd.shape[1]
    capacity = 5 * tokens_here // (4 * node_count)
    rows_each = node_count * capacity
    w_gu = w_gate_up[0, 0]
    w_dn = w_down[0, 0]
    hidden_units = w_dn.shape[0]
    tokens_a = act_fwd[0]
    placer_a = place_matrix(routes_fwd[0, :, 0], node_count, capacity)
    cotangent = grad_bwd[0]
    placer_b = place_matrix(routes_bwd[0, :, 0], node_count, capacity)
    scaled = (weight_bwd[0][:, None] * cotangent.astype(jnp.float32)).astype(jnp.bfloat16)
    packed_a = pack_rows(placer_a, tokens_a, node_count, capacity)
    packed_b = pack_rows(placer_b, scaled, node_count, capacity)
    rows_a, rows_b = send_rows((packed_a, packed_b), local_count)
    saved_packed = pack_rows(placer_b, saved_bwd[0], node_count, capacity)
    saved_rows = lax.all_to_all(
        saved_packed, "node", split_axis=0, concat_axis=0, tiled=True
    ).reshape(rows_each, -1)
    row_block = rows_a
    preact = lax.psum_scatter(
        jnp.dot(row_block, w_gu, preferred_element_type=jnp.float32).astype(jnp.bfloat16),
        "local",
        scatter_dimension=0,
        tiled=True,
    ).astype(jnp.float32)
    row_block = rows_b
    grad_hidden = lax.psum_scatter(
        lax.dot_general(
            row_block, w_dn, (((1,), (1,)), ((), ())), preferred_element_type=jnp.float32
        ).astype(jnp.bfloat16),
        "local",
        scatter_dimension=0,
        tiled=True,
    ).astype(jnp.float32)
    hidden = (jax.nn.silu(preact[:, :hidden_units]) * preact[:, hidden_units:]).astype(jnp.bfloat16)
    done_a = jnp.dot(
        lax.all_gather(hidden, "local", axis=0, tiled=True),
        w_dn,
        preferred_element_type=jnp.float32,
    ).astype(jnp.bfloat16)
    gate_pre = saved_rows[:, :hidden_units].astype(jnp.float32)
    up_pre = saved_rows[:, hidden_units:].astype(jnp.float32)
    sigmoid_g = 1.0 / (1.0 + jnp.exp(-gate_pre))
    grad_gate = grad_hidden * up_pre * sigmoid_g * (1.0 + gate_pre * (1.0 - sigmoid_g))
    grad_up = grad_hidden * gate_pre * sigmoid_g
    grad_gu = jnp.concatenate([grad_gate, grad_up], axis=1).astype(jnp.bfloat16)
    product = lax.dot_general(
        lax.all_gather(grad_gu, "local", axis=0, tiled=True),
        w_gu,
        (((1,), (1,)), ((), ())),
        preferred_element_type=jnp.float32,
    )
    done_b = product.astype(jnp.bfloat16)
    back_a, back_b = return_rows((done_a, done_b), node_count, capacity, local_count)
    moe_a = unpack_rows(placer_a, back_a)
    result_a = tokens_a.astype(jnp.float32) + weight_fwd[0][:, None] * moe_a.astype(jnp.float32)
    result_a = result_a.astype(jnp.bfloat16)
    moe_b = unpack_rows(placer_b, back_b)
    result_b = (cotangent.astype(jnp.float32) + moe_b.astype(jnp.float32)).astype(jnp.bfloat16)
    next_input = from_behind(result_a[None], "pp", 1)
    prev_grad = from_behind(result_b[None], "pp", -1)
    return (next_input, prev_grad)


def solution(mesh):
    in_specs = (
        P("pp", ("node", "local"), None),
        P("pp", ("node", "local"), None),
        P("pp", ("node", "local")),
        P("pp", ("node", "local"), None),
        P("pp", ("node", "local"), None),
        P("pp", ("node", "local")),
        P("pp", ("node", "local"), None),
        P("pp", "node", "local", None),
        P("pp", "node", None, "local"),
    )
    out_specs = (P("pp", ("node", "local"), None), P("pp", ("node", "local"), None))
    paired = mesh.shape["node"] == 2 and mesh.shape["local"] == 4
    plan = body_pair if paired else body
    return jax.shard_map(plan, mesh=mesh, in_specs=in_specs, out_specs=out_specs, check_vma=False)
```

```python
import jax
import jax.numpy as jnp
from jax import lax
from jax.experimental import pallas as pl
from jax.experimental.pallas import tpu as pltpu
from jax.sharding import PartitionSpec as P

F32 = jnp.float32
BF16 = jnp.bfloat16
AXES = ("pp", "node", "local")


def move(value, by_pp=0, by_node=0, by_local=0, wrap=True, first=0, last=None):
    pps, nodes, locs = (lax.axis_size(a) for a in AXES)
    last = locs - 1 if last is None else last
    pairs = []
    for s in range(pps):
        for n in range(nodes):
            for l in range(locs):
                to = l + by_local
                if not wrap and not (first <= l <= last and 0 <= to < locs):
                    continue
                source = (s * nodes + n) * locs + l
                target = (((s + by_pp) % pps) * nodes + (n ^ by_node)) * locs + to % locs
                pairs.append((source, target))
    return lax.ppermute(value, AXES, pairs)


def sorted_places(route):
    ones = route.astype(F32)
    count = route.shape[0]
    earlier = (jnp.arange(count)[None, :] < jnp.arange(count)[:, None]).astype(F32)
    ones_before = jnp.dot(earlier, ones[:, None], preferred_element_type=F32)[:, 0]
    zeros = count - jnp.sum(ones)
    index = jnp.arange(count, dtype=F32)
    place = jnp.where(route == 0, index - ones_before, zeros + ones_before)
    return place.astype(jnp.int32)


def sorter(route):
    place = sorted_places(route)
    rows = jnp.arange(route.shape[0], dtype=jnp.int32)
    return (rows[:, None] == place[None, :]).astype(BF16)


def window_rows(route, first, capacity):
    place = sorted_places(route)
    start = route.shape[0] - capacity
    in_window = place - jnp.where(route == 1, start, 0)
    return jnp.where(route == first, in_window, in_window + capacity)


def one_hot(row, count):
    return (row[:, None] == jnp.arange(count, dtype=jnp.int32)[None, :]).astype(BF16)


def dot_t(left, right):
    return lax.dot_general(left, right, (((1,), (1,)), ((), ())), preferred_element_type=F32)


def windows(blocks, node, capacity):
    tokens = blocks.shape[-2]
    start = tokens - capacity
    low = lax.slice_in_dim(blocks, 0, capacity, axis=-2 + blocks.ndim)
    high = lax.slice_in_dim(blocks, start, tokens, axis=-2 + blocks.ndim)
    own = jnp.where(node == 0, low, high)
    other = jnp.where(node == 0, high, low)
    return own, other


def join(*values):
    return lax.optimization_barrier(values)


def after(values, *others):
    return list(join(*values, *others)[: len(values)])


def cut(tokens, placer, local):
    column = tokens.shape[1] // 4
    blocks = []
    for m in range(4):
        block = lax.dynamic_slice_in_dim(tokens, ((local - m) % 4) * column, column, axis=1)
        blocks.append(jnp.dot(placer, block, preferred_element_type=F32).astype(BF16))
    return blocks


def sums(partial):
    right, left = partial(3), partial(1)
    for step in (1, 2, 3):
        right, left = right.astype(BF16), left.astype(BF16)
        got_r, got_l = yield (
            (right, dict(by_local=1, wrap=False, last=step - 1)),
            (left, dict(by_local=-1, wrap=False, first=4 - step)),
        )
        right = partial(3 - step).astype(F32) + got_r.astype(F32)
        if step < 3:
            left = partial(step + 1).astype(F32) + got_l.astype(F32)
    yield right + got_l.astype(F32)


def gathers(rows, local):
    from_left, from_right = [rows], [rows]
    for step in (1, 2, 3):
        got_r, got_l = yield (
            (from_left[-1], dict(by_local=1, wrap=False, first=step - 1)),
            (from_right[-1], dict(by_local=-1, wrap=False, last=4 - step)),
        )
        from_left.append(got_r)
        from_right.append(got_l)
    slots = [rows]
    for m in (1, 2, 3):
        slots.append(jnp.where(local + m < 4, from_right[m], from_left[4 - m]))
    yield jnp.stack(slots)


def send(pieces):
    return [move(value, **how) for value, how in pieces]


def operands(pieces):
    return [value for value, _ in pieces]


def returns(done, by_pp):
    pieces = []
    for m in (2, 1, 3, 0):
        pieces.append((done(m, 0), dict(by_pp=by_pp, by_local=m)))
        pieces.append((done(m, 1), dict(by_pp=by_pp, by_node=1, by_local=m)))
    return pieces


def later(pieces, *others):
    values = after(operands(pieces), *others)
    return [(value, how) for value, (_, how) in zip(values, pieces)]


def finish_kernel(count, at_ref, residual_ref, weight_ref, pick_ref, *refs):
    out_ref = refs[-1]
    capacity, column = refs[0].shape[-2:]
    for i in range(count):
        cols = pl.ds(pl.multiple_of(at_ref[i] * column, column), column)
        rows = [refs[2 * i][...].reshape(capacity, column), refs[2 * i + 1][...].reshape(capacity, column)]
        moe = sum(
            jnp.dot(pick_ref[k], rows[k], preferred_element_type=F32) for k in (0, 1)
        )
        total = residual_ref[:, cols].astype(F32) + weight_ref[...] * moe
        out_ref[:, cols] = total.astype(out_ref.dtype)


def finish(residual, weight, row, blocks, at):
    capacity, column = blocks[0].shape[-2:]
    count = len(blocks) // 2
    tokens, features = residual.shape
    pick = one_hot(row, 2 * capacity).reshape(tokens, 2, capacity).transpose(1, 0, 2)
    vmem = pl.BlockSpec(memory_space=pltpu.VMEM)
    return pl.pallas_call(
        lambda *refs: finish_kernel(count, *refs),
        out_shape=jax.ShapeDtypeStruct((tokens, features), BF16),
        in_specs=[pl.BlockSpec(memory_space=pltpu.SMEM)] + [vmem] * (3 + 2 * count),
        out_specs=vmem,
        compiler_params=pltpu.CompilerParams(vmem_limit_bytes=24 * 2**20),
        name="finish",
    )(at, residual, weight[:, None], pick, *blocks)


def body_pair(
    act_fwd, routes_fwd, weight_fwd, grad_bwd, routes_bwd, weight_bwd, saved_bwd, w_gate_up, w_down
):
    node = lax.axis_index("node")
    local = lax.axis_index("local")
    tokens_here = act_fwd.shape[1]
    capacity = 5 * tokens_here // 8
    w_gu = w_gate_up[0, 0]
    w_dn = w_down[0, 0]
    hidden_units = w_dn.shape[0]
    shape = (4, 2, capacity)

    act, grad = act_fwd[0], grad_bwd[0]
    route_a, route_b = routes_fwd[0, :, 0], routes_bwd[0, :, 0]
    sort_b = sorter(route_b)
    column = act.shape[1] // 4

    dy = (weight_bwd[0][:, None] * grad.astype(F32)).astype(BF16)
    cut_b = cut(dy, sort_b, local)
    got_b = [move(cut_b[m], by_local=-m) for m in (2, 1, 3)]
    saved = jnp.dot(sort_b, saved_bwd[0], preferred_element_type=F32).astype(BF16)
    (saved,) = after([saved], *cut_b[1:])
    saved_own, saved_other = windows(saved, node, capacity)
    saved_got = move(saved_other, by_node=1)
    placer_a = one_hot(window_rows(route_a, 0, capacity), 2 * capacity)
    packed_a = jnp.stack(
        [
            lax.dot_general(
                placer_a,
                act[:, j * column : (j + 1) * column],
                (((0,), (0,)), ((), ())),
                preferred_element_type=F32,
            )
            .astype(BF16)
            .reshape(2, capacity, column)
            for j in range(4)
        ],
        axis=1,
    ).reshape(8, capacity, column)
    *got_b, saved_got, packed_a = join(*got_b, saved_got, packed_a)

    def by_node(own, got, axis):
        return jnp.stack([jnp.where(node == 0, own, got), jnp.where(node == 0, got, own)], axis=axis)

    def homes(array, axis):
        return lambda slot: lax.dynamic_index_in_dim(
            array, (local + slot) % 4, axis=axis, keepdims=False
        )

    own_b, other_b = windows(
        jnp.stack([cut_b[0], got_b[1], got_b[0], got_b[2]]), node, capacity
    )
    got_bx = move(other_b, by_node=1)

    got_a = lax.all_to_all(packed_a, ("node", "local"), split_axis=0, concat_axis=0, tiled=True)
    act_wait, small_wait = after([act, jnp.stack([route_a.astype(F32), weight_fwd[0]])], other_b)
    act_next = move(act_wait, by_pp=1)
    small_next = move(small_wait, by_pp=1)

    rows_b = by_node(own_b, got_bx, 1).reshape(-1, column)
    part_b = dot_t(rows_b, w_dn).astype(BF16).reshape(shape + (hidden_units,))
    chain_b = sums(lambda slot: part_b[slot])
    pieces_b = next(chain_b)
    back_b = send(pieces_b)
    *back_b, act_next, small_next = join(*back_b, act_next, small_next)
    pieces_b = chain_b.send(back_b)
    back_b = send(pieces_b)

    part_a = jnp.dot(got_a.reshape(-1, column), w_gu, preferred_element_type=F32).astype(BF16)
    chain_a = sums(homes(part_a.reshape(2, 4, capacity, 2 * hidden_units), 1))
    pieces_a = next(chain_a)
    back_a = send(pieces_a)
    pieces_b = chain_b.send(back_b)
    back_b = send(pieces_b)
    back_a = after(back_a, *operands(pieces_b))
    back_b = after(back_b, *operands(pieces_a))
    dh = chain_b.send(back_b)

    saved_rows = by_node(saved_own, saved_got, 0)
    g = saved_rows[..., :hidden_units].astype(F32)
    u = saved_rows[..., hidden_units:].astype(F32)
    q = 1.0 / (1.0 + jnp.exp(-g))
    grad_gu = jnp.concatenate([dh * u * q * (1.0 + g * (1.0 - q)), dh * g * q], axis=-1).astype(
        BF16
    )
    chain_b = gathers(grad_gu, local)
    pieces_b = next(chain_b)
    back_b = send(pieces_b)
    for _ in (2, 3):
        back_a = after(back_a, *operands(pieces_b))
        pieces_a = chain_a.send(back_a)
        back_a = send(pieces_a)
        back_b = after(back_b, *operands(pieces_a))
        pieces_b = chain_b.send(back_b)
        back_b = send(pieces_b)
    back_a = after(back_a, *operands(pieces_b))
    preact = chain_a.send(back_a)
    hidden = (jax.nn.silu(preact[..., :hidden_units]) * preact[..., hidden_units:]).astype(BF16)
    all_hidden = [hidden] + [move(hidden, by_local=-m) for m in (1, 2, 3)]
    back_b = after(back_b, hidden)
    all_gu = chain_b.send(back_b)
    done_b = dot_t(all_gu.reshape(-1, 2 * hidden_units), w_gu).astype(BF16)
    done_b = done_b.reshape(shape + (column,))
    out_b = lax.dynamic_slice_in_dim(jnp.concatenate([done_b, done_b]), (4 - local) % 4, 4, axis=0)
    out_b = out_b.transpose(1, 0, 2, 3).reshape(8, capacity, column)
    home_b = lax.all_to_all(out_b, ("node", "local"), split_axis=0, concat_axis=0, tiled=True)

    all_hidden = after(all_hidden, out_b)
    done_a = jnp.dot(
        jnp.stack(all_hidden).reshape(-1, hidden_units), w_dn, preferred_element_type=F32
    ).astype(BF16)
    done_a = done_a.reshape(shape + (column,))
    home_a = send(
        returns(
            lambda slot, other: lax.dynamic_index_in_dim(done_a[slot], node ^ other, keepdims=False), 1
        )
    )

    blocks_b = [home_b[4 * n + j] for j in range(4) for n in (0, 1)]
    ones = jnp.ones((tokens_here,), F32)
    result_b = finish(
        grad, ones, window_rows(route_b, 0, capacity), blocks_b, jnp.arange(4, dtype=jnp.int32)
    )
    prev_grad = move(result_b, by_pp=-1)
    row_a = window_rows(small_next[0].astype(jnp.int32), node, capacity)
    at = jnp.stack([(local - m) % 4 for m in (2, 1, 3, 0)]).astype(jnp.int32)
    next_input = finish(act_next, small_next[1], row_a, home_a, at)
    return next_input[None], prev_grad[None]


def from_behind(value, axis, by):
    length = lax.axis_size(axis)
    return lax.ppermute(value, axis, [(i, (i + by) % length) for i in range(length)])


def place_matrix(route, expert_count, capacity):
    onehot = (route[:, None] == jnp.arange(expert_count, dtype=jnp.int32)[None, :]).astype(
        jnp.int32
    )
    before = jnp.cumsum(onehot, axis=0) - onehot
    slot_index = jnp.sum(before * onehot, axis=1)
    target = route * capacity + slot_index
    positions = jnp.arange(expert_count * capacity, dtype=jnp.int32)
    return (positions[:, None] == target[None, :]).astype(jnp.bfloat16)


def pack_rows(placer, values, expert_count, capacity):
    packed = jnp.dot(placer, values, preferred_element_type=jnp.float32).astype(jnp.bfloat16)
    return packed.reshape(expert_count, capacity, values.shape[1])


def unpack_rows(placer, packed):
    flattened = packed.reshape(-1, packed.shape[-1])
    result = lax.dot_general(
        placer, flattened, (((0,), (0,)), ((), ())), preferred_element_type=jnp.float32
    )
    return result.astype(jnp.bfloat16)


def flat_outgoing(packed, local_count):
    expert_count, capacity, feature_count = packed.shape
    column = feature_count // local_count
    outgoing = packed.reshape(expert_count, capacity, local_count, column).transpose(0, 2, 1, 3)
    return outgoing.reshape(expert_count * local_count, capacity, column)


def flat_layout(received, expert_count, local_count):
    capacity = received.shape[1]
    column = received.shape[2]
    rows_in = received.reshape(expert_count, local_count, capacity, column).transpose(1, 0, 2, 3)
    return rows_in.reshape(-1, column)


def send_rows(packs, local_count):
    expert_count = packs[0].shape[0]
    outgoing = tuple((flat_outgoing(packed, local_count) for packed in packs))
    received = (
        lax.all_to_all(outgoing[0], ("node", "local"), split_axis=0, concat_axis=0, tiled=True),
        lax.all_to_all(outgoing[1], ("node", "local"), split_axis=0, concat_axis=0, tiled=True),
    )
    return tuple((flat_layout(item, expert_count, local_count) for item in received))


def return_rows(finished_pair, expert_count, capacity, local_count):
    column = finished_pair[0].shape[1]
    blocks = tuple(
        (item.reshape(local_count, expert_count, capacity, column) for item in finished_pair)
    )
    outgoing = tuple(
        (
            item.transpose(1, 0, 2, 3).reshape(expert_count * local_count, capacity, column)
            for item in blocks
        )
    )
    received = (
        lax.all_to_all(outgoing[0], ("node", "local"), split_axis=0, concat_axis=0, tiled=True),
        lax.all_to_all(outgoing[1], ("node", "local"), split_axis=0, concat_axis=0, tiled=True),
    )
    results = []
    for item in received:
        arranged = item.reshape(expert_count, local_count, capacity, column).transpose(0, 2, 1, 3)
        results.append(arranged.reshape(expert_count, capacity, local_count * column))
    return tuple(results)


def body(
    act_fwd, routes_fwd, weight_fwd, grad_bwd, routes_bwd, weight_bwd, saved_bwd, w_gate_up, w_down
):
    node_count = lax.axis_size("node")
    local_count = lax.axis_size("local")
    tokens_here = act_fwd.shape[1]
    capacity = 5 * tokens_here // (4 * node_count)
    rows_each = node_count * capacity
    w_gu = w_gate_up[0, 0]
    w_dn = w_down[0, 0]
    hidden_units = w_dn.shape[0]
    tokens_a = act_fwd[0]
    placer_a = place_matrix(routes_fwd[0, :, 0], node_count, capacity)
    cotangent = grad_bwd[0]
    placer_b = place_matrix(routes_bwd[0, :, 0], node_count, capacity)
    scaled = (weight_bwd[0][:, None] * cotangent.astype(jnp.float32)).astype(jnp.bfloat16)
    packed_a = pack_rows(placer_a, tokens_a, node_count, capacity)
    packed_b = pack_rows(placer_b, scaled, node_count, capacity)
    rows_a, rows_b = send_rows((packed_a, packed_b), local_count)
    saved_packed = pack_rows(placer_b, saved_bwd[0], node_count, capacity)
    saved_rows = lax.all_to_all(
        saved_packed, "node", split_axis=0, concat_axis=0, tiled=True
    ).reshape(rows_each, -1)
    row_block = rows_a
    preact = lax.psum_scatter(
        jnp.dot(row_block, w_gu, preferred_element_type=jnp.float32).astype(jnp.bfloat16),
        "local",
        scatter_dimension=0,
        tiled=True,
    ).astype(jnp.float32)
    row_block = rows_b
    grad_hidden = lax.psum_scatter(
        lax.dot_general(
            row_block, w_dn, (((1,), (1,)), ((), ())), preferred_element_type=jnp.float32
        ).astype(jnp.bfloat16),
        "local",
        scatter_dimension=0,
        tiled=True,
    ).astype(jnp.float32)
    hidden = (jax.nn.silu(preact[:, :hidden_units]) * preact[:, hidden_units:]).astype(jnp.bfloat16)
    done_a = jnp.dot(
        lax.all_gather(hidden, "local", axis=0, tiled=True),
        w_dn,
        preferred_element_type=jnp.float32,
    ).astype(jnp.bfloat16)
    gate_pre = saved_rows[:, :hidden_units].astype(jnp.float32)
    up_pre = saved_rows[:, hidden_units:].astype(jnp.float32)
    sigmoid_g = 1.0 / (1.0 + jnp.exp(-gate_pre))
    grad_gate = grad_hidden * up_pre * sigmoid_g * (1.0 + gate_pre * (1.0 - sigmoid_g))
    grad_up = grad_hidden * gate_pre * sigmoid_g
    grad_gu = jnp.concatenate([grad_gate, grad_up], axis=1).astype(jnp.bfloat16)
    product = lax.dot_general(
        lax.all_gather(grad_gu, "local", axis=0, tiled=True),
        w_gu,
        (((1,), (1,)), ((), ())),
        preferred_element_type=jnp.float32,
    )
    done_b = product.astype(jnp.bfloat16)
    back_a, back_b = return_rows((done_a, done_b), node_count, capacity, local_count)
    moe_a = unpack_rows(placer_a, back_a)
    result_a = tokens_a.astype(jnp.float32) + weight_fwd[0][:, None] * moe_a.astype(jnp.float32)
    result_a = result_a.astype(jnp.bfloat16)
    moe_b = unpack_rows(placer_b, back_b)
    result_b = (cotangent.astype(jnp.float32) + moe_b.astype(jnp.float32)).astype(jnp.bfloat16)
    next_input = from_behind(result_a[None], "pp", 1)
    prev_grad = from_behind(result_b[None], "pp", -1)
    return (next_input, prev_grad)


def solution(mesh):
    in_specs = (
        P("pp", ("node", "local"), None),
        P("pp", ("node", "local"), None),
        P("pp", ("node", "local")),
        P("pp", ("node", "local"), None),
        P("pp", ("node", "local"), None),
        P("pp", ("node", "local")),
        P("pp", ("node", "local"), None),
        P("pp", "node", "local", None),
        P("pp", "node", None, "local"),
    )
    out_specs = (P("pp", ("node", "local"), None), P("pp", ("node", "local"), None))
    paired = mesh.shape["node"] == 2 and mesh.shape["local"] == 4
    plan = body_pair if paired else body
    return jax.shard_map(plan, mesh=mesh, in_specs=in_specs, out_specs=out_specs, check_vma=False)
```

```python
import jax
import jax.numpy as jnp
from jax import lax
from jax.experimental import pallas as pl
from jax.experimental.pallas import tpu as pltpu
from jax.sharding import PartitionSpec as P

F32 = jnp.float32
BF16 = jnp.bfloat16
AXES = ("pp", "node", "local")


def move(value, by_pp=0, by_node=0, by_local=0, wrap=True, first=0, last=None):
    pps, nodes, locs = (lax.axis_size(a) for a in AXES)
    last = locs - 1 if last is None else last
    pairs = []
    for s in range(pps):
        for n in range(nodes):
            for l in range(locs):
                to = l + by_local
                if not wrap and not (first <= l <= last and 0 <= to < locs):
                    continue
                source = (s * nodes + n) * locs + l
                target = (((s + by_pp) % pps) * nodes + (n ^ by_node)) * locs + to % locs
                pairs.append((source, target))
    return lax.ppermute(value, AXES, pairs)


def sorted_places(route):
    ones = route.astype(F32)
    count = route.shape[0]
    earlier = (jnp.arange(count)[None, :] < jnp.arange(count)[:, None]).astype(F32)
    ones_before = jnp.dot(earlier, ones[:, None], preferred_element_type=F32)[:, 0]
    zeros = count - jnp.sum(ones)
    index = jnp.arange(count, dtype=F32)
    place = jnp.where(route == 0, index - ones_before, zeros + ones_before)
    return place.astype(jnp.int32)


def sorter(route):
    place = sorted_places(route)
    rows = jnp.arange(route.shape[0], dtype=jnp.int32)
    return (rows[:, None] == place[None, :]).astype(BF16)


def window_rows(route, first, capacity):
    place = sorted_places(route)
    start = route.shape[0] - capacity
    in_window = place - jnp.where(route == 1, start, 0)
    return jnp.where(route == first, in_window, in_window + capacity)


def one_hot(row, count):
    return (row[:, None] == jnp.arange(count, dtype=jnp.int32)[None, :]).astype(BF16)


def dot_t(left, right):
    return lax.dot_general(left, right, (((1,), (1,)), ((), ())), preferred_element_type=F32)


def windows(blocks, node, capacity):
    tokens = blocks.shape[-2]
    start = tokens - capacity
    low = lax.slice_in_dim(blocks, 0, capacity, axis=-2 + blocks.ndim)
    high = lax.slice_in_dim(blocks, start, tokens, axis=-2 + blocks.ndim)
    own = jnp.where(node == 0, low, high)
    other = jnp.where(node == 0, high, low)
    return own, other


def join(*values):
    return lax.optimization_barrier(values)


def after(values, *others):
    return list(join(*values, *others)[: len(values)])


def cut(tokens, placer, local):
    column = tokens.shape[1] // 4
    blocks = []
    for m in range(4):
        block = lax.dynamic_slice_in_dim(tokens, ((local - m) % 4) * column, column, axis=1)
        blocks.append(jnp.dot(placer, block, preferred_element_type=F32).astype(BF16))
    return blocks


def sums(partial):
    right, left = partial(3), partial(1)
    for step in (1, 2, 3):
        right, left = right.astype(BF16), left.astype(BF16)
        got_r, got_l = yield (
            (right, dict(by_local=1, wrap=False, last=step - 1)),
            (left, dict(by_local=-1, wrap=False, first=4 - step)),
        )
        right = partial(3 - step).astype(F32) + got_r.astype(F32)
        if step < 3:
            left = partial(step + 1).astype(F32) + got_l.astype(F32)
    yield right + got_l.astype(F32)


def gathers(rows, local):
    from_left, from_right = [rows], [rows]
    for step in (1, 2, 3):
        got_r, got_l = yield (
            (from_left[-1], dict(by_local=1, wrap=False, first=step - 1)),
            (from_right[-1], dict(by_local=-1, wrap=False, last=4 - step)),
        )
        from_left.append(got_r)
        from_right.append(got_l)
    slots = [rows]
    for m in (1, 2, 3):
        slots.append(jnp.where(local + m < 4, from_right[m], from_left[4 - m]))
    yield jnp.stack(slots)


def send(pieces):
    return [move(value, **how) for value, how in pieces]


def operands(pieces):
    return [value for value, _ in pieces]


def returns(done, by_pp):
    pieces = []
    for m in (2, 1, 3, 0):
        pieces.append((done(m, 0), dict(by_pp=by_pp, by_local=m)))
        pieces.append((done(m, 1), dict(by_pp=by_pp, by_node=1, by_local=m)))
    return pieces


def later(pieces, *others):
    values = after(operands(pieces), *others)
    return [(value, how) for value, (_, how) in zip(values, pieces)]


def finish_kernel(count, at_ref, residual_ref, weight_ref, pick_ref, *refs):
    out_ref = refs[-1]
    capacity, column = refs[0].shape[-2:]
    for i in range(count):
        cols = pl.ds(pl.multiple_of(at_ref[i] * column, column), column)
        rows = [refs[2 * i][...].reshape(capacity, column), refs[2 * i + 1][...].reshape(capacity, column)]
        moe = sum(
            jnp.dot(pick_ref[k], rows[k], preferred_element_type=F32) for k in (0, 1)
        )
        total = residual_ref[:, cols].astype(F32) + weight_ref[...] * moe
        out_ref[0, :, cols] = total.astype(out_ref.dtype)


def finish(residual, weight, row, blocks, at):
    capacity, column = blocks[0].shape[-2:]
    count = len(blocks) // 2
    tokens, features = residual.shape
    pick = one_hot(row, 2 * capacity).reshape(tokens, 2, capacity).transpose(1, 0, 2)
    vmem = pl.BlockSpec(memory_space=pltpu.VMEM)
    return pl.pallas_call(
        lambda *refs: finish_kernel(count, *refs),
        out_shape=jax.ShapeDtypeStruct((1, tokens, features), BF16),
        in_specs=[pl.BlockSpec(memory_space=pltpu.SMEM)] + [vmem] * (3 + 2 * count),
        out_specs=vmem,
        compiler_params=pltpu.CompilerParams(vmem_limit_bytes=8 * 2**20),
        name="finish",
    )(at, residual, weight[:, None], pick, *blocks)


def body_pair(
    act_fwd, routes_fwd, weight_fwd, grad_bwd, routes_bwd, weight_bwd, saved_bwd, w_gate_up, w_down
):
    node = lax.axis_index("node")
    local = lax.axis_index("local")
    tokens_here = act_fwd.shape[1]
    capacity = 5 * tokens_here // 8
    w_gu = w_gate_up[0, 0]
    w_dn = w_down[0, 0]
    hidden_units = w_dn.shape[0]
    shape = (4, 2, capacity)

    act, grad = act_fwd[0], grad_bwd[0]
    route_a, route_b = routes_fwd[0, :, 0], routes_bwd[0, :, 0]
    sort_b = sorter(route_b)
    column = act.shape[1] // 4

    dy = (weight_bwd[0][:, None] * grad.astype(F32)).astype(BF16)
    cut_b = cut(dy, sort_b, local)
    got_b = [move(cut_b[m], by_local=-m) for m in (2, 1, 3)]
    saved = jnp.dot(sort_b, saved_bwd[0], preferred_element_type=F32).astype(BF16)
    (saved,) = after([saved], *cut_b[1:])
    saved_own, saved_other = windows(saved, node, capacity)
    saved_got = move(saved_other, by_node=1)
    placer_a = one_hot(window_rows(route_a, 0, capacity), 2 * capacity)
    packed_a = jnp.stack(
        [
            lax.dot_general(
                placer_a,
                act[:, j * column : (j + 1) * column],
                (((0,), (0,)), ((), ())),
                preferred_element_type=F32,
            )
            .astype(BF16)
            .reshape(2, capacity, column)
            for j in range(4)
        ],
        axis=1,
    ).reshape(8, capacity, column)
    *got_b, saved_got, packed_a = join(*got_b, saved_got, packed_a)

    def by_node(own, got, axis):
        return jnp.stack([jnp.where(node == 0, own, got), jnp.where(node == 0, got, own)], axis=axis)

    def homes(array, axis):
        return lambda slot: lax.dynamic_index_in_dim(
            array, (local + slot) % 4, axis=axis, keepdims=False
        )

    own_b, other_b = windows(
        jnp.stack([cut_b[0], got_b[1], got_b[0], got_b[2]]), node, capacity
    )
    got_bx = move(other_b, by_node=1)

    got_a = lax.all_to_all(packed_a, ("node", "local"), split_axis=0, concat_axis=0, tiled=True)
    act_wait, small_wait = after([act, jnp.stack([route_a.astype(F32), weight_fwd[0]])], other_b)
    act_next = move(act_wait, by_pp=1)
    small_next = move(small_wait, by_pp=1)

    rows_b = by_node(own_b, got_bx, 1).reshape(-1, column)
    part_b = dot_t(rows_b, w_dn).astype(BF16).reshape(shape + (hidden_units,))
    chain_b = sums(lambda slot: part_b[slot])
    pieces_b = next(chain_b)
    back_b = send(pieces_b)
    *back_b, act_next, small_next = join(*back_b, act_next, small_next)
    pieces_b = chain_b.send(back_b)
    back_b = send(pieces_b)

    part_a = jnp.dot(got_a.reshape(-1, column), w_gu, preferred_element_type=F32).astype(BF16)
    chain_a = sums(homes(part_a.reshape(2, 4, capacity, 2 * hidden_units), 1))
    pieces_a = next(chain_a)
    back_a = send(pieces_a)
    pieces_b = chain_b.send(back_b)
    back_b = send(pieces_b)
    back_a = after(back_a, *operands(pieces_b))
    back_b = after(back_b, *operands(pieces_a))
    dh = chain_b.send(back_b)

    saved_rows = by_node(saved_own, saved_got, 0)
    g = saved_rows[..., :hidden_units].astype(F32)
    u = saved_rows[..., hidden_units:].astype(F32)
    q = 1.0 / (1.0 + jnp.exp(-g))
    grad_gu = jnp.concatenate([dh * u * q * (1.0 + g * (1.0 - q)), dh * g * q], axis=-1).astype(
        BF16
    )
    chain_b = gathers(grad_gu, local)
    pieces_b = next(chain_b)
    back_b = send(pieces_b)
    for _ in (2, 3):
        back_a = after(back_a, *operands(pieces_b))
        pieces_a = chain_a.send(back_a)
        back_a = send(pieces_a)
        back_b = after(back_b, *operands(pieces_a))
        pieces_b = chain_b.send(back_b)
        back_b = send(pieces_b)
    back_a = after(back_a, *operands(pieces_b))
    preact = chain_a.send(back_a)
    hidden = (jax.nn.silu(preact[..., :hidden_units]) * preact[..., hidden_units:]).astype(BF16)
    all_hidden = [hidden] + [move(hidden, by_local=-m) for m in (1, 2, 3)]
    back_b = after(back_b, hidden)
    all_gu = chain_b.send(back_b)
    done_b = dot_t(all_gu.reshape(-1, 2 * hidden_units), w_gu).astype(BF16)
    done_b = done_b.reshape(shape + (column,))
    out_b = lax.dynamic_slice_in_dim(jnp.concatenate([done_b, done_b]), (4 - local) % 4, 4, axis=0)
    out_b = out_b.transpose(1, 0, 2, 3).reshape(8, capacity, column)
    home_b = lax.all_to_all(out_b, ("node", "local"), split_axis=0, concat_axis=0, tiled=True)

    done_a = jnp.dot(
        jnp.stack(all_hidden).reshape(-1, hidden_units), w_dn, preferred_element_type=F32
    ).astype(BF16)
    done_a = done_a.reshape(shape + (column,))
    home_a = send(
        returns(
            lambda slot, other: lax.dynamic_index_in_dim(done_a[slot], node ^ other, keepdims=False), 1
        )
    )

    blocks_b = [home_b[4 * n + j] for j in range(4) for n in (0, 1)]
    ones = jnp.ones((tokens_here,), F32)
    result_b = finish(
        grad, ones, window_rows(route_b, 0, capacity), blocks_b, jnp.arange(4, dtype=jnp.int32)
    )
    prev_grad = move(result_b, by_pp=-1)
    row_a = window_rows(small_next[0].astype(jnp.int32), node, capacity)
    at = jnp.stack([(local - m) % 4 for m in (2, 1, 3, 0)]).astype(jnp.int32)
    next_input = finish(act_next, small_next[1], row_a, home_a, at)
    return next_input, prev_grad


def from_behind(value, axis, by):
    length = lax.axis_size(axis)
    return lax.ppermute(value, axis, [(i, (i + by) % length) for i in range(length)])


def place_matrix(route, expert_count, capacity):
    onehot = (route[:, None] == jnp.arange(expert_count, dtype=jnp.int32)[None, :]).astype(
        jnp.int32
    )
    before = jnp.cumsum(onehot, axis=0) - onehot
    slot_index = jnp.sum(before * onehot, axis=1)
    target = route * capacity + slot_index
    positions = jnp.arange(expert_count * capacity, dtype=jnp.int32)
    return (positions[:, None] == target[None, :]).astype(jnp.bfloat16)


def pack_rows(placer, values, expert_count, capacity):
    packed = jnp.dot(placer, values, preferred_element_type=jnp.float32).astype(jnp.bfloat16)
    return packed.reshape(expert_count, capacity, values.shape[1])


def unpack_rows(placer, packed):
    flattened = packed.reshape(-1, packed.shape[-1])
    result = lax.dot_general(
        placer, flattened, (((0,), (0,)), ((), ())), preferred_element_type=jnp.float32
    )
    return result.astype(jnp.bfloat16)


def flat_outgoing(packed, local_count):
    expert_count, capacity, feature_count = packed.shape
    column = feature_count // local_count
    outgoing = packed.reshape(expert_count, capacity, local_count, column).transpose(0, 2, 1, 3)
    return outgoing.reshape(expert_count * local_count, capacity, column)


def flat_layout(received, expert_count, local_count):
    capacity = received.shape[1]
    column = received.shape[2]
    rows_in = received.reshape(expert_count, local_count, capacity, column).transpose(1, 0, 2, 3)
    return rows_in.reshape(-1, column)


def send_rows(packs, local_count):
    expert_count = packs[0].shape[0]
    outgoing = tuple((flat_outgoing(packed, local_count) for packed in packs))
    received = (
        lax.all_to_all(outgoing[0], ("node", "local"), split_axis=0, concat_axis=0, tiled=True),
        lax.all_to_all(outgoing[1], ("node", "local"), split_axis=0, concat_axis=0, tiled=True),
    )
    return tuple((flat_layout(item, expert_count, local_count) for item in received))


def return_rows(finished_pair, expert_count, capacity, local_count):
    column = finished_pair[0].shape[1]
    blocks = tuple(
        (item.reshape(local_count, expert_count, capacity, column) for item in finished_pair)
    )
    outgoing = tuple(
        (
            item.transpose(1, 0, 2, 3).reshape(expert_count * local_count, capacity, column)
            for item in blocks
        )
    )
    received = (
        lax.all_to_all(outgoing[0], ("node", "local"), split_axis=0, concat_axis=0, tiled=True),
        lax.all_to_all(outgoing[1], ("node", "local"), split_axis=0, concat_axis=0, tiled=True),
    )
    results = []
    for item in received:
        arranged = item.reshape(expert_count, local_count, capacity, column).transpose(0, 2, 1, 3)
        results.append(arranged.reshape(expert_count, capacity, local_count * column))
    return tuple(results)


def body(
    act_fwd, routes_fwd, weight_fwd, grad_bwd, routes_bwd, weight_bwd, saved_bwd, w_gate_up, w_down
):
    node_count = lax.axis_size("node")
    local_count = lax.axis_size("local")
    tokens_here = act_fwd.shape[1]
    capacity = 5 * tokens_here // (4 * node_count)
    rows_each = node_count * capacity
    w_gu = w_gate_up[0, 0]
    w_dn = w_down[0, 0]
    hidden_units = w_dn.shape[0]
    tokens_a = act_fwd[0]
    placer_a = place_matrix(routes_fwd[0, :, 0], node_count, capacity)
    cotangent = grad_bwd[0]
    placer_b = place_matrix(routes_bwd[0, :, 0], node_count, capacity)
    scaled = (weight_bwd[0][:, None] * cotangent.astype(jnp.float32)).astype(jnp.bfloat16)
    packed_a = pack_rows(placer_a, tokens_a, node_count, capacity)
    packed_b = pack_rows(placer_b, scaled, node_count, capacity)
    rows_a, rows_b = send_rows((packed_a, packed_b), local_count)
    saved_packed = pack_rows(placer_b, saved_bwd[0], node_count, capacity)
    saved_rows = lax.all_to_all(
        saved_packed, "node", split_axis=0, concat_axis=0, tiled=True
    ).reshape(rows_each, -1)
    row_block = rows_a
    preact = lax.psum_scatter(
        jnp.dot(row_block, w_gu, preferred_element_type=jnp.float32).astype(jnp.bfloat16),
        "local",
        scatter_dimension=0,
        tiled=True,
    ).astype(jnp.float32)
    row_block = rows_b
    grad_hidden = lax.psum_scatter(
        lax.dot_general(
            row_block, w_dn, (((1,), (1,)), ((), ())), preferred_element_type=jnp.float32
        ).astype(jnp.bfloat16),
        "local",
        scatter_dimension=0,
        tiled=True,
    ).astype(jnp.float32)
    hidden = (jax.nn.silu(preact[:, :hidden_units]) * preact[:, hidden_units:]).astype(jnp.bfloat16)
    done_a = jnp.dot(
        lax.all_gather(hidden, "local", axis=0, tiled=True),
        w_dn,
        preferred_element_type=jnp.float32,
    ).astype(jnp.bfloat16)
    gate_pre = saved_rows[:, :hidden_units].astype(jnp.float32)
    up_pre = saved_rows[:, hidden_units:].astype(jnp.float32)
    sigmoid_g = 1.0 / (1.0 + jnp.exp(-gate_pre))
    grad_gate = grad_hidden * up_pre * sigmoid_g * (1.0 + gate_pre * (1.0 - sigmoid_g))
    grad_up = grad_hidden * gate_pre * sigmoid_g
    grad_gu = jnp.concatenate([grad_gate, grad_up], axis=1).astype(jnp.bfloat16)
    product = lax.dot_general(
        lax.all_gather(grad_gu, "local", axis=0, tiled=True),
        w_gu,
        (((1,), (1,)), ((), ())),
        preferred_element_type=jnp.float32,
    )
    done_b = product.astype(jnp.bfloat16)
    back_a, back_b = return_rows((done_a, done_b), node_count, capacity, local_count)
    moe_a = unpack_rows(placer_a, back_a)
    result_a = tokens_a.astype(jnp.float32) + weight_fwd[0][:, None] * moe_a.astype(jnp.float32)
    result_a = result_a.astype(jnp.bfloat16)
    moe_b = unpack_rows(placer_b, back_b)
    result_b = (cotangent.astype(jnp.float32) + moe_b.astype(jnp.float32)).astype(jnp.bfloat16)
    next_input = from_behind(result_a[None], "pp", 1)
    prev_grad = from_behind(result_b[None], "pp", -1)
    return (next_input, prev_grad)


def solution(mesh):
    in_specs = (
        P("pp", ("node", "local"), None),
        P("pp", ("node", "local"), None),
        P("pp", ("node", "local")),
        P("pp", ("node", "local"), None),
        P("pp", ("node", "local"), None),
        P("pp", ("node", "local")),
        P("pp", ("node", "local"), None),
        P("pp", "node", "local", None),
        P("pp", "node", None, "local"),
    )
    out_specs = (P("pp", ("node", "local"), None), P("pp", ("node", "local"), None))
    paired = mesh.shape["node"] == 2 and mesh.shape["local"] == 4
    plan = body_pair if paired else body
    return jax.shard_map(plan, mesh=mesh, in_specs=in_specs, out_specs=out_specs, check_vma=False)
```

```python
import jax
import jax.numpy as jnp
from jax import lax
from jax.experimental import pallas as pl
from jax.experimental.pallas import tpu as pltpu
from jax.sharding import PartitionSpec as P

F32 = jnp.float32
BF16 = jnp.bfloat16
AXES = ("pp", "node", "local")


def move(value, by_pp=0, by_node=0, by_local=0, wrap=True, first=0, last=None):
    pps, nodes, locs = (lax.axis_size(a) for a in AXES)
    last = locs - 1 if last is None else last
    pairs = []
    for s in range(pps):
        for n in range(nodes):
            for l in range(locs):
                to = l + by_local
                if not wrap and not (first <= l <= last and 0 <= to < locs):
                    continue
                source = (s * nodes + n) * locs + l
                target = (((s + by_pp) % pps) * nodes + (n ^ by_node)) * locs + to % locs
                pairs.append((source, target))
    return lax.ppermute(value, AXES, pairs)


def sorted_places(route):
    ones = route.astype(F32)
    count = route.shape[0]
    earlier = (jnp.arange(count)[None, :] < jnp.arange(count)[:, None]).astype(F32)
    ones_before = jnp.dot(earlier, ones[:, None], preferred_element_type=F32)[:, 0]
    zeros = count - jnp.sum(ones)
    index = jnp.arange(count, dtype=F32)
    place = jnp.where(route == 0, index - ones_before, zeros + ones_before)
    return place.astype(jnp.int32)


def sorter(route):
    place = sorted_places(route)
    rows = jnp.arange(route.shape[0], dtype=jnp.int32)
    return (rows[:, None] == place[None, :]).astype(BF16)


def window_rows(route, first, capacity):
    place = sorted_places(route)
    start = route.shape[0] - capacity
    in_window = place - jnp.where(route == 1, start, 0)
    return jnp.where(route == first, in_window, in_window + capacity)


def one_hot(row, count):
    return (row[:, None] == jnp.arange(count, dtype=jnp.int32)[None, :]).astype(BF16)


def dot_t(left, right):
    return lax.dot_general(left, right, (((1,), (1,)), ((), ())), preferred_element_type=F32)


def windows(blocks, node, capacity):
    tokens = blocks.shape[-2]
    start = tokens - capacity
    low = lax.slice_in_dim(blocks, 0, capacity, axis=-2 + blocks.ndim)
    high = lax.slice_in_dim(blocks, start, tokens, axis=-2 + blocks.ndim)
    own = jnp.where(node == 0, low, high)
    other = jnp.where(node == 0, high, low)
    return own, other


def join(*values):
    return lax.optimization_barrier(values)


def after(values, *others):
    return list(join(*values, *others)[: len(values)])


def cut(tokens, placer, local):
    column = tokens.shape[1] // 4
    blocks = []
    for m in range(4):
        block = lax.dynamic_slice_in_dim(tokens, ((local - m) % 4) * column, column, axis=1)
        blocks.append(jnp.dot(placer, block, preferred_element_type=F32).astype(BF16))
    return blocks


def sums(partial):
    right, left = partial(3), partial(1)
    for step in (1, 2, 3):
        right, left = right.astype(BF16), left.astype(BF16)
        got_r, got_l = yield (
            (right, dict(by_local=1, wrap=False, last=step - 1)),
            (left, dict(by_local=-1, wrap=False, first=4 - step)),
        )
        right = partial(3 - step).astype(F32) + got_r.astype(F32)
        if step < 3:
            left = partial(step + 1).astype(F32) + got_l.astype(F32)
    yield right + got_l.astype(F32)


def gathers(rows, local):
    from_left, from_right = [rows], [rows]
    for step in (1, 2, 3):
        got_r, got_l = yield (
            (from_left[-1], dict(by_local=1, wrap=False, first=step - 1)),
            (from_right[-1], dict(by_local=-1, wrap=False, last=4 - step)),
        )
        from_left.append(got_r)
        from_right.append(got_l)
    slots = [rows]
    for m in (1, 2, 3):
        slots.append(jnp.where(local + m < 4, from_right[m], from_left[4 - m]))
    yield jnp.stack(slots)


def send(pieces):
    return [move(value, **how) for value, how in pieces]


def operands(pieces):
    return [value for value, _ in pieces]


def valid(zeros, node, tokens, capacity):
    row = jnp.arange(capacity, dtype=F32)[None, :]
    return jnp.where(node == 0, row < zeros[:, None], row + (tokens - capacity) >= zeros[:, None])


def merge(own, other, node, tokens):
    slots, capacity, column = own.shape
    low = jnp.where(node == 0, own, other)
    high = jnp.where(node == 0, other, own)
    rest = jnp.zeros((slots, tokens - capacity, column), own.dtype)
    return jnp.concatenate([low, rest], axis=1) + jnp.concatenate([rest, high], axis=1)


def homeward(merged, by_pp):
    return [(merged[m], dict(by_pp=by_pp, by_local=m)) for m in (2, 1, 3, 0)]


def finish_kernel(at_ref, residual_ref, weight_ref, pick_ref, *refs):
    *blocks, out_ref, rows, sem = refs
    count = len(blocks)
    column = rows.shape[-1]
    copies = [pltpu.make_async_copy(blocks[i], rows.at[i], sem.at[i]) for i in range(count)]
    for copy in copies:
        copy.start()
    for i in range(count):
        copies[i].wait()
        cols = pl.ds(pl.multiple_of(at_ref[i] * column, column), column)
        moe = jnp.dot(pick_ref[...], rows[i], preferred_element_type=F32)
        total = residual_ref[:, cols].astype(F32) + weight_ref[...] * moe
        out_ref[0, :, cols] = total.astype(out_ref.dtype)


def finish(residual, weight, place, blocks, at):
    column = blocks[0].shape[-1]
    tokens, features = residual.shape
    vmem = pl.BlockSpec(memory_space=pltpu.VMEM)
    anywhere = pl.BlockSpec(memory_space=pl.ANY)
    return pl.pallas_call(
        finish_kernel,
        out_shape=jax.ShapeDtypeStruct((1, tokens, features), BF16),
        in_specs=[pl.BlockSpec(memory_space=pltpu.SMEM)] + [vmem] * 3 + [anywhere] * len(blocks),
        out_specs=vmem,
        scratch_shapes=[
            pltpu.VMEM((len(blocks), tokens, column), BF16),
            pltpu.SemaphoreType.DMA((len(blocks),)),
        ],
        compiler_params=pltpu.CompilerParams(vmem_limit_bytes=8 * 2**20),
        name="finish",
    )(at, residual, weight[:, None], one_hot(place, tokens), *blocks)


def body_pair(
    act_fwd, routes_fwd, weight_fwd, grad_bwd, routes_bwd, weight_bwd, saved_bwd, w_gate_up, w_down
):
    node = lax.axis_index("node")
    local = lax.axis_index("local")
    tokens_here = act_fwd.shape[1]
    capacity = 5 * tokens_here // 8
    w_gu = w_gate_up[0, 0]
    w_dn = w_down[0, 0]
    hidden_units = w_dn.shape[0]
    shape = (4, 2, capacity)

    act, grad = act_fwd[0], grad_bwd[0]
    route_a, route_b = routes_fwd[0, :, 0], routes_bwd[0, :, 0]
    sort_b = sorter(route_b)
    zeros = tokens_here - jnp.stack([jnp.sum(route_a), jnp.sum(route_b)]).astype(F32)
    column = act.shape[1] // 4

    dy = (weight_bwd[0][:, None] * grad.astype(F32)).astype(BF16)
    cut_b = cut(dy, sort_b, local)
    got_b = [move(cut_b[m], by_local=-m) for m in (2, 1, 3)]
    saved = jnp.dot(sort_b, saved_bwd[0], preferred_element_type=F32).astype(BF16)
    (saved,) = after([saved], *cut_b[1:])
    saved_own, saved_other = windows(saved, node, capacity)
    saved_got = move(saved_other, by_node=1)
    zeros_got = move(after([zeros], saved_other)[0], by_node=1)
    placer_a = one_hot(window_rows(route_a, 0, capacity), 2 * capacity)
    packed_a = jnp.stack(
        [
            lax.dot_general(
                placer_a,
                act[:, j * column : (j + 1) * column],
                (((0,), (0,)), ((), ())),
                preferred_element_type=F32,
            )
            .astype(BF16)
            .reshape(2, capacity, column)
            for j in range(4)
        ],
        axis=1,
    ).reshape(8, capacity, column)
    *got_b, saved_got, zeros_got, packed_a = join(*got_b, saved_got, zeros_got, packed_a)

    def by_node(own, got, axis):
        return jnp.stack([jnp.where(node == 0, own, got), jnp.where(node == 0, got, own)], axis=axis)

    def homes(array, axis):
        return lambda slot: lax.dynamic_index_in_dim(
            array, (local + slot) % 4, axis=axis, keepdims=False
        )

    zeros = by_node(zeros, zeros_got, 0)

    own_b, other_b = windows(
        jnp.stack([cut_b[0], got_b[1], got_b[0], got_b[2]]), node, capacity
    )
    got_bx = move(other_b, by_node=1)

    got_a = lax.all_to_all(packed_a, ("node", "local"), split_axis=0, concat_axis=0, tiled=True)
    act_wait, small_wait = after([act, jnp.stack([route_a.astype(F32), weight_fwd[0]])], other_b)
    act_next = move(act_wait, by_pp=1)
    small_next = move(small_wait, by_pp=1)

    rows_b = by_node(own_b, got_bx, 1).reshape(-1, column)
    part_b = dot_t(rows_b, w_dn).astype(BF16).reshape(shape + (hidden_units,))
    chain_b = sums(lambda slot: part_b[slot])
    pieces_b = next(chain_b)
    back_b = send(pieces_b)
    *back_b, got_a, act_next, small_next = join(*back_b, got_a, act_next, small_next)
    pieces_b = chain_b.send(back_b)
    back_b = send(pieces_b)

    part_a = jnp.dot(got_a.reshape(-1, column), w_gu, preferred_element_type=F32).astype(BF16)
    chain_a = sums(homes(part_a.reshape(2, 4, capacity, 2 * hidden_units), 1))
    pieces_a = next(chain_a)
    back_a = send(pieces_a)
    pieces_b = chain_b.send(back_b)
    back_b = send(pieces_b)
    grad_wait, route_wait = after([grad, route_b], *operands(pieces_a))
    grad_next = move(grad_wait, by_pp=-1)
    route_b_next = move(route_wait, by_pp=-1)
    back_a = after(back_a, *operands(pieces_b))
    dh = chain_b.send(back_b)

    saved_rows = by_node(saved_own, saved_got, 0)
    g = saved_rows[..., :hidden_units].astype(F32)
    u = saved_rows[..., hidden_units:].astype(F32)
    q = 1.0 / (1.0 + jnp.exp(-g))
    dh = jnp.where(valid(zeros[:, 1], node, tokens_here, capacity)[..., None], dh, 0.0)
    grad_gu = jnp.concatenate([dh * u * q * (1.0 + g * (1.0 - q)), dh * g * q], axis=-1).astype(
        BF16
    )
    chain_b = gathers(grad_gu, local)
    pieces_b = next(chain_b)
    back_b = send(pieces_b)
    *back_a, grad_next, route_b_next = join(*back_a, grad_next, route_b_next, *operands(pieces_b))[:4]
    for _ in (2, 3):
        back_a = after(back_a, *operands(pieces_b))
        pieces_a = chain_a.send(back_a)
        back_a = send(pieces_a)
        back_b = after(back_b, *operands(pieces_a))
        pieces_b = chain_b.send(back_b)
        back_b = send(pieces_b)
    back_a = after(back_a, *operands(pieces_b))
    preact = chain_a.send(back_a)
    preact = jnp.where(valid(zeros[:, 0], node, tokens_here, capacity)[..., None], preact, 0.0)
    hidden = (jax.nn.silu(preact[..., :hidden_units]) * preact[..., hidden_units:]).astype(BF16)
    all_hidden = [hidden] + [move(hidden, by_local=-m) for m in (1, 2, 3)]
    back_b = after(back_b, hidden)
    all_gu = chain_b.send(back_b)
    done_b = dot_t(all_gu.reshape(-1, 2 * hidden_units), w_gu).astype(BF16)
    done_b = done_b.reshape(shape + (column,))

    def split(done):
        own = lax.dynamic_index_in_dim(done, node, axis=1, keepdims=False)
        other = lax.dynamic_index_in_dim(done, 1 - node, axis=1, keepdims=False)
        return own, other

    own_b, other_b = split(done_b)
    got_b = move(other_b, by_node=1)
    all_hidden = after(all_hidden, other_b)
    done_a = jnp.dot(
        jnp.stack(all_hidden).reshape(-1, hidden_units), w_dn, preferred_element_type=F32
    ).astype(BF16)
    own_a, other_a = split(done_a.reshape(shape + (column,)))
    got_a = move(other_a, by_node=1)
    home_b = send(homeward(merge(own_b, got_b, node, tokens_here), -1))
    home_a = send(homeward(merge(own_a, got_a, node, tokens_here), 1))

    at = jnp.stack([(local - m) % 4 for m in (2, 1, 3, 0)]).astype(jnp.int32)
    ones = jnp.ones((tokens_here,), F32)
    prev_grad = finish(grad_next, ones, sorted_places(route_b_next), home_b, at)
    place_a = sorted_places(small_next[0].astype(jnp.int32))
    next_input = finish(act_next, small_next[1], place_a, home_a, at)
    return next_input, prev_grad


def from_behind(value, axis, by):
    length = lax.axis_size(axis)
    return lax.ppermute(value, axis, [(i, (i + by) % length) for i in range(length)])


def place_matrix(route, expert_count, capacity):
    onehot = (route[:, None] == jnp.arange(expert_count, dtype=jnp.int32)[None, :]).astype(
        jnp.int32
    )
    before = jnp.cumsum(onehot, axis=0) - onehot
    slot_index = jnp.sum(before * onehot, axis=1)
    target = route * capacity + slot_index
    positions = jnp.arange(expert_count * capacity, dtype=jnp.int32)
    return (positions[:, None] == target[None, :]).astype(jnp.bfloat16)


def pack_rows(placer, values, expert_count, capacity):
    packed = jnp.dot(placer, values, preferred_element_type=jnp.float32).astype(jnp.bfloat16)
    return packed.reshape(expert_count, capacity, values.shape[1])


def unpack_rows(placer, packed):
    flattened = packed.reshape(-1, packed.shape[-1])
    result = lax.dot_general(
        placer, flattened, (((0,), (0,)), ((), ())), preferred_element_type=jnp.float32
    )
    return result.astype(jnp.bfloat16)


def flat_outgoing(packed, local_count):
    expert_count, capacity, feature_count = packed.shape
    column = feature_count // local_count
    outgoing = packed.reshape(expert_count, capacity, local_count, column).transpose(0, 2, 1, 3)
    return outgoing.reshape(expert_count * local_count, capacity, column)


def flat_layout(received, expert_count, local_count):
    capacity = received.shape[1]
    column = received.shape[2]
    rows_in = received.reshape(expert_count, local_count, capacity, column).transpose(1, 0, 2, 3)
    return rows_in.reshape(-1, column)


def send_rows(packs, local_count):
    expert_count = packs[0].shape[0]
    outgoing = tuple((flat_outgoing(packed, local_count) for packed in packs))
    received = (
        lax.all_to_all(outgoing[0], ("node", "local"), split_axis=0, concat_axis=0, tiled=True),
        lax.all_to_all(outgoing[1], ("node", "local"), split_axis=0, concat_axis=0, tiled=True),
    )
    return tuple((flat_layout(item, expert_count, local_count) for item in received))


def return_rows(finished_pair, expert_count, capacity, local_count):
    column = finished_pair[0].shape[1]
    blocks = tuple(
        (item.reshape(local_count, expert_count, capacity, column) for item in finished_pair)
    )
    outgoing = tuple(
        (
            item.transpose(1, 0, 2, 3).reshape(expert_count * local_count, capacity, column)
            for item in blocks
        )
    )
    received = (
        lax.all_to_all(outgoing[0], ("node", "local"), split_axis=0, concat_axis=0, tiled=True),
        lax.all_to_all(outgoing[1], ("node", "local"), split_axis=0, concat_axis=0, tiled=True),
    )
    results = []
    for item in received:
        arranged = item.reshape(expert_count, local_count, capacity, column).transpose(0, 2, 1, 3)
        results.append(arranged.reshape(expert_count, capacity, local_count * column))
    return tuple(results)


def body(
    act_fwd, routes_fwd, weight_fwd, grad_bwd, routes_bwd, weight_bwd, saved_bwd, w_gate_up, w_down
):
    node_count = lax.axis_size("node")
    local_count = lax.axis_size("local")
    tokens_here = act_fwd.shape[1]
    capacity = 5 * tokens_here // (4 * node_count)
    rows_each = node_count * capacity
    w_gu = w_gate_up[0, 0]
    w_dn = w_down[0, 0]
    hidden_units = w_dn.shape[0]
    tokens_a = act_fwd[0]
    placer_a = place_matrix(routes_fwd[0, :, 0], node_count, capacity)
    cotangent = grad_bwd[0]
    placer_b = place_matrix(routes_bwd[0, :, 0], node_count, capacity)
    scaled = (weight_bwd[0][:, None] * cotangent.astype(jnp.float32)).astype(jnp.bfloat16)
    packed_a = pack_rows(placer_a, tokens_a, node_count, capacity)
    packed_b = pack_rows(placer_b, scaled, node_count, capacity)
    rows_a, rows_b = send_rows((packed_a, packed_b), local_count)
    saved_packed = pack_rows(placer_b, saved_bwd[0], node_count, capacity)
    saved_rows = lax.all_to_all(
        saved_packed, "node", split_axis=0, concat_axis=0, tiled=True
    ).reshape(rows_each, -1)
    row_block = rows_a
    preact = lax.psum_scatter(
        jnp.dot(row_block, w_gu, preferred_element_type=jnp.float32).astype(jnp.bfloat16),
        "local",
        scatter_dimension=0,
        tiled=True,
    ).astype(jnp.float32)
    row_block = rows_b
    grad_hidden = lax.psum_scatter(
        lax.dot_general(
            row_block, w_dn, (((1,), (1,)), ((), ())), preferred_element_type=jnp.float32
        ).astype(jnp.bfloat16),
        "local",
        scatter_dimension=0,
        tiled=True,
    ).astype(jnp.float32)
    hidden = (jax.nn.silu(preact[:, :hidden_units]) * preact[:, hidden_units:]).astype(jnp.bfloat16)
    done_a = jnp.dot(
        lax.all_gather(hidden, "local", axis=0, tiled=True),
        w_dn,
        preferred_element_type=jnp.float32,
    ).astype(jnp.bfloat16)
    gate_pre = saved_rows[:, :hidden_units].astype(jnp.float32)
    up_pre = saved_rows[:, hidden_units:].astype(jnp.float32)
    sigmoid_g = 1.0 / (1.0 + jnp.exp(-gate_pre))
    grad_gate = grad_hidden * up_pre * sigmoid_g * (1.0 + gate_pre * (1.0 - sigmoid_g))
    grad_up = grad_hidden * gate_pre * sigmoid_g
    grad_gu = jnp.concatenate([grad_gate, grad_up], axis=1).astype(jnp.bfloat16)
    product = lax.dot_general(
        lax.all_gather(grad_gu, "local", axis=0, tiled=True),
        w_gu,
        (((1,), (1,)), ((), ())),
        preferred_element_type=jnp.float32,
    )
    done_b = product.astype(jnp.bfloat16)
    back_a, back_b = return_rows((done_a, done_b), node_count, capacity, local_count)
    moe_a = unpack_rows(placer_a, back_a)
    result_a = tokens_a.astype(jnp.float32) + weight_fwd[0][:, None] * moe_a.astype(jnp.float32)
    result_a = result_a.astype(jnp.bfloat16)
    moe_b = unpack_rows(placer_b, back_b)
    result_b = (cotangent.astype(jnp.float32) + moe_b.astype(jnp.float32)).astype(jnp.bfloat16)
    next_input = from_behind(result_a[None], "pp", 1)
    prev_grad = from_behind(result_b[None], "pp", -1)
    return (next_input, prev_grad)


def solution(mesh):
    in_specs = (
        P("pp", ("node", "local"), None),
        P("pp", ("node", "local"), None),
        P("pp", ("node", "local")),
        P("pp", ("node", "local"), None),
        P("pp", ("node", "local"), None),
        P("pp", ("node", "local")),
        P("pp", ("node", "local"), None),
        P("pp", "node", "local", None),
        P("pp", "node", None, "local"),
    )
    out_specs = (P("pp", ("node", "local"), None), P("pp", ("node", "local"), None))
    paired = mesh.shape["node"] == 2 and mesh.shape["local"] == 4
    plan = body_pair if paired else body
    return jax.shard_map(plan, mesh=mesh, in_specs=in_specs, out_specs=out_specs, check_vma=False)
```

```python
import jax
import jax.numpy as jnp
from jax import lax
from jax.experimental import pallas as pl
from jax.experimental.pallas import tpu as pltpu
from jax.sharding import PartitionSpec as P

F32 = jnp.float32
BF16 = jnp.bfloat16
AXES = ("pp", "node", "local")


def move(value, by_pp=0, by_node=0, by_local=0, wrap=True, first=0, last=None):
    pps, nodes, locs = (lax.axis_size(a) for a in AXES)
    last = locs - 1 if last is None else last
    pairs = []
    for s in range(pps):
        for n in range(nodes):
            for l in range(locs):
                to = l + by_local
                if not wrap and not (first <= l <= last and 0 <= to < locs):
                    continue
                source = (s * nodes + n) * locs + l
                target = (((s + by_pp) % pps) * nodes + (n ^ by_node)) * locs + to % locs
                pairs.append((source, target))
    return lax.ppermute(value, AXES, pairs)


def sorted_places(route):
    ones = route.astype(F32)
    count = route.shape[0]
    earlier = (jnp.arange(count)[None, :] < jnp.arange(count)[:, None]).astype(F32)
    ones_before = jnp.dot(earlier, ones[:, None], preferred_element_type=F32)[:, 0]
    zeros = count - jnp.sum(ones)
    index = jnp.arange(count, dtype=F32)
    place = jnp.where(route == 0, index - ones_before, zeros + ones_before)
    return place.astype(jnp.int32)


def sorter(route):
    place = sorted_places(route)
    rows = jnp.arange(route.shape[0], dtype=jnp.int32)
    return (rows[:, None] == place[None, :]).astype(BF16)


def one_hot(row, count):
    return (row[:, None] == jnp.arange(count, dtype=jnp.int32)[None, :]).astype(BF16)


def dot_t(left, right):
    return lax.dot_general(left, right, (((1,), (1,)), ((), ())), preferred_element_type=F32)


def windows(blocks, node, capacity):
    tokens = blocks.shape[-2]
    start = tokens - capacity
    low = lax.slice_in_dim(blocks, 0, capacity, axis=-2 + blocks.ndim)
    high = lax.slice_in_dim(blocks, start, tokens, axis=-2 + blocks.ndim)
    own = jnp.where(node == 0, low, high)
    other = jnp.where(node == 0, high, low)
    return own, other


def join(*values):
    return lax.optimization_barrier(values)


def after(values, *others):
    return list(join(*values, *others)[: len(values)])


def cut(tokens, placer, local):
    column = tokens.shape[1] // 4
    blocks = []
    for m in range(4):
        block = lax.dynamic_slice_in_dim(tokens, ((local - m) % 4) * column, column, axis=1)
        blocks.append(jnp.dot(placer, block, preferred_element_type=F32).astype(BF16))
    return blocks


def sums(partial):
    right, left = partial(3), partial(1)
    for step in (1, 2, 3):
        right, left = right.astype(BF16), left.astype(BF16)
        got_r, got_l = yield (
            (right, dict(by_local=1, wrap=False, last=step - 1)),
            (left, dict(by_local=-1, wrap=False, first=4 - step)),
        )
        right = partial(3 - step).astype(F32) + got_r.astype(F32)
        if step < 3:
            left = partial(step + 1).astype(F32) + got_l.astype(F32)
    yield right + got_l.astype(F32)


def gathers(rows, local):
    from_left, from_right = [rows], [rows]
    for step in (1, 2, 3):
        got_r, got_l = yield (
            (from_left[-1], dict(by_local=1, wrap=False, first=step - 1)),
            (from_right[-1], dict(by_local=-1, wrap=False, last=4 - step)),
        )
        from_left.append(got_r)
        from_right.append(got_l)
    slots = [rows]
    for m in (1, 2, 3):
        slots.append(jnp.where(local + m < 4, from_right[m], from_left[4 - m]))
    yield jnp.stack(slots)


def send(pieces):
    return [move(value, **how) for value, how in pieces]


def operands(pieces):
    return [value for value, _ in pieces]


def valid(zeros, node, tokens, capacity):
    row = jnp.arange(capacity, dtype=F32)[None, :]
    return jnp.where(node == 0, row < zeros[:, None], row + (tokens - capacity) >= zeros[:, None])


def merge(own, other, node, tokens):
    slots, capacity, column = own.shape
    low = jnp.where(node == 0, own, other)
    high = jnp.where(node == 0, other, own)
    rest = jnp.zeros((slots, tokens - capacity, column), own.dtype)
    return jnp.concatenate([low, rest], axis=1) + jnp.concatenate([rest, high], axis=1)


def homeward(merged, by_pp):
    return [(merged[m], dict(by_pp=by_pp, by_local=m)) for m in (2, 1, 3, 0)]


def finish_kernel(at_ref, residual_ref, weight_ref, pick_ref, *refs):
    *blocks, out_ref, rows, sem = refs
    count = len(blocks)
    column = rows.shape[-1]
    copies = [pltpu.make_async_copy(blocks[i], rows.at[i], sem.at[i]) for i in range(count)]
    for copy in copies:
        copy.start()
    for i in range(count):
        copies[i].wait()
        cols = pl.ds(pl.multiple_of(at_ref[i] * column, column), column)
        moe = jnp.dot(pick_ref[...], rows[i], preferred_element_type=F32)
        total = residual_ref[:, cols].astype(F32) + weight_ref[...] * moe
        out_ref[0, :, cols] = total.astype(out_ref.dtype)


def finish(residual, weight, place, blocks, at):
    column = blocks[0].shape[-1]
    tokens, features = residual.shape
    vmem = pl.BlockSpec(memory_space=pltpu.VMEM)
    anywhere = pl.BlockSpec(memory_space=pl.ANY)
    return pl.pallas_call(
        finish_kernel,
        out_shape=jax.ShapeDtypeStruct((1, tokens, features), BF16),
        in_specs=[pl.BlockSpec(memory_space=pltpu.SMEM)] + [vmem] * 3 + [anywhere] * len(blocks),
        out_specs=vmem,
        scratch_shapes=[
            pltpu.VMEM((len(blocks), tokens, column), BF16),
            pltpu.SemaphoreType.DMA((len(blocks),)),
        ],
        compiler_params=pltpu.CompilerParams(vmem_limit_bytes=8 * 2**20),
        name="finish",
    )(at, residual, weight[:, None], one_hot(place, tokens), *blocks)


def body_pair(
    act_fwd, routes_fwd, weight_fwd, grad_bwd, routes_bwd, weight_bwd, saved_bwd, w_gate_up, w_down
):
    node = lax.axis_index("node")
    local = lax.axis_index("local")
    tokens_here = act_fwd.shape[1]
    capacity = 5 * tokens_here // 8
    w_gu = w_gate_up[0, 0]
    w_dn = w_down[0, 0]
    hidden_units = w_dn.shape[0]
    shape = (4, 2, capacity)

    act, grad = act_fwd[0], grad_bwd[0]
    route_a, route_b = routes_fwd[0, :, 0], routes_bwd[0, :, 0]
    sort_a, sort_b = sorter(route_a), sorter(route_b)
    zeros = tokens_here - jnp.stack([jnp.sum(route_a), jnp.sum(route_b)]).astype(F32)

    def in_rows(cuts, got):
        return windows(jnp.stack([cuts[0], got[1], got[0], got[2]]), node, capacity)

    def by_node(own, got, axis):
        return jnp.stack([jnp.where(node == 0, own, got), jnp.where(node == 0, got, own)], axis=axis)

    def split(done):
        own = lax.dynamic_index_in_dim(done, node, axis=1, keepdims=False)
        other = lax.dynamic_index_in_dim(done, 1 - node, axis=1, keepdims=False)
        return own, other

    def turn(chain, back, *others):
        pieces = chain.send(after(back, *others))
        return operands(pieces), send(pieces)

    cut_a = cut(act, sort_a, local)
    got_a = [move(cut_a[m], by_local=-m) for m in (2, 1, 3)]
    dy = (weight_bwd[0][:, None] * grad.astype(F32)).astype(BF16)
    cut_b = cut(dy, sort_b, local)
    *got_a, b0, b1, b2, b3 = join(*got_a, *cut_b)
    cut_b = [b0, b1, b2, b3]
    got_b = [move(cut_b[m], by_local=-m) for m in (2, 1, 3)]
    own_a, other_a = in_rows(cut_a, got_a)
    column = own_a.shape[-1]
    got_ax = move(other_a, by_node=1)
    act_next = move(after([act], other_a)[0], by_pp=1)
    *got_b, got_ax, act_next = join(*got_b, got_ax, act_next)

    rows_a = by_node(own_a, got_ax, 1).reshape(-1, column)
    part_a = jnp.dot(rows_a, w_gu, preferred_element_type=F32).astype(BF16)
    part_a = part_a.reshape(shape + (2 * hidden_units,))
    own_b, other_b = in_rows(cut_b, got_b)
    got_bx = move(other_b, by_node=1)
    chain_a = sums(lambda slot: part_a[slot])
    pieces = next(chain_a)
    back_a = send(pieces)
    small, zeros_wait = after(
        [jnp.stack([route_a.astype(F32), weight_fwd[0]]), zeros], *operands(pieces)
    )
    small_next = move(small, by_pp=1)
    zeros_got = move(zeros_wait, by_node=1)
    *back_a, got_bx, small_next, zeros_got = join(*back_a, got_bx, small_next, zeros_got)
    zeros = by_node(zeros, zeros_got, 0)

    values_a, back_a = turn(chain_a, back_a)
    rows_b = by_node(own_b, got_bx, 1).reshape(-1, column)
    part_b = dot_t(rows_b, w_dn).astype(BF16).reshape(shape + (hidden_units,))
    chain_b = sums(lambda slot: part_b[slot])
    pieces = next(chain_b)
    back_b = send(pieces)
    saved = jnp.dot(sort_b, saved_bwd[0], preferred_element_type=F32).astype(BF16)
    saved_own, saved_other = windows(saved, node, capacity)
    (saved_other,) = after([saved_other], *values_a)
    saved_got = move(saved_other, by_node=1)
    *back_b, saved_got = join(*back_b, saved_got, *values_a)[:3]

    values_b, back_b = turn(chain_b, back_b)
    grad_wait, route_wait = after([grad, route_b], *values_b)
    grad_next = move(grad_wait, by_pp=-1)
    route_b_next = move(route_wait, by_pp=-1)
    values_a, back_a = turn(chain_a, back_a, *values_b)
    *back_b, grad_next, route_b_next = join(*back_b, grad_next, route_b_next, *values_a)[:4]
    values_b, back_b = turn(chain_b, back_b)

    preact = chain_a.send(after(back_a, *values_b))
    preact = jnp.where(valid(zeros[:, 0], node, tokens_here, capacity)[..., None], preact, 0.0)
    hidden = (jax.nn.silu(preact[..., :hidden_units]) * preact[..., hidden_units:]).astype(BF16)
    all_hidden = [move(hidden, by_local=-m) for m in (1, 2, 3)]

    dh = chain_b.send(after(back_b, hidden))
    dh = jnp.where(valid(zeros[:, 1], node, tokens_here, capacity)[..., None], dh, 0.0)
    saved_rows = by_node(saved_own, saved_got, 0)
    g = saved_rows[..., :hidden_units].astype(F32)
    u = saved_rows[..., hidden_units:].astype(F32)
    q = 1.0 / (1.0 + jnp.exp(-g))
    grad_gu = jnp.concatenate([dh * u * q * (1.0 + g * (1.0 - q)), dh * g * q], axis=-1).astype(
        BF16
    )
    chain_b = gathers(grad_gu, local)
    pieces = next(chain_b)
    back_b = send(pieces)
    *back_b, h1, h2, h3 = join(*back_b, *all_hidden)
    all_hidden = jnp.stack([hidden, h1, h2, h3])
    values_b, back_b = turn(chain_b, back_b)

    done_a = jnp.dot(
        all_hidden.reshape(-1, hidden_units), w_dn, preferred_element_type=F32
    ).astype(BF16)
    own_a, other_a = split(done_a.reshape(shape + (column,)))
    got_a = move(other_a, by_node=1)
    *back_b, got_a = join(*back_b, got_a)
    values_b, back_b = turn(chain_b, back_b)
    home_a = send(homeward(merge(own_a, got_a, node, tokens_here), 1))
    all_gu = chain_b.send(back_b)
    done_b = dot_t(all_gu.reshape(-1, 2 * hidden_units), w_gu).astype(BF16)
    own_b, other_b = split(done_b.reshape(shape + (column,)))
    got_b = move(other_b, by_node=1)
    home_b = send(homeward(merge(own_b, got_b, node, tokens_here), -1))

    at = jnp.stack([(local - m) % 4 for m in (2, 1, 3, 0)]).astype(jnp.int32)
    place_a = sorted_places(small_next[0].astype(jnp.int32))
    next_input = finish(act_next, small_next[1], place_a, home_a, at)
    ones = jnp.ones((tokens_here,), F32)
    prev_grad = finish(grad_next, ones, sorted_places(route_b_next), home_b, at)
    return next_input, prev_grad


def from_behind(value, axis, by):
    length = lax.axis_size(axis)
    return lax.ppermute(value, axis, [(i, (i + by) % length) for i in range(length)])


def place_matrix(route, expert_count, capacity):
    onehot = (route[:, None] == jnp.arange(expert_count, dtype=jnp.int32)[None, :]).astype(
        jnp.int32
    )
    before = jnp.cumsum(onehot, axis=0) - onehot
    slot_index = jnp.sum(before * onehot, axis=1)
    target = route * capacity + slot_index
    positions = jnp.arange(expert_count * capacity, dtype=jnp.int32)
    return (positions[:, None] == target[None, :]).astype(jnp.bfloat16)


def pack_rows(placer, values, expert_count, capacity):
    packed = jnp.dot(placer, values, preferred_element_type=jnp.float32).astype(jnp.bfloat16)
    return packed.reshape(expert_count, capacity, values.shape[1])


def unpack_rows(placer, packed):
    flattened = packed.reshape(-1, packed.shape[-1])
    result = lax.dot_general(
        placer, flattened, (((0,), (0,)), ((), ())), preferred_element_type=jnp.float32
    )
    return result.astype(jnp.bfloat16)


def flat_outgoing(packed, local_count):
    expert_count, capacity, feature_count = packed.shape
    column = feature_count // local_count
    outgoing = packed.reshape(expert_count, capacity, local_count, column).transpose(0, 2, 1, 3)
    return outgoing.reshape(expert_count * local_count, capacity, column)


def flat_layout(received, expert_count, local_count):
    capacity = received.shape[1]
    column = received.shape[2]
    rows_in = received.reshape(expert_count, local_count, capacity, column).transpose(1, 0, 2, 3)
    return rows_in.reshape(-1, column)


def send_rows(packs, local_count):
    expert_count = packs[0].shape[0]
    outgoing = tuple((flat_outgoing(packed, local_count) for packed in packs))
    received = (
        lax.all_to_all(outgoing[0], ("node", "local"), split_axis=0, concat_axis=0, tiled=True),
        lax.all_to_all(outgoing[1], ("node", "local"), split_axis=0, concat_axis=0, tiled=True),
    )
    return tuple((flat_layout(item, expert_count, local_count) for item in received))


def return_rows(finished_pair, expert_count, capacity, local_count):
    column = finished_pair[0].shape[1]
    blocks = tuple(
        (item.reshape(local_count, expert_count, capacity, column) for item in finished_pair)
    )
    outgoing = tuple(
        (
            item.transpose(1, 0, 2, 3).reshape(expert_count * local_count, capacity, column)
            for item in blocks
        )
    )
    received = (
        lax.all_to_all(outgoing[0], ("node", "local"), split_axis=0, concat_axis=0, tiled=True),
        lax.all_to_all(outgoing[1], ("node", "local"), split_axis=0, concat_axis=0, tiled=True),
    )
    results = []
    for item in received:
        arranged = item.reshape(expert_count, local_count, capacity, column).transpose(0, 2, 1, 3)
        results.append(arranged.reshape(expert_count, capacity, local_count * column))
    return tuple(results)


def body(
    act_fwd, routes_fwd, weight_fwd, grad_bwd, routes_bwd, weight_bwd, saved_bwd, w_gate_up, w_down
):
    node_count = lax.axis_size("node")
    local_count = lax.axis_size("local")
    tokens_here = act_fwd.shape[1]
    capacity = 5 * tokens_here // (4 * node_count)
    rows_each = node_count * capacity
    w_gu = w_gate_up[0, 0]
    w_dn = w_down[0, 0]
    hidden_units = w_dn.shape[0]
    tokens_a = act_fwd[0]
    placer_a = place_matrix(routes_fwd[0, :, 0], node_count, capacity)
    cotangent = grad_bwd[0]
    placer_b = place_matrix(routes_bwd[0, :, 0], node_count, capacity)
    scaled = (weight_bwd[0][:, None] * cotangent.astype(jnp.float32)).astype(jnp.bfloat16)
    packed_a = pack_rows(placer_a, tokens_a, node_count, capacity)
    packed_b = pack_rows(placer_b, scaled, node_count, capacity)
    rows_a, rows_b = send_rows((packed_a, packed_b), local_count)
    saved_packed = pack_rows(placer_b, saved_bwd[0], node_count, capacity)
    saved_rows = lax.all_to_all(
        saved_packed, "node", split_axis=0, concat_axis=0, tiled=True
    ).reshape(rows_each, -1)
    row_block = rows_a
    preact = lax.psum_scatter(
        jnp.dot(row_block, w_gu, preferred_element_type=jnp.float32).astype(jnp.bfloat16),
        "local",
        scatter_dimension=0,
        tiled=True,
    ).astype(jnp.float32)
    row_block = rows_b
    grad_hidden = lax.psum_scatter(
        lax.dot_general(
            row_block, w_dn, (((1,), (1,)), ((), ())), preferred_element_type=jnp.float32
        ).astype(jnp.bfloat16),
        "local",
        scatter_dimension=0,
        tiled=True,
    ).astype(jnp.float32)
    hidden = (jax.nn.silu(preact[:, :hidden_units]) * preact[:, hidden_units:]).astype(jnp.bfloat16)
    done_a = jnp.dot(
        lax.all_gather(hidden, "local", axis=0, tiled=True),
        w_dn,
        preferred_element_type=jnp.float32,
    ).astype(jnp.bfloat16)
    gate_pre = saved_rows[:, :hidden_units].astype(jnp.float32)
    up_pre = saved_rows[:, hidden_units:].astype(jnp.float32)
    sigmoid_g = 1.0 / (1.0 + jnp.exp(-gate_pre))
    grad_gate = grad_hidden * up_pre * sigmoid_g * (1.0 + gate_pre * (1.0 - sigmoid_g))
    grad_up = grad_hidden * gate_pre * sigmoid_g
    grad_gu = jnp.concatenate([grad_gate, grad_up], axis=1).astype(jnp.bfloat16)
    product = lax.dot_general(
        lax.all_gather(grad_gu, "local", axis=0, tiled=True),
        w_gu,
        (((1,), (1,)), ((), ())),
        preferred_element_type=jnp.float32,
    )
    done_b = product.astype(jnp.bfloat16)
    back_a, back_b = return_rows((done_a, done_b), node_count, capacity, local_count)
    moe_a = unpack_rows(placer_a, back_a)
    result_a = tokens_a.astype(jnp.float32) + weight_fwd[0][:, None] * moe_a.astype(jnp.float32)
    result_a = result_a.astype(jnp.bfloat16)
    moe_b = unpack_rows(placer_b, back_b)
    result_b = (cotangent.astype(jnp.float32) + moe_b.astype(jnp.float32)).astype(jnp.bfloat16)
    next_input = from_behind(result_a[None], "pp", 1)
    prev_grad = from_behind(result_b[None], "pp", -1)
    return (next_input, prev_grad)


def solution(mesh):
    in_specs = (
        P("pp", ("node", "local"), None),
        P("pp", ("node", "local"), None),
        P("pp", ("node", "local")),
        P("pp", ("node", "local"), None),
        P("pp", ("node", "local"), None),
        P("pp", ("node", "local")),
        P("pp", ("node", "local"), None),
        P("pp", "node", "local", None),
        P("pp", "node", None, "local"),
    )
    out_specs = (P("pp", ("node", "local"), None), P("pp", ("node", "local"), None))
    paired = mesh.shape["node"] == 2 and mesh.shape["local"] == 4
    plan = body_pair if paired else body
    return jax.shard_map(plan, mesh=mesh, in_specs=in_specs, out_specs=out_specs, check_vma=False)
```

```python
import jax
import jax.numpy as jnp
from jax import lax
from jax.experimental import pallas as pl
from jax.experimental.pallas import tpu as pltpu
from jax.sharding import PartitionSpec as P

F32 = jnp.float32
BF16 = jnp.bfloat16
AXES = ("pp", "node", "local")


def move(value, by_pp=0, by_node=0, by_local=0, wrap=True, first=0, last=None):
    pps, nodes, locs = (lax.axis_size(a) for a in AXES)
    last = locs - 1 if last is None else last
    pairs = []
    for s in range(pps):
        for n in range(nodes):
            for l in range(locs):
                to = l + by_local
                if not wrap and not (first <= l <= last and 0 <= to < locs):
                    continue
                source = (s * nodes + n) * locs + l
                target = (((s + by_pp) % pps) * nodes + (n ^ by_node)) * locs + to % locs
                pairs.append((source, target))
    return lax.ppermute(value, AXES, pairs)


def sorted_places(route):
    ones = route.astype(F32)
    count = route.shape[0]
    earlier = (jnp.arange(count)[None, :] < jnp.arange(count)[:, None]).astype(F32)
    ones_before = jnp.dot(earlier, ones[:, None], preferred_element_type=F32)[:, 0]
    zeros = count - jnp.sum(ones)
    index = jnp.arange(count, dtype=F32)
    place = jnp.where(route == 0, index - ones_before, zeros + ones_before)
    return place.astype(jnp.int32)


def sorter(route):
    place = sorted_places(route)
    rows = jnp.arange(route.shape[0], dtype=jnp.int32)
    return (rows[:, None] == place[None, :]).astype(BF16)


def one_hot(row, count):
    return (row[:, None] == jnp.arange(count, dtype=jnp.int32)[None, :]).astype(BF16)


def dot_t(left, right):
    return lax.dot_general(left, right, (((1,), (1,)), ((), ())), preferred_element_type=F32)


def windows(blocks, node, capacity):
    tokens = blocks.shape[-2]
    start = tokens - capacity
    low = lax.slice_in_dim(blocks, 0, capacity, axis=-2 + blocks.ndim)
    high = lax.slice_in_dim(blocks, start, tokens, axis=-2 + blocks.ndim)
    own = jnp.where(node == 0, low, high)
    other = jnp.where(node == 0, high, low)
    return own, other


def join(*values):
    return lax.optimization_barrier(values)


def after(values, *others):
    return list(join(*values, *others)[: len(values)])


def cut(tokens, placer, local):
    column = tokens.shape[1] // 4
    blocks = []
    for m in range(4):
        block = lax.dynamic_slice_in_dim(tokens, ((local - m) % 4) * column, column, axis=1)
        blocks.append(jnp.dot(placer, block, preferred_element_type=F32).astype(BF16))
    return blocks


def sums(partial):
    right, left = partial(3), partial(1)
    for step in (1, 2, 3):
        right, left = right.astype(BF16), left.astype(BF16)
        got_r, got_l = yield (
            (right, dict(by_local=1, wrap=False, last=step - 1)),
            (left, dict(by_local=-1, wrap=False, first=4 - step)),
        )
        right = partial(3 - step).astype(F32) + got_r.astype(F32)
        if step < 3:
            left = partial(step + 1).astype(F32) + got_l.astype(F32)
    yield right + got_l.astype(F32)


def gathers(rows, local):
    from_left, from_right = [rows], [rows]
    for step in (1, 2, 3):
        got_r, got_l = yield (
            (from_left[-1], dict(by_local=1, wrap=False, first=step - 1)),
            (from_right[-1], dict(by_local=-1, wrap=False, last=4 - step)),
        )
        from_left.append(got_r)
        from_right.append(got_l)
    slots = [rows]
    for m in (1, 2, 3):
        slots.append(jnp.where(local + m < 4, from_right[m], from_left[4 - m]))
    yield jnp.stack(slots)


def send(pieces):
    return [move(value, **how) for value, how in pieces]


def operands(pieces):
    return [value for value, _ in pieces]


def valid(zeros, node, tokens, capacity):
    row = jnp.arange(capacity, dtype=F32)[None, :]
    return jnp.where(node == 0, row < zeros[:, None], row + (tokens - capacity) >= zeros[:, None])


def merge(own, other, node, tokens):
    slots, capacity, column = own.shape
    low = jnp.where(node == 0, own, other)
    high = jnp.where(node == 0, other, own)
    rest = jnp.zeros((slots, tokens - capacity, column), own.dtype)
    return jnp.concatenate([low, rest], axis=1) + jnp.concatenate([rest, high], axis=1)


def homeward(merged, by_pp):
    return [(merged[m], dict(by_pp=by_pp, by_local=m)) for m in (2, 1, 3, 0)]


def finish_kernel(at_ref, residual_ref, weight_ref, pick_ref, *refs):
    *blocks, out_ref, rows, sem = refs
    count = len(blocks)
    column = rows.shape[-1]
    copies = [pltpu.make_async_copy(blocks[i], rows.at[i], sem.at[i]) for i in range(count)]
    for copy in copies:
        copy.start()
    for i in range(count):
        copies[i].wait()
        cols = pl.ds(pl.multiple_of(at_ref[i] * column, column), column)
        moe = jnp.dot(pick_ref[...], rows[i], preferred_element_type=F32)
        total = residual_ref[:, cols].astype(F32) + weight_ref[...] * moe
        out_ref[0, :, cols] = total.astype(out_ref.dtype)


def finish(residual, weight, place, blocks, at):
    column = blocks[0].shape[-1]
    tokens, features = residual.shape
    vmem = pl.BlockSpec(memory_space=pltpu.VMEM)
    anywhere = pl.BlockSpec(memory_space=pl.ANY)
    return pl.pallas_call(
        finish_kernel,
        out_shape=jax.ShapeDtypeStruct((1, tokens, features), BF16),
        in_specs=[pl.BlockSpec(memory_space=pltpu.SMEM)] + [vmem] * 3 + [anywhere] * len(blocks),
        out_specs=vmem,
        scratch_shapes=[
            pltpu.VMEM((len(blocks), tokens, column), BF16),
            pltpu.SemaphoreType.DMA((len(blocks),)),
        ],
        compiler_params=pltpu.CompilerParams(vmem_limit_bytes=8 * 2**20),
        name="finish",
    )(at, residual, weight[:, None], one_hot(place, tokens), *blocks)


def body_pair(
    act_fwd, routes_fwd, weight_fwd, grad_bwd, routes_bwd, weight_bwd, saved_bwd, w_gate_up, w_down
):
    node = lax.axis_index("node")
    local = lax.axis_index("local")
    tokens_here = act_fwd.shape[1]
    capacity = 5 * tokens_here // 8
    w_gu = w_gate_up[0, 0]
    w_dn = w_down[0, 0]
    hidden_units = w_dn.shape[0]
    shape = (4, 2, capacity)

    act, grad = act_fwd[0], grad_bwd[0]
    route_a, route_b = routes_fwd[0, :, 0], routes_bwd[0, :, 0]
    sort_a, sort_b = sorter(route_a), sorter(route_b)
    zeros = tokens_here - jnp.stack([jnp.sum(route_a), jnp.sum(route_b)]).astype(F32)

    def in_rows(cuts, got):
        return windows(jnp.stack([cuts[0], got[1], got[0], got[2]]), node, capacity)

    def by_node(own, got, axis):
        return jnp.stack([jnp.where(node == 0, own, got), jnp.where(node == 0, got, own)], axis=axis)

    def split(done):
        own = lax.dynamic_index_in_dim(done, node, axis=1, keepdims=False)
        other = lax.dynamic_index_in_dim(done, 1 - node, axis=1, keepdims=False)
        return own, other

    def turn(chain, back, *others):
        pieces = chain.send(after(back, *others))
        return operands(pieces), send(pieces)

    dy = (weight_bwd[0][:, None] * grad.astype(F32)).astype(BF16)
    cut_b = cut(dy, sort_b, local)
    got_b = [move(cut_b[m], by_local=-m) for m in (2, 1, 3)]
    saved = jnp.dot(sort_b, saved_bwd[0], preferred_element_type=F32).astype(BF16)
    saved_own, saved_other = windows(saved, node, capacity)
    saved_got = move(saved_other, by_node=1)
    (zeros_wait,) = after([zeros], saved_other)
    zeros_got = move(zeros_wait, by_node=1)
    cut_a = cut(act, sort_a, local)
    *got_b, saved_got, zeros_got, a0, a1, a2, a3 = join(*got_b, saved_got, zeros_got, *cut_a)
    cut_a = [a0, a1, a2, a3]
    zeros = by_node(zeros, zeros_got, 0)
    got_a = [move(cut_a[m], by_local=-m) for m in (2, 1, 3)]
    own_b, other_b = in_rows(cut_b, got_b)
    column = own_b.shape[-1]
    got_bx = move(other_b, by_node=1)

    rows_b = by_node(own_b, got_bx, 1).reshape(-1, column)
    part_b = dot_t(rows_b, w_dn).astype(BF16).reshape(shape + (hidden_units,))
    chain_b = sums(lambda slot: part_b[slot])
    back_b = send(next(chain_b))
    *back_b, g0, g1, g2 = join(*back_b, *got_a)
    own_a, other_a = in_rows(cut_a, [g0, g1, g2])
    got_ax = move(other_a, by_node=1)
    act_next = move(after([act], other_a)[0], by_pp=1)
    values_b, back_b = turn(chain_b, back_b)
    values_b, back_b = turn(chain_b, back_b)
    *back_b, got_ax, act_next = join(*back_b, got_ax, act_next)
    dh = chain_b.send(back_b)
    dh = jnp.where(valid(zeros[:, 1], node, tokens_here, capacity)[..., None], dh, 0.0)
    saved_rows = by_node(saved_own, saved_got, 0)
    g = saved_rows[..., :hidden_units].astype(F32)
    u = saved_rows[..., hidden_units:].astype(F32)
    q = 1.0 / (1.0 + jnp.exp(-g))
    grad_gu = jnp.concatenate([dh * u * q * (1.0 + g * (1.0 - q)), dh * g * q], axis=-1).astype(
        BF16
    )

    chain_b = gathers(grad_gu, local)
    back_b = send(next(chain_b))
    grad_wait, route_wait, small_wait = after(
        [grad, route_b, jnp.stack([route_a.astype(F32), weight_fwd[0]])], grad_gu
    )
    grad_next = move(grad_wait, by_pp=-1)
    route_b_next = move(route_wait, by_pp=-1)
    small_next = move(small_wait, by_pp=1)
    rows_a = by_node(own_a, got_ax, 1).reshape(-1, column)
    part_a = jnp.dot(rows_a, w_gu, preferred_element_type=F32).astype(BF16)
    *back_b, part_a, grad_next, route_b_next, small_next = join(
        *back_b, part_a, grad_next, route_b_next, small_next
    )
    part_a = part_a.reshape(shape + (2 * hidden_units,))
    chain_a = sums(lambda slot: part_a[slot])
    values_b, back_b = turn(chain_b, back_b)
    back_a = send(next(chain_a))
    values_b, back_b = turn(chain_b, back_b)
    values_a, back_a = turn(chain_a, back_a)
    values_a, back_a = turn(chain_a, back_a)
    all_gu = chain_b.send(back_b)
    done_b = dot_t(all_gu.reshape(-1, 2 * hidden_units), w_gu).astype(BF16)
    own_b, other_b = split(done_b.reshape(shape + (column,)))
    got_b = move(other_b, by_node=1)
    *back_a, got_b = join(*back_a, got_b)

    preact = chain_a.send(back_a)
    preact = jnp.where(valid(zeros[:, 0], node, tokens_here, capacity)[..., None], preact, 0.0)
    hidden = (jax.nn.silu(preact[..., :hidden_units]) * preact[..., hidden_units:]).astype(BF16)
    all_hidden = [move(hidden, by_local=-m) for m in (1, 2, 3)]
    merged_b = merge(own_b, got_b, node, tokens_here)
    h1, h2, h3, merged_b = join(*all_hidden, merged_b)
    all_hidden = jnp.stack([hidden, h1, h2, h3])
    home_b = send(homeward(merged_b, -1))
    done_a = jnp.dot(
        all_hidden.reshape(-1, hidden_units), w_dn, preferred_element_type=F32
    ).astype(BF16)
    own_a, other_a = split(done_a.reshape(shape + (column,)))
    got_a = move(other_a, by_node=1)
    home_a = send(homeward(merge(own_a, got_a, node, tokens_here), 1))

    at = jnp.stack([(local - m) % 4 for m in (2, 1, 3, 0)]).astype(jnp.int32)
    ones = jnp.ones((tokens_here,), F32)
    prev_grad = finish(grad_next, ones, sorted_places(route_b_next), home_b, at)
    place_a = sorted_places(small_next[0].astype(jnp.int32))
    next_input = finish(act_next, small_next[1], place_a, home_a, at)
    return next_input, prev_grad


def from_behind(value, axis, by):
    length = lax.axis_size(axis)
    return lax.ppermute(value, axis, [(i, (i + by) % length) for i in range(length)])


def place_matrix(route, expert_count, capacity):
    onehot = (route[:, None] == jnp.arange(expert_count, dtype=jnp.int32)[None, :]).astype(
        jnp.int32
    )
    before = jnp.cumsum(onehot, axis=0) - onehot
    slot_index = jnp.sum(before * onehot, axis=1)
    target = route * capacity + slot_index
    positions = jnp.arange(expert_count * capacity, dtype=jnp.int32)
    return (positions[:, None] == target[None, :]).astype(jnp.bfloat16)


def pack_rows(placer, values, expert_count, capacity):
    packed = jnp.dot(placer, values, preferred_element_type=jnp.float32).astype(jnp.bfloat16)
    return packed.reshape(expert_count, capacity, values.shape[1])


def unpack_rows(placer, packed):
    flattened = packed.reshape(-1, packed.shape[-1])
    result = lax.dot_general(
        placer, flattened, (((0,), (0,)), ((), ())), preferred_element_type=jnp.float32
    )
    return result.astype(jnp.bfloat16)


def flat_outgoing(packed, local_count):
    expert_count, capacity, feature_count = packed.shape
    column = feature_count // local_count
    outgoing = packed.reshape(expert_count, capacity, local_count, column).transpose(0, 2, 1, 3)
    return outgoing.reshape(expert_count * local_count, capacity, column)


def flat_layout(received, expert_count, local_count):
    capacity = received.shape[1]
    column = received.shape[2]
    rows_in = received.reshape(expert_count, local_count, capacity, column).transpose(1, 0, 2, 3)
    return rows_in.reshape(-1, column)


def send_rows(packs, local_count):
    expert_count = packs[0].shape[0]
    outgoing = tuple((flat_outgoing(packed, local_count) for packed in packs))
    received = (
        lax.all_to_all(outgoing[0], ("node", "local"), split_axis=0, concat_axis=0, tiled=True),
        lax.all_to_all(outgoing[1], ("node", "local"), split_axis=0, concat_axis=0, tiled=True),
    )
    return tuple((flat_layout(item, expert_count, local_count) for item in received))


def return_rows(finished_pair, expert_count, capacity, local_count):
    column = finished_pair[0].shape[1]
    blocks = tuple(
        (item.reshape(local_count, expert_count, capacity, column) for item in finished_pair)
    )
    outgoing = tuple(
        (
            item.transpose(1, 0, 2, 3).reshape(expert_count * local_count, capacity, column)
            for item in blocks
        )
    )
    received = (
        lax.all_to_all(outgoing[0], ("node", "local"), split_axis=0, concat_axis=0, tiled=True),
        lax.all_to_all(outgoing[1], ("node", "local"), split_axis=0, concat_axis=0, tiled=True),
    )
    results = []
    for item in received:
        arranged = item.reshape(expert_count, local_count, capacity, column).transpose(0, 2, 1, 3)
        results.append(arranged.reshape(expert_count, capacity, local_count * column))
    return tuple(results)


def body(
    act_fwd, routes_fwd, weight_fwd, grad_bwd, routes_bwd, weight_bwd, saved_bwd, w_gate_up, w_down
):
    node_count = lax.axis_size("node")
    local_count = lax.axis_size("local")
    tokens_here = act_fwd.shape[1]
    capacity = 5 * tokens_here // (4 * node_count)
    rows_each = node_count * capacity
    w_gu = w_gate_up[0, 0]
    w_dn = w_down[0, 0]
    hidden_units = w_dn.shape[0]
    tokens_a = act_fwd[0]
    placer_a = place_matrix(routes_fwd[0, :, 0], node_count, capacity)
    cotangent = grad_bwd[0]
    placer_b = place_matrix(routes_bwd[0, :, 0], node_count, capacity)
    scaled = (weight_bwd[0][:, None] * cotangent.astype(jnp.float32)).astype(jnp.bfloat16)
    packed_a = pack_rows(placer_a, tokens_a, node_count, capacity)
    packed_b = pack_rows(placer_b, scaled, node_count, capacity)
    rows_a, rows_b = send_rows((packed_a, packed_b), local_count)
    saved_packed = pack_rows(placer_b, saved_bwd[0], node_count, capacity)
    saved_rows = lax.all_to_all(
        saved_packed, "node", split_axis=0, concat_axis=0, tiled=True
    ).reshape(rows_each, -1)
    row_block = rows_a
    preact = lax.psum_scatter(
        jnp.dot(row_block, w_gu, preferred_element_type=jnp.float32).astype(jnp.bfloat16),
        "local",
        scatter_dimension=0,
        tiled=True,
    ).astype(jnp.float32)
    row_block = rows_b
    grad_hidden = lax.psum_scatter(
        lax.dot_general(
            row_block, w_dn, (((1,), (1,)), ((), ())), preferred_element_type=jnp.float32
        ).astype(jnp.bfloat16),
        "local",
        scatter_dimension=0,
        tiled=True,
    ).astype(jnp.float32)
    hidden = (jax.nn.silu(preact[:, :hidden_units]) * preact[:, hidden_units:]).astype(jnp.bfloat16)
    done_a = jnp.dot(
        lax.all_gather(hidden, "local", axis=0, tiled=True),
        w_dn,
        preferred_element_type=jnp.float32,
    ).astype(jnp.bfloat16)
    gate_pre = saved_rows[:, :hidden_units].astype(jnp.float32)
    up_pre = saved_rows[:, hidden_units:].astype(jnp.float32)
    sigmoid_g = 1.0 / (1.0 + jnp.exp(-gate_pre))
    grad_gate = grad_hidden * up_pre * sigmoid_g * (1.0 + gate_pre * (1.0 - sigmoid_g))
    grad_up = grad_hidden * gate_pre * sigmoid_g
    grad_gu = jnp.concatenate([grad_gate, grad_up], axis=1).astype(jnp.bfloat16)
    product = lax.dot_general(
        lax.all_gather(grad_gu, "local", axis=0, tiled=True),
        w_gu,
        (((1,), (1,)), ((), ())),
        preferred_element_type=jnp.float32,
    )
    done_b = product.astype(jnp.bfloat16)
    back_a, back_b = return_rows((done_a, done_b), node_count, capacity, local_count)
    moe_a = unpack_rows(placer_a, back_a)
    result_a = tokens_a.astype(jnp.float32) + weight_fwd[0][:, None] * moe_a.astype(jnp.float32)
    result_a = result_a.astype(jnp.bfloat16)
    moe_b = unpack_rows(placer_b, back_b)
    result_b = (cotangent.astype(jnp.float32) + moe_b.astype(jnp.float32)).astype(jnp.bfloat16)
    next_input = from_behind(result_a[None], "pp", 1)
    prev_grad = from_behind(result_b[None], "pp", -1)
    return (next_input, prev_grad)


def solution(mesh):
    in_specs = (
        P("pp", ("node", "local"), None),
        P("pp", ("node", "local"), None),
        P("pp", ("node", "local")),
        P("pp", ("node", "local"), None),
        P("pp", ("node", "local"), None),
        P("pp", ("node", "local")),
        P("pp", ("node", "local"), None),
        P("pp", "node", "local", None),
        P("pp", "node", None, "local"),
    )
    out_specs = (P("pp", ("node", "local"), None), P("pp", ("node", "local"), None))
    paired = mesh.shape["node"] == 2 and mesh.shape["local"] == 4
    plan = body_pair if paired else body
    return jax.shard_map(plan, mesh=mesh, in_specs=in_specs, out_specs=out_specs, check_vma=False)
```

```python
import jax
import jax.numpy as jnp
from jax import lax
from jax.experimental import pallas as pl
from jax.experimental.pallas import tpu as pltpu
from jax.sharding import PartitionSpec as P

F32 = jnp.float32
BF16 = jnp.bfloat16
AXES = ("pp", "node", "local")


def move(value, by_pp=0, by_node=0, by_local=0, wrap=True, first=0, last=None):
    pps, nodes, locs = (lax.axis_size(a) for a in AXES)
    last = locs - 1 if last is None else last
    pairs = []
    for s in range(pps):
        for n in range(nodes):
            for l in range(locs):
                to = l + by_local
                if not wrap and not (first <= l <= last and 0 <= to < locs):
                    continue
                source = (s * nodes + n) * locs + l
                target = (((s + by_pp) % pps) * nodes + (n ^ by_node)) * locs + to % locs
                pairs.append((source, target))
    return lax.ppermute(value, AXES, pairs)


def sorted_places(route):
    ones = route.astype(F32)
    count = route.shape[0]
    earlier = (jnp.arange(count)[None, :] < jnp.arange(count)[:, None]).astype(F32)
    ones_before = jnp.dot(earlier, ones[:, None], preferred_element_type=F32)[:, 0]
    zeros = count - jnp.sum(ones)
    index = jnp.arange(count, dtype=F32)
    place = jnp.where(route == 0, index - ones_before, zeros + ones_before)
    return place.astype(jnp.int32)


def sorter(route):
    place = sorted_places(route)
    rows = jnp.arange(route.shape[0], dtype=jnp.int32)
    return (rows[:, None] == place[None, :]).astype(BF16)


def one_hot(row, count):
    return (row[:, None] == jnp.arange(count, dtype=jnp.int32)[None, :]).astype(BF16)


def window_placer(route, first, capacity):
    place = sorted_places(route)
    start = route.shape[0] - capacity
    in_window = place - jnp.where(route == 1, start, 0)
    row = jnp.where(route == first, in_window, in_window + capacity)
    rows = jnp.arange(2 * capacity, dtype=jnp.int32)
    return (rows[:, None] == row[None, :]).astype(BF16)


def dot_t(left, right):
    return lax.dot_general(left, right, (((1,), (1,)), ((), ())), preferred_element_type=F32)


def windows(blocks, node, capacity):
    tokens = blocks.shape[-2]
    start = tokens - capacity
    low = lax.slice_in_dim(blocks, 0, capacity, axis=-2 + blocks.ndim)
    high = lax.slice_in_dim(blocks, start, tokens, axis=-2 + blocks.ndim)
    own = jnp.where(node == 0, low, high)
    other = jnp.where(node == 0, high, low)
    return own, other


def join(*values):
    return lax.optimization_barrier(values)


def after(values, *others):
    return list(join(*values, *others)[: len(values)])


def cut(tokens, placer, local):
    column = tokens.shape[1] // 4
    blocks = []
    for m in range(4):
        block = lax.dynamic_slice_in_dim(tokens, ((local - m) % 4) * column, column, axis=1)
        blocks.append(jnp.dot(placer, block, preferred_element_type=F32).astype(BF16))
    return blocks


def sums(partial):
    right, left = partial(3), partial(1)
    for step in (1, 2, 3):
        right, left = right.astype(BF16), left.astype(BF16)
        got_r, got_l = yield (
            (right, dict(by_local=1, wrap=False, last=step - 1)),
            (left, dict(by_local=-1, wrap=False, first=4 - step)),
        )
        right = partial(3 - step).astype(F32) + got_r.astype(F32)
        if step < 3:
            left = partial(step + 1).astype(F32) + got_l.astype(F32)
    yield right + got_l.astype(F32)


def gathers(rows, local):
    from_left, from_right = [rows], [rows]
    for step in (1, 2, 3):
        got_r, got_l = yield (
            (from_left[-1], dict(by_local=1, wrap=False, first=step - 1)),
            (from_right[-1], dict(by_local=-1, wrap=False, last=4 - step)),
        )
        from_left.append(got_r)
        from_right.append(got_l)
    slots = [rows]
    for m in (1, 2, 3):
        slots.append(jnp.where(local + m < 4, from_right[m], from_left[4 - m]))
    yield jnp.stack(slots)


def send(pieces):
    return [move(value, **how) for value, how in pieces]


def operands(pieces):
    return [value for value, _ in pieces]


def valid(zeros, node, tokens, capacity):
    row = jnp.arange(capacity, dtype=F32)[None, :]
    return jnp.where(node == 0, row < zeros[:, None], row + (tokens - capacity) >= zeros[:, None])


def merge(own, other, node, tokens):
    slots, capacity, column = own.shape
    low = jnp.where(node == 0, own, other)
    high = jnp.where(node == 0, other, own)
    rest = jnp.zeros((slots, tokens - capacity, column), own.dtype)
    return jnp.concatenate([low, rest], axis=1) + jnp.concatenate([rest, high], axis=1)


def homeward(merged, by_pp):
    return [(merged[m], dict(by_pp=by_pp, by_local=m)) for m in (2, 1, 3, 0)]


def finish_kernel(at_ref, residual_ref, weight_ref, pick_ref, *refs):
    *blocks, out_ref, rows, sem = refs
    count = len(blocks)
    column = rows.shape[-1]
    copies = [pltpu.make_async_copy(blocks[i], rows.at[i], sem.at[i]) for i in range(count)]
    for copy in copies:
        copy.start()
    for i in range(count):
        copies[i].wait()
        cols = pl.ds(pl.multiple_of(at_ref[i] * column, column), column)
        moe = jnp.dot(pick_ref[...], rows[i], preferred_element_type=F32)
        total = residual_ref[:, cols].astype(F32) + weight_ref[...] * moe
        out_ref[0, :, cols] = total.astype(out_ref.dtype)


def finish(residual, weight, place, blocks, at):
    column = blocks[0].shape[-1]
    tokens, features = residual.shape
    vmem = pl.BlockSpec(memory_space=pltpu.VMEM)
    anywhere = pl.BlockSpec(memory_space=pl.ANY)
    return pl.pallas_call(
        finish_kernel,
        out_shape=jax.ShapeDtypeStruct((1, tokens, features), BF16),
        in_specs=[pl.BlockSpec(memory_space=pltpu.SMEM)] + [vmem] * 3 + [anywhere] * len(blocks),
        out_specs=vmem,
        scratch_shapes=[
            pltpu.VMEM((len(blocks), tokens, column), BF16),
            pltpu.SemaphoreType.DMA((len(blocks),)),
        ],
        compiler_params=pltpu.CompilerParams(vmem_limit_bytes=8 * 2**20),
        name="finish",
    )(at, residual, weight[:, None], one_hot(place, tokens), *blocks)


def body_pair(
    act_fwd, routes_fwd, weight_fwd, grad_bwd, routes_bwd, weight_bwd, saved_bwd, w_gate_up, w_down
):
    node = lax.axis_index("node")
    local = lax.axis_index("local")
    tokens_here = act_fwd.shape[1]
    capacity = 5 * tokens_here // 8
    w_gu = w_gate_up[0, 0]
    w_dn = w_down[0, 0]
    hidden_units = w_dn.shape[0]
    shape = (4, 2, capacity)

    act, grad = act_fwd[0], grad_bwd[0]
    route_a, route_b = routes_fwd[0, :, 0], routes_bwd[0, :, 0]
    sort_a = sorter(route_a)
    zeros = tokens_here - jnp.stack([jnp.sum(route_a), jnp.sum(route_b)]).astype(F32)

    def in_rows(cuts, got):
        return windows(jnp.stack([cuts[0], got[1], got[0], got[2]]), node, capacity)

    def by_node(own, got, axis):
        return jnp.stack([jnp.where(node == 0, own, got), jnp.where(node == 0, got, own)], axis=axis)

    def split(done):
        own = lax.dynamic_index_in_dim(done, node, axis=1, keepdims=False)
        other = lax.dynamic_index_in_dim(done, 1 - node, axis=1, keepdims=False)
        return own, other

    def turn(chain, back, *others):
        pieces = chain.send(after(back, *others))
        return operands(pieces), send(pieces)

    dy = (weight_bwd[0][:, None] * grad.astype(F32)).astype(BF16)
    pack_b = cut(dy, window_placer(route_b, node, capacity), local)
    own_b = [pack_b[0][:capacity]] + [move(pack_b[m][:capacity], by_local=-m) for m in (1, 2, 3)]
    got_b = [move(pack_b[m][capacity:], by_node=1, by_local=-m) for m in range(4)]
    saved = jnp.dot(sorter(route_b), saved_bwd[0], preferred_element_type=F32).astype(BF16)
    saved_own, saved_other = windows(saved, node, capacity)
    extra = jnp.broadcast_to(jnp.repeat(zeros, 8)[:, None], (16, saved.shape[1])).astype(BF16)
    saved_got = move(jnp.concatenate([saved_other, extra], axis=0), by_node=1)
    cut_a = cut(act, sort_a, local)
    *blocks, saved_got, a0, a1, a2, a3 = join(*own_b, *got_b, saved_got, *cut_a)
    own_b, got_b = jnp.stack(blocks[:4]), jnp.stack(blocks[4:])
    cut_a = [a0, a1, a2, a3]
    zeros_got = saved_got[capacity::8, 0].astype(F32)
    saved_got = saved_got[:capacity]
    zeros = by_node(zeros, zeros_got, 0)
    got_a = [move(cut_a[m], by_local=-m) for m in (2, 1, 3)]
    column = own_b.shape[-1]

    rows_b = by_node(own_b, got_b, 1).reshape(-1, column)
    part_b = dot_t(rows_b, w_dn).astype(BF16).reshape(shape + (hidden_units,))
    chain_b = sums(lambda slot: part_b[slot])
    back_b = send(next(chain_b))
    *back_b, g0, g1, g2 = join(*back_b, *got_a)
    own_a, other_a = in_rows(cut_a, [g0, g1, g2])
    got_ax = move(other_a, by_node=1)
    values_b, back_b = turn(chain_b, back_b)
    small_wait, route_wait = after(
        [jnp.stack([route_a.astype(F32), weight_fwd[0]]), route_b], *values_b, other_a
    )
    small_next = move(small_wait, by_pp=1)
    route_b_next = move(route_wait, by_pp=-1)
    *back_b, small_next, route_b_next = join(*back_b, small_next, route_b_next)
    values_b, back_b = turn(chain_b, back_b)
    act_next = move(after([act], *values_b)[0], by_pp=1)
    *back_b, got_ax = join(*back_b, got_ax)
    dh = chain_b.send(back_b)
    dh = jnp.where(valid(zeros[:, 1], node, tokens_here, capacity)[..., None], dh, 0.0)
    saved_rows = by_node(saved_own, saved_got, 0)
    g = saved_rows[..., :hidden_units].astype(F32)
    u = saved_rows[..., hidden_units:].astype(F32)
    q = 1.0 / (1.0 + jnp.exp(-g))
    grad_gu = jnp.concatenate([dh * u * q * (1.0 + g * (1.0 - q)), dh * g * q], axis=-1).astype(
        BF16
    )

    chain_b = gathers(grad_gu, local)
    back_b = send(next(chain_b))
    rows_a = by_node(own_a, got_ax, 1).reshape(-1, column)
    part_a = jnp.dot(rows_a, w_gu, preferred_element_type=F32).astype(BF16)
    *back_b, part_a, act_next = join(*back_b, part_a, act_next)
    part_a = part_a.reshape(shape + (2 * hidden_units,))
    chain_a = sums(lambda slot: part_a[slot])
    values_b, back_b = turn(chain_b, back_b)
    pieces = next(chain_a)
    back_a = send(pieces)
    grad_next = move(after([grad], *operands(pieces))[0], by_pp=-1)
    *back_b, grad_next = join(*back_b, grad_next)
    values_b, back_b = turn(chain_b, back_b)
    values_a, back_a = turn(chain_a, back_a)
    values_a, back_a = turn(chain_a, back_a)
    all_gu = chain_b.send(back_b)
    done_b = dot_t(all_gu.reshape(-1, 2 * hidden_units), w_gu).astype(BF16)
    own_b, other_b = split(done_b.reshape(shape + (column,)))
    got_b = move(other_b, by_node=1)

    preact = chain_a.send(back_a)
    preact = jnp.where(valid(zeros[:, 0], node, tokens_here, capacity)[..., None], preact, 0.0)
    hidden = (jax.nn.silu(preact[..., :hidden_units]) * preact[..., hidden_units:]).astype(BF16)
    all_hidden = [move(hidden, by_local=-m) for m in (1, 2, 3)]
    merged_b = merge(own_b, got_b, node, tokens_here)
    h1, h2, h3, merged_b = join(*all_hidden, merged_b)
    all_hidden = jnp.stack([hidden, h1, h2, h3])
    home_b = send(homeward(merged_b, -1))
    done_a = jnp.dot(
        all_hidden.reshape(-1, hidden_units), w_dn, preferred_element_type=F32
    ).astype(BF16)
    own_a, other_a = split(done_a.reshape(shape + (column,)))
    got_a = move(other_a, by_node=1)
    home_a = send(homeward(merge(own_a, got_a, node, tokens_here), 1))

    at = jnp.stack([(local - m) % 4 for m in (2, 1, 3, 0)]).astype(jnp.int32)
    ones = jnp.ones((tokens_here,), F32)
    prev_grad = finish(grad_next, ones, sorted_places(route_b_next), home_b, at)
    place_a = sorted_places(small_next[0].astype(jnp.int32))
    next_input = finish(act_next, small_next[1], place_a, home_a, at)
    return next_input, prev_grad


def from_behind(value, axis, by):
    length = lax.axis_size(axis)
    return lax.ppermute(value, axis, [(i, (i + by) % length) for i in range(length)])


def place_matrix(route, expert_count, capacity):
    onehot = (route[:, None] == jnp.arange(expert_count, dtype=jnp.int32)[None, :]).astype(
        jnp.int32
    )
    before = jnp.cumsum(onehot, axis=0) - onehot
    slot_index = jnp.sum(before * onehot, axis=1)
    target = route * capacity + slot_index
    positions = jnp.arange(expert_count * capacity, dtype=jnp.int32)
    return (positions[:, None] == target[None, :]).astype(jnp.bfloat16)


def pack_rows(placer, values, expert_count, capacity):
    packed = jnp.dot(placer, values, preferred_element_type=jnp.float32).astype(jnp.bfloat16)
    return packed.reshape(expert_count, capacity, values.shape[1])


def unpack_rows(placer, packed):
    flattened = packed.reshape(-1, packed.shape[-1])
    result = lax.dot_general(
        placer, flattened, (((0,), (0,)), ((), ())), preferred_element_type=jnp.float32
    )
    return result.astype(jnp.bfloat16)


def flat_outgoing(packed, local_count):
    expert_count, capacity, feature_count = packed.shape
    column = feature_count // local_count
    outgoing = packed.reshape(expert_count, capacity, local_count, column).transpose(0, 2, 1, 3)
    return outgoing.reshape(expert_count * local_count, capacity, column)


def flat_layout(received, expert_count, local_count):
    capacity = received.shape[1]
    column = received.shape[2]
    rows_in = received.reshape(expert_count, local_count, capacity, column).transpose(1, 0, 2, 3)
    return rows_in.reshape(-1, column)


def send_rows(packs, local_count):
    expert_count = packs[0].shape[0]
    outgoing = tuple((flat_outgoing(packed, local_count) for packed in packs))
    received = (
        lax.all_to_all(outgoing[0], ("node", "local"), split_axis=0, concat_axis=0, tiled=True),
        lax.all_to_all(outgoing[1], ("node", "local"), split_axis=0, concat_axis=0, tiled=True),
    )
    return tuple((flat_layout(item, expert_count, local_count) for item in received))


def return_rows(finished_pair, expert_count, capacity, local_count):
    column = finished_pair[0].shape[1]
    blocks = tuple(
        (item.reshape(local_count, expert_count, capacity, column) for item in finished_pair)
    )
    outgoing = tuple(
        (
            item.transpose(1, 0, 2, 3).reshape(expert_count * local_count, capacity, column)
            for item in blocks
        )
    )
    received = (
        lax.all_to_all(outgoing[0], ("node", "local"), split_axis=0, concat_axis=0, tiled=True),
        lax.all_to_all(outgoing[1], ("node", "local"), split_axis=0, concat_axis=0, tiled=True),
    )
    results = []
    for item in received:
        arranged = item.reshape(expert_count, local_count, capacity, column).transpose(0, 2, 1, 3)
        results.append(arranged.reshape(expert_count, capacity, local_count * column))
    return tuple(results)


def body(
    act_fwd, routes_fwd, weight_fwd, grad_bwd, routes_bwd, weight_bwd, saved_bwd, w_gate_up, w_down
):
    node_count = lax.axis_size("node")
    local_count = lax.axis_size("local")
    tokens_here = act_fwd.shape[1]
    capacity = 5 * tokens_here // (4 * node_count)
    rows_each = node_count * capacity
    w_gu = w_gate_up[0, 0]
    w_dn = w_down[0, 0]
    hidden_units = w_dn.shape[0]
    tokens_a = act_fwd[0]
    placer_a = place_matrix(routes_fwd[0, :, 0], node_count, capacity)
    cotangent = grad_bwd[0]
    placer_b = place_matrix(routes_bwd[0, :, 0], node_count, capacity)
    scaled = (weight_bwd[0][:, None] * cotangent.astype(jnp.float32)).astype(jnp.bfloat16)
    packed_a = pack_rows(placer_a, tokens_a, node_count, capacity)
    packed_b = pack_rows(placer_b, scaled, node_count, capacity)
    rows_a, rows_b = send_rows((packed_a, packed_b), local_count)
    saved_packed = pack_rows(placer_b, saved_bwd[0], node_count, capacity)
    saved_rows = lax.all_to_all(
        saved_packed, "node", split_axis=0, concat_axis=0, tiled=True
    ).reshape(rows_each, -1)
    row_block = rows_a
    preact = lax.psum_scatter(
        jnp.dot(row_block, w_gu, preferred_element_type=jnp.float32).astype(jnp.bfloat16),
        "local",
        scatter_dimension=0,
        tiled=True,
    ).astype(jnp.float32)
    row_block = rows_b
    grad_hidden = lax.psum_scatter(
        lax.dot_general(
            row_block, w_dn, (((1,), (1,)), ((), ())), preferred_element_type=jnp.float32
        ).astype(jnp.bfloat16),
        "local",
        scatter_dimension=0,
        tiled=True,
    ).astype(jnp.float32)
    hidden = (jax.nn.silu(preact[:, :hidden_units]) * preact[:, hidden_units:]).astype(jnp.bfloat16)
    done_a = jnp.dot(
        lax.all_gather(hidden, "local", axis=0, tiled=True),
        w_dn,
        preferred_element_type=jnp.float32,
    ).astype(jnp.bfloat16)
    gate_pre = saved_rows[:, :hidden_units].astype(jnp.float32)
    up_pre = saved_rows[:, hidden_units:].astype(jnp.float32)
    sigmoid_g = 1.0 / (1.0 + jnp.exp(-gate_pre))
    grad_gate = grad_hidden * up_pre * sigmoid_g * (1.0 + gate_pre * (1.0 - sigmoid_g))
    grad_up = grad_hidden * gate_pre * sigmoid_g
    grad_gu = jnp.concatenate([grad_gate, grad_up], axis=1).astype(jnp.bfloat16)
    product = lax.dot_general(
        lax.all_gather(grad_gu, "local", axis=0, tiled=True),
        w_gu,
        (((1,), (1,)), ((), ())),
        preferred_element_type=jnp.float32,
    )
    done_b = product.astype(jnp.bfloat16)
    back_a, back_b = return_rows((done_a, done_b), node_count, capacity, local_count)
    moe_a = unpack_rows(placer_a, back_a)
    result_a = tokens_a.astype(jnp.float32) + weight_fwd[0][:, None] * moe_a.astype(jnp.float32)
    result_a = result_a.astype(jnp.bfloat16)
    moe_b = unpack_rows(placer_b, back_b)
    result_b = (cotangent.astype(jnp.float32) + moe_b.astype(jnp.float32)).astype(jnp.bfloat16)
    next_input = from_behind(result_a[None], "pp", 1)
    prev_grad = from_behind(result_b[None], "pp", -1)
    return (next_input, prev_grad)


def solution(mesh):
    in_specs = (
        P("pp", ("node", "local"), None),
        P("pp", ("node", "local"), None),
        P("pp", ("node", "local")),
        P("pp", ("node", "local"), None),
        P("pp", ("node", "local"), None),
        P("pp", ("node", "local")),
        P("pp", ("node", "local"), None),
        P("pp", "node", "local", None),
        P("pp", "node", None, "local"),
    )
    out_specs = (P("pp", ("node", "local"), None), P("pp", ("node", "local"), None))
    paired = mesh.shape["node"] == 2 and mesh.shape["local"] == 4
    plan = body_pair if paired else body
    return jax.shard_map(plan, mesh=mesh, in_specs=in_specs, out_specs=out_specs, check_vma=False)
```

```python
import jax
import jax.numpy as jnp
from jax import lax
from jax.experimental import pallas as pl
from jax.experimental.pallas import tpu as pltpu
from jax.sharding import PartitionSpec as P

F32 = jnp.float32
BF16 = jnp.bfloat16
AXES = ("pp", "node", "local")


def move(value, by_pp=0, by_node=0, by_local=0, wrap=True, first=0, last=None):
    pps, nodes, locs = (lax.axis_size(a) for a in AXES)
    last = locs - 1 if last is None else last
    pairs = []
    for s in range(pps):
        for n in range(nodes):
            for l in range(locs):
                to = l + by_local
                if not wrap and not (first <= l <= last and 0 <= to < locs):
                    continue
                source = (s * nodes + n) * locs + l
                target = (((s + by_pp) % pps) * nodes + (n ^ by_node)) * locs + to % locs
                pairs.append((source, target))
    return lax.ppermute(value, AXES, pairs)


def sorted_places(route):
    ones = route.astype(F32)
    count = route.shape[0]
    earlier = (jnp.arange(count)[None, :] < jnp.arange(count)[:, None]).astype(F32)
    ones_before = jnp.dot(earlier, ones[:, None], preferred_element_type=F32)[:, 0]
    zeros = count - jnp.sum(ones)
    index = jnp.arange(count, dtype=F32)
    place = jnp.where(route == 0, index - ones_before, zeros + ones_before)
    return place.astype(jnp.int32)


def sorter(route):
    place = sorted_places(route)
    rows = jnp.arange(route.shape[0], dtype=jnp.int32)
    return (rows[:, None] == place[None, :]).astype(BF16)


def one_hot(row, count):
    return (row[:, None] == jnp.arange(count, dtype=jnp.int32)[None, :]).astype(BF16)


def dot_t(left, right):
    return lax.dot_general(left, right, (((1,), (1,)), ((), ())), preferred_element_type=F32)


def windows(blocks, node, capacity):
    tokens = blocks.shape[-2]
    start = tokens - capacity
    low = lax.slice_in_dim(blocks, 0, capacity, axis=-2 + blocks.ndim)
    high = lax.slice_in_dim(blocks, start, tokens, axis=-2 + blocks.ndim)
    own = jnp.where(node == 0, low, high)
    other = jnp.where(node == 0, high, low)
    return own, other


def join(*values):
    return lax.optimization_barrier(values)


def after(values, *others):
    return list(join(*values, *others)[: len(values)])


def cut(tokens, placer, local):
    column = tokens.shape[1] // 4
    blocks = []
    for m in range(4):
        block = lax.dynamic_slice_in_dim(tokens, ((local - m) % 4) * column, column, axis=1)
        blocks.append(jnp.dot(placer, block, preferred_element_type=F32).astype(BF16))
    return blocks


def sums(partial):
    right, left = partial(3), partial(1)
    for step in (1, 2, 3):
        right, left = right.astype(BF16), left.astype(BF16)
        got_r, got_l = yield (
            (right, dict(by_local=1, wrap=False, last=step - 1)),
            (left, dict(by_local=-1, wrap=False, first=4 - step)),
        )
        right = partial(3 - step).astype(F32) + got_r.astype(F32)
        if step < 3:
            left = partial(step + 1).astype(F32) + got_l.astype(F32)
    yield right + got_l.astype(F32)


def gathers(rows, local):
    from_left, from_right = [rows], [rows]
    for step in (1, 2, 3):
        got_r, got_l = yield (
            (from_left[-1], dict(by_local=1, wrap=False, first=step - 1)),
            (from_right[-1], dict(by_local=-1, wrap=False, last=4 - step)),
        )
        from_left.append(got_r)
        from_right.append(got_l)
    slots = [rows]
    for m in (1, 2, 3):
        slots.append(jnp.where(local + m < 4, from_right[m], from_left[4 - m]))
    yield jnp.stack(slots)


def send(pieces):
    return [move(value, **how) for value, how in pieces]


def operands(pieces):
    return [value for value, _ in pieces]


def valid(zeros, node, tokens, capacity):
    row = jnp.arange(capacity, dtype=F32)[None, :]
    return jnp.where(node == 0, row < zeros[:, None], row + (tokens - capacity) >= zeros[:, None])


def merge(own, other, node, tokens):
    slots, capacity, column = own.shape
    low = jnp.where(node == 0, own, other)
    high = jnp.where(node == 0, other, own)
    rest = jnp.zeros((slots, tokens - capacity, column), own.dtype)
    return jnp.concatenate([low, rest], axis=1) + jnp.concatenate([rest, high], axis=1)


def homeward(merged, by_pp):
    return [(merged[m], dict(by_pp=by_pp, by_local=m)) for m in (2, 1, 3, 0)]


def finish_kernel(at_ref, residual_ref, weight_ref, pick_ref, *refs):
    *blocks, out_ref, rows, sem = refs
    count = len(blocks)
    column = rows.shape[-1]
    copies = [pltpu.make_async_copy(blocks[i], rows.at[i], sem.at[i]) for i in range(count)]
    for copy in copies:
        copy.start()
    for i in range(count):
        copies[i].wait()
        cols = pl.ds(pl.multiple_of(at_ref[i] * column, column), column)
        moe = jnp.dot(pick_ref[...], rows[i], preferred_element_type=F32)
        total = residual_ref[:, cols].astype(F32) + weight_ref[...] * moe
        out_ref[0, :, cols] = total.astype(out_ref.dtype)


def finish(residual, weight, place, blocks, at):
    column = blocks[0].shape[-1]
    tokens, features = residual.shape
    vmem = pl.BlockSpec(memory_space=pltpu.VMEM)
    anywhere = pl.BlockSpec(memory_space=pl.ANY)
    return pl.pallas_call(
        finish_kernel,
        out_shape=jax.ShapeDtypeStruct((1, tokens, features), BF16),
        in_specs=[pl.BlockSpec(memory_space=pltpu.SMEM)] + [vmem] * 3 + [anywhere] * len(blocks),
        out_specs=vmem,
        scratch_shapes=[
            pltpu.VMEM((len(blocks), tokens, column), BF16),
            pltpu.SemaphoreType.DMA((len(blocks),)),
        ],
        compiler_params=pltpu.CompilerParams(vmem_limit_bytes=8 * 2**20),
        name="finish",
    )(at, residual, weight[:, None], one_hot(place, tokens), *blocks)


def body_pair(
    act_fwd, routes_fwd, weight_fwd, grad_bwd, routes_bwd, weight_bwd, saved_bwd, w_gate_up, w_down
):
    node = lax.axis_index("node")
    local = lax.axis_index("local")
    tokens_here = act_fwd.shape[1]
    capacity = 5 * tokens_here // 8
    w_gu = w_gate_up[0, 0]
    w_dn = w_down[0, 0]
    hidden_units = w_dn.shape[0]
    shape = (4, 2, capacity)

    act, grad = act_fwd[0], grad_bwd[0]
    route_a, route_b = routes_fwd[0, :, 0], routes_bwd[0, :, 0]
    sort_a = sorter(route_a)
    zeros = tokens_here - jnp.stack([jnp.sum(route_a), jnp.sum(route_b)]).astype(F32)

    def in_rows(cuts, got):
        return windows(jnp.stack([cuts[0], got[1], got[0], got[2]]), node, capacity)

    def by_node(own, got, axis):
        return jnp.stack([jnp.where(node == 0, own, got), jnp.where(node == 0, got, own)], axis=axis)

    def split(done):
        own = lax.dynamic_index_in_dim(done, node, axis=1, keepdims=False)
        other = lax.dynamic_index_in_dim(done, 1 - node, axis=1, keepdims=False)
        return own, other

    def turn(chain, back, *others):
        pieces = chain.send(after(back, *others))
        return operands(pieces), send(pieces)

    dy = (weight_bwd[0][:, None] * grad.astype(F32)).astype(BF16)
    sort_b = sorter(route_b)
    cut_b = cut(dy, sort_b, local)
    got_b = [move(cut_b[m], by_local=-m) for m in (2, 1, 3)]
    saved = jnp.dot(sort_b, saved_bwd[0], preferred_element_type=F32).astype(BF16)
    saved_own, saved_other = windows(saved, node, capacity)
    extra = jnp.broadcast_to(jnp.repeat(zeros, 8)[:, None], (16, saved.shape[1])).astype(BF16)
    saved_got = move(jnp.concatenate([saved_other, extra], axis=0), by_node=1)
    cut_a = cut(act, sort_a, local)
    *got_b, saved_got, a0, a1, a2, a3 = join(*got_b, saved_got, *cut_a)
    cut_a = [a0, a1, a2, a3]
    zeros_got = saved_got[capacity::8, 0].astype(F32)
    saved_got = saved_got[:capacity]
    zeros = by_node(zeros, zeros_got, 0)
    got_a = [move(cut_a[m], by_local=-m) for m in (2, 1, 3)]
    own_b, other_b = in_rows(cut_b, got_b)
    column = own_b.shape[-1]
    got_bx = move(other_b, by_node=1)

    rows_b = by_node(own_b, got_bx, 1).reshape(-1, column)
    part_b = dot_t(rows_b, w_dn).astype(BF16).reshape(shape + (hidden_units,))
    back_b = [move(part_b[m], by_local=m) for m in (2, 1, 3)]
    both = join(*back_b, *got_a)
    back_b, got_a = both[:3], both[3:]
    own_a, other_a = in_rows(cut_a, got_a)
    got_ax = move(other_a, by_node=1)
    dh = part_b[0].astype(F32) + sum(part.astype(F32) for part in back_b)
    dh = jnp.where(valid(zeros[:, 1], node, tokens_here, capacity)[..., None], dh, 0.0)
    saved_rows = by_node(saved_own, saved_got, 0)
    g = saved_rows[..., :hidden_units].astype(F32)
    u = saved_rows[..., hidden_units:].astype(F32)
    q = 1.0 / (1.0 + jnp.exp(-g))
    grad_gu = jnp.concatenate([dh * u * q * (1.0 + g * (1.0 - q)), dh * g * q], axis=-1).astype(
        BF16
    )

    chain_b = gathers(grad_gu, local)
    back_b = send(next(chain_b))
    small_wait, route_wait = after(
        [jnp.stack([route_a.astype(F32), weight_fwd[0]]), route_b], grad_gu
    )
    small_next = move(small_wait, by_pp=1)
    route_b_next = move(route_wait, by_pp=-1)
    rows_a = by_node(own_a, got_ax, 1).reshape(-1, column)
    part_a = jnp.dot(rows_a, w_gu, preferred_element_type=F32).astype(BF16)
    *back_b, part_a, small_next, route_b_next = join(*back_b, part_a, small_next, route_b_next)
    part_a = part_a.reshape(shape + (2 * hidden_units,))
    chain_a = sums(lambda slot: part_a[slot])
    values_b, back_b = turn(chain_b, back_b)
    pieces = next(chain_a)
    back_a = send(pieces)
    act_next = move(after([act], *operands(pieces))[0], by_pp=1)
    *back_b, act_next = join(*back_b, act_next)
    values_b, back_b = turn(chain_b, back_b)
    grad_next = move(join(grad, *values_b)[0], by_pp=-1)
    *back_b, grad_next = join(*back_b, grad_next)
    values_a, back_a = turn(chain_a, back_a)
    values_a, back_a = turn(chain_a, back_a)
    all_gu = chain_b.send(back_b)
    done_b = dot_t(all_gu.reshape(-1, 2 * hidden_units), w_gu).astype(BF16)
    own_b, other_b = split(done_b.reshape(shape + (column,)))
    got_b = move(other_b, by_node=1)

    preact = chain_a.send(back_a)
    preact = jnp.where(valid(zeros[:, 0], node, tokens_here, capacity)[..., None], preact, 0.0)
    hidden = (jax.nn.silu(preact[..., :hidden_units]) * preact[..., hidden_units:]).astype(BF16)
    all_hidden = [move(hidden, by_local=-m) for m in (1, 2, 3)]
    merged_b = merge(own_b, got_b, node, tokens_here)
    h1, h2, h3, merged_b = join(*all_hidden, merged_b)
    all_hidden = jnp.stack([hidden, h1, h2, h3])
    home_b = send(homeward(merged_b, -1))
    done_a = jnp.dot(
        all_hidden.reshape(-1, hidden_units), w_dn, preferred_element_type=F32
    ).astype(BF16)
    own_a, other_a = split(done_a.reshape(shape + (column,)))
    got_a = move(other_a, by_node=1)
    home_a = send(homeward(merge(own_a, got_a, node, tokens_here), 1))

    at = jnp.stack([(local - m) % 4 for m in (2, 1, 3, 0)]).astype(jnp.int32)
    ones = jnp.ones((tokens_here,), F32)
    prev_grad = finish(grad_next, ones, sorted_places(route_b_next), home_b, at)
    place_a = sorted_places(small_next[0].astype(jnp.int32))
    next_input = finish(act_next, small_next[1], place_a, home_a, at)
    return next_input, prev_grad


def from_behind(value, axis, by):
    length = lax.axis_size(axis)
    return lax.ppermute(value, axis, [(i, (i + by) % length) for i in range(length)])


def place_matrix(route, expert_count, capacity):
    onehot = (route[:, None] == jnp.arange(expert_count, dtype=jnp.int32)[None, :]).astype(
        jnp.int32
    )
    before = jnp.cumsum(onehot, axis=0) - onehot
    slot_index = jnp.sum(before * onehot, axis=1)
    target = route * capacity + slot_index
    positions = jnp.arange(expert_count * capacity, dtype=jnp.int32)
    return (positions[:, None] == target[None, :]).astype(jnp.bfloat16)


def pack_rows(placer, values, expert_count, capacity):
    packed = jnp.dot(placer, values, preferred_element_type=jnp.float32).astype(jnp.bfloat16)
    return packed.reshape(expert_count, capacity, values.shape[1])


def unpack_rows(placer, packed):
    flattened = packed.reshape(-1, packed.shape[-1])
    result = lax.dot_general(
        placer, flattened, (((0,), (0,)), ((), ())), preferred_element_type=jnp.float32
    )
    return result.astype(jnp.bfloat16)


def flat_outgoing(packed, local_count):
    expert_count, capacity, feature_count = packed.shape
    column = feature_count // local_count
    outgoing = packed.reshape(expert_count, capacity, local_count, column).transpose(0, 2, 1, 3)
    return outgoing.reshape(expert_count * local_count, capacity, column)


def flat_layout(received, expert_count, local_count):
    capacity = received.shape[1]
    column = received.shape[2]
    rows_in = received.reshape(expert_count, local_count, capacity, column).transpose(1, 0, 2, 3)
    return rows_in.reshape(-1, column)


def send_rows(packs, local_count):
    expert_count = packs[0].shape[0]
    outgoing = tuple((flat_outgoing(packed, local_count) for packed in packs))
    received = (
        lax.all_to_all(outgoing[0], ("node", "local"), split_axis=0, concat_axis=0, tiled=True),
        lax.all_to_all(outgoing[1], ("node", "local"), split_axis=0, concat_axis=0, tiled=True),
    )
    return tuple((flat_layout(item, expert_count, local_count) for item in received))


def return_rows(finished_pair, expert_count, capacity, local_count):
    column = finished_pair[0].shape[1]
    blocks = tuple(
        (item.reshape(local_count, expert_count, capacity, column) for item in finished_pair)
    )
    outgoing = tuple(
        (
            item.transpose(1, 0, 2, 3).reshape(expert_count * local_count, capacity, column)
            for item in blocks
        )
    )
    received = (
        lax.all_to_all(outgoing[0], ("node", "local"), split_axis=0, concat_axis=0, tiled=True),
        lax.all_to_all(outgoing[1], ("node", "local"), split_axis=0, concat_axis=0, tiled=True),
    )
    results = []
    for item in received:
        arranged = item.reshape(expert_count, local_count, capacity, column).transpose(0, 2, 1, 3)
        results.append(arranged.reshape(expert_count, capacity, local_count * column))
    return tuple(results)


def body(
    act_fwd, routes_fwd, weight_fwd, grad_bwd, routes_bwd, weight_bwd, saved_bwd, w_gate_up, w_down
):
    node_count = lax.axis_size("node")
    local_count = lax.axis_size("local")
    tokens_here = act_fwd.shape[1]
    capacity = 5 * tokens_here // (4 * node_count)
    rows_each = node_count * capacity
    w_gu = w_gate_up[0, 0]
    w_dn = w_down[0, 0]
    hidden_units = w_dn.shape[0]
    tokens_a = act_fwd[0]
    placer_a = place_matrix(routes_fwd[0, :, 0], node_count, capacity)
    cotangent = grad_bwd[0]
    placer_b = place_matrix(routes_bwd[0, :, 0], node_count, capacity)
    scaled = (weight_bwd[0][:, None] * cotangent.astype(jnp.float32)).astype(jnp.bfloat16)
    packed_a = pack_rows(placer_a, tokens_a, node_count, capacity)
    packed_b = pack_rows(placer_b, scaled, node_count, capacity)
    rows_a, rows_b = send_rows((packed_a, packed_b), local_count)
    saved_packed = pack_rows(placer_b, saved_bwd[0], node_count, capacity)
    saved_rows = lax.all_to_all(
        saved_packed, "node", split_axis=0, concat_axis=0, tiled=True
    ).reshape(rows_each, -1)
    row_block = rows_a
    preact = lax.psum_scatter(
        jnp.dot(row_block, w_gu, preferred_element_type=jnp.float32).astype(jnp.bfloat16),
        "local",
        scatter_dimension=0,
        tiled=True,
    ).astype(jnp.float32)
    row_block = rows_b
    grad_hidden = lax.psum_scatter(
        lax.dot_general(
            row_block, w_dn, (((1,), (1,)), ((), ())), preferred_element_type=jnp.float32
        ).astype(jnp.bfloat16),
        "local",
        scatter_dimension=0,
        tiled=True,
    ).astype(jnp.float32)
    hidden = (jax.nn.silu(preact[:, :hidden_units]) * preact[:, hidden_units:]).astype(jnp.bfloat16)
    done_a = jnp.dot(
        lax.all_gather(hidden, "local", axis=0, tiled=True),
        w_dn,
        preferred_element_type=jnp.float32,
    ).astype(jnp.bfloat16)
    gate_pre = saved_rows[:, :hidden_units].astype(jnp.float32)
    up_pre = saved_rows[:, hidden_units:].astype(jnp.float32)
    sigmoid_g = 1.0 / (1.0 + jnp.exp(-gate_pre))
    grad_gate = grad_hidden * up_pre * sigmoid_g * (1.0 + gate_pre * (1.0 - sigmoid_g))
    grad_up = grad_hidden * gate_pre * sigmoid_g
    grad_gu = jnp.concatenate([grad_gate, grad_up], axis=1).astype(jnp.bfloat16)
    product = lax.dot_general(
        lax.all_gather(grad_gu, "local", axis=0, tiled=True),
        w_gu,
        (((1,), (1,)), ((), ())),
        preferred_element_type=jnp.float32,
    )
    done_b = product.astype(jnp.bfloat16)
    back_a, back_b = return_rows((done_a, done_b), node_count, capacity, local_count)
    moe_a = unpack_rows(placer_a, back_a)
    result_a = tokens_a.astype(jnp.float32) + weight_fwd[0][:, None] * moe_a.astype(jnp.float32)
    result_a = result_a.astype(jnp.bfloat16)
    moe_b = unpack_rows(placer_b, back_b)
    result_b = (cotangent.astype(jnp.float32) + moe_b.astype(jnp.float32)).astype(jnp.bfloat16)
    next_input = from_behind(result_a[None], "pp", 1)
    prev_grad = from_behind(result_b[None], "pp", -1)
    return (next_input, prev_grad)


def solution(mesh):
    in_specs = (
        P("pp", ("node", "local"), None),
        P("pp", ("node", "local"), None),
        P("pp", ("node", "local")),
        P("pp", ("node", "local"), None),
        P("pp", ("node", "local"), None),
        P("pp", ("node", "local")),
        P("pp", ("node", "local"), None),
        P("pp", "node", "local", None),
        P("pp", "node", None, "local"),
    )
    out_specs = (P("pp", ("node", "local"), None), P("pp", ("node", "local"), None))
    paired = mesh.shape["node"] == 2 and mesh.shape["local"] == 4
    plan = body_pair if paired else body
    return jax.shard_map(plan, mesh=mesh, in_specs=in_specs, out_specs=out_specs, check_vma=False)
```

```python
import jax
import jax.numpy as jnp
from jax import lax
from jax.experimental import pallas as pl
from jax.experimental.pallas import tpu as pltpu
from jax.sharding import PartitionSpec as P

F32 = jnp.float32
BF16 = jnp.bfloat16
AXES = ("pp", "node", "local")


def move(value, by_pp=0, by_node=0, by_local=0, wrap=True):
    pps, nodes, locs = (lax.axis_size(a) for a in AXES)
    pairs = []
    for s in range(pps):
        for n in range(nodes):
            for l in range(locs):
                to = l + by_local
                if not wrap and not 0 <= to < locs:
                    continue
                source = (s * nodes + n) * locs + l
                target = (((s + by_pp) % pps) * nodes + (n ^ by_node)) * locs + to % locs
                pairs.append((source, target))
    return lax.ppermute(value, AXES, pairs)


def sorted_places(route):
    ones = route.astype(F32)
    count = route.shape[0]
    earlier = (jnp.arange(count)[None, :] < jnp.arange(count)[:, None]).astype(F32)
    ones_before = jnp.dot(earlier, ones[:, None], preferred_element_type=F32)[:, 0]
    zeros = count - jnp.sum(ones)
    index = jnp.arange(count, dtype=F32)
    place = jnp.where(route == 0, index - ones_before, zeros + ones_before)
    return place.astype(jnp.int32)


def sorter(route):
    place = sorted_places(route)
    rows = jnp.arange(route.shape[0], dtype=jnp.int32)
    return (rows[:, None] == place[None, :]).astype(BF16)


def one_hot(row, count):
    return (row[:, None] == jnp.arange(count, dtype=jnp.int32)[None, :]).astype(BF16)


def dot_t(left, right):
    return lax.dot_general(left, right, (((1,), (1,)), ((), ())), preferred_element_type=F32)


def windows(blocks, node, capacity):
    tokens = blocks.shape[-2]
    start = tokens - capacity
    low = lax.slice_in_dim(blocks, 0, capacity, axis=-2 + blocks.ndim)
    high = lax.slice_in_dim(blocks, start, tokens, axis=-2 + blocks.ndim)
    own = jnp.where(node == 0, low, high)
    other = jnp.where(node == 0, high, low)
    return own, other


def join(*values):
    return lax.optimization_barrier(values)


def picker_of(route_ref):
    tokens = route_ref.shape[1]
    row = lax.broadcasted_iota(jnp.int32, (tokens, tokens), 0)
    col = lax.broadcasted_iota(jnp.int32, (tokens, tokens), 1)
    ones = route_ref[...].astype(F32)
    before = jnp.dot(
        jnp.broadcast_to(ones, (8, tokens)).astype(BF16),
        (row < col).astype(BF16),
        preferred_element_type=F32,
    )[0:1]
    zeros = tokens - jnp.sum(ones, axis=1, keepdims=True)
    index = col[0:1].astype(F32)
    place = jnp.where(ones == 0.0, index - before, zeros + before).astype(jnp.int32)
    return (row == place).astype(BF16), zeros


def cut_kernel(at_ref, route_ref, weight_ref, values_ref, *rest):
    blocks = rest[-4:]
    column = blocks[0].shape[1]
    picker, zeros = picker_of(route_ref)
    for i, block_ref in enumerate(blocks):
        cols = pl.ds(pl.multiple_of(at_ref[i] * column, column), column)
        block = (weight_ref[...] * values_ref[:, cols].astype(F32)).astype(BF16)
        block_ref[...] = jnp.dot(picker, block, preferred_element_type=F32).astype(BF16)
    if len(rest) > 4:
        other_route_ref, saved_ref, own_ref, other_ref = rest[:4]
        capacity, width = own_ref.shape
        saved = jnp.dot(picker, saved_ref[...], preferred_element_type=F32)
        low, high = saved[:capacity], saved[saved.shape[0] - capacity :]
        first = at_ref[4] == 0
        own_ref[...] = jnp.where(first, low, high).astype(BF16)
        other_ref[:capacity] = jnp.where(first, high, low).astype(BF16)
        zeros_other = other_route_ref.shape[1] - jnp.sum(
            other_route_ref[...].astype(F32), axis=1, keepdims=True
        )
        upper = lax.broadcasted_iota(jnp.int32, (16, width), 0) < 8
        other_ref[capacity:] = jnp.where(upper, zeros_other, zeros).astype(BF16)


def cut(tokens, weight, route, node, local, capacity, other_route=None, saved=None):
    rows, features = tokens.shape
    vmem = pl.BlockSpec(memory_space=pltpu.VMEM)
    at = jnp.stack([(local - m) % 4 for m in range(4)] + [node]).astype(jnp.int32)
    out_shape = [jax.ShapeDtypeStruct((rows, features // 4), BF16)] * 4
    more = []
    if saved is not None:
        more = [other_route[None, :], saved]
        width = saved.shape[1]
        out_shape = [
            jax.ShapeDtypeStruct((capacity, width), BF16),
            jax.ShapeDtypeStruct((capacity + 16, width), BF16),
        ] + out_shape
    return list(
        pl.pallas_call(
            cut_kernel,
            out_shape=out_shape,
            in_specs=[pl.BlockSpec(memory_space=pltpu.SMEM)] + [vmem] * (3 + len(more)),
            out_specs=[vmem] * len(out_shape),
            compiler_params=pltpu.CompilerParams(vmem_limit_bytes=10 * 2**20),
            name="cut",
        )(at, route[None, :], weight[:, None], tokens, *more)
    )


def send(pieces):
    return [move(value, **how) for value, how in pieces]


def both_ways(right, left):
    right, left = right.astype(BF16), left.astype(BF16)
    return move(right, by_local=1, wrap=False), move(left, by_local=-1, wrap=False)


def valid(zeros, node, tokens, capacity):
    row = jnp.arange(capacity, dtype=F32)[None, :]
    return jnp.where(node == 0, row < zeros[:, None], row + (tokens - capacity) >= zeros[:, None])


def merge(own, other, node, tokens):
    slots, capacity, column = own.shape
    low = jnp.where(node == 0, own, other)
    high = jnp.where(node == 0, other, own)
    rest = jnp.zeros((slots, tokens - capacity, column), own.dtype)
    return jnp.concatenate([low, rest], axis=1) + jnp.concatenate([rest, high], axis=1)


def homeward(merged, by_pp):
    return [(merged[m], dict(by_pp=by_pp, by_local=m)) for m in (2, 1, 3, 0)]


def finish_kernel(at_ref, residual_ref, weight_ref, pick_ref, *refs):
    *blocks, out_ref, rows, sem = refs
    count = len(blocks)
    column = rows.shape[-1]
    copies = [pltpu.make_async_copy(blocks[i], rows.at[i], sem.at[i]) for i in range(count)]
    for copy in copies:
        copy.start()
    for i in range(count):
        copies[i].wait()
        cols = pl.ds(pl.multiple_of(at_ref[i] * column, column), column)
        moe = jnp.dot(pick_ref[...], rows[i], preferred_element_type=F32)
        total = residual_ref[:, cols].astype(F32) + weight_ref[...] * moe
        out_ref[0, :, cols] = total.astype(out_ref.dtype)


def finish(residual, weight, place, blocks, at):
    column = blocks[0].shape[-1]
    tokens, features = residual.shape
    vmem = pl.BlockSpec(memory_space=pltpu.VMEM)
    anywhere = pl.BlockSpec(memory_space=pl.ANY)
    return pl.pallas_call(
        finish_kernel,
        out_shape=jax.ShapeDtypeStruct((1, tokens, features), BF16),
        in_specs=[pl.BlockSpec(memory_space=pltpu.SMEM)] + [vmem] * 3 + [anywhere] * len(blocks),
        out_specs=vmem,
        scratch_shapes=[
            pltpu.VMEM((len(blocks), tokens, column), BF16),
            pltpu.SemaphoreType.DMA((len(blocks),)),
        ],
        compiler_params=pltpu.CompilerParams(vmem_limit_bytes=8 * 2**20),
        name="finish",
    )(at, residual, weight[:, None], one_hot(place, tokens), *blocks)


def body_pair(
    act_fwd, routes_fwd, weight_fwd, grad_bwd, routes_bwd, weight_bwd, saved_bwd, w_gate_up, w_down
):
    node = lax.axis_index("node")
    local = lax.axis_index("local")
    tokens_here = act_fwd.shape[1]
    capacity = 5 * tokens_here // 8
    w_gu = w_gate_up[0, 0]
    w_dn = w_down[0, 0]
    hidden_units = w_dn.shape[0]
    shape = (4, 2, capacity)

    act, grad = act_fwd[0], grad_bwd[0]
    route_a, route_b = routes_fwd[0, :, 0], routes_bwd[0, :, 0]
    zeros = tokens_here - jnp.stack([jnp.sum(route_a), jnp.sum(route_b)]).astype(F32)

    def in_rows(cuts, got):
        return windows(jnp.stack([cuts[0], got[1], got[0], got[2]]), node, capacity)

    def by_node(own, got, axis):
        return jnp.stack([jnp.where(node == 0, own, got), jnp.where(node == 0, got, own)], axis=axis)

    def split(done):
        own = lax.dynamic_index_in_dim(done, node, axis=1, keepdims=False)
        other = lax.dynamic_index_in_dim(done, 1 - node, axis=1, keepdims=False)
        return own, other

    saved_own, saved_other, *cut_b = cut(
        grad, weight_bwd[0], route_b, node, local, capacity, route_a, saved_bwd[0]
    )
    got_b = [move(cut_b[m], by_local=-m) for m in (2, 1, 3)]
    saved_got = move(saved_other, by_node=1)
    cut_a = cut(act, jnp.ones((tokens_here,), F32), route_a, node, local, capacity)
    *got_b, saved_got, a0, a1, a2, a3 = join(*got_b, saved_got, *cut_a)
    cut_a = [a0, a1, a2, a3]
    got_a = [move(cut_a[m], by_local=-m) for m in (2, 1, 3)]
    own_b, other_b = in_rows(cut_b, got_b)
    column = own_b.shape[-1]
    got_bx = move(other_b, by_node=1)

    rows_b = by_node(own_b, got_bx, 1).reshape(-1, column)
    part_b = dot_t(rows_b, w_dn).astype(BF16).reshape(shape + (hidden_units,))
    back_b = [move(part_b[m], by_local=m) for m in (2, 1, 3)]
    both = join(*back_b, *got_a)
    back_b, got_a = both[:3], both[3:]
    zeros_got = saved_got[capacity::8, 0].astype(F32)
    saved_got = saved_got[:capacity]
    zeros = by_node(zeros, zeros_got, 0)
    own_a, other_a = in_rows(cut_a, got_a)
    got_ax = move(other_a, by_node=1)
    dh = part_b[0].astype(F32) + sum(part.astype(F32) for part in back_b)
    dh = jnp.where(valid(zeros[:, 1], node, tokens_here, capacity)[..., None], dh, 0.0)
    saved_rows = by_node(saved_own, saved_got, 0)
    g = saved_rows[..., :hidden_units].astype(F32)
    u = saved_rows[..., hidden_units:].astype(F32)
    q = 1.0 / (1.0 + jnp.exp(-g))
    grad_gu = jnp.concatenate([dh * u * q * (1.0 + g * (1.0 - q)), dh * g * q], axis=-1).astype(
        BF16
    )

    small = jnp.stack([route_a.astype(F32), weight_fwd[0]])
    grad_gu, small, route_next = join(grad_gu, small, route_b)
    got_r, got_l = both_ways(grad_gu, grad_gu)
    small_next = move(small, by_pp=1)
    route_b_next = move(route_next, by_pp=-1)
    rows_a = by_node(own_a, got_ax, 1).reshape(-1, column)
    part_a = jnp.dot(rows_a, w_gu, preferred_element_type=F32).astype(BF16)
    got_r, got_l, part_a, small_next, route_b_next, act_in, grad_in = join(
        got_r, got_l, part_a, small_next, route_b_next, act, grad
    )
    part_a = part_a.reshape(shape + (2 * hidden_units,))
    lefts, rights = [grad_gu, got_r], [grad_gu, got_l]

    got_r, got_l = both_ways(
        jnp.where(local == 0, part_a[3], got_r),
        jnp.where(local == 3, part_a[1], got_l),
    )
    act_next = move(act_in, by_pp=1)
    got_r, got_l, act_next, grad_in = join(got_r, got_l, act_next, grad_in)
    lefts.append(got_r)
    rights.append(got_l)

    got_r, got_l = got_r.astype(F32), got_l.astype(F32)
    got_r, got_l = both_ways(
        jnp.where(local == 2, 0.0, part_a[2].astype(F32)) + jnp.where(local == 0, 0.0, got_r),
        jnp.where(local == 1, 0.0, part_a[2].astype(F32)) + jnp.where(local == 3, 0.0, got_l),
    )
    grad_next = move(grad_in, by_pp=-1)
    got_r, got_l, grad_next = join(got_r, got_l, grad_next)
    lefts.append(got_r)
    rights.append(got_l)

    middle = (local == 1) | (local == 2)
    got_r, got_l = both_ways(
        part_a[1].astype(F32) + jnp.where(middle, got_r.astype(F32), 0.0),
        part_a[3].astype(F32) + jnp.where(middle, got_l.astype(F32), 0.0),
    )
    preact = part_a[0].astype(F32) + got_r.astype(F32) + got_l.astype(F32)

    all_gu = jnp.stack(
        [grad_gu] + [jnp.where(local + m < 4, rights[m], lefts[4 - m]) for m in (1, 2, 3)]
    )
    done_b = dot_t(all_gu.reshape(-1, 2 * hidden_units), w_gu).astype(BF16)
    own_b, other_b = split(done_b.reshape(shape + (column,)))
    got_b = move(other_b, by_node=1)

    preact = jnp.where(valid(zeros[:, 0], node, tokens_here, capacity)[..., None], preact, 0.0)
    hidden = (jax.nn.silu(preact[..., :hidden_units]) * preact[..., hidden_units:]).astype(BF16)
    all_hidden = [move(hidden, by_local=-m) for m in (1, 2, 3)]
    merged_b = merge(own_b, got_b, node, tokens_here)
    h1, h2, h3, merged_b = join(*all_hidden, merged_b)
    all_hidden = jnp.stack([hidden, h1, h2, h3])
    home_b = send(homeward(merged_b, -1))
    done_a = jnp.dot(
        all_hidden.reshape(-1, hidden_units), w_dn, preferred_element_type=F32
    ).astype(BF16)
    own_a, other_a = split(done_a.reshape(shape + (column,)))
    got_a = move(other_a, by_node=1)
    home_a = send(homeward(merge(own_a, got_a, node, tokens_here), 1))

    at = jnp.stack([(local - m) % 4 for m in (2, 1, 3, 0)]).astype(jnp.int32)
    ones = jnp.ones((tokens_here,), F32)
    prev_grad = finish(grad_next, ones, sorted_places(route_b_next), home_b, at)
    place_a = sorted_places(small_next[0].astype(jnp.int32))
    next_input = finish(act_next, small_next[1], place_a, home_a, at)
    return next_input, prev_grad


def from_behind(value, axis, by):
    length = lax.axis_size(axis)
    return lax.ppermute(value, axis, [(i, (i + by) % length) for i in range(length)])


def place_matrix(route, expert_count, capacity):
    onehot = (route[:, None] == jnp.arange(expert_count, dtype=jnp.int32)[None, :]).astype(
        jnp.int32
    )
    before = jnp.cumsum(onehot, axis=0) - onehot
    slot_index = jnp.sum(before * onehot, axis=1)
    target = route * capacity + slot_index
    positions = jnp.arange(expert_count * capacity, dtype=jnp.int32)
    return (positions[:, None] == target[None, :]).astype(jnp.bfloat16)


def pack_rows(placer, values, expert_count, capacity):
    packed = jnp.dot(placer, values, preferred_element_type=jnp.float32).astype(jnp.bfloat16)
    return packed.reshape(expert_count, capacity, values.shape[1])


def unpack_rows(placer, packed):
    flattened = packed.reshape(-1, packed.shape[-1])
    result = lax.dot_general(
        placer, flattened, (((0,), (0,)), ((), ())), preferred_element_type=jnp.float32
    )
    return result.astype(jnp.bfloat16)


def flat_outgoing(packed, local_count):
    expert_count, capacity, feature_count = packed.shape
    column = feature_count // local_count
    outgoing = packed.reshape(expert_count, capacity, local_count, column).transpose(0, 2, 1, 3)
    return outgoing.reshape(expert_count * local_count, capacity, column)


def flat_layout(received, expert_count, local_count):
    capacity = received.shape[1]
    column = received.shape[2]
    rows_in = received.reshape(expert_count, local_count, capacity, column).transpose(1, 0, 2, 3)
    return rows_in.reshape(-1, column)


def send_rows(packs, local_count):
    expert_count = packs[0].shape[0]
    outgoing = tuple((flat_outgoing(packed, local_count) for packed in packs))
    received = (
        lax.all_to_all(outgoing[0], ("node", "local"), split_axis=0, concat_axis=0, tiled=True),
        lax.all_to_all(outgoing[1], ("node", "local"), split_axis=0, concat_axis=0, tiled=True),
    )
    return tuple((flat_layout(item, expert_count, local_count) for item in received))


def return_rows(finished_pair, expert_count, capacity, local_count):
    column = finished_pair[0].shape[1]
    blocks = tuple(
        (item.reshape(local_count, expert_count, capacity, column) for item in finished_pair)
    )
    outgoing = tuple(
        (
            item.transpose(1, 0, 2, 3).reshape(expert_count * local_count, capacity, column)
            for item in blocks
        )
    )
    received = (
        lax.all_to_all(outgoing[0], ("node", "local"), split_axis=0, concat_axis=0, tiled=True),
        lax.all_to_all(outgoing[1], ("node", "local"), split_axis=0, concat_axis=0, tiled=True),
    )
    results = []
    for item in received:
        arranged = item.reshape(expert_count, local_count, capacity, column).transpose(0, 2, 1, 3)
        results.append(arranged.reshape(expert_count, capacity, local_count * column))
    return tuple(results)


def body(
    act_fwd, routes_fwd, weight_fwd, grad_bwd, routes_bwd, weight_bwd, saved_bwd, w_gate_up, w_down
):
    node_count = lax.axis_size("node")
    local_count = lax.axis_size("local")
    tokens_here = act_fwd.shape[1]
    capacity = 5 * tokens_here // (4 * node_count)
    rows_each = node_count * capacity
    w_gu = w_gate_up[0, 0]
    w_dn = w_down[0, 0]
    hidden_units = w_dn.shape[0]
    tokens_a = act_fwd[0]
    placer_a = place_matrix(routes_fwd[0, :, 0], node_count, capacity)
    cotangent = grad_bwd[0]
    placer_b = place_matrix(routes_bwd[0, :, 0], node_count, capacity)
    scaled = (weight_bwd[0][:, None] * cotangent.astype(jnp.float32)).astype(jnp.bfloat16)
    packed_a = pack_rows(placer_a, tokens_a, node_count, capacity)
    packed_b = pack_rows(placer_b, scaled, node_count, capacity)
    rows_a, rows_b = send_rows((packed_a, packed_b), local_count)
    saved_packed = pack_rows(placer_b, saved_bwd[0], node_count, capacity)
    saved_rows = lax.all_to_all(
        saved_packed, "node", split_axis=0, concat_axis=0, tiled=True
    ).reshape(rows_each, -1)
    row_block = rows_a
    preact = lax.psum_scatter(
        jnp.dot(row_block, w_gu, preferred_element_type=jnp.float32).astype(jnp.bfloat16),
        "local",
        scatter_dimension=0,
        tiled=True,
    ).astype(jnp.float32)
    row_block = rows_b
    grad_hidden = lax.psum_scatter(
        lax.dot_general(
            row_block, w_dn, (((1,), (1,)), ((), ())), preferred_element_type=jnp.float32
        ).astype(jnp.bfloat16),
        "local",
        scatter_dimension=0,
        tiled=True,
    ).astype(jnp.float32)
    hidden = (jax.nn.silu(preact[:, :hidden_units]) * preact[:, hidden_units:]).astype(jnp.bfloat16)
    done_a = jnp.dot(
        lax.all_gather(hidden, "local", axis=0, tiled=True),
        w_dn,
        preferred_element_type=jnp.float32,
    ).astype(jnp.bfloat16)
    gate_pre = saved_rows[:, :hidden_units].astype(jnp.float32)
    up_pre = saved_rows[:, hidden_units:].astype(jnp.float32)
    sigmoid_g = 1.0 / (1.0 + jnp.exp(-gate_pre))
    grad_gate = grad_hidden * up_pre * sigmoid_g * (1.0 + gate_pre * (1.0 - sigmoid_g))
    grad_up = grad_hidden * gate_pre * sigmoid_g
    grad_gu = jnp.concatenate([grad_gate, grad_up], axis=1).astype(jnp.bfloat16)
    product = lax.dot_general(
        lax.all_gather(grad_gu, "local", axis=0, tiled=True),
        w_gu,
        (((1,), (1,)), ((), ())),
        preferred_element_type=jnp.float32,
    )
    done_b = product.astype(jnp.bfloat16)
    back_a, back_b = return_rows((done_a, done_b), node_count, capacity, local_count)
    moe_a = unpack_rows(placer_a, back_a)
    result_a = tokens_a.astype(jnp.float32) + weight_fwd[0][:, None] * moe_a.astype(jnp.float32)
    result_a = result_a.astype(jnp.bfloat16)
    moe_b = unpack_rows(placer_b, back_b)
    result_b = (cotangent.astype(jnp.float32) + moe_b.astype(jnp.float32)).astype(jnp.bfloat16)
    next_input = from_behind(result_a[None], "pp", 1)
    prev_grad = from_behind(result_b[None], "pp", -1)
    return (next_input, prev_grad)


def solution(mesh):
    in_specs = (
        P("pp", ("node", "local"), None),
        P("pp", ("node", "local"), None),
        P("pp", ("node", "local")),
        P("pp", ("node", "local"), None),
        P("pp", ("node", "local"), None),
        P("pp", ("node", "local")),
        P("pp", ("node", "local"), None),
        P("pp", "node", "local", None),
        P("pp", "node", None, "local"),
    )
    out_specs = (P("pp", ("node", "local"), None), P("pp", ("node", "local"), None))
    paired = mesh.shape["node"] == 2 and mesh.shape["local"] == 4
    plan = body_pair if paired else body
    return jax.shard_map(plan, mesh=mesh, in_specs=in_specs, out_specs=out_specs, check_vma=False)
```

```python
import jax
import jax.numpy as jnp
from jax import lax
from jax.experimental import pallas as pl
from jax.experimental.pallas import tpu as pltpu
from jax.sharding import PartitionSpec as P

F32 = jnp.float32
BF16 = jnp.bfloat16
AXES = ("pp", "node", "local")


def move(value, by_pp=0, by_node=0, by_local=0, wrap=True):
    pps, nodes, locs = (lax.axis_size(a) for a in AXES)
    pairs = []
    for s in range(pps):
        for n in range(nodes):
            for l in range(locs):
                to = l + by_local
                if not wrap and not 0 <= to < locs:
                    continue
                source = (s * nodes + n) * locs + l
                target = (((s + by_pp) % pps) * nodes + (n ^ by_node)) * locs + to % locs
                pairs.append((source, target))
    return lax.ppermute(value, AXES, pairs)


def sorted_places(route):
    ones = route.astype(F32)
    count = route.shape[0]
    earlier = (jnp.arange(count)[None, :] < jnp.arange(count)[:, None]).astype(F32)
    ones_before = jnp.dot(earlier, ones[:, None], preferred_element_type=F32)[:, 0]
    zeros = count - jnp.sum(ones)
    index = jnp.arange(count, dtype=F32)
    place = jnp.where(route == 0, index - ones_before, zeros + ones_before)
    return place.astype(jnp.int32)


def sorter(route):
    place = sorted_places(route)
    rows = jnp.arange(route.shape[0], dtype=jnp.int32)
    return (rows[:, None] == place[None, :]).astype(BF16)


def one_hot(row, count):
    return (row[:, None] == jnp.arange(count, dtype=jnp.int32)[None, :]).astype(BF16)


def dot_t(left, right):
    return lax.dot_general(left, right, (((1,), (1,)), ((), ())), preferred_element_type=F32)


def windows(blocks, node, capacity):
    tokens = blocks.shape[-2]
    start = tokens - capacity
    low = lax.slice_in_dim(blocks, 0, capacity, axis=-2 + blocks.ndim)
    high = lax.slice_in_dim(blocks, start, tokens, axis=-2 + blocks.ndim)
    own = jnp.where(node == 0, low, high)
    other = jnp.where(node == 0, high, low)
    return own, other


def join(*values):
    return lax.optimization_barrier(values)


def picker_of(route_ref):
    tokens = route_ref.shape[1]
    row = lax.broadcasted_iota(jnp.int32, (tokens, tokens), 0)
    col = lax.broadcasted_iota(jnp.int32, (tokens, tokens), 1)
    ones = route_ref[...].astype(F32)
    before = jnp.dot(
        jnp.broadcast_to(ones, (8, tokens)).astype(BF16),
        (row < col).astype(BF16),
        preferred_element_type=F32,
    )[0:1]
    zeros = tokens - jnp.sum(ones, axis=1, keepdims=True)
    index = col[0:1].astype(F32)
    place = jnp.where(ones == 0.0, index - before, zeros + before).astype(jnp.int32)
    return (row == place).astype(BF16), zeros


def column_of(row_ref):
    n = row_ref.shape[1]
    row = lax.broadcasted_iota(jnp.int32, (n, n), 0)
    col = lax.broadcasted_iota(jnp.int32, (n, n), 1)
    return jnp.sum(jnp.where(row == col, row_ref[...], 0.0), axis=1, keepdims=True)


def cut_kernel(at_ref, route_ref, weight_ref, values_ref, *rest):
    blocks = rest[-4:]
    column = blocks[0].shape[1]
    picker, zeros = picker_of(route_ref)
    weight = column_of(weight_ref)
    for i, block_ref in enumerate(blocks):
        cols = pl.ds(pl.multiple_of(at_ref[i] * column, column), column)
        block = (weight * values_ref[:, cols].astype(F32)).astype(BF16)
        block_ref[...] = jnp.dot(picker, block, preferred_element_type=F32).astype(BF16)
    if len(rest) > 4:
        other_route_ref, saved_ref, own_ref, other_ref = rest[:4]
        capacity, width = own_ref.shape
        saved = jnp.dot(picker, saved_ref[...], preferred_element_type=F32)
        low, high = saved[:capacity], saved[saved.shape[0] - capacity :]
        first = at_ref[4] == 0
        own_ref[...] = jnp.where(first, low, high).astype(BF16)
        other_ref[:capacity] = jnp.where(first, high, low).astype(BF16)
        zeros_other = other_route_ref.shape[1] - jnp.sum(
            other_route_ref[...].astype(F32), axis=1, keepdims=True
        )
        upper = lax.broadcasted_iota(jnp.int32, (16, width), 0) < 8
        other_ref[capacity:] = jnp.where(upper, zeros_other, zeros).astype(BF16)


def cut(tokens, weight, route, node, local, capacity, other_route=None, saved=None):
    rows, features = tokens.shape
    vmem = pl.BlockSpec(memory_space=pltpu.VMEM)
    at = jnp.stack([(local - m) % 4 for m in range(4)] + [node]).astype(jnp.int32)
    out_shape = [jax.ShapeDtypeStruct((rows, features // 4), BF16)] * 4
    more = []
    if saved is not None:
        more = [other_route[None, :], saved]
        width = saved.shape[1]
        out_shape = [
            jax.ShapeDtypeStruct((capacity, width), BF16),
            jax.ShapeDtypeStruct((capacity + 16, width), BF16),
        ] + out_shape
    return list(
        pl.pallas_call(
            cut_kernel,
            out_shape=out_shape,
            in_specs=[pl.BlockSpec(memory_space=pltpu.SMEM)] + [vmem] * (3 + len(more)),
            out_specs=[vmem] * len(out_shape),
            compiler_params=pltpu.CompilerParams(vmem_limit_bytes=48 * 2**20),
            name="cut",
        )(at, route[None, :], weight[None, :], tokens, *more)
    )


def send(pieces):
    return [move(value, **how) for value, how in pieces]


def both_ways(right, left):
    right, left = right.astype(BF16), left.astype(BF16)
    return move(right, by_local=1, wrap=False), move(left, by_local=-1, wrap=False)


def valid(zeros, node, tokens, capacity):
    row = jnp.arange(capacity, dtype=F32)
    zeros = zeros[..., None]
    return jnp.where(node == 0, row < zeros, row + (tokens - capacity) >= zeros)


def merge(own, other, node, tokens):
    slots, capacity, column = own.shape
    low = jnp.where(node == 0, own, other)
    high = jnp.where(node == 0, other, own)
    rest = jnp.zeros((slots, tokens - capacity, column), own.dtype)
    return jnp.concatenate([low, rest], axis=1) + jnp.concatenate([rest, high], axis=1)


def homeward(merged, by_pp):
    return [(merged[m], dict(by_pp=by_pp, by_local=m)) for m in (2, 1, 3, 0)]


def finish_kernel(at_ref, residual_ref, weight_ref, pick_ref, *refs):
    *blocks, out_ref, rows, sem = refs
    count = len(blocks)
    column = rows.shape[-1]
    copies = [pltpu.make_async_copy(blocks[i], rows.at[i], sem.at[i]) for i in range(count)]
    for copy in copies:
        copy.start()
    weight = column_of(weight_ref)
    for i in range(count):
        copies[i].wait()
        cols = pl.ds(pl.multiple_of(at_ref[i] * column, column), column)
        moe = jnp.dot(pick_ref[...], rows[i], preferred_element_type=F32)
        total = residual_ref[:, cols].astype(F32) + weight * moe
        out_ref[0, :, cols] = total.astype(out_ref.dtype)


def finish(residual, weight, place, blocks, at):
    column = blocks[0].shape[-1]
    tokens, features = residual.shape
    vmem = pl.BlockSpec(memory_space=pltpu.VMEM)
    anywhere = pl.BlockSpec(memory_space=pl.ANY)
    return pl.pallas_call(
        finish_kernel,
        out_shape=jax.ShapeDtypeStruct((1, tokens, features), BF16),
        in_specs=[pl.BlockSpec(memory_space=pltpu.SMEM)] + [vmem] * 3 + [anywhere] * len(blocks),
        out_specs=vmem,
        scratch_shapes=[
            pltpu.VMEM((len(blocks), tokens, column), BF16),
            pltpu.SemaphoreType.DMA((len(blocks),)),
        ],
        compiler_params=pltpu.CompilerParams(vmem_limit_bytes=8 * 2**20),
        name="finish",
    )(at, residual, weight[None, :], one_hot(place, tokens), *blocks)


def body_pair(
    act_fwd, routes_fwd, weight_fwd, grad_bwd, routes_bwd, weight_bwd, saved_bwd, w_gate_up, w_down
):
    node = lax.axis_index("node")
    local = lax.axis_index("local")
    tokens_here = act_fwd.shape[1]
    capacity = 5 * tokens_here // 8
    w_gu = w_gate_up[0, 0]
    w_dn = w_down[0, 0]
    hidden_units = w_dn.shape[0]
    shape = (2, 4, capacity)

    act, grad = act_fwd[0], grad_bwd[0]
    route_a, route_b = routes_fwd[0, :, 0], routes_bwd[0, :, 0]
    zeros = tokens_here - jnp.stack([jnp.sum(route_a), jnp.sum(route_b)]).astype(F32)

    def in_rows(cuts, got):
        return windows(jnp.stack([cuts[0], got[1], got[0], got[2]]), node, capacity)

    def by_node(own, got, axis):
        return jnp.stack([jnp.where(node == 0, own, got), jnp.where(node == 0, got, own)], axis=axis)

    saved_own, saved_other, *cut_b = cut(
        grad, weight_bwd[0], route_b, node, local, capacity, route_a, saved_bwd[0]
    )
    got_b = [move(cut_b[m], by_local=-m) for m in (2, 1, 3)]
    saved_got = move(saved_other, by_node=1)
    cut_a = cut(act, jnp.ones((tokens_here,), F32), route_a, node, local, capacity)
    *got_b, saved_got, a0, a1, a2, a3 = join(*got_b, saved_got, *cut_a)
    cut_a = [a0, a1, a2, a3]
    got_a = [move(cut_a[m], by_local=-m) for m in (2, 1, 3)]
    own_b, other_b = in_rows(cut_b, got_b)
    column = own_b.shape[-1]
    got_bx = move(other_b, by_node=1)

    rows_b = by_node(own_b, got_bx, 0).reshape(-1, column)
    part_b = dot_t(rows_b, w_dn).astype(BF16).reshape(shape + (hidden_units,))
    back_b = [move(part_b[:, m], by_local=m) for m in (2, 1, 3)]
    both = join(*back_b, *got_a)
    back_b, got_a = both[:3], both[3:]
    zeros_got = saved_got[capacity::8, 0].astype(F32)
    saved_got = saved_got[:capacity]
    zeros = by_node(zeros, zeros_got, 0)
    own_a, other_a = in_rows(cut_a, got_a)
    got_ax = move(other_a, by_node=1)
    saved_rows = by_node(saved_own, saved_got, 0)
    own_rows = valid(zeros, node, tokens_here, capacity)

    def gate_up_grad(home):
        dh = part_b[home, 0].astype(F32) + sum(part[home].astype(F32) for part in back_b)
        dh = jnp.where(own_rows[home, 1][:, None], dh, 0.0)
        g = saved_rows[home, :, :hidden_units].astype(F32)
        u = saved_rows[home, :, hidden_units:].astype(F32)
        q = 1.0 / (1.0 + jnp.exp(-g))
        both = [dh * u * q * (1.0 + g * (1.0 - q)), dh * g * q]
        return jnp.concatenate(both, axis=-1).astype(BF16)

    def hidden_of(preact, home):
        preact = jnp.where(own_rows[home, 0][:, None], preact, 0.0)
        gate, up = preact[:, :hidden_units], preact[:, hidden_units:]
        return (jax.nn.silu(gate) * up).astype(BF16)

    homes = (0, 1)
    grad_gu = [gate_up_grad(home) for home in homes]
    first = [both_ways(rows, rows) for rows in grad_gu]
    rows_a = by_node(own_a, got_ax, 0).reshape(-1, column)
    part_a = jnp.dot(rows_a, w_gu, preferred_element_type=F32).astype(BF16)
    part_a = part_a.reshape(shape + (2 * hidden_units,))

    def second_round(home):
        got_r, got_l = first[home]
        return both_ways(
            jnp.where(local == 0, part_a[home, 3], got_r),
            jnp.where(local == 3, part_a[home, 1], got_l),
        )

    def third_round(home):
        got_r, got_l = second[home]
        part = part_a[home, 2].astype(F32)
        return both_ways(
            jnp.where(local == 2, 0.0, part) + jnp.where(local == 0, 0.0, got_r.astype(F32)),
            jnp.where(local == 1, 0.0, part) + jnp.where(local == 3, 0.0, got_l.astype(F32)),
        )

    def fourth_round(home):
        got_r, got_l = third[home]
        middle = (local == 1) | (local == 2)
        return both_ways(
            part_a[home, 1].astype(F32) + jnp.where(middle, got_r.astype(F32), 0.0),
            part_a[home, 3].astype(F32) + jnp.where(middle, got_l.astype(F32), 0.0),
        )

    kept = [[None], [None]]
    r, l, *rest = join(*first[1], *first[0], act, grad)
    first[1], kept[0], (act_in, grad_in) = (r, l), kept[0] + [rest[:2]], rest[2:]
    second = [second_round(home) for home in homes]
    act_next = move(act_in, by_pp=1)
    r, l, *rest = join(*second[0], *first[1])
    second[0], kept[1] = (r, l), kept[1] + [rest]
    third = [third_round(0)]
    r, l, *rest = join(*second[1], *second[0], act_next, grad_in)
    second[1], kept[0], (act_next, grad_in) = (r, l), kept[0] + [rest[:2]], rest[2:]
    third.append(third_round(1))
    grad_next = move(grad_in, by_pp=-1)
    r, l, *rest = join(*third[0], *second[1])
    third[0], kept[1] = (r, l), kept[1] + [rest]
    fourth = [fourth_round(0)]
    small = jnp.stack([route_a.astype(F32), weight_fwd[0]])
    r, l, *rest = join(*third[1], *third[0], grad_next, small, route_b)
    third[1], kept[0], (grad_next, small, route_next) = (r, l), kept[0] + [rest[:2]], rest[2:]
    fourth.append(fourth_round(1))
    kept[1].append(third[1])
    small_next = move(small, by_pp=1)
    route_b_next = move(route_next, by_pp=-1)

    def by_expert(blocks):
        return jnp.where(node == 0, blocks[0], blocks[1]), jnp.where(node == 0, blocks[1], blocks[0])

    done_b = []
    for home in homes:
        blocks = [grad_gu[home]] + [
            jnp.where(local + m < 4, kept[home][m][1], kept[home][4 - m][0]) for m in (1, 2, 3)
        ]
        done = dot_t(jnp.stack(blocks).reshape(-1, 2 * hidden_units), w_gu).astype(BF16)
        done_b.append(done.reshape(4, capacity, column))
    own_b, other_b = by_expert(done_b)
    got_b = move(other_b, by_node=1)
    r, l, small_next, route_b_next = join(*fourth[1], small_next, route_b_next)
    fourth[1] = (r, l)

    all_hidden = []
    for home in homes:
        got_r, got_l = fourth[home]
        hidden = hidden_of(part_a[home, 0].astype(F32) + got_r.astype(F32) + got_l.astype(F32), home)
        all_hidden += [hidden] + [move(hidden, by_local=-m) for m in (1, 2, 3)]
    merged_b = merge(own_b, got_b, node, tokens_here)
    *all_hidden, merged_b = join(*all_hidden, merged_b)
    home_b = send(homeward(merged_b, -1))
    done_a = []
    for home in homes:
        blocks = jnp.stack(all_hidden[4 * home : 4 * home + 4]).reshape(-1, hidden_units)
        done = jnp.dot(blocks, w_dn, preferred_element_type=F32).astype(BF16)
        done_a.append(done.reshape(4, capacity, column))
    own_a, other_a = by_expert(done_a)
    got_a = move(other_a, by_node=1)
    home_a = send(homeward(merge(own_a, got_a, node, tokens_here), 1))

    at = jnp.stack([(local - m) % 4 for m in (2, 1, 3, 0)]).astype(jnp.int32)
    ones = jnp.ones((tokens_here,), F32)
    prev_grad = finish(grad_next, ones, sorted_places(route_b_next), home_b, at)
    place_a = sorted_places(small_next[0].astype(jnp.int32))
    next_input = finish(act_next, small_next[1], place_a, home_a, at)
    return next_input, prev_grad


def from_behind(value, axis, by):
    length = lax.axis_size(axis)
    return lax.ppermute(value, axis, [(i, (i + by) % length) for i in range(length)])


def place_matrix(route, expert_count, capacity):
    onehot = (route[:, None] == jnp.arange(expert_count, dtype=jnp.int32)[None, :]).astype(
        jnp.int32
    )
    before = jnp.cumsum(onehot, axis=0) - onehot
    slot_index = jnp.sum(before * onehot, axis=1)
    target = route * capacity + slot_index
    positions = jnp.arange(expert_count * capacity, dtype=jnp.int32)
    return (positions[:, None] == target[None, :]).astype(jnp.bfloat16)


def pack_rows(placer, values, expert_count, capacity):
    packed = jnp.dot(placer, values, preferred_element_type=jnp.float32).astype(jnp.bfloat16)
    return packed.reshape(expert_count, capacity, values.shape[1])


def unpack_rows(placer, packed):
    flattened = packed.reshape(-1, packed.shape[-1])
    result = lax.dot_general(
        placer, flattened, (((0,), (0,)), ((), ())), preferred_element_type=jnp.float32
    )
    return result.astype(jnp.bfloat16)


def flat_outgoing(packed, local_count):
    expert_count, capacity, feature_count = packed.shape
    column = feature_count // local_count
    outgoing = packed.reshape(expert_count, capacity, local_count, column).transpose(0, 2, 1, 3)
    return outgoing.reshape(expert_count * local_count, capacity, column)


def flat_layout(received, expert_count, local_count):
    capacity = received.shape[1]
    column = received.shape[2]
    rows_in = received.reshape(expert_count, local_count, capacity, column).transpose(1, 0, 2, 3)
    return rows_in.reshape(-1, column)


def send_rows(packs, local_count):
    expert_count = packs[0].shape[0]
    outgoing = tuple((flat_outgoing(packed, local_count) for packed in packs))
    received = (
        lax.all_to_all(outgoing[0], ("node", "local"), split_axis=0, concat_axis=0, tiled=True),
        lax.all_to_all(outgoing[1], ("node", "local"), split_axis=0, concat_axis=0, tiled=True),
    )
    return tuple((flat_layout(item, expert_count, local_count) for item in received))


def return_rows(finished_pair, expert_count, capacity, local_count):
    column = finished_pair[0].shape[1]
    blocks = tuple(
        (item.reshape(local_count, expert_count, capacity, column) for item in finished_pair)
    )
    outgoing = tuple(
        (
            item.transpose(1, 0, 2, 3).reshape(expert_count * local_count, capacity, column)
            for item in blocks
        )
    )
    received = (
        lax.all_to_all(outgoing[0], ("node", "local"), split_axis=0, concat_axis=0, tiled=True),
        lax.all_to_all(outgoing[1], ("node", "local"), split_axis=0, concat_axis=0, tiled=True),
    )
    results = []
    for item in received:
        arranged = item.reshape(expert_count, local_count, capacity, column).transpose(0, 2, 1, 3)
        results.append(arranged.reshape(expert_count, capacity, local_count * column))
    return tuple(results)


def body(
    act_fwd, routes_fwd, weight_fwd, grad_bwd, routes_bwd, weight_bwd, saved_bwd, w_gate_up, w_down
):
    node_count = lax.axis_size("node")
    local_count = lax.axis_size("local")
    tokens_here = act_fwd.shape[1]
    capacity = 5 * tokens_here // (4 * node_count)
    rows_each = node_count * capacity
    w_gu = w_gate_up[0, 0]
    w_dn = w_down[0, 0]
    hidden_units = w_dn.shape[0]
    tokens_a = act_fwd[0]
    placer_a = place_matrix(routes_fwd[0, :, 0], node_count, capacity)
    cotangent = grad_bwd[0]
    placer_b = place_matrix(routes_bwd[0, :, 0], node_count, capacity)
    scaled = (weight_bwd[0][:, None] * cotangent.astype(jnp.float32)).astype(jnp.bfloat16)
    packed_a = pack_rows(placer_a, tokens_a, node_count, capacity)
    packed_b = pack_rows(placer_b, scaled, node_count, capacity)
    rows_a, rows_b = send_rows((packed_a, packed_b), local_count)
    saved_packed = pack_rows(placer_b, saved_bwd[0], node_count, capacity)
    saved_rows = lax.all_to_all(
        saved_packed, "node", split_axis=0, concat_axis=0, tiled=True
    ).reshape(rows_each, -1)
    row_block = rows_a
    preact = lax.psum_scatter(
        jnp.dot(row_block, w_gu, preferred_element_type=jnp.float32).astype(jnp.bfloat16),
        "local",
        scatter_dimension=0,
        tiled=True,
    ).astype(jnp.float32)
    row_block = rows_b
    grad_hidden = lax.psum_scatter(
        lax.dot_general(
            row_block, w_dn, (((1,), (1,)), ((), ())), preferred_element_type=jnp.float32
        ).astype(jnp.bfloat16),
        "local",
        scatter_dimension=0,
        tiled=True,
    ).astype(jnp.float32)
    hidden = (jax.nn.silu(preact[:, :hidden_units]) * preact[:, hidden_units:]).astype(jnp.bfloat16)
    done_a = jnp.dot(
        lax.all_gather(hidden, "local", axis=0, tiled=True),
        w_dn,
        preferred_element_type=jnp.float32,
    ).astype(jnp.bfloat16)
    gate_pre = saved_rows[:, :hidden_units].astype(jnp.float32)
    up_pre = saved_rows[:, hidden_units:].astype(jnp.float32)
    sigmoid_g = 1.0 / (1.0 + jnp.exp(-gate_pre))
    grad_gate = grad_hidden * up_pre * sigmoid_g * (1.0 + gate_pre * (1.0 - sigmoid_g))
    grad_up = grad_hidden * gate_pre * sigmoid_g
    grad_gu = jnp.concatenate([grad_gate, grad_up], axis=1).astype(jnp.bfloat16)
    product = lax.dot_general(
        lax.all_gather(grad_gu, "local", axis=0, tiled=True),
        w_gu,
        (((1,), (1,)), ((), ())),
        preferred_element_type=jnp.float32,
    )
    done_b = product.astype(jnp.bfloat16)
    back_a, back_b = return_rows((done_a, done_b), node_count, capacity, local_count)
    moe_a = unpack_rows(placer_a, back_a)
    result_a = tokens_a.astype(jnp.float32) + weight_fwd[0][:, None] * moe_a.astype(jnp.float32)
    result_a = result_a.astype(jnp.bfloat16)
    moe_b = unpack_rows(placer_b, back_b)
    result_b = (cotangent.astype(jnp.float32) + moe_b.astype(jnp.float32)).astype(jnp.bfloat16)
    next_input = from_behind(result_a[None], "pp", 1)
    prev_grad = from_behind(result_b[None], "pp", -1)
    return (next_input, prev_grad)


def solution(mesh):
    in_specs = (
        P("pp", ("node", "local"), None),
        P("pp", ("node", "local"), None),
        P("pp", ("node", "local")),
        P("pp", ("node", "local"), None),
        P("pp", ("node", "local"), None),
        P("pp", ("node", "local")),
        P("pp", ("node", "local"), None),
        P("pp", "node", "local", None),
        P("pp", "node", None, "local"),
    )
    out_specs = (P("pp", ("node", "local"), None), P("pp", ("node", "local"), None))
    paired = mesh.shape["node"] == 2 and mesh.shape["local"] == 4
    plan = body_pair if paired else body
    return jax.shard_map(plan, mesh=mesh, in_specs=in_specs, out_specs=out_specs, check_vma=False)
```

```python
import jax
import jax.numpy as jnp
from jax import lax
from jax.experimental import pallas as pl
from jax.experimental.pallas import tpu as pltpu
from jax.sharding import PartitionSpec as P

F32 = jnp.float32
BF16 = jnp.bfloat16
AXES = ("pp", "node", "local")


def move(value, by_pp=0, by_node=0, by_local=0, wrap=True, first=0, last=None):
    pps, nodes, locs = (lax.axis_size(a) for a in AXES)
    last = locs - 1 if last is None else last
    pairs = []
    for s in range(pps):
        for n in range(nodes):
            for l in range(locs):
                to = l + by_local
                if not wrap and not (first <= l <= last and 0 <= to < locs):
                    continue
                source = (s * nodes + n) * locs + l
                target = (((s + by_pp) % pps) * nodes + (n ^ by_node)) * locs + to % locs
                pairs.append((source, target))
    return lax.ppermute(value, AXES, pairs)


def sorted_places(route):
    ones = route.astype(F32)
    count = route.shape[0]
    earlier = (jnp.arange(count)[None, :] < jnp.arange(count)[:, None]).astype(F32)
    ones_before = jnp.dot(earlier, ones[:, None], preferred_element_type=F32)[:, 0]
    zeros = count - jnp.sum(ones)
    index = jnp.arange(count, dtype=F32)
    place = jnp.where(route == 0, index - ones_before, zeros + ones_before)
    return place.astype(jnp.int32)


def sorter(route):
    place = sorted_places(route)
    rows = jnp.arange(route.shape[0], dtype=jnp.int32)
    return (rows[:, None] == place[None, :]).astype(BF16)


def one_hot(row, count):
    return (row[:, None] == jnp.arange(count, dtype=jnp.int32)[None, :]).astype(BF16)


def dot_t(left, right):
    return lax.dot_general(left, right, (((1,), (1,)), ((), ())), preferred_element_type=F32)


def windows(blocks, node, capacity):
    tokens = blocks.shape[-2]
    start = tokens - capacity
    low = lax.slice_in_dim(blocks, 0, capacity, axis=-2 + blocks.ndim)
    high = lax.slice_in_dim(blocks, start, tokens, axis=-2 + blocks.ndim)
    own = jnp.where(node == 0, low, high)
    other = jnp.where(node == 0, high, low)
    return own, other


def join(*values):
    return lax.optimization_barrier(values)


def after(values, *others):
    return list(join(*values, *others)[: len(values)])


def cut(tokens, placer, local):
    column = tokens.shape[1] // 4
    blocks = []
    for m in range(4):
        block = lax.dynamic_slice_in_dim(tokens, ((local - m) % 4) * column, column, axis=1)
        blocks.append(jnp.dot(placer, block, preferred_element_type=F32).astype(BF16))
    return blocks


def sums(partial):
    right, left = partial(3), partial(1)
    for step in (1, 2, 3):
        right, left = right.astype(BF16), left.astype(BF16)
        got_r, got_l = yield (
            (right, dict(by_local=1, wrap=False, last=step - 1)),
            (left, dict(by_local=-1, wrap=False, first=4 - step)),
        )
        right = partial(3 - step).astype(F32) + got_r.astype(F32)
        if step < 3:
            left = partial(step + 1).astype(F32) + got_l.astype(F32)
    yield right + got_l.astype(F32)


def gathers(rows, local):
    from_left, from_right = [rows], [rows]
    for step in (1, 2, 3):
        got_r, got_l = yield (
            (from_left[-1], dict(by_local=1, wrap=False, first=step - 1)),
            (from_right[-1], dict(by_local=-1, wrap=False, last=4 - step)),
        )
        from_left.append(got_r)
        from_right.append(got_l)
    slots = [rows]
    for m in (1, 2, 3):
        slots.append(jnp.where(local + m < 4, from_right[m], from_left[4 - m]))
    yield jnp.stack(slots)


def send(pieces):
    return [move(value, **how) for value, how in pieces]


def operands(pieces):
    return [value for value, _ in pieces]


def valid(zeros, node, tokens, capacity):
    row = jnp.arange(capacity, dtype=F32)[None, :]
    return jnp.where(node == 0, row < zeros[:, None], row + (tokens - capacity) >= zeros[:, None])


def merge(own, other, node, tokens):
    slots, capacity, column = own.shape
    low = jnp.where(node == 0, own, other)
    high = jnp.where(node == 0, other, own)
    rest = jnp.zeros((slots, tokens - capacity, column), own.dtype)
    return jnp.concatenate([low, rest], axis=1) + jnp.concatenate([rest, high], axis=1)


def homeward(merged, by_pp):
    return [(merged[m], dict(by_pp=by_pp, by_local=m)) for m in (2, 1, 3, 0)]


def finish_kernel(at_ref, residual_ref, weight_ref, pick_ref, *refs):
    *blocks, out_ref, rows, sem = refs
    count = len(blocks)
    column = rows.shape[-1]
    copies = [pltpu.make_async_copy(blocks[i], rows.at[i], sem.at[i]) for i in range(count)]
    for copy in copies:
        copy.start()
    for i in range(count):
        copies[i].wait()
        cols = pl.ds(pl.multiple_of(at_ref[i] * column, column), column)
        moe = jnp.dot(pick_ref[...], rows[i], preferred_element_type=F32)
        total = residual_ref[:, cols].astype(F32) + weight_ref[...] * moe
        out_ref[0, :, cols] = total.astype(out_ref.dtype)


def finish(residual, weight, place, blocks, at):
    column = blocks[0].shape[-1]
    tokens, features = residual.shape
    vmem = pl.BlockSpec(memory_space=pltpu.VMEM)
    anywhere = pl.BlockSpec(memory_space=pl.ANY)
    return pl.pallas_call(
        finish_kernel,
        out_shape=jax.ShapeDtypeStruct((1, tokens, features), BF16),
        in_specs=[pl.BlockSpec(memory_space=pltpu.SMEM)] + [vmem] * 3 + [anywhere] * len(blocks),
        out_specs=vmem,
        scratch_shapes=[
            pltpu.VMEM((len(blocks), tokens, column), BF16),
            pltpu.SemaphoreType.DMA((len(blocks),)),
        ],
        compiler_params=pltpu.CompilerParams(vmem_limit_bytes=8 * 2**20),
        name="finish",
    )(at, residual, weight[:, None], one_hot(place, tokens), *blocks)


def body_pair(
    act_fwd, routes_fwd, weight_fwd, grad_bwd, routes_bwd, weight_bwd, saved_bwd, w_gate_up, w_down
):
    node = lax.axis_index("node")
    local = lax.axis_index("local")
    tokens_here = act_fwd.shape[1]
    capacity = 5 * tokens_here // 8
    w_gu = w_gate_up[0, 0]
    w_dn = w_down[0, 0]
    hidden_units = w_dn.shape[0]
    shape = (4, 2, capacity)

    act, grad = act_fwd[0], grad_bwd[0]
    route_a, route_b = routes_fwd[0, :, 0], routes_bwd[0, :, 0]
    sort_a, sort_b = sorter(route_a), sorter(route_b)
    zeros = tokens_here - jnp.stack([jnp.sum(route_a), jnp.sum(route_b)]).astype(F32)

    def in_rows(cuts, got):
        return windows(jnp.stack([cuts[0], got[1], got[0], got[2]]), node, capacity)

    def by_node(own, got, axis):
        return jnp.stack([jnp.where(node == 0, own, got), jnp.where(node == 0, got, own)], axis=axis)

    def split(done):
        own = lax.dynamic_index_in_dim(done, node, axis=1, keepdims=False)
        other = lax.dynamic_index_in_dim(done, 1 - node, axis=1, keepdims=False)
        return own, other

    def turn(chain, back, *others):
        pieces = chain.send(after(back, *others))
        return operands(pieces), send(pieces)

    dy = (weight_bwd[0][:, None] * grad.astype(F32)).astype(BF16)
    cut_b = cut(dy, sort_b, local)
    c1, c2, c3, saved_in = join(*cut_b[1:], saved_bwd[0])
    got_b = [move(c2, by_local=-2), move(c1, by_local=-1), move(c3, by_local=-3)]
    saved = jnp.dot(sort_b, saved_in, preferred_element_type=F32).astype(BF16)
    saved_own, saved_other = windows(saved, node, capacity)
    saved_got = move(saved_other, by_node=1)
    (zeros_wait,) = after([zeros], saved_other)
    zeros_got = move(zeros_wait, by_node=1)
    cut_a = cut(act, sort_a, local)
    *got_b, saved_got, zeros_got, a0, a1, a2, a3 = join(*got_b, saved_got, zeros_got, *cut_a)
    cut_a = [a0, a1, a2, a3]
    zeros = by_node(zeros, zeros_got, 0)
    got_a = [move(cut_a[m], by_local=-m) for m in (2, 1, 3)]
    own_b, other_b = in_rows(cut_b, got_b)
    column = own_b.shape[-1]
    got_bx = move(other_b, by_node=1)

    rows_b = by_node(own_b, got_bx, 1).reshape(-1, column)
    part_b = dot_t(rows_b, w_dn).astype(BF16).reshape(shape + (hidden_units,))
    back_b = [move(part_b[m], by_local=m) for m in (2, 1, 3)]
    both = join(*back_b, *got_a)
    back_b, got_a = both[:3], both[3:]
    own_a, other_a = in_rows(cut_a, got_a)
    got_ax = move(other_a, by_node=1)
    dh = part_b[0].astype(F32) + sum(part.astype(F32) for part in back_b)
    dh = jnp.where(valid(zeros[:, 1], node, tokens_here, capacity)[..., None], dh, 0.0)
    saved_rows = by_node(saved_own, saved_got, 0)
    g = saved_rows[..., :hidden_units].astype(F32)
    u = saved_rows[..., hidden_units:].astype(F32)
    q = 1.0 / (1.0 + jnp.exp(-g))
    grad_gu = jnp.concatenate([dh * u * q * (1.0 + g * (1.0 - q)), dh * g * q], axis=-1).astype(
        BF16
    )

    chain_b = gathers(grad_gu, local)
    back_b = send(next(chain_b))
    small_wait, route_wait = after(
        [jnp.stack([route_a.astype(F32), weight_fwd[0]]), route_b], grad_gu
    )
    small_next = move(small_wait, by_pp=1)
    route_b_next = move(route_wait, by_pp=-1)
    rows_a = by_node(own_a, got_ax, 1).reshape(-1, column)
    part_a = jnp.dot(rows_a, w_gu, preferred_element_type=F32).astype(BF16)
    *back_b, part_a, small_next, route_b_next = join(*back_b, part_a, small_next, route_b_next)
    part_a = part_a.reshape(shape + (2 * hidden_units,))
    chain_a = sums(lambda slot: part_a[slot])
    values_b, back_b = turn(chain_b, back_b)
    pieces = next(chain_a)
    back_a = send(pieces)
    act_next = move(after([act], *operands(pieces))[0], by_pp=1)
    *back_b, act_next = join(*back_b, act_next)
    values_b, back_b = turn(chain_b, back_b)
    grad_next = move(join(grad, *values_b)[0], by_pp=-1)
    *back_b, grad_next = join(*back_b, grad_next)
    values_a, back_a = turn(chain_a, back_a)
    values_a, back_a = turn(chain_a, back_a)
    all_gu = chain_b.send(back_b)
    done_b = dot_t(all_gu.reshape(-1, 2 * hidden_units), w_gu).astype(BF16)
    own_b, other_b = split(done_b.reshape(shape + (column,)))
    got_b = move(other_b, by_node=1)

    preact = chain_a.send(back_a)
    preact = jnp.where(valid(zeros[:, 0], node, tokens_here, capacity)[..., None], preact, 0.0)
    hidden = (jax.nn.silu(preact[..., :hidden_units]) * preact[..., hidden_units:]).astype(BF16)
    all_hidden = [move(hidden, by_local=-m) for m in (1, 2, 3)]
    merged_b = merge(own_b, got_b, node, tokens_here)
    h1, h2, h3, merged_b = join(*all_hidden, merged_b)
    all_hidden = jnp.stack([hidden, h1, h2, h3])
    home_b = send(homeward(merged_b, -1))
    done_a = jnp.dot(
        all_hidden.reshape(-1, hidden_units), w_dn, preferred_element_type=F32
    ).astype(BF16)
    own_a, other_a = split(done_a.reshape(shape + (column,)))
    got_a = move(other_a, by_node=1)
    home_a = send(homeward(merge(own_a, got_a, node, tokens_here), 1))

    at = jnp.stack([(local - m) % 4 for m in (2, 1, 3, 0)]).astype(jnp.int32)
    ones = jnp.ones((tokens_here,), F32)
    prev_grad = finish(grad_next, ones, sorted_places(route_b_next), home_b, at)
    place_a = sorted_places(small_next[0].astype(jnp.int32))
    next_input = finish(act_next, small_next[1], place_a, home_a, at)
    return next_input, prev_grad


def from_behind(value, axis, by):
    length = lax.axis_size(axis)
    return lax.ppermute(value, axis, [(i, (i + by) % length) for i in range(length)])


def place_matrix(route, expert_count, capacity):
    onehot = (route[:, None] == jnp.arange(expert_count, dtype=jnp.int32)[None, :]).astype(
        jnp.int32
    )
    before = jnp.cumsum(onehot, axis=0) - onehot
    slot_index = jnp.sum(before * onehot, axis=1)
    target = route * capacity + slot_index
    positions = jnp.arange(expert_count * capacity, dtype=jnp.int32)
    return (positions[:, None] == target[None, :]).astype(jnp.bfloat16)


def pack_rows(placer, values, expert_count, capacity):
    packed = jnp.dot(placer, values, preferred_element_type=jnp.float32).astype(jnp.bfloat16)
    return packed.reshape(expert_count, capacity, values.shape[1])


def unpack_rows(placer, packed):
    flattened = packed.reshape(-1, packed.shape[-1])
    result = lax.dot_general(
        placer, flattened, (((0,), (0,)), ((), ())), preferred_element_type=jnp.float32
    )
    return result.astype(jnp.bfloat16)


def flat_outgoing(packed, local_count):
    expert_count, capacity, feature_count = packed.shape
    column = feature_count // local_count
    outgoing = packed.reshape(expert_count, capacity, local_count, column).transpose(0, 2, 1, 3)
    return outgoing.reshape(expert_count * local_count, capacity, column)


def flat_layout(received, expert_count, local_count):
    capacity = received.shape[1]
    column = received.shape[2]
    rows_in = received.reshape(expert_count, local_count, capacity, column).transpose(1, 0, 2, 3)
    return rows_in.reshape(-1, column)


def send_rows(packs, local_count):
    expert_count = packs[0].shape[0]
    outgoing = tuple((flat_outgoing(packed, local_count) for packed in packs))
    received = (
        lax.all_to_all(outgoing[0], ("node", "local"), split_axis=0, concat_axis=0, tiled=True),
        lax.all_to_all(outgoing[1], ("node", "local"), split_axis=0, concat_axis=0, tiled=True),
    )
    return tuple((flat_layout(item, expert_count, local_count) for item in received))


def return_rows(finished_pair, expert_count, capacity, local_count):
    column = finished_pair[0].shape[1]
    blocks = tuple(
        (item.reshape(local_count, expert_count, capacity, column) for item in finished_pair)
    )
    outgoing = tuple(
        (
            item.transpose(1, 0, 2, 3).reshape(expert_count * local_count, capacity, column)
            for item in blocks
        )
    )
    received = (
        lax.all_to_all(outgoing[0], ("node", "local"), split_axis=0, concat_axis=0, tiled=True),
        lax.all_to_all(outgoing[1], ("node", "local"), split_axis=0, concat_axis=0, tiled=True),
    )
    results = []
    for item in received:
        arranged = item.reshape(expert_count, local_count, capacity, column).transpose(0, 2, 1, 3)
        results.append(arranged.reshape(expert_count, capacity, local_count * column))
    return tuple(results)


def body(
    act_fwd, routes_fwd, weight_fwd, grad_bwd, routes_bwd, weight_bwd, saved_bwd, w_gate_up, w_down
):
    node_count = lax.axis_size("node")
    local_count = lax.axis_size("local")
    tokens_here = act_fwd.shape[1]
    capacity = 5 * tokens_here // (4 * node_count)
    rows_each = node_count * capacity
    w_gu = w_gate_up[0, 0]
    w_dn = w_down[0, 0]
    hidden_units = w_dn.shape[0]
    tokens_a = act_fwd[0]
    placer_a = place_matrix(routes_fwd[0, :, 0], node_count, capacity)
    cotangent = grad_bwd[0]
    placer_b = place_matrix(routes_bwd[0, :, 0], node_count, capacity)
    scaled = (weight_bwd[0][:, None] * cotangent.astype(jnp.float32)).astype(jnp.bfloat16)
    packed_a = pack_rows(placer_a, tokens_a, node_count, capacity)
    packed_b = pack_rows(placer_b, scaled, node_count, capacity)
    rows_a, rows_b = send_rows((packed_a, packed_b), local_count)
    saved_packed = pack_rows(placer_b, saved_bwd[0], node_count, capacity)
    saved_rows = lax.all_to_all(
        saved_packed, "node", split_axis=0, concat_axis=0, tiled=True
    ).reshape(rows_each, -1)
    row_block = rows_a
    preact = lax.psum_scatter(
        jnp.dot(row_block, w_gu, preferred_element_type=jnp.float32).astype(jnp.bfloat16),
        "local",
        scatter_dimension=0,
        tiled=True,
    ).astype(jnp.float32)
    row_block = rows_b
    grad_hidden = lax.psum_scatter(
        lax.dot_general(
            row_block, w_dn, (((1,), (1,)), ((), ())), preferred_element_type=jnp.float32
        ).astype(jnp.bfloat16),
        "local",
        scatter_dimension=0,
        tiled=True,
    ).astype(jnp.float32)
    hidden = (jax.nn.silu(preact[:, :hidden_units]) * preact[:, hidden_units:]).astype(jnp.bfloat16)
    done_a = jnp.dot(
        lax.all_gather(hidden, "local", axis=0, tiled=True),
        w_dn,
        preferred_element_type=jnp.float32,
    ).astype(jnp.bfloat16)
    gate_pre = saved_rows[:, :hidden_units].astype(jnp.float32)
    up_pre = saved_rows[:, hidden_units:].astype(jnp.float32)
    sigmoid_g = 1.0 / (1.0 + jnp.exp(-gate_pre))
    grad_gate = grad_hidden * up_pre * sigmoid_g * (1.0 + gate_pre * (1.0 - sigmoid_g))
    grad_up = grad_hidden * gate_pre * sigmoid_g
    grad_gu = jnp.concatenate([grad_gate, grad_up], axis=1).astype(jnp.bfloat16)
    product = lax.dot_general(
        lax.all_gather(grad_gu, "local", axis=0, tiled=True),
        w_gu,
        (((1,), (1,)), ((), ())),
        preferred_element_type=jnp.float32,
    )
    done_b = product.astype(jnp.bfloat16)
    back_a, back_b = return_rows((done_a, done_b), node_count, capacity, local_count)
    moe_a = unpack_rows(placer_a, back_a)
    result_a = tokens_a.astype(jnp.float32) + weight_fwd[0][:, None] * moe_a.astype(jnp.float32)
    result_a = result_a.astype(jnp.bfloat16)
    moe_b = unpack_rows(placer_b, back_b)
    result_b = (cotangent.astype(jnp.float32) + moe_b.astype(jnp.float32)).astype(jnp.bfloat16)
    next_input = from_behind(result_a[None], "pp", 1)
    prev_grad = from_behind(result_b[None], "pp", -1)
    return (next_input, prev_grad)


def solution(mesh):
    in_specs = (
        P("pp", ("node", "local"), None),
        P("pp", ("node", "local"), None),
        P("pp", ("node", "local")),
        P("pp", ("node", "local"), None),
        P("pp", ("node", "local"), None),
        P("pp", ("node", "local")),
        P("pp", ("node", "local"), None),
        P("pp", "node", "local", None),
        P("pp", "node", None, "local"),
    )
    out_specs = (P("pp", ("node", "local"), None), P("pp", ("node", "local"), None))
    paired = mesh.shape["node"] == 2 and mesh.shape["local"] == 4
    plan = body_pair if paired else body
    return jax.shard_map(plan, mesh=mesh, in_specs=in_specs, out_specs=out_specs, check_vma=False)
```

```python
import jax
import jax.numpy as jnp
from jax import lax
from jax.experimental import pallas as pl
from jax.experimental.pallas import tpu as pltpu
from jax.sharding import PartitionSpec as P

F32 = jnp.float32
BF16 = jnp.bfloat16
AXES = ("pp", "node", "local")


def move(value, by_pp=0, by_node=0, by_local=0, wrap=True, first=0, last=None):
    pps, nodes, locs = (lax.axis_size(a) for a in AXES)
    last = locs - 1 if last is None else last
    pairs = []
    for s in range(pps):
        for n in range(nodes):
            for l in range(locs):
                to = l + by_local
                if not wrap and not (first <= l <= last and 0 <= to < locs):
                    continue
                source = (s * nodes + n) * locs + l
                target = (((s + by_pp) % pps) * nodes + (n ^ by_node)) * locs + to % locs
                pairs.append((source, target))
    return lax.ppermute(value, AXES, pairs)


def sorted_places(route):
    ones = route.astype(F32)
    count = route.shape[0]
    earlier = (jnp.arange(count)[None, :] < jnp.arange(count)[:, None]).astype(F32)
    ones_before = jnp.dot(earlier, ones[:, None], preferred_element_type=F32)[:, 0]
    zeros = count - jnp.sum(ones)
    index = jnp.arange(count, dtype=F32)
    place = jnp.where(route == 0, index - ones_before, zeros + ones_before)
    return place.astype(jnp.int32)


def sorter(route):
    place = sorted_places(route)
    rows = jnp.arange(route.shape[0], dtype=jnp.int32)
    return (rows[:, None] == place[None, :]).astype(BF16)


def one_hot(row, count):
    return (row[:, None] == jnp.arange(count, dtype=jnp.int32)[None, :]).astype(BF16)


def dot_t(left, right):
    return lax.dot_general(left, right, (((1,), (1,)), ((), ())), preferred_element_type=F32)


def windows(blocks, node, capacity):
    tokens = blocks.shape[-2]
    start = tokens - capacity
    low = lax.slice_in_dim(blocks, 0, capacity, axis=-2 + blocks.ndim)
    high = lax.slice_in_dim(blocks, start, tokens, axis=-2 + blocks.ndim)
    own = jnp.where(node == 0, low, high)
    other = jnp.where(node == 0, high, low)
    return own, other


def join(*values):
    return lax.optimization_barrier(values)


def after(values, *others):
    return list(join(*values, *others)[: len(values)])


def cut(tokens, placer, local):
    column = tokens.shape[1] // 4
    blocks = []
    for m in range(4):
        block = lax.dynamic_slice_in_dim(tokens, ((local - m) % 4) * column, column, axis=1)
        blocks.append(jnp.dot(placer, block, preferred_element_type=F32).astype(BF16))
    return blocks


def sums(partial):
    right, left = partial(3), partial(1)
    for step in (1, 2, 3):
        right, left = right.astype(BF16), left.astype(BF16)
        got_r, got_l = yield (
            (right, dict(by_local=1, wrap=False, last=step - 1)),
            (left, dict(by_local=-1, wrap=False, first=4 - step)),
        )
        right = partial(3 - step).astype(F32) + got_r.astype(F32)
        if step < 3:
            left = partial(step + 1).astype(F32) + got_l.astype(F32)
    yield right + got_l.astype(F32)


def gathers(rows, local):
    from_left, from_right = [rows], [rows]
    for step in (1, 2, 3):
        got_r, got_l = yield (
            (from_left[-1], dict(by_local=1, wrap=False, first=step - 1)),
            (from_right[-1], dict(by_local=-1, wrap=False, last=4 - step)),
        )
        from_left.append(got_r)
        from_right.append(got_l)
    slots = [rows]
    for m in (1, 2, 3):
        slots.append(jnp.where(local + m < 4, from_right[m], from_left[4 - m]))
    yield jnp.stack(slots)


def send(pieces):
    return [move(value, **how) for value, how in pieces]


def operands(pieces):
    return [value for value, _ in pieces]


def valid(zeros, node, tokens, capacity):
    row = jnp.arange(capacity, dtype=F32)[None, :]
    return jnp.where(node == 0, row < zeros[:, None], row + (tokens - capacity) >= zeros[:, None])


def merge(own, other, node, tokens):
    slots, capacity, column = own.shape
    low = jnp.where(node == 0, own, other)
    high = jnp.where(node == 0, other, own)
    rest = jnp.zeros((slots, tokens - capacity, column), own.dtype)
    return jnp.concatenate([low, rest], axis=1) + jnp.concatenate([rest, high], axis=1)


def homeward(merged, by_pp):
    return [(merged[m], dict(by_pp=by_pp, by_local=m)) for m in (2, 1, 3, 0)]


def column_of(row_ref):
    n = row_ref.shape[1]
    row = lax.broadcasted_iota(jnp.int32, (n, n), 0)
    col = lax.broadcasted_iota(jnp.int32, (n, n), 1)
    return jnp.sum(jnp.where(row == col, row_ref[...], 0.0), axis=1, keepdims=True)


def cut_kernel(at_ref, route_ref, weight_ref, values_ref, *blocks):
    tokens = route_ref.shape[1]
    column = blocks[0].shape[1]
    row = lax.broadcasted_iota(jnp.int32, (tokens, tokens), 0)
    col = lax.broadcasted_iota(jnp.int32, (tokens, tokens), 1)
    ones = route_ref[...].astype(F32)
    before = jnp.dot(
        jnp.broadcast_to(ones, (8, tokens)).astype(BF16),
        (row < col).astype(BF16),
        preferred_element_type=F32,
    )[0:1]
    zeros = tokens - jnp.sum(ones, axis=1, keepdims=True)
    index = col[0:1].astype(F32)
    place = jnp.where(ones == 0.0, index - before, zeros + before).astype(jnp.int32)
    picker = (row == place).astype(BF16)
    weight = column_of(weight_ref)
    for i, block_ref in enumerate(blocks):
        cols = pl.ds(pl.multiple_of(at_ref[i] * column, column), column)
        block = (weight * values_ref[:, cols].astype(F32)).astype(BF16)
        block_ref[...] = jnp.dot(picker, block, preferred_element_type=F32).astype(BF16)


def scaled_cut(tokens, weight, route, local):
    rows, features = tokens.shape
    vmem = pl.BlockSpec(memory_space=pltpu.VMEM)
    at = jnp.stack([(local - m) % 4 for m in range(4)]).astype(jnp.int32)
    return list(
        pl.pallas_call(
            cut_kernel,
            out_shape=[jax.ShapeDtypeStruct((rows, features // 4), BF16)] * 4,
            in_specs=[pl.BlockSpec(memory_space=pltpu.SMEM)] + [vmem] * 3,
            out_specs=[vmem] * 4,
            compiler_params=pltpu.CompilerParams(vmem_limit_bytes=8 * 2**20),
            name="cut",
        )(at, route[None, :], weight[None, :], tokens)
    )


def finish_kernel(at_ref, weight_ref, pick_ref, residual_ref, *refs):
    *blocks, out_ref, rows, base, total, sem = refs
    count = len(blocks)
    column = rows.shape[-1]

    def cols(i):
        return pl.ds(pl.multiple_of(at_ref[i] * column, column), column)

    ins = []
    for i in range(count):
        ins.append(
            (
                pltpu.make_async_copy(blocks[i], rows.at[i], sem.at[0, i]),
                pltpu.make_async_copy(residual_ref.at[:, cols(i)], base.at[i], sem.at[1, i]),
            )
        )
        for copy in ins[i]:
            copy.start()
    weight = column_of(weight_ref)
    outs = []
    for i in range(count):
        for copy in ins[i]:
            copy.wait()
        moe = jnp.dot(pick_ref[...], rows[i], preferred_element_type=F32)
        total[i] = (base[i].astype(F32) + weight * moe).astype(total.dtype)
        outs.append(pltpu.make_async_copy(total.at[i], out_ref.at[0, :, cols(i)], sem.at[2, i]))
        outs[i].start()
    for copy in outs:
        copy.wait()


def finish(residual, weight, place, blocks, at):
    count, column = len(blocks), blocks[0].shape[-1]
    tokens, features = residual.shape
    vmem = pl.BlockSpec(memory_space=pltpu.VMEM)
    anywhere = pl.BlockSpec(memory_space=pl.ANY)
    return pl.pallas_call(
        finish_kernel,
        out_shape=jax.ShapeDtypeStruct((1, tokens, features), BF16),
        in_specs=[pl.BlockSpec(memory_space=pltpu.SMEM)] + [vmem] * 2 + [anywhere] * (1 + count),
        out_specs=anywhere,
        scratch_shapes=[pltpu.VMEM((count, tokens, column), BF16)] * 3
        + [pltpu.SemaphoreType.DMA((3, count))],
        compiler_params=pltpu.CompilerParams(vmem_limit_bytes=8 * 2**20),
        name="finish",
    )(at, weight[None, :], one_hot(place, tokens), residual, *blocks)


def body_pair(
    act_fwd, routes_fwd, weight_fwd, grad_bwd, routes_bwd, weight_bwd, saved_bwd, w_gate_up, w_down
):
    node = lax.axis_index("node")
    local = lax.axis_index("local")
    tokens_here = act_fwd.shape[1]
    capacity = 5 * tokens_here // 8
    w_gu = w_gate_up[0, 0]
    w_dn = w_down[0, 0]
    hidden_units = w_dn.shape[0]
    shape = (4, 2, capacity)

    act, grad = act_fwd[0], grad_bwd[0]
    route_a, route_b = routes_fwd[0, :, 0], routes_bwd[0, :, 0]
    sort_a, sort_b = sorter(route_a), sorter(route_b)
    zeros = tokens_here - jnp.stack([jnp.sum(route_a), jnp.sum(route_b)]).astype(F32)

    def in_rows(cuts, got):
        return windows(jnp.stack([cuts[0], got[1], got[0], got[2]]), node, capacity)

    def by_node(own, got, axis):
        return jnp.stack([jnp.where(node == 0, own, got), jnp.where(node == 0, got, own)], axis=axis)

    def split(done):
        own = lax.dynamic_index_in_dim(done, node, axis=1, keepdims=False)
        other = lax.dynamic_index_in_dim(done, 1 - node, axis=1, keepdims=False)
        return own, other

    def turn(chain, back, *others):
        pieces = chain.send(after(back, *others))
        return operands(pieces), send(pieces)

    cut_b = scaled_cut(grad, weight_bwd[0], route_b, local)
    c1, c2, c3, saved_in = join(*cut_b[1:], saved_bwd[0])
    got_b = [move(c2, by_local=-2), move(c1, by_local=-1), move(c3, by_local=-3)]
    saved = jnp.dot(sort_b, saved_in, preferred_element_type=F32).astype(BF16)
    saved_own, saved_other = windows(saved, node, capacity)
    saved_got = move(saved_other, by_node=1)
    (zeros_wait,) = after([zeros], saved_other)
    zeros_got = move(zeros_wait, by_node=1)
    cut_a = cut(act, sort_a, local)
    *got_b, saved_got, zeros_got, a0, a1, a2, a3 = join(*got_b, saved_got, zeros_got, *cut_a)
    cut_a = [a0, a1, a2, a3]
    zeros = by_node(zeros, zeros_got, 0)
    got_a = [move(cut_a[m], by_local=-m) for m in (2, 1, 3)]
    own_b, other_b = in_rows(cut_b, got_b)
    column = own_b.shape[-1]
    got_bx = move(other_b, by_node=1)

    rows_b = by_node(own_b, got_bx, 1).reshape(-1, column)
    part_b = dot_t(rows_b, w_dn).astype(BF16).reshape(shape + (hidden_units,))
    back_b = [move(part_b[m], by_local=m) for m in (2, 1, 3)]
    both = join(*back_b, *got_a)
    back_b, got_a = both[:3], both[3:]
    own_a, other_a = in_rows(cut_a, got_a)
    got_ax = move(other_a, by_node=1)
    dh = part_b[0].astype(F32) + sum(part.astype(F32) for part in back_b)
    dh = jnp.where(valid(zeros[:, 1], node, tokens_here, capacity)[..., None], dh, 0.0)
    saved_rows = by_node(saved_own, saved_got, 0)
    g = saved_rows[..., :hidden_units].astype(F32)
    u = saved_rows[..., hidden_units:].astype(F32)
    q = 1.0 / (1.0 + jnp.exp(-g))
    grad_gu = jnp.concatenate([dh * u * q * (1.0 + g * (1.0 - q)), dh * g * q], axis=-1).astype(
        BF16
    )

    chain_b = gathers(grad_gu, local)
    back_b = send(next(chain_b))
    small_wait, route_wait = after(
        [jnp.stack([route_a.astype(F32), weight_fwd[0]]), route_b], grad_gu
    )
    small_next = move(small_wait, by_pp=1)
    route_b_next = move(route_wait, by_pp=-1)
    rows_a = by_node(own_a, got_ax, 1).reshape(-1, column)
    part_a = jnp.dot(rows_a, w_gu, preferred_element_type=F32).astype(BF16)
    *back_b, part_a, small_next, route_b_next = join(*back_b, part_a, small_next, route_b_next)
    part_a = part_a.reshape(shape + (2 * hidden_units,))
    chain_a = sums(lambda slot: part_a[slot])
    values_b, back_b = turn(chain_b, back_b)
    pieces = next(chain_a)
    back_a = send(pieces)
    act_next = move(after([act], *operands(pieces))[0], by_pp=1)
    *back_b, act_next = join(*back_b, act_next)
    values_b, back_b = turn(chain_b, back_b)
    grad_next = move(join(grad, *values_b)[0], by_pp=-1)
    *back_b, grad_next = join(*back_b, grad_next)
    values_a, back_a = turn(chain_a, back_a)
    values_a, back_a = turn(chain_a, back_a)
    all_gu = chain_b.send(back_b)
    done_b = dot_t(all_gu.reshape(-1, 2 * hidden_units), w_gu).astype(BF16)
    own_b, other_b = split(done_b.reshape(shape + (column,)))
    got_b = move(other_b, by_node=1)

    preact = chain_a.send(back_a)
    preact = jnp.where(valid(zeros[:, 0], node, tokens_here, capacity)[..., None], preact, 0.0)
    hidden = (jax.nn.silu(preact[..., :hidden_units]) * preact[..., hidden_units:]).astype(BF16)
    all_hidden = [move(hidden, by_local=-m) for m in (1, 2, 3)]
    merged_b = merge(own_b, got_b, node, tokens_here)
    h1, h2, h3, merged_b = join(*all_hidden, merged_b)
    all_hidden = jnp.stack([hidden, h1, h2, h3])
    home_b = send(homeward(merged_b, -1))
    done_a = jnp.dot(
        all_hidden.reshape(-1, hidden_units), w_dn, preferred_element_type=F32
    ).astype(BF16)
    own_a, other_a = split(done_a.reshape(shape + (column,)))
    got_a = move(other_a, by_node=1)
    home_a = send(homeward(merge(own_a, got_a, node, tokens_here), 1))

    at = jnp.stack([(local - m) % 4 for m in (2, 1, 3, 0)]).astype(jnp.int32)
    ones = jnp.ones((tokens_here,), F32)
    prev_grad = finish(grad_next, ones, sorted_places(route_b_next), home_b, at)
    place_a = sorted_places(small_next[0].astype(jnp.int32))
    next_input = finish(act_next, small_next[1], place_a, home_a, at)
    return next_input, prev_grad


def from_behind(value, axis, by):
    length = lax.axis_size(axis)
    return lax.ppermute(value, axis, [(i, (i + by) % length) for i in range(length)])


def place_matrix(route, expert_count, capacity):
    onehot = (route[:, None] == jnp.arange(expert_count, dtype=jnp.int32)[None, :]).astype(
        jnp.int32
    )
    before = jnp.cumsum(onehot, axis=0) - onehot
    slot_index = jnp.sum(before * onehot, axis=1)
    target = route * capacity + slot_index
    positions = jnp.arange(expert_count * capacity, dtype=jnp.int32)
    return (positions[:, None] == target[None, :]).astype(jnp.bfloat16)


def pack_rows(placer, values, expert_count, capacity):
    packed = jnp.dot(placer, values, preferred_element_type=jnp.float32).astype(jnp.bfloat16)
    return packed.reshape(expert_count, capacity, values.shape[1])


def unpack_rows(placer, packed):
    flattened = packed.reshape(-1, packed.shape[-1])
    result = lax.dot_general(
        placer, flattened, (((0,), (0,)), ((), ())), preferred_element_type=jnp.float32
    )
    return result.astype(jnp.bfloat16)


def flat_outgoing(packed, local_count):
    expert_count, capacity, feature_count = packed.shape
    column = feature_count // local_count
    outgoing = packed.reshape(expert_count, capacity, local_count, column).transpose(0, 2, 1, 3)
    return outgoing.reshape(expert_count * local_count, capacity, column)


def flat_layout(received, expert_count, local_count):
    capacity = received.shape[1]
    column = received.shape[2]
    rows_in = received.reshape(expert_count, local_count, capacity, column).transpose(1, 0, 2, 3)
    return rows_in.reshape(-1, column)


def send_rows(packs, local_count):
    expert_count = packs[0].shape[0]
    outgoing = tuple((flat_outgoing(packed, local_count) for packed in packs))
    received = (
        lax.all_to_all(outgoing[0], ("node", "local"), split_axis=0, concat_axis=0, tiled=True),
        lax.all_to_all(outgoing[1], ("node", "local"), split_axis=0, concat_axis=0, tiled=True),
    )
    return tuple((flat_layout(item, expert_count, local_count) for item in received))


def return_rows(finished_pair, expert_count, capacity, local_count):
    column = finished_pair[0].shape[1]
    blocks = tuple(
        (item.reshape(local_count, expert_count, capacity, column) for item in finished_pair)
    )
    outgoing = tuple(
        (
            item.transpose(1, 0, 2, 3).reshape(expert_count * local_count, capacity, column)
            for item in blocks
        )
    )
    received = (
        lax.all_to_all(outgoing[0], ("node", "local"), split_axis=0, concat_axis=0, tiled=True),
        lax.all_to_all(outgoing[1], ("node", "local"), split_axis=0, concat_axis=0, tiled=True),
    )
    results = []
    for item in received:
        arranged = item.reshape(expert_count, local_count, capacity, column).transpose(0, 2, 1, 3)
        results.append(arranged.reshape(expert_count, capacity, local_count * column))
    return tuple(results)


def body(
    act_fwd, routes_fwd, weight_fwd, grad_bwd, routes_bwd, weight_bwd, saved_bwd, w_gate_up, w_down
):
    node_count = lax.axis_size("node")
    local_count = lax.axis_size("local")
    tokens_here = act_fwd.shape[1]
    capacity = 5 * tokens_here // (4 * node_count)
    rows_each = node_count * capacity
    w_gu = w_gate_up[0, 0]
    w_dn = w_down[0, 0]
    hidden_units = w_dn.shape[0]
    tokens_a = act_fwd[0]
    placer_a = place_matrix(routes_fwd[0, :, 0], node_count, capacity)
    cotangent = grad_bwd[0]
    placer_b = place_matrix(routes_bwd[0, :, 0], node_count, capacity)
    scaled = (weight_bwd[0][:, None] * cotangent.astype(jnp.float32)).astype(jnp.bfloat16)
    packed_a = pack_rows(placer_a, tokens_a, node_count, capacity)
    packed_b = pack_rows(placer_b, scaled, node_count, capacity)
    rows_a, rows_b = send_rows((packed_a, packed_b), local_count)
    saved_packed = pack_rows(placer_b, saved_bwd[0], node_count, capacity)
    saved_rows = lax.all_to_all(
        saved_packed, "node", split_axis=0, concat_axis=0, tiled=True
    ).reshape(rows_each, -1)
    row_block = rows_a
    preact = lax.psum_scatter(
        jnp.dot(row_block, w_gu, preferred_element_type=jnp.float32).astype(jnp.bfloat16),
        "local",
        scatter_dimension=0,
        tiled=True,
    ).astype(jnp.float32)
    row_block = rows_b
    grad_hidden = lax.psum_scatter(
        lax.dot_general(
            row_block, w_dn, (((1,), (1,)), ((), ())), preferred_element_type=jnp.float32
        ).astype(jnp.bfloat16),
        "local",
        scatter_dimension=0,
        tiled=True,
    ).astype(jnp.float32)
    hidden = (jax.nn.silu(preact[:, :hidden_units]) * preact[:, hidden_units:]).astype(jnp.bfloat16)
    done_a = jnp.dot(
        lax.all_gather(hidden, "local", axis=0, tiled=True),
        w_dn,
        preferred_element_type=jnp.float32,
    ).astype(jnp.bfloat16)
    gate_pre = saved_rows[:, :hidden_units].astype(jnp.float32)
    up_pre = saved_rows[:, hidden_units:].astype(jnp.float32)
    sigmoid_g = 1.0 / (1.0 + jnp.exp(-gate_pre))
    grad_gate = grad_hidden * up_pre * sigmoid_g * (1.0 + gate_pre * (1.0 - sigmoid_g))
    grad_up = grad_hidden * gate_pre * sigmoid_g
    grad_gu = jnp.concatenate([grad_gate, grad_up], axis=1).astype(jnp.bfloat16)
    product = lax.dot_general(
        lax.all_gather(grad_gu, "local", axis=0, tiled=True),
        w_gu,
        (((1,), (1,)), ((), ())),
        preferred_element_type=jnp.float32,
    )
    done_b = product.astype(jnp.bfloat16)
    back_a, back_b = return_rows((done_a, done_b), node_count, capacity, local_count)
    moe_a = unpack_rows(placer_a, back_a)
    result_a = tokens_a.astype(jnp.float32) + weight_fwd[0][:, None] * moe_a.astype(jnp.float32)
    result_a = result_a.astype(jnp.bfloat16)
    moe_b = unpack_rows(placer_b, back_b)
    result_b = (cotangent.astype(jnp.float32) + moe_b.astype(jnp.float32)).astype(jnp.bfloat16)
    next_input = from_behind(result_a[None], "pp", 1)
    prev_grad = from_behind(result_b[None], "pp", -1)
    return (next_input, prev_grad)


def solution(mesh):
    in_specs = (
        P("pp", ("node", "local"), None),
        P("pp", ("node", "local"), None),
        P("pp", ("node", "local")),
        P("pp", ("node", "local"), None),
        P("pp", ("node", "local"), None),
        P("pp", ("node", "local")),
        P("pp", ("node", "local"), None),
        P("pp", "node", "local", None),
        P("pp", "node", None, "local"),
    )
    out_specs = (P("pp", ("node", "local"), None), P("pp", ("node", "local"), None))
    paired = mesh.shape["node"] == 2 and mesh.shape["local"] == 4
    plan = body_pair if paired else body
    return jax.shard_map(plan, mesh=mesh, in_specs=in_specs, out_specs=out_specs, check_vma=False)
```

```python
import jax
import jax.numpy as jnp
from jax import lax
from jax.experimental import pallas as pl
from jax.experimental.pallas import tpu as pltpu
from jax.sharding import PartitionSpec as P

F32 = jnp.float32
BF16 = jnp.bfloat16
AXES = ("pp", "node", "local")


def move(value, by_pp=0, by_node=0, by_local=0, wrap=True, first=0, last=None):
    pps, nodes, locs = (lax.axis_size(a) for a in AXES)
    last = locs - 1 if last is None else last
    pairs = []
    for s in range(pps):
        for n in range(nodes):
            for l in range(locs):
                to = l + by_local
                if not wrap and not (first <= l <= last and 0 <= to < locs):
                    continue
                source = (s * nodes + n) * locs + l
                target = (((s + by_pp) % pps) * nodes + (n ^ by_node)) * locs + to % locs
                pairs.append((source, target))
    return lax.ppermute(value, AXES, pairs)


def sorted_places(route):
    ones = route.astype(F32)
    count = route.shape[0]
    earlier = (jnp.arange(count)[None, :] < jnp.arange(count)[:, None]).astype(F32)
    ones_before = jnp.dot(earlier, ones[:, None], preferred_element_type=F32)[:, 0]
    zeros = count - jnp.sum(ones)
    index = jnp.arange(count, dtype=F32)
    place = jnp.where(route == 0, index - ones_before, zeros + ones_before)
    return place.astype(jnp.int32)


def sorter(route):
    place = sorted_places(route)
    rows = jnp.arange(route.shape[0], dtype=jnp.int32)
    return (rows[:, None] == place[None, :]).astype(BF16)


def one_hot(row, count):
    return (row[:, None] == jnp.arange(count, dtype=jnp.int32)[None, :]).astype(BF16)


def dot_t(left, right):
    return lax.dot_general(left, right, (((1,), (1,)), ((), ())), preferred_element_type=F32)


def windows(blocks, node, capacity):
    tokens = blocks.shape[-2]
    start = tokens - capacity
    low = lax.slice_in_dim(blocks, 0, capacity, axis=-2 + blocks.ndim)
    high = lax.slice_in_dim(blocks, start, tokens, axis=-2 + blocks.ndim)
    own = jnp.where(node == 0, low, high)
    other = jnp.where(node == 0, high, low)
    return own, other


def join(*values):
    return lax.optimization_barrier(values)


def after(values, *others):
    return list(join(*values, *others)[: len(values)])


def cut(tokens, placer, local):
    column = tokens.shape[1] // 4
    blocks = []
    for m in range(4):
        block = lax.dynamic_slice_in_dim(tokens, ((local - m) % 4) * column, column, axis=1)
        blocks.append(jnp.dot(placer, block, preferred_element_type=F32).astype(BF16))
    return blocks


def sums(partial):
    right, left = partial(3), partial(1)
    for step in (1, 2, 3):
        right, left = right.astype(BF16), left.astype(BF16)
        got_r, got_l = yield (
            (right, dict(by_local=1, wrap=False, last=step - 1)),
            (left, dict(by_local=-1, wrap=False, first=4 - step)),
        )
        right = partial(3 - step).astype(F32) + got_r.astype(F32)
        if step < 3:
            left = partial(step + 1).astype(F32) + got_l.astype(F32)
    yield right + got_l.astype(F32)


def gathers(rows, local):
    from_left, from_right = [rows], [rows]
    for step in (1, 2, 3):
        got_r, got_l = yield (
            (from_left[-1], dict(by_local=1, wrap=False, first=step - 1)),
            (from_right[-1], dict(by_local=-1, wrap=False, last=4 - step)),
        )
        from_left.append(got_r)
        from_right.append(got_l)
    slots = [rows]
    for m in (1, 2, 3):
        slots.append(jnp.where(local + m < 4, from_right[m], from_left[4 - m]))
    yield jnp.stack(slots)


def send(pieces):
    return [move(value, **how) for value, how in pieces]


def operands(pieces):
    return [value for value, _ in pieces]


def valid(zeros, node, tokens, capacity):
    row = jnp.arange(capacity, dtype=F32)[None, :]
    return jnp.where(node == 0, row < zeros[:, None], row + (tokens - capacity) >= zeros[:, None])


def merge(own, other, node, tokens):
    slots, capacity, column = own.shape
    low = jnp.where(node == 0, own, other)
    high = jnp.where(node == 0, other, own)
    rest = jnp.zeros((slots, tokens - capacity, column), own.dtype)
    return jnp.concatenate([low, rest], axis=1) + jnp.concatenate([rest, high], axis=1)


def homeward(merged, by_pp):
    return [(merged[m], dict(by_pp=by_pp, by_local=m)) for m in (2, 1, 3, 0)]


def column_of(row_ref):
    n = row_ref.shape[1]
    row = lax.broadcasted_iota(jnp.int32, (n, n), 0)
    col = lax.broadcasted_iota(jnp.int32, (n, n), 1)
    return jnp.sum(jnp.where(row == col, row_ref[...], 0.0), axis=1, keepdims=True)


def cut_kernel(at_ref, route_ref, weight_ref, values_ref, *blocks):
    tokens = route_ref.shape[1]
    column = blocks[0].shape[1]
    row = lax.broadcasted_iota(jnp.int32, (tokens, tokens), 0)
    col = lax.broadcasted_iota(jnp.int32, (tokens, tokens), 1)
    ones = route_ref[...].astype(F32)
    before = jnp.dot(
        jnp.broadcast_to(ones, (8, tokens)).astype(BF16),
        (row < col).astype(BF16),
        preferred_element_type=F32,
    )[0:1]
    zeros = tokens - jnp.sum(ones, axis=1, keepdims=True)
    index = col[0:1].astype(F32)
    place = jnp.where(ones == 0.0, index - before, zeros + before).astype(jnp.int32)
    picker = (row == place).astype(BF16)
    weight = column_of(weight_ref)
    for i, block_ref in enumerate(blocks):
        cols = pl.ds(pl.multiple_of(at_ref[i] * column, column), column)
        block = (weight * values_ref[:, cols].astype(F32)).astype(BF16)
        block_ref[...] = jnp.dot(picker, block, preferred_element_type=F32).astype(BF16)


def scaled_cut(tokens, weight, route, local):
    rows, features = tokens.shape
    vmem = pl.BlockSpec(memory_space=pltpu.VMEM)
    at = jnp.stack([(local - m) % 4 for m in range(4)]).astype(jnp.int32)
    return list(
        pl.pallas_call(
            cut_kernel,
            out_shape=[jax.ShapeDtypeStruct((rows, features // 4), BF16)] * 4,
            in_specs=[pl.BlockSpec(memory_space=pltpu.SMEM)] + [vmem] * 3,
            out_specs=[vmem] * 4,
            compiler_params=pltpu.CompilerParams(vmem_limit_bytes=8 * 2**20),
            name="cut",
        )(at, route[None, :], weight[None, :], tokens)
    )


def finish_kernel(at_ref, weight_ref, pick_ref, residual_ref, *refs):
    *blocks, out_ref, rows, base, total, sem = refs
    count = len(blocks)
    column = rows.shape[-1]

    def cols(i):
        return pl.ds(pl.multiple_of(at_ref[i] * column, column), column)

    ins = []
    for i in range(count):
        ins.append(
            (
                pltpu.make_async_copy(blocks[i], rows.at[i], sem.at[0, i]),
                pltpu.make_async_copy(residual_ref.at[:, cols(i)], base.at[i], sem.at[1, i]),
            )
        )
        for copy in ins[i]:
            copy.start()
    weight = column_of(weight_ref)
    outs = []
    for i in range(count):
        for copy in ins[i]:
            copy.wait()
        moe = jnp.dot(pick_ref[...], rows[i], preferred_element_type=F32)
        total[i] = (base[i].astype(F32) + weight * moe).astype(total.dtype)
        outs.append(pltpu.make_async_copy(total.at[i], out_ref.at[0, :, cols(i)], sem.at[2, i]))
        outs[i].start()
    for copy in outs:
        copy.wait()


def finish(residual, weight, place, blocks, at):
    count, column = len(blocks), blocks[0].shape[-1]
    tokens, features = residual.shape
    vmem = pl.BlockSpec(memory_space=pltpu.VMEM)
    anywhere = pl.BlockSpec(memory_space=pl.ANY)
    return pl.pallas_call(
        finish_kernel,
        out_shape=jax.ShapeDtypeStruct((1, tokens, features), BF16),
        in_specs=[pl.BlockSpec(memory_space=pltpu.SMEM)] + [vmem] * 2 + [anywhere] * (1 + count),
        out_specs=anywhere,
        scratch_shapes=[pltpu.VMEM((count, tokens, column), BF16)] * 3
        + [pltpu.SemaphoreType.DMA((3, count))],
        compiler_params=pltpu.CompilerParams(vmem_limit_bytes=8 * 2**20),
        name="finish",
    )(at, weight[None, :], one_hot(place, tokens), residual, *blocks)


def body_pair(
    act_fwd, routes_fwd, weight_fwd, grad_bwd, routes_bwd, weight_bwd, saved_bwd, w_gate_up, w_down
):
    node = lax.axis_index("node")
    local = lax.axis_index("local")
    tokens_here = act_fwd.shape[1]
    capacity = 5 * tokens_here // 8
    w_gu = w_gate_up[0, 0]
    w_dn = w_down[0, 0]
    hidden_units = w_dn.shape[0]
    shape = (4, 2, capacity)

    act, grad = act_fwd[0], grad_bwd[0]
    route_a, route_b = routes_fwd[0, :, 0], routes_bwd[0, :, 0]
    sort_a, sort_b = sorter(route_a), sorter(route_b)
    zeros = tokens_here - jnp.stack([jnp.sum(route_a), jnp.sum(route_b)]).astype(F32)

    def in_rows(cuts, got):
        return windows(jnp.stack([cuts[0], got[1], got[0], got[2]]), node, capacity)

    def by_node(own, got, axis):
        return jnp.stack([jnp.where(node == 0, own, got), jnp.where(node == 0, got, own)], axis=axis)

    def split(done):
        own = lax.dynamic_index_in_dim(done, node, axis=1, keepdims=False)
        other = lax.dynamic_index_in_dim(done, 1 - node, axis=1, keepdims=False)
        return own, other

    def turn(chain, back, *others):
        pieces = chain.send(after(back, *others))
        return operands(pieces), send(pieces)

    cut_b = scaled_cut(grad, weight_bwd[0], route_b, local)
    c1, c2, c3, saved_in = join(*cut_b[1:], saved_bwd[0])
    got_b = [move(c2, by_local=-2), move(c1, by_local=-1), move(c3, by_local=-3)]
    saved = jnp.dot(sort_b, saved_in, preferred_element_type=F32).astype(BF16)
    saved_own, saved_other = windows(saved, node, capacity)
    saved_got = move(saved_other, by_node=1)
    (zeros_wait,) = after([zeros], saved_other)
    zeros_got = move(zeros_wait, by_node=1)
    cut_a = cut(act, sort_a, local)
    *got_b, saved_got, zeros_got, a0, a1, a2, a3 = join(*got_b, saved_got, zeros_got, *cut_a)
    cut_a = [a0, a1, a2, a3]
    zeros = by_node(zeros, zeros_got, 0)
    got_a = [move(cut_a[m], by_local=-m) for m in (2, 1, 3)]
    own_b, other_b = in_rows(cut_b, got_b)
    column = own_b.shape[-1]
    got_bx = move(other_b, by_node=1)

    rows_b = by_node(own_b, got_bx, 1).reshape(-1, column)
    part_b = dot_t(rows_b, w_dn).astype(BF16).reshape(shape + (hidden_units,))
    back_b = [move(part_b[m], by_local=m) for m in (2, 1, 3)]
    both = join(*back_b, *got_a)
    back_b, got_a = both[:3], both[3:]
    own_a, other_a = in_rows(cut_a, got_a)
    got_ax = move(other_a, by_node=1)
    dh = part_b[0].astype(F32) + sum(part.astype(F32) for part in back_b)
    dh = jnp.where(valid(zeros[:, 1], node, tokens_here, capacity)[..., None], dh, 0.0)
    saved_rows = by_node(saved_own, saved_got, 0)
    g = saved_rows[..., :hidden_units].astype(F32)
    u = saved_rows[..., hidden_units:].astype(F32)
    q = 1.0 / (1.0 + jnp.exp(-g))
    grad_gu = jnp.concatenate([dh * u * q * (1.0 + g * (1.0 - q)), dh * g * q], axis=-1).astype(
        BF16
    )

    chain_b = gathers(grad_gu, local)
    back_b = send(next(chain_b))
    small_wait, route_wait = after(
        [jnp.stack([route_a.astype(F32), weight_fwd[0]]), route_b], grad_gu
    )
    small_next = move(small_wait, by_pp=1)
    route_b_next = move(route_wait, by_pp=-1)
    part_a = []
    for m in range(4):
        rows = by_node(own_a[m], got_ax[m], 0).reshape(-1, column)
        part = jnp.dot(rows, w_gu, preferred_element_type=F32).astype(BF16)
        part_a.append(part.reshape(2, capacity, 2 * hidden_units))
    r, l, *part_a, small_next, route_b_next = join(*back_b, *part_a, small_next, route_b_next)
    back_b = [r, l]
    chain_a = sums(lambda slot: part_a[slot])
    values_b, back_b = turn(chain_b, back_b)
    pieces = next(chain_a)
    back_a = send(pieces)
    act_next = move(after([act], *operands(pieces))[0], by_pp=1)
    *back_b, act_next = join(*back_b, act_next)
    values_b, back_b = turn(chain_b, back_b)
    grad_next = move(join(grad, *values_b)[0], by_pp=-1)
    *back_b, grad_next = join(*back_b, grad_next)
    values_a, back_a = turn(chain_a, back_a)
    values_a, back_a = turn(chain_a, back_a)
    all_gu = chain_b.send(back_b)
    done_b = dot_t(all_gu.reshape(-1, 2 * hidden_units), w_gu).astype(BF16)
    own_b, other_b = split(done_b.reshape(shape + (column,)))
    got_b = move(other_b, by_node=1)

    preact = chain_a.send(back_a)
    preact = jnp.where(valid(zeros[:, 0], node, tokens_here, capacity)[..., None], preact, 0.0)
    hidden = (jax.nn.silu(preact[..., :hidden_units]) * preact[..., hidden_units:]).astype(BF16)
    all_hidden = [move(hidden, by_local=-m) for m in (1, 2, 3)]
    merged_b = merge(own_b, got_b, node, tokens_here)
    h1, h2, h3, merged_b = join(*all_hidden, merged_b)
    all_hidden = jnp.stack([hidden, h1, h2, h3])
    home_b = send(homeward(merged_b, -1))
    done_a = jnp.dot(
        all_hidden.reshape(-1, hidden_units), w_dn, preferred_element_type=F32
    ).astype(BF16)
    own_a, other_a = split(done_a.reshape(shape + (column,)))
    got_a = move(other_a, by_node=1)
    home_a = send(homeward(merge(own_a, got_a, node, tokens_here), 1))

    at = jnp.stack([(local - m) % 4 for m in (2, 1, 3, 0)]).astype(jnp.int32)
    ones = jnp.ones((tokens_here,), F32)
    prev_grad = finish(grad_next, ones, sorted_places(route_b_next), home_b, at)
    place_a = sorted_places(small_next[0].astype(jnp.int32))
    next_input = finish(act_next, small_next[1], place_a, home_a, at)
    return next_input, prev_grad


def from_behind(value, axis, by):
    length = lax.axis_size(axis)
    return lax.ppermute(value, axis, [(i, (i + by) % length) for i in range(length)])


def place_matrix(route, expert_count, capacity):
    onehot = (route[:, None] == jnp.arange(expert_count, dtype=jnp.int32)[None, :]).astype(
        jnp.int32
    )
    before = jnp.cumsum(onehot, axis=0) - onehot
    slot_index = jnp.sum(before * onehot, axis=1)
    target = route * capacity + slot_index
    positions = jnp.arange(expert_count * capacity, dtype=jnp.int32)
    return (positions[:, None] == target[None, :]).astype(jnp.bfloat16)


def pack_rows(placer, values, expert_count, capacity):
    packed = jnp.dot(placer, values, preferred_element_type=jnp.float32).astype(jnp.bfloat16)
    return packed.reshape(expert_count, capacity, values.shape[1])


def unpack_rows(placer, packed):
    flattened = packed.reshape(-1, packed.shape[-1])
    result = lax.dot_general(
        placer, flattened, (((0,), (0,)), ((), ())), preferred_element_type=jnp.float32
    )
    return result.astype(jnp.bfloat16)


def flat_outgoing(packed, local_count):
    expert_count, capacity, feature_count = packed.shape
    column = feature_count // local_count
    outgoing = packed.reshape(expert_count, capacity, local_count, column).transpose(0, 2, 1, 3)
    return outgoing.reshape(expert_count * local_count, capacity, column)


def flat_layout(received, expert_count, local_count):
    capacity = received.shape[1]
    column = received.shape[2]
    rows_in = received.reshape(expert_count, local_count, capacity, column).transpose(1, 0, 2, 3)
    return rows_in.reshape(-1, column)


def send_rows(packs, local_count):
    expert_count = packs[0].shape[0]
    outgoing = tuple((flat_outgoing(packed, local_count) for packed in packs))
    received = (
        lax.all_to_all(outgoing[0], ("node", "local"), split_axis=0, concat_axis=0, tiled=True),
        lax.all_to_all(outgoing[1], ("node", "local"), split_axis=0, concat_axis=0, tiled=True),
    )
    return tuple((flat_layout(item, expert_count, local_count) for item in received))


def return_rows(finished_pair, expert_count, capacity, local_count):
    column = finished_pair[0].shape[1]
    blocks = tuple(
        (item.reshape(local_count, expert_count, capacity, column) for item in finished_pair)
    )
    outgoing = tuple(
        (
            item.transpose(1, 0, 2, 3).reshape(expert_count * local_count, capacity, column)
            for item in blocks
        )
    )
    received = (
        lax.all_to_all(outgoing[0], ("node", "local"), split_axis=0, concat_axis=0, tiled=True),
        lax.all_to_all(outgoing[1], ("node", "local"), split_axis=0, concat_axis=0, tiled=True),
    )
    results = []
    for item in received:
        arranged = item.reshape(expert_count, local_count, capacity, column).transpose(0, 2, 1, 3)
        results.append(arranged.reshape(expert_count, capacity, local_count * column))
    return tuple(results)


def body(
    act_fwd, routes_fwd, weight_fwd, grad_bwd, routes_bwd, weight_bwd, saved_bwd, w_gate_up, w_down
):
    node_count = lax.axis_size("node")
    local_count = lax.axis_size("local")
    tokens_here = act_fwd.shape[1]
    capacity = 5 * tokens_here // (4 * node_count)
    rows_each = node_count * capacity
    w_gu = w_gate_up[0, 0]
    w_dn = w_down[0, 0]
    hidden_units = w_dn.shape[0]
    tokens_a = act_fwd[0]
    placer_a = place_matrix(routes_fwd[0, :, 0], node_count, capacity)
    cotangent = grad_bwd[0]
    placer_b = place_matrix(routes_bwd[0, :, 0], node_count, capacity)
    scaled = (weight_bwd[0][:, None] * cotangent.astype(jnp.float32)).astype(jnp.bfloat16)
    packed_a = pack_rows(placer_a, tokens_a, node_count, capacity)
    packed_b = pack_rows(placer_b, scaled, node_count, capacity)
    rows_a, rows_b = send_rows((packed_a, packed_b), local_count)
    saved_packed = pack_rows(placer_b, saved_bwd[0], node_count, capacity)
    saved_rows = lax.all_to_all(
        saved_packed, "node", split_axis=0, concat_axis=0, tiled=True
    ).reshape(rows_each, -1)
    row_block = rows_a
    preact = lax.psum_scatter(
        jnp.dot(row_block, w_gu, preferred_element_type=jnp.float32).astype(jnp.bfloat16),
        "local",
        scatter_dimension=0,
        tiled=True,
    ).astype(jnp.float32)
    row_block = rows_b
    grad_hidden = lax.psum_scatter(
        lax.dot_general(
            row_block, w_dn, (((1,), (1,)), ((), ())), preferred_element_type=jnp.float32
        ).astype(jnp.bfloat16),
        "local",
        scatter_dimension=0,
        tiled=True,
    ).astype(jnp.float32)
    hidden = (jax.nn.silu(preact[:, :hidden_units]) * preact[:, hidden_units:]).astype(jnp.bfloat16)
    done_a = jnp.dot(
        lax.all_gather(hidden, "local", axis=0, tiled=True),
        w_dn,
        preferred_element_type=jnp.float32,
    ).astype(jnp.bfloat16)
    gate_pre = saved_rows[:, :hidden_units].astype(jnp.float32)
    up_pre = saved_rows[:, hidden_units:].astype(jnp.float32)
    sigmoid_g = 1.0 / (1.0 + jnp.exp(-gate_pre))
    grad_gate = grad_hidden * up_pre * sigmoid_g * (1.0 + gate_pre * (1.0 - sigmoid_g))
    grad_up = grad_hidden * gate_pre * sigmoid_g
    grad_gu = jnp.concatenate([grad_gate, grad_up], axis=1).astype(jnp.bfloat16)
    product = lax.dot_general(
        lax.all_gather(grad_gu, "local", axis=0, tiled=True),
        w_gu,
        (((1,), (1,)), ((), ())),
        preferred_element_type=jnp.float32,
    )
    done_b = product.astype(jnp.bfloat16)
    back_a, back_b = return_rows((done_a, done_b), node_count, capacity, local_count)
    moe_a = unpack_rows(placer_a, back_a)
    result_a = tokens_a.astype(jnp.float32) + weight_fwd[0][:, None] * moe_a.astype(jnp.float32)
    result_a = result_a.astype(jnp.bfloat16)
    moe_b = unpack_rows(placer_b, back_b)
    result_b = (cotangent.astype(jnp.float32) + moe_b.astype(jnp.float32)).astype(jnp.bfloat16)
    next_input = from_behind(result_a[None], "pp", 1)
    prev_grad = from_behind(result_b[None], "pp", -1)
    return (next_input, prev_grad)


def solution(mesh):
    in_specs = (
        P("pp", ("node", "local"), None),
        P("pp", ("node", "local"), None),
        P("pp", ("node", "local")),
        P("pp", ("node", "local"), None),
        P("pp", ("node", "local"), None),
        P("pp", ("node", "local")),
        P("pp", ("node", "local"), None),
        P("pp", "node", "local", None),
        P("pp", "node", None, "local"),
    )
    out_specs = (P("pp", ("node", "local"), None), P("pp", ("node", "local"), None))
    paired = mesh.shape["node"] == 2 and mesh.shape["local"] == 4
    plan = body_pair if paired else body
    return jax.shard_map(plan, mesh=mesh, in_specs=in_specs, out_specs=out_specs, check_vma=False)
```

```python
import jax
import jax.numpy as jnp
from jax import lax
from jax.experimental import pallas as pl
from jax.experimental.pallas import tpu as pltpu
from jax.sharding import PartitionSpec as P

F32 = jnp.float32
BF16 = jnp.bfloat16
AXES = ("pp", "node", "local")


def move(value, by_pp=0, by_node=0, by_local=0, wrap=True, first=0, last=None):
    pps, nodes, locs = (lax.axis_size(a) for a in AXES)
    last = locs - 1 if last is None else last
    pairs = []
    for s in range(pps):
        for n in range(nodes):
            for l in range(locs):
                to = l + by_local
                if not wrap and not (first <= l <= last and 0 <= to < locs):
                    continue
                source = (s * nodes + n) * locs + l
                target = (((s + by_pp) % pps) * nodes + (n ^ by_node)) * locs + to % locs
                pairs.append((source, target))
    return lax.ppermute(value, AXES, pairs)


def sorted_places(route):
    ones = route.astype(F32)
    count = route.shape[0]
    earlier = (jnp.arange(count)[None, :] < jnp.arange(count)[:, None]).astype(F32)
    ones_before = jnp.dot(earlier, ones[:, None], preferred_element_type=F32)[:, 0]
    zeros = count - jnp.sum(ones)
    index = jnp.arange(count, dtype=F32)
    place = jnp.where(route == 0, index - ones_before, zeros + ones_before)
    return place.astype(jnp.int32)


def sorter(route):
    place = sorted_places(route)
    rows = jnp.arange(route.shape[0], dtype=jnp.int32)
    return (rows[:, None] == place[None, :]).astype(BF16)


def one_hot(row, count):
    return (row[:, None] == jnp.arange(count, dtype=jnp.int32)[None, :]).astype(BF16)


def dot_t(left, right):
    return lax.dot_general(left, right, (((1,), (1,)), ((), ())), preferred_element_type=F32)


def windows(blocks, node, capacity):
    tokens = blocks.shape[-2]
    start = tokens - capacity
    low = lax.slice_in_dim(blocks, 0, capacity, axis=-2 + blocks.ndim)
    high = lax.slice_in_dim(blocks, start, tokens, axis=-2 + blocks.ndim)
    own = jnp.where(node == 0, low, high)
    other = jnp.where(node == 0, high, low)
    return own, other


def join(*values):
    return lax.optimization_barrier(values)


def after(values, *others):
    return list(join(*values, *others)[: len(values)])


def cut(tokens, placer, local):
    column = tokens.shape[1] // 4
    blocks = []
    for m in range(4):
        block = lax.dynamic_slice_in_dim(tokens, ((local - m) % 4) * column, column, axis=1)
        blocks.append(jnp.dot(placer, block, preferred_element_type=F32).astype(BF16))
    return blocks


def sums(partial):
    right, left = partial(3), partial(1)
    for step in (1, 2, 3):
        right, left = right.astype(BF16), left.astype(BF16)
        got_r, got_l = yield (
            (right, dict(by_local=1, wrap=False, last=step - 1)),
            (left, dict(by_local=-1, wrap=False, first=4 - step)),
        )
        right = partial(3 - step).astype(F32) + got_r.astype(F32)
        if step < 3:
            left = partial(step + 1).astype(F32) + got_l.astype(F32)
    yield right + got_l.astype(F32)


def gathers(rows, local):
    from_left, from_right = [rows], [rows]
    for step in (1, 2, 3):
        got_r, got_l = yield (
            (from_left[-1], dict(by_local=1, wrap=False, first=step - 1)),
            (from_right[-1], dict(by_local=-1, wrap=False, last=4 - step)),
        )
        from_left.append(got_r)
        from_right.append(got_l)
    slots = [rows]
    for m in (1, 2, 3):
        slots.append(jnp.where(local + m < 4, from_right[m], from_left[4 - m]))
    yield jnp.stack(slots)


def send(pieces):
    return [move(value, **how) for value, how in pieces]


def operands(pieces):
    return [value for value, _ in pieces]


def valid(zeros, node, tokens, capacity):
    row = jnp.arange(capacity, dtype=F32)[None, :]
    return jnp.where(node == 0, row < zeros[:, None], row + (tokens - capacity) >= zeros[:, None])


def merge(own, other, node, tokens):
    slots, capacity, column = own.shape
    low = jnp.where(node == 0, own, other)
    high = jnp.where(node == 0, other, own)
    rest = jnp.zeros((slots, tokens - capacity, column), own.dtype)
    return jnp.concatenate([low, rest], axis=1) + jnp.concatenate([rest, high], axis=1)


def homeward(merged, by_pp):
    return [(merged[m], dict(by_pp=by_pp, by_local=m)) for m in (2, 1, 3, 0)]


def column_of(row_ref):
    n = row_ref.shape[1]
    row = lax.broadcasted_iota(jnp.int32, (n, n), 0)
    col = lax.broadcasted_iota(jnp.int32, (n, n), 1)
    return jnp.sum(jnp.where(row == col, row_ref[...], 0.0), axis=1, keepdims=True)


def cut_kernel(at_ref, route_ref, weight_ref, values_ref, *blocks):
    tokens = route_ref.shape[1]
    column = blocks[0].shape[1]
    row = lax.broadcasted_iota(jnp.int32, (tokens, tokens), 0)
    col = lax.broadcasted_iota(jnp.int32, (tokens, tokens), 1)
    ones = route_ref[...].astype(F32)
    before = jnp.dot(
        jnp.broadcast_to(ones, (8, tokens)).astype(BF16),
        (row < col).astype(BF16),
        preferred_element_type=F32,
    )[0:1]
    zeros = tokens - jnp.sum(ones, axis=1, keepdims=True)
    index = col[0:1].astype(F32)
    place = jnp.where(ones == 0.0, index - before, zeros + before).astype(jnp.int32)
    picker = (row == place).astype(BF16)
    weight = column_of(weight_ref)
    for i, block_ref in enumerate(blocks):
        cols = pl.ds(pl.multiple_of(at_ref[i] * column, column), column)
        block = (weight * values_ref[:, cols].astype(F32)).astype(BF16)
        block_ref[...] = jnp.dot(picker, block, preferred_element_type=F32).astype(BF16)


def scaled_cut(tokens, weight, route, local):
    rows, features = tokens.shape
    vmem = pl.BlockSpec(memory_space=pltpu.VMEM)
    at = jnp.stack([(local - m) % 4 for m in range(4)]).astype(jnp.int32)
    return list(
        pl.pallas_call(
            cut_kernel,
            out_shape=[jax.ShapeDtypeStruct((rows, features // 4), BF16)] * 4,
            in_specs=[pl.BlockSpec(memory_space=pltpu.SMEM)] + [vmem] * 3,
            out_specs=[vmem] * 4,
            compiler_params=pltpu.CompilerParams(vmem_limit_bytes=8 * 2**20),
            name="cut",
        )(at, route[None, :], weight[None, :], tokens)
    )


def finish_kernel(at_ref, weight_ref, pick_ref, residual_ref, *refs):
    *blocks, out_ref, rows, base, total, sem = refs
    count = len(blocks)
    column = rows.shape[-1]

    def cols(i):
        return pl.ds(pl.multiple_of(at_ref[i] * column, column), column)

    ins = []
    for i in range(count):
        ins.append(
            (
                pltpu.make_async_copy(blocks[i], rows.at[i], sem.at[0, i]),
                pltpu.make_async_copy(residual_ref.at[:, cols(i)], base.at[i], sem.at[1, i]),
            )
        )
        for copy in ins[i]:
            copy.start()
    weight = column_of(weight_ref)
    outs = []
    for i in range(count):
        for copy in ins[i]:
            copy.wait()
        moe = jnp.dot(pick_ref[...], rows[i], preferred_element_type=F32)
        total[i] = (base[i].astype(F32) + weight * moe).astype(total.dtype)
        outs.append(pltpu.make_async_copy(total.at[i], out_ref.at[0, :, cols(i)], sem.at[2, i]))
        outs[i].start()
    for copy in outs:
        copy.wait()


def finish(residual, weight, place, blocks, at):
    count, column = len(blocks), blocks[0].shape[-1]
    tokens, features = residual.shape
    vmem = pl.BlockSpec(memory_space=pltpu.VMEM)
    anywhere = pl.BlockSpec(memory_space=pl.ANY)
    return pl.pallas_call(
        finish_kernel,
        out_shape=jax.ShapeDtypeStruct((1, tokens, features), BF16),
        in_specs=[pl.BlockSpec(memory_space=pltpu.SMEM)] + [vmem] * 2 + [anywhere] * (1 + count),
        out_specs=anywhere,
        scratch_shapes=[pltpu.VMEM((count, tokens, column), BF16)] * 3
        + [pltpu.SemaphoreType.DMA((3, count))],
        compiler_params=pltpu.CompilerParams(vmem_limit_bytes=8 * 2**20),
        name="finish",
    )(at, weight[None, :], one_hot(place, tokens), residual, *blocks)


def body_pair(
    act_fwd, routes_fwd, weight_fwd, grad_bwd, routes_bwd, weight_bwd, saved_bwd, w_gate_up, w_down
):
    node = lax.axis_index("node")
    local = lax.axis_index("local")
    tokens_here = act_fwd.shape[1]
    capacity = 5 * tokens_here // 8
    w_gu = w_gate_up[0, 0]
    w_dn = w_down[0, 0]
    hidden_units = w_dn.shape[0]
    shape = (4, 2, capacity)

    act, grad = act_fwd[0], grad_bwd[0]
    route_a, route_b = routes_fwd[0, :, 0], routes_bwd[0, :, 0]
    sort_b = sorter(route_b)
    zeros = tokens_here - jnp.stack([jnp.sum(route_a), jnp.sum(route_b)]).astype(F32)

    def in_rows(cuts, got):
        return windows(jnp.stack([cuts[0], got[1], got[0], got[2]]), node, capacity)

    def by_node(own, got, axis):
        return jnp.stack([jnp.where(node == 0, own, got), jnp.where(node == 0, got, own)], axis=axis)

    def split(done):
        own = lax.dynamic_index_in_dim(done, node, axis=1, keepdims=False)
        other = lax.dynamic_index_in_dim(done, 1 - node, axis=1, keepdims=False)
        return own, other

    def turn(chain, back, *others):
        pieces = chain.send(after(back, *others))
        return operands(pieces), send(pieces)

    cut_a = scaled_cut(act, jnp.ones((tokens_here,), F32), route_a, local)
    c1, c2, c3, saved_in, grad_in = join(*cut_a[1:], saved_bwd[0], grad)
    got_a = [move(c2, by_local=-2), move(c1, by_local=-1), move(c3, by_local=-3)]
    saved = jnp.dot(sort_b, saved_in, preferred_element_type=F32).astype(BF16)
    saved_own, saved_other = windows(saved, node, capacity)
    saved_got = move(saved_other, by_node=1)
    zeros_got = move(zeros, by_node=1)
    cut_b = scaled_cut(grad_in, weight_bwd[0], route_b, local)
    *got_a, saved_got, zeros_got, b0, b1, b2, b3 = join(*got_a, saved_got, zeros_got, *cut_b)
    cut_b = [b0, b1, b2, b3]
    zeros = by_node(zeros, zeros_got, 0)
    got_b = [move(cut_b[m], by_local=-m) for m in (2, 1, 3)]
    own_a, other_a = in_rows(cut_a, got_a)
    column = own_a.shape[-1]
    got_ax = move(other_a, by_node=1)
    *got_b, got_ax, act_in, small, route_in, grad_in = join(
        *got_b, got_ax, act, jnp.stack([route_a.astype(F32), weight_fwd[0]]), route_b, grad
    )

    own_b, other_b = in_rows(cut_b, got_b)
    got_bx = move(other_b, by_node=1)
    part_a = []
    for m in range(4):
        rows = by_node(own_a[m], got_ax[m], 0).reshape(-1, column)
        part = jnp.dot(rows, w_gu, preferred_element_type=F32).astype(BF16)
        part_a.append(part.reshape(2, capacity, 2 * hidden_units))
    chain_a = sums(lambda slot: part_a[slot])
    back_a = send(next(chain_a))
    act_next = move(act_in, by_pp=1)
    *back_a, got_bx, act_next = join(*back_a, got_bx, act_next)

    back_a = send(chain_a.send(back_a))
    rows_b = by_node(own_b, got_bx, 1).reshape(-1, column)
    part_b = dot_t(rows_b, w_dn).astype(BF16).reshape(shape + (hidden_units,))
    back_b = [move(part_b[m], by_local=m) for m in (2, 1, 3)]
    back_a = send(chain_a.send(back_a))
    preact = chain_a.send(back_a)
    preact = jnp.where(valid(zeros[:, 0], node, tokens_here, capacity)[..., None], preact, 0.0)
    hidden = (jax.nn.silu(preact[..., :hidden_units]) * preact[..., hidden_units:]).astype(BF16)
    all_hidden = [move(hidden, by_local=-m) for m in (1, 2, 3)]

    dh = part_b[0].astype(F32) + sum(part.astype(F32) for part in back_b)
    dh = jnp.where(valid(zeros[:, 1], node, tokens_here, capacity)[..., None], dh, 0.0)
    saved_rows = by_node(saved_own, saved_got, 0)
    g = saved_rows[..., :hidden_units].astype(F32)
    u = saved_rows[..., hidden_units:].astype(F32)
    q = 1.0 / (1.0 + jnp.exp(-g))
    grad_gu = jnp.concatenate([dh * u * q * (1.0 + g * (1.0 - q)), dh * g * q], axis=-1).astype(
        BF16
    )

    chain_b = gathers(grad_gu, local)
    back_b = send(next(chain_b))
    *back_b, h1, h2, h3, small, route_in, grad_in = join(
        *back_b, *all_hidden, small, route_in, grad_in
    )
    back_b = send(chain_b.send(back_b))
    all_hidden = jnp.stack([hidden, h1, h2, h3])
    done_a = jnp.dot(
        all_hidden.reshape(-1, hidden_units), w_dn, preferred_element_type=F32
    ).astype(BF16)
    own_a, other_a = split(done_a.reshape(shape + (column,)))
    got_a = move(other_a, by_node=1)
    small_next = move(small, by_pp=1)
    route_b_next = move(route_in, by_pp=-1)
    *back_b, got_a, small_next, route_b_next = join(*back_b, got_a, small_next, route_b_next)
    back_b = send(chain_b.send(back_b))
    home_a = send(homeward(merge(own_a, got_a, node, tokens_here), 1))
    *back_b, h0, h1, h2, h3 = join(*back_b, *home_a)
    home_a = [h0, h1, h2, h3]
    grad_next = move(grad_in, by_pp=-1)
    all_gu = chain_b.send(back_b)
    done_b = dot_t(all_gu.reshape(-1, 2 * hidden_units), w_gu).astype(BF16)
    own_b, other_b = split(done_b.reshape(shape + (column,)))
    got_b = move(other_b, by_node=1)
    got_b, grad_next = join(got_b, grad_next)
    home_b = send(homeward(merge(own_b, got_b, node, tokens_here), -1))

    at = jnp.stack([(local - m) % 4 for m in (2, 1, 3, 0)]).astype(jnp.int32)
    place_a = sorted_places(small_next[0].astype(jnp.int32))
    next_input = finish(act_next, small_next[1], place_a, home_a, at)
    ones = jnp.ones((tokens_here,), F32)
    prev_grad = finish(grad_next, ones, sorted_places(route_b_next), home_b, at)
    return next_input, prev_grad


def from_behind(value, axis, by):
    length = lax.axis_size(axis)
    return lax.ppermute(value, axis, [(i, (i + by) % length) for i in range(length)])


def place_matrix(route, expert_count, capacity):
    onehot = (route[:, None] == jnp.arange(expert_count, dtype=jnp.int32)[None, :]).astype(
        jnp.int32
    )
    before = jnp.cumsum(onehot, axis=0) - onehot
    slot_index = jnp.sum(before * onehot, axis=1)
    target = route * capacity + slot_index
    positions = jnp.arange(expert_count * capacity, dtype=jnp.int32)
    return (positions[:, None] == target[None, :]).astype(jnp.bfloat16)


def pack_rows(placer, values, expert_count, capacity):
    packed = jnp.dot(placer, values, preferred_element_type=jnp.float32).astype(jnp.bfloat16)
    return packed.reshape(expert_count, capacity, values.shape[1])


def unpack_rows(placer, packed):
    flattened = packed.reshape(-1, packed.shape[-1])
    result = lax.dot_general(
        placer, flattened, (((0,), (0,)), ((), ())), preferred_element_type=jnp.float32
    )
    return result.astype(jnp.bfloat16)


def flat_outgoing(packed, local_count):
    expert_count, capacity, feature_count = packed.shape
    column = feature_count // local_count
    outgoing = packed.reshape(expert_count, capacity, local_count, column).transpose(0, 2, 1, 3)
    return outgoing.reshape(expert_count * local_count, capacity, column)


def flat_layout(received, expert_count, local_count):
    capacity = received.shape[1]
    column = received.shape[2]
    rows_in = received.reshape(expert_count, local_count, capacity, column).transpose(1, 0, 2, 3)
    return rows_in.reshape(-1, column)


def send_rows(packs, local_count):
    expert_count = packs[0].shape[0]
    outgoing = tuple((flat_outgoing(packed, local_count) for packed in packs))
    received = (
        lax.all_to_all(outgoing[0], ("node", "local"), split_axis=0, concat_axis=0, tiled=True),
        lax.all_to_all(outgoing[1], ("node", "local"), split_axis=0, concat_axis=0, tiled=True),
    )
    return tuple((flat_layout(item, expert_count, local_count) for item in received))


def return_rows(finished_pair, expert_count, capacity, local_count):
    column = finished_pair[0].shape[1]
    blocks = tuple(
        (item.reshape(local_count, expert_count, capacity, column) for item in finished_pair)
    )
    outgoing = tuple(
        (
            item.transpose(1, 0, 2, 3).reshape(expert_count * local_count, capacity, column)
            for item in blocks
        )
    )
    received = (
        lax.all_to_all(outgoing[0], ("node", "local"), split_axis=0, concat_axis=0, tiled=True),
        lax.all_to_all(outgoing[1], ("node", "local"), split_axis=0, concat_axis=0, tiled=True),
    )
    results = []
    for item in received:
        arranged = item.reshape(expert_count, local_count, capacity, column).transpose(0, 2, 1, 3)
        results.append(arranged.reshape(expert_count, capacity, local_count * column))
    return tuple(results)


def body(
    act_fwd, routes_fwd, weight_fwd, grad_bwd, routes_bwd, weight_bwd, saved_bwd, w_gate_up, w_down
):
    node_count = lax.axis_size("node")
    local_count = lax.axis_size("local")
    tokens_here = act_fwd.shape[1]
    capacity = 5 * tokens_here // (4 * node_count)
    rows_each = node_count * capacity
    w_gu = w_gate_up[0, 0]
    w_dn = w_down[0, 0]
    hidden_units = w_dn.shape[0]
    tokens_a = act_fwd[0]
    placer_a = place_matrix(routes_fwd[0, :, 0], node_count, capacity)
    cotangent = grad_bwd[0]
    placer_b = place_matrix(routes_bwd[0, :, 0], node_count, capacity)
    scaled = (weight_bwd[0][:, None] * cotangent.astype(jnp.float32)).astype(jnp.bfloat16)
    packed_a = pack_rows(placer_a, tokens_a, node_count, capacity)
    packed_b = pack_rows(placer_b, scaled, node_count, capacity)
    rows_a, rows_b = send_rows((packed_a, packed_b), local_count)
    saved_packed = pack_rows(placer_b, saved_bwd[0], node_count, capacity)
    saved_rows = lax.all_to_all(
        saved_packed, "node", split_axis=0, concat_axis=0, tiled=True
    ).reshape(rows_each, -1)
    row_block = rows_a
    preact = lax.psum_scatter(
        jnp.dot(row_block, w_gu, preferred_element_type=jnp.float32).astype(jnp.bfloat16),
        "local",
        scatter_dimension=0,
        tiled=True,
    ).astype(jnp.float32)
    row_block = rows_b
    grad_hidden = lax.psum_scatter(
        lax.dot_general(
            row_block, w_dn, (((1,), (1,)), ((), ())), preferred_element_type=jnp.float32
        ).astype(jnp.bfloat16),
        "local",
        scatter_dimension=0,
        tiled=True,
    ).astype(jnp.float32)
    hidden = (jax.nn.silu(preact[:, :hidden_units]) * preact[:, hidden_units:]).astype(jnp.bfloat16)
    done_a = jnp.dot(
        lax.all_gather(hidden, "local", axis=0, tiled=True),
        w_dn,
        preferred_element_type=jnp.float32,
    ).astype(jnp.bfloat16)
    gate_pre = saved_rows[:, :hidden_units].astype(jnp.float32)
    up_pre = saved_rows[:, hidden_units:].astype(jnp.float32)
    sigmoid_g = 1.0 / (1.0 + jnp.exp(-gate_pre))
    grad_gate = grad_hidden * up_pre * sigmoid_g * (1.0 + gate_pre * (1.0 - sigmoid_g))
    grad_up = grad_hidden * gate_pre * sigmoid_g
    grad_gu = jnp.concatenate([grad_gate, grad_up], axis=1).astype(jnp.bfloat16)
    product = lax.dot_general(
        lax.all_gather(grad_gu, "local", axis=0, tiled=True),
        w_gu,
        (((1,), (1,)), ((), ())),
        preferred_element_type=jnp.float32,
    )
    done_b = product.astype(jnp.bfloat16)
    back_a, back_b = return_rows((done_a, done_b), node_count, capacity, local_count)
    moe_a = unpack_rows(placer_a, back_a)
    result_a = tokens_a.astype(jnp.float32) + weight_fwd[0][:, None] * moe_a.astype(jnp.float32)
    result_a = result_a.astype(jnp.bfloat16)
    moe_b = unpack_rows(placer_b, back_b)
    result_b = (cotangent.astype(jnp.float32) + moe_b.astype(jnp.float32)).astype(jnp.bfloat16)
    next_input = from_behind(result_a[None], "pp", 1)
    prev_grad = from_behind(result_b[None], "pp", -1)
    return (next_input, prev_grad)


def solution(mesh):
    in_specs = (
        P("pp", ("node", "local"), None),
        P("pp", ("node", "local"), None),
        P("pp", ("node", "local")),
        P("pp", ("node", "local"), None),
        P("pp", ("node", "local"), None),
        P("pp", ("node", "local")),
        P("pp", ("node", "local"), None),
        P("pp", "node", "local", None),
        P("pp", "node", None, "local"),
    )
    out_specs = (P("pp", ("node", "local"), None), P("pp", ("node", "local"), None))
    paired = mesh.shape["node"] == 2 and mesh.shape["local"] == 4
    plan = body_pair if paired else body
    return jax.shard_map(plan, mesh=mesh, in_specs=in_specs, out_specs=out_specs, check_vma=False)
```

```python
import jax
import jax.numpy as jnp
from jax import lax
from jax.experimental import pallas as pl
from jax.experimental.pallas import tpu as pltpu
from jax.sharding import PartitionSpec as P

F32 = jnp.float32
BF16 = jnp.bfloat16
AXES = ("pp", "node", "local")


def move(value, by_pp=0, by_node=0, by_local=0, wrap=True, first=0, last=None):
    pps, nodes, locs = (lax.axis_size(a) for a in AXES)
    last = locs - 1 if last is None else last
    pairs = []
    for s in range(pps):
        for n in range(nodes):
            for l in range(locs):
                to = l + by_local
                if not wrap and not (first <= l <= last and 0 <= to < locs):
                    continue
                source = (s * nodes + n) * locs + l
                target = (((s + by_pp) % pps) * nodes + (n ^ by_node)) * locs + to % locs
                pairs.append((source, target))
    return lax.ppermute(value, AXES, pairs)


def sorted_places(route):
    ones = route.astype(F32)
    count = route.shape[0]
    earlier = (jnp.arange(count)[None, :] < jnp.arange(count)[:, None]).astype(F32)
    ones_before = jnp.dot(earlier, ones[:, None], preferred_element_type=F32)[:, 0]
    zeros = count - jnp.sum(ones)
    index = jnp.arange(count, dtype=F32)
    place = jnp.where(route == 0, index - ones_before, zeros + ones_before)
    return place.astype(jnp.int32)


def sorter(route):
    place = sorted_places(route)
    rows = jnp.arange(route.shape[0], dtype=jnp.int32)
    return (rows[:, None] == place[None, :]).astype(BF16)


def one_hot(row, count):
    return (row[:, None] == jnp.arange(count, dtype=jnp.int32)[None, :]).astype(BF16)


def dot_t(left, right):
    return lax.dot_general(left, right, (((1,), (1,)), ((), ())), preferred_element_type=F32)


def windows(blocks, node, capacity):
    tokens = blocks.shape[-2]
    start = tokens - capacity
    low = lax.slice_in_dim(blocks, 0, capacity, axis=-2 + blocks.ndim)
    high = lax.slice_in_dim(blocks, start, tokens, axis=-2 + blocks.ndim)
    own = jnp.where(node == 0, low, high)
    other = jnp.where(node == 0, high, low)
    return own, other


def join(*values):
    return lax.optimization_barrier(values)


def after(values, *others):
    return list(join(*values, *others)[: len(values)])


def cut(tokens, placer, local):
    column = tokens.shape[1] // 4
    blocks = []
    for m in range(4):
        block = lax.dynamic_slice_in_dim(tokens, ((local - m) % 4) * column, column, axis=1)
        blocks.append(jnp.dot(placer, block, preferred_element_type=F32).astype(BF16))
    return blocks


def sums(partial):
    right, left = partial(3), partial(1)
    for step in (1, 2, 3):
        right, left = right.astype(BF16), left.astype(BF16)
        got_r, got_l = yield (
            (right, dict(by_local=1, wrap=False, last=step - 1)),
            (left, dict(by_local=-1, wrap=False, first=4 - step)),
        )
        right = partial(3 - step).astype(F32) + got_r.astype(F32)
        if step < 3:
            left = partial(step + 1).astype(F32) + got_l.astype(F32)
    yield right + got_l.astype(F32)


def gathers(rows, local):
    from_left, from_right = [rows], [rows]
    for step in (1, 2, 3):
        got_r, got_l = yield (
            (from_left[-1], dict(by_local=1, wrap=False, first=step - 1)),
            (from_right[-1], dict(by_local=-1, wrap=False, last=4 - step)),
        )
        from_left.append(got_r)
        from_right.append(got_l)
    slots = [rows]
    for m in (1, 2, 3):
        slots.append(jnp.where(local + m < 4, from_right[m], from_left[4 - m]))
    yield jnp.stack(slots)


def send(pieces):
    return [move(value, **how) for value, how in pieces]


def operands(pieces):
    return [value for value, _ in pieces]


def valid(zeros, node, tokens, capacity):
    row = jnp.arange(capacity, dtype=F32)[None, :]
    return jnp.where(node == 0, row < zeros[:, None], row + (tokens - capacity) >= zeros[:, None])


def merge(own, other, node, tokens):
    slots, capacity, column = own.shape
    low = jnp.where(node == 0, own, other)
    high = jnp.where(node == 0, other, own)
    rest = jnp.zeros((slots, tokens - capacity, column), own.dtype)
    return jnp.concatenate([low, rest], axis=1) + jnp.concatenate([rest, high], axis=1)


def homeward(merged, by_pp):
    return [(merged[m], dict(by_pp=by_pp, by_local=m)) for m in (2, 1, 3, 0)]


def column_of(row_ref):
    n = row_ref.shape[1]
    row = lax.broadcasted_iota(jnp.int32, (n, n), 0)
    col = lax.broadcasted_iota(jnp.int32, (n, n), 1)
    return jnp.sum(jnp.where(row == col, row_ref[...], 0.0), axis=1, keepdims=True)


def cut_kernel(at_ref, route_ref, weight_ref, values_ref, *refs):
    *blocks, values, sem = refs
    tokens = route_ref.shape[1]
    column = blocks[0].shape[1]
    copies = []
    for i in range(len(blocks)):
        cols = pl.ds(pl.multiple_of(at_ref[i] * column, column), column)
        copies.append(pltpu.make_async_copy(values_ref.at[:, cols], values.at[i], sem.at[i]))
        copies[i].start()
    row = lax.broadcasted_iota(jnp.int32, (tokens, tokens), 0)
    col = lax.broadcasted_iota(jnp.int32, (tokens, tokens), 1)
    ones = route_ref[...].astype(F32)
    before = jnp.dot(
        jnp.broadcast_to(ones, (8, tokens)).astype(BF16),
        (row < col).astype(BF16),
        preferred_element_type=F32,
    )[0:1]
    zeros = tokens - jnp.sum(ones, axis=1, keepdims=True)
    index = col[0:1].astype(F32)
    place = jnp.where(ones == 0.0, index - before, zeros + before).astype(jnp.int32)
    picker = (row == place).astype(BF16)
    weight = column_of(weight_ref)
    for i, block_ref in enumerate(blocks):
        copies[i].wait()
        block = (weight * values[i].astype(F32)).astype(BF16)
        block_ref[...] = jnp.dot(picker, block, preferred_element_type=F32).astype(BF16)


def scaled_cut(tokens, weight, route, local):
    rows, features = tokens.shape
    vmem = pl.BlockSpec(memory_space=pltpu.VMEM)
    at = jnp.stack([(local - m) % 4 for m in range(4)]).astype(jnp.int32)
    return list(
        pl.pallas_call(
            cut_kernel,
            out_shape=[jax.ShapeDtypeStruct((rows, features // 4), BF16)] * 4,
            in_specs=[pl.BlockSpec(memory_space=pltpu.SMEM)]
            + [vmem] * 2
            + [pl.BlockSpec(memory_space=pl.ANY)],
            out_specs=[vmem] * 4,
            scratch_shapes=[
                pltpu.VMEM((4, rows, features // 4), BF16),
                pltpu.SemaphoreType.DMA((4,)),
            ],
            compiler_params=pltpu.CompilerParams(vmem_limit_bytes=56 * 2**20),
            name="cut",
        )(at, route[None, :], weight[None, :], tokens)
    )


def finish_kernel(at_ref, weight_ref, pick_ref, residual_ref, *refs):
    *blocks, out_ref, rows, base, total, sem = refs
    count = len(blocks)
    column = rows.shape[-1]

    def cols(i):
        return pl.ds(pl.multiple_of(at_ref[i] * column, column), column)

    ins = []
    for i in range(count):
        ins.append(
            (
                pltpu.make_async_copy(blocks[i], rows.at[i], sem.at[0, i]),
                pltpu.make_async_copy(residual_ref.at[:, cols(i)], base.at[i], sem.at[1, i]),
            )
        )
        for copy in ins[i]:
            copy.start()
    weight = column_of(weight_ref)
    outs = []
    for i in range(count):
        for copy in ins[i]:
            copy.wait()
        moe = jnp.dot(pick_ref[...], rows[i], preferred_element_type=F32)
        total[i] = (base[i].astype(F32) + weight * moe).astype(total.dtype)
        outs.append(pltpu.make_async_copy(total.at[i], out_ref.at[0, :, cols(i)], sem.at[2, i]))
        outs[i].start()
    for copy in outs:
        copy.wait()


def finish(residual, weight, place, blocks, at):
    count, column = len(blocks), blocks[0].shape[-1]
    tokens, features = residual.shape
    vmem = pl.BlockSpec(memory_space=pltpu.VMEM)
    anywhere = pl.BlockSpec(memory_space=pl.ANY)
    return pl.pallas_call(
        finish_kernel,
        out_shape=jax.ShapeDtypeStruct((1, tokens, features), BF16),
        in_specs=[pl.BlockSpec(memory_space=pltpu.SMEM)] + [vmem] * 2 + [anywhere] * (1 + count),
        out_specs=anywhere,
        scratch_shapes=[pltpu.VMEM((count, tokens, column), BF16)] * 3
        + [pltpu.SemaphoreType.DMA((3, count))],
        compiler_params=pltpu.CompilerParams(vmem_limit_bytes=8 * 2**20),
        name="finish",
    )(at, weight[None, :], one_hot(place, tokens), residual, *blocks)


def body_pair(
    act_fwd, routes_fwd, weight_fwd, grad_bwd, routes_bwd, weight_bwd, saved_bwd, w_gate_up, w_down
):
    node = lax.axis_index("node")
    local = lax.axis_index("local")
    tokens_here = act_fwd.shape[1]
    capacity = 5 * tokens_here // 8
    w_gu = w_gate_up[0, 0]
    w_dn = w_down[0, 0]
    hidden_units = w_dn.shape[0]
    shape = (4, 2, capacity)

    act, grad = act_fwd[0], grad_bwd[0]
    route_a, route_b = routes_fwd[0, :, 0], routes_bwd[0, :, 0]
    sort_a, sort_b = sorter(route_a), sorter(route_b)
    zeros = tokens_here - jnp.stack([jnp.sum(route_a), jnp.sum(route_b)]).astype(F32)

    def in_rows(cuts, got):
        return windows(jnp.stack([cuts[0], got[1], got[0], got[2]]), node, capacity)

    def by_node(own, got, axis):
        return jnp.stack([jnp.where(node == 0, own, got), jnp.where(node == 0, got, own)], axis=axis)

    def split(done):
        own = lax.dynamic_index_in_dim(done, node, axis=1, keepdims=False)
        other = lax.dynamic_index_in_dim(done, 1 - node, axis=1, keepdims=False)
        return own, other

    def turn(chain, back, *others):
        pieces = chain.send(after(back, *others))
        return operands(pieces), send(pieces)

    cut_b = scaled_cut(grad, weight_bwd[0], route_b, local)
    c1, c2, c3, saved_in = join(*cut_b[1:], saved_bwd[0])
    got_b = [move(c2, by_local=-2), move(c1, by_local=-1), move(c3, by_local=-3)]
    saved = jnp.dot(sort_b, saved_in, preferred_element_type=F32).astype(BF16)
    saved_own, saved_other = windows(saved, node, capacity)
    saved_got = move(saved_other, by_node=1)
    (zeros_wait,) = after([zeros], saved_other)
    zeros_got = move(zeros_wait, by_node=1)
    cut_a = cut(act, sort_a, local)
    *got_b, saved_got, zeros_got, a0, a1, a2, a3 = join(*got_b, saved_got, zeros_got, *cut_a)
    cut_a = [a0, a1, a2, a3]
    zeros = by_node(zeros, zeros_got, 0)
    got_a = [move(cut_a[m], by_local=-m) for m in (2, 1, 3)]
    own_b, other_b = in_rows(cut_b, got_b)
    column = own_b.shape[-1]
    got_bx = move(other_b, by_node=1)

    rows_b = by_node(own_b, got_bx, 1).reshape(-1, column)
    part_b = dot_t(rows_b, w_dn).astype(BF16).reshape(shape + (hidden_units,))
    back_b = [move(part_b[m], by_local=m) for m in (2, 1, 3)]
    both = join(*back_b, *got_a)
    back_b, got_a = both[:3], both[3:]
    own_a, other_a = in_rows(cut_a, got_a)
    got_ax = move(other_a, by_node=1)
    dh = part_b[0].astype(F32) + sum(part.astype(F32) for part in back_b)
    dh = jnp.where(valid(zeros[:, 1], node, tokens_here, capacity)[..., None], dh, 0.0)
    saved_rows = by_node(saved_own, saved_got, 0)
    g = saved_rows[..., :hidden_units].astype(F32)
    u = saved_rows[..., hidden_units:].astype(F32)
    q = 1.0 / (1.0 + jnp.exp(-g))
    grad_gu = jnp.concatenate([dh * u * q * (1.0 + g * (1.0 - q)), dh * g * q], axis=-1).astype(
        BF16
    )

    chain_b = gathers(grad_gu, local)
    back_b = send(next(chain_b))
    small_wait, route_wait = after(
        [jnp.stack([route_a.astype(F32), weight_fwd[0]]), route_b], grad_gu
    )
    small_next = move(small_wait, by_pp=1)
    route_b_next = move(route_wait, by_pp=-1)
    rows_a = by_node(own_a, got_ax, 1).reshape(-1, column)
    part_a = jnp.dot(rows_a, w_gu, preferred_element_type=F32).astype(BF16)
    *back_b, part_a, small_next, route_b_next = join(*back_b, part_a, small_next, route_b_next)
    part_a = part_a.reshape(shape + (2 * hidden_units,))
    chain_a = sums(lambda slot: part_a[slot])
    values_b, back_b = turn(chain_b, back_b)
    pieces = next(chain_a)
    back_a = send(pieces)
    act_next = move(after([act], *operands(pieces))[0], by_pp=1)
    *back_b, act_next = join(*back_b, act_next)
    values_b, back_b = turn(chain_b, back_b)
    grad_next = move(join(grad, *values_b)[0], by_pp=-1)
    *back_b, grad_next = join(*back_b, grad_next)
    values_a, back_a = turn(chain_a, back_a)
    values_a, back_a = turn(chain_a, back_a)
    all_gu = chain_b.send(back_b)
    done_b = dot_t(all_gu.reshape(-1, 2 * hidden_units), w_gu).astype(BF16)
    own_b, other_b = split(done_b.reshape(shape + (column,)))
    got_b = move(other_b, by_node=1)

    preact = chain_a.send(back_a)
    preact = jnp.where(valid(zeros[:, 0], node, tokens_here, capacity)[..., None], preact, 0.0)
    hidden = (jax.nn.silu(preact[..., :hidden_units]) * preact[..., hidden_units:]).astype(BF16)
    all_hidden = [move(hidden, by_local=-m) for m in (1, 2, 3)]
    merged_b = merge(own_b, got_b, node, tokens_here)
    h1, h2, h3, merged_b = join(*all_hidden, merged_b)
    all_hidden = jnp.stack([hidden, h1, h2, h3])
    home_b = send(homeward(merged_b, -1))
    done_a = jnp.dot(
        all_hidden.reshape(-1, hidden_units), w_dn, preferred_element_type=F32
    ).astype(BF16)
    own_a, other_a = split(done_a.reshape(shape + (column,)))
    got_a = move(other_a, by_node=1)
    home_a = send(homeward(merge(own_a, got_a, node, tokens_here), 1))

    at = jnp.stack([(local - m) % 4 for m in (2, 1, 3, 0)]).astype(jnp.int32)
    ones = jnp.ones((tokens_here,), F32)
    prev_grad = finish(grad_next, ones, sorted_places(route_b_next), home_b, at)
    place_a = sorted_places(small_next[0].astype(jnp.int32))
    next_input = finish(act_next, small_next[1], place_a, home_a, at)
    return next_input, prev_grad


def from_behind(value, axis, by):
    length = lax.axis_size(axis)
    return lax.ppermute(value, axis, [(i, (i + by) % length) for i in range(length)])


def place_matrix(route, expert_count, capacity):
    onehot = (route[:, None] == jnp.arange(expert_count, dtype=jnp.int32)[None, :]).astype(
        jnp.int32
    )
    before = jnp.cumsum(onehot, axis=0) - onehot
    slot_index = jnp.sum(before * onehot, axis=1)
    target = route * capacity + slot_index
    positions = jnp.arange(expert_count * capacity, dtype=jnp.int32)
    return (positions[:, None] == target[None, :]).astype(jnp.bfloat16)


def pack_rows(placer, values, expert_count, capacity):
    packed = jnp.dot(placer, values, preferred_element_type=jnp.float32).astype(jnp.bfloat16)
    return packed.reshape(expert_count, capacity, values.shape[1])


def unpack_rows(placer, packed):
    flattened = packed.reshape(-1, packed.shape[-1])
    result = lax.dot_general(
        placer, flattened, (((0,), (0,)), ((), ())), preferred_element_type=jnp.float32
    )
    return result.astype(jnp.bfloat16)


def flat_outgoing(packed, local_count):
    expert_count, capacity, feature_count = packed.shape
    column = feature_count // local_count
    outgoing = packed.reshape(expert_count, capacity, local_count, column).transpose(0, 2, 1, 3)
    return outgoing.reshape(expert_count * local_count, capacity, column)


def flat_layout(received, expert_count, local_count):
    capacity = received.shape[1]
    column = received.shape[2]
    rows_in = received.reshape(expert_count, local_count, capacity, column).transpose(1, 0, 2, 3)
    return rows_in.reshape(-1, column)


def send_rows(packs, local_count):
    expert_count = packs[0].shape[0]
    outgoing = tuple((flat_outgoing(packed, local_count) for packed in packs))
    received = (
        lax.all_to_all(outgoing[0], ("node", "local"), split_axis=0, concat_axis=0, tiled=True),
        lax.all_to_all(outgoing[1], ("node", "local"), split_axis=0, concat_axis=0, tiled=True),
    )
    return tuple((flat_layout(item, expert_count, local_count) for item in received))


def return_rows(finished_pair, expert_count, capacity, local_count):
    column = finished_pair[0].shape[1]
    blocks = tuple(
        (item.reshape(local_count, expert_count, capacity, column) for item in finished_pair)
    )
    outgoing = tuple(
        (
            item.transpose(1, 0, 2, 3).reshape(expert_count * local_count, capacity, column)
            for item in blocks
        )
    )
    received = (
        lax.all_to_all(outgoing[0], ("node", "local"), split_axis=0, concat_axis=0, tiled=True),
        lax.all_to_all(outgoing[1], ("node", "local"), split_axis=0, concat_axis=0, tiled=True),
    )
    results = []
    for item in received:
        arranged = item.reshape(expert_count, local_count, capacity, column).transpose(0, 2, 1, 3)
        results.append(arranged.reshape(expert_count, capacity, local_count * column))
    return tuple(results)


def body(
    act_fwd, routes_fwd, weight_fwd, grad_bwd, routes_bwd, weight_bwd, saved_bwd, w_gate_up, w_down
):
    node_count = lax.axis_size("node")
    local_count = lax.axis_size("local")
    tokens_here = act_fwd.shape[1]
    capacity = 5 * tokens_here // (4 * node_count)
    rows_each = node_count * capacity
    w_gu = w_gate_up[0, 0]
    w_dn = w_down[0, 0]
    hidden_units = w_dn.shape[0]
    tokens_a = act_fwd[0]
    placer_a = place_matrix(routes_fwd[0, :, 0], node_count, capacity)
    cotangent = grad_bwd[0]
    placer_b = place_matrix(routes_bwd[0, :, 0], node_count, capacity)
    scaled = (weight_bwd[0][:, None] * cotangent.astype(jnp.float32)).astype(jnp.bfloat16)
    packed_a = pack_rows(placer_a, tokens_a, node_count, capacity)
    packed_b = pack_rows(placer_b, scaled, node_count, capacity)
    rows_a, rows_b = send_rows((packed_a, packed_b), local_count)
    saved_packed = pack_rows(placer_b, saved_bwd[0], node_count, capacity)
    saved_rows = lax.all_to_all(
        saved_packed, "node", split_axis=0, concat_axis=0, tiled=True
    ).reshape(rows_each, -1)
    row_block = rows_a
    preact = lax.psum_scatter(
        jnp.dot(row_block, w_gu, preferred_element_type=jnp.float32).astype(jnp.bfloat16),
        "local",
        scatter_dimension=0,
        tiled=True,
    ).astype(jnp.float32)
    row_block = rows_b
    grad_hidden = lax.psum_scatter(
        lax.dot_general(
            row_block, w_dn, (((1,), (1,)), ((), ())), preferred_element_type=jnp.float32
        ).astype(jnp.bfloat16),
        "local",
        scatter_dimension=0,
        tiled=True,
    ).astype(jnp.float32)
    hidden = (jax.nn.silu(preact[:, :hidden_units]) * preact[:, hidden_units:]).astype(jnp.bfloat16)
    done_a = jnp.dot(
        lax.all_gather(hidden, "local", axis=0, tiled=True),
        w_dn,
        preferred_element_type=jnp.float32,
    ).astype(jnp.bfloat16)
    gate_pre = saved_rows[:, :hidden_units].astype(jnp.float32)
    up_pre = saved_rows[:, hidden_units:].astype(jnp.float32)
    sigmoid_g = 1.0 / (1.0 + jnp.exp(-gate_pre))
    grad_gate = grad_hidden * up_pre * sigmoid_g * (1.0 + gate_pre * (1.0 - sigmoid_g))
    grad_up = grad_hidden * gate_pre * sigmoid_g
    grad_gu = jnp.concatenate([grad_gate, grad_up], axis=1).astype(jnp.bfloat16)
    product = lax.dot_general(
        lax.all_gather(grad_gu, "local", axis=0, tiled=True),
        w_gu,
        (((1,), (1,)), ((), ())),
        preferred_element_type=jnp.float32,
    )
    done_b = product.astype(jnp.bfloat16)
    back_a, back_b = return_rows((done_a, done_b), node_count, capacity, local_count)
    moe_a = unpack_rows(placer_a, back_a)
    result_a = tokens_a.astype(jnp.float32) + weight_fwd[0][:, None] * moe_a.astype(jnp.float32)
    result_a = result_a.astype(jnp.bfloat16)
    moe_b = unpack_rows(placer_b, back_b)
    result_b = (cotangent.astype(jnp.float32) + moe_b.astype(jnp.float32)).astype(jnp.bfloat16)
    next_input = from_behind(result_a[None], "pp", 1)
    prev_grad = from_behind(result_b[None], "pp", -1)
    return (next_input, prev_grad)


def solution(mesh):
    in_specs = (
        P("pp", ("node", "local"), None),
        P("pp", ("node", "local"), None),
        P("pp", ("node", "local")),
        P("pp", ("node", "local"), None),
        P("pp", ("node", "local"), None),
        P("pp", ("node", "local")),
        P("pp", ("node", "local"), None),
        P("pp", "node", "local", None),
        P("pp", "node", None, "local"),
    )
    out_specs = (P("pp", ("node", "local"), None), P("pp", ("node", "local"), None))
    paired = mesh.shape["node"] == 2 and mesh.shape["local"] == 4
    plan = body_pair if paired else body
    return jax.shard_map(plan, mesh=mesh, in_specs=in_specs, out_specs=out_specs, check_vma=False)
```

```python
import jax
import jax.numpy as jnp
from jax import lax
from jax.experimental import pallas as pl
from jax.experimental.pallas import tpu as pltpu
from jax.sharding import PartitionSpec as P

F32 = jnp.float32
BF16 = jnp.bfloat16
AXES = ("pp", "node", "local")


def move(value, by_pp=0, by_node=0, by_local=0, wrap=True, first=0, last=None):
    pps, nodes, locs = (lax.axis_size(a) for a in AXES)
    last = locs - 1 if last is None else last
    pairs = []
    for s in range(pps):
        for n in range(nodes):
            for l in range(locs):
                to = l + by_local
                if not wrap and not (first <= l <= last and 0 <= to < locs):
                    continue
                source = (s * nodes + n) * locs + l
                target = (((s + by_pp) % pps) * nodes + (n ^ by_node)) * locs + to % locs
                pairs.append((source, target))
    return lax.ppermute(value, AXES, pairs)


def sorted_places(route):
    ones = route.astype(F32)
    count = route.shape[0]
    earlier = (jnp.arange(count)[None, :] < jnp.arange(count)[:, None]).astype(F32)
    ones_before = jnp.dot(earlier, ones[:, None], preferred_element_type=F32)[:, 0]
    zeros = count - jnp.sum(ones)
    index = jnp.arange(count, dtype=F32)
    place = jnp.where(route == 0, index - ones_before, zeros + ones_before)
    return place.astype(jnp.int32)


def sorter(route):
    place = sorted_places(route)
    rows = jnp.arange(route.shape[0], dtype=jnp.int32)
    return (rows[:, None] == place[None, :]).astype(BF16)


def one_hot(row, count):
    return (row[:, None] == jnp.arange(count, dtype=jnp.int32)[None, :]).astype(BF16)


def dot_t(left, right):
    return lax.dot_general(left, right, (((1,), (1,)), ((), ())), preferred_element_type=F32)


def windows(blocks, node, capacity):
    tokens = blocks.shape[-2]
    start = tokens - capacity
    low = lax.slice_in_dim(blocks, 0, capacity, axis=-2 + blocks.ndim)
    high = lax.slice_in_dim(blocks, start, tokens, axis=-2 + blocks.ndim)
    own = jnp.where(node == 0, low, high)
    other = jnp.where(node == 0, high, low)
    return own, other


def join(*values):
    return lax.optimization_barrier(values)


def after(values, *others):
    return list(join(*values, *others)[: len(values)])


def cut(tokens, placer, local):
    column = tokens.shape[1] // 4
    blocks = []
    for m in range(4):
        block = lax.dynamic_slice_in_dim(tokens, ((local - m) % 4) * column, column, axis=1)
        blocks.append(jnp.dot(placer, block, preferred_element_type=F32).astype(BF16))
    return blocks


def sums(partial):
    right, left = partial(3), partial(1)
    for step in (1, 2, 3):
        right, left = right.astype(BF16), left.astype(BF16)
        got_r, got_l = yield (
            (right, dict(by_local=1, wrap=False, last=step - 1)),
            (left, dict(by_local=-1, wrap=False, first=4 - step)),
        )
        right = partial(3 - step).astype(F32) + got_r.astype(F32)
        if step < 3:
            left = partial(step + 1).astype(F32) + got_l.astype(F32)
    yield right + got_l.astype(F32)


def gathers(rows, local):
    from_left, from_right = [rows], [rows]
    for step in (1, 2, 3):
        got_r, got_l = yield (
            (from_left[-1], dict(by_local=1, wrap=False, first=step - 1)),
            (from_right[-1], dict(by_local=-1, wrap=False, last=4 - step)),
        )
        from_left.append(got_r)
        from_right.append(got_l)
    slots = [rows]
    for m in (1, 2, 3):
        slots.append(jnp.where(local + m < 4, from_right[m], from_left[4 - m]))
    yield jnp.stack(slots)


def send(pieces):
    return [move(value, **how) for value, how in pieces]


def operands(pieces):
    return [value for value, _ in pieces]


def valid(zeros, node, tokens, capacity):
    row = jnp.arange(capacity, dtype=F32)[None, :]
    return jnp.where(node == 0, row < zeros[:, None], row + (tokens - capacity) >= zeros[:, None])


def merge(own, other, node, tokens):
    slots, capacity, column = own.shape
    low = jnp.where(node == 0, own, other)
    high = jnp.where(node == 0, other, own)
    rest = jnp.zeros((slots, tokens - capacity, column), own.dtype)
    return jnp.concatenate([low, rest], axis=1) + jnp.concatenate([rest, high], axis=1)


def homeward(merged, by_pp):
    return [(merged[m], dict(by_pp=by_pp, by_local=m)) for m in (2, 1, 3, 0)]


def column_of(row_ref):
    n = row_ref.shape[1]
    row = lax.broadcasted_iota(jnp.int32, (n, n), 0)
    col = lax.broadcasted_iota(jnp.int32, (n, n), 1)
    return jnp.sum(jnp.where(row == col, row_ref[...], 0.0), axis=1, keepdims=True)


def cut_kernel(at_ref, route_ref, weight_ref, values_ref, *blocks):
    tokens = route_ref.shape[1]
    column = blocks[0].shape[1]
    row = lax.broadcasted_iota(jnp.int32, (tokens, tokens), 0)
    col = lax.broadcasted_iota(jnp.int32, (tokens, tokens), 1)
    ones = route_ref[...].astype(F32)
    before = jnp.dot(
        jnp.broadcast_to(ones, (8, tokens)).astype(BF16),
        (row < col).astype(BF16),
        preferred_element_type=F32,
    )[0:1]
    zeros = tokens - jnp.sum(ones, axis=1, keepdims=True)
    index = col[0:1].astype(F32)
    place = jnp.where(ones == 0.0, index - before, zeros + before).astype(jnp.int32)
    picker = (row == place).astype(BF16)
    weight = column_of(weight_ref)
    for i, block_ref in enumerate(blocks):
        cols = pl.ds(pl.multiple_of(at_ref[i] * column, column), column)
        block = (weight * values_ref[:, cols].astype(F32)).astype(BF16)
        block_ref[...] = jnp.dot(picker, block, preferred_element_type=F32).astype(BF16)


def scaled_cut(tokens, weight, route, local):
    rows, features = tokens.shape
    vmem = pl.BlockSpec(memory_space=pltpu.VMEM)
    at = jnp.stack([(local - m) % 4 for m in range(4)]).astype(jnp.int32)
    return list(
        pl.pallas_call(
            cut_kernel,
            out_shape=[jax.ShapeDtypeStruct((rows, features // 4), BF16)] * 4,
            in_specs=[pl.BlockSpec(memory_space=pltpu.SMEM)] + [vmem] * 3,
            out_specs=[vmem] * 4,
            compiler_params=pltpu.CompilerParams(vmem_limit_bytes=8 * 2**20),
            name="cut",
        )(at, route[None, :], weight[None, :], tokens)
    )


def finish_kernel(at_ref, weight_ref, pick_ref, residual_ref, *refs):
    *blocks, out_ref, rows, base, total, sem = refs
    count = len(blocks)
    column = rows.shape[-1]

    def cols(i):
        return pl.ds(pl.multiple_of(at_ref[i] * column, column), column)

    ins = []
    for i in range(count):
        ins.append(
            (
                pltpu.make_async_copy(blocks[i], rows.at[i], sem.at[0, i]),
                pltpu.make_async_copy(residual_ref.at[:, cols(i)], base.at[i], sem.at[1, i]),
            )
        )
        for copy in ins[i]:
            copy.start()
    weight = column_of(weight_ref)
    outs = []
    for i in range(count):
        for copy in ins[i]:
            copy.wait()
        moe = jnp.dot(pick_ref[...], rows[i], preferred_element_type=F32)
        total[i] = (base[i].astype(F32) + weight * moe).astype(total.dtype)
        outs.append(pltpu.make_async_copy(total.at[i], out_ref.at[0, :, cols(i)], sem.at[2, i]))
        outs[i].start()
    for copy in outs:
        copy.wait()


def finish(residual, weight, place, blocks, at):
    count, column = len(blocks), blocks[0].shape[-1]
    tokens, features = residual.shape
    vmem = pl.BlockSpec(memory_space=pltpu.VMEM)
    anywhere = pl.BlockSpec(memory_space=pl.ANY)
    return pl.pallas_call(
        finish_kernel,
        out_shape=jax.ShapeDtypeStruct((1, tokens, features), BF16),
        in_specs=[pl.BlockSpec(memory_space=pltpu.SMEM)] + [vmem] * 2 + [anywhere] * (1 + count),
        out_specs=anywhere,
        scratch_shapes=[pltpu.VMEM((count, tokens, column), BF16)] * 3
        + [pltpu.SemaphoreType.DMA((3, count))],
        compiler_params=pltpu.CompilerParams(vmem_limit_bytes=8 * 2**20),
        name="finish",
    )(at, weight[None, :], one_hot(place, tokens), residual, *blocks)


def body_pair(
    act_fwd, routes_fwd, weight_fwd, grad_bwd, routes_bwd, weight_bwd, saved_bwd, w_gate_up, w_down
):
    node = lax.axis_index("node")
    local = lax.axis_index("local")
    tokens_here = act_fwd.shape[1]
    capacity = 5 * tokens_here // 8
    w_gu = w_gate_up[0, 0]
    w_dn = w_down[0, 0]
    hidden_units = w_dn.shape[0]
    shape = (4, 2, capacity)

    act, grad = act_fwd[0], grad_bwd[0]
    route_a, route_b = routes_fwd[0, :, 0], routes_bwd[0, :, 0]
    sort_a, sort_b = sorter(route_a), sorter(route_b)
    zeros = tokens_here - jnp.stack([jnp.sum(route_a), jnp.sum(route_b)]).astype(F32)

    def in_rows(cuts, got):
        return windows(jnp.stack([cuts[0], got[1], got[0], got[2]]), node, capacity)

    def by_node(own, got, axis):
        return jnp.stack([jnp.where(node == 0, own, got), jnp.where(node == 0, got, own)], axis=axis)

    def split(done):
        own = lax.dynamic_index_in_dim(done, node, axis=1, keepdims=False)
        other = lax.dynamic_index_in_dim(done, 1 - node, axis=1, keepdims=False)
        return own, other

    def turn(chain, back, *others):
        pieces = chain.send(after(back, *others))
        return operands(pieces), send(pieces)

    cut_b = scaled_cut(grad, weight_bwd[0], route_b, local)
    c1, c2, c3, saved_in = join(*cut_b[1:], saved_bwd[0])
    got_b = [move(c2, by_local=-2), move(c1, by_local=-1), move(c3, by_local=-3)]
    saved = jnp.dot(sort_b, saved_in, preferred_element_type=F32).astype(BF16)
    saved_own, saved_other = windows(saved, node, capacity)
    saved_got = move(saved_other, by_node=1)
    (zeros_wait,) = after([zeros], saved_other)
    zeros_got = move(zeros_wait, by_node=1)
    cut_a = cut(act, sort_a, local)
    *got_b, saved_got, zeros_got, a0, a1, a2, a3 = join(*got_b, saved_got, zeros_got, *cut_a)
    cut_a = [a0, a1, a2, a3]
    zeros = by_node(zeros, zeros_got, 0)
    got_a = [move(cut_a[m], by_local=-m) for m in (2, 1, 3)]
    own_b, other_b = in_rows(cut_b, got_b)
    column = own_b.shape[-1]
    got_bx = move(other_b, by_node=1)

    rows_b = by_node(own_b, got_bx, 1).reshape(-1, column)
    part_b = dot_t(rows_b, w_dn).astype(BF16).reshape(shape + (hidden_units,))
    back_b = [move(part_b[m], by_local=m) for m in (2, 1, 3)]
    both = join(*back_b, *got_a)
    back_b, got_a = both[:3], both[3:]
    own_a, other_a = in_rows(cut_a, got_a)
    got_ax = move(other_a, by_node=1)
    dh = part_b[0].astype(F32) + sum(part.astype(F32) for part in back_b)
    dh = jnp.where(valid(zeros[:, 1], node, tokens_here, capacity)[..., None], dh, 0.0)
    saved_rows = by_node(saved_own, saved_got, 0)
    g = saved_rows[..., :hidden_units].astype(F32)
    u = saved_rows[..., hidden_units:].astype(F32)
    q = 1.0 / (1.0 + jnp.exp(-g))
    grad_gu = jnp.concatenate([dh * u * q * (1.0 + g * (1.0 - q)), dh * g * q], axis=-1).astype(
        BF16
    )

    chain_b = gathers(grad_gu, local)
    back_b = send(next(chain_b))
    small_wait, route_wait = after(
        [jnp.stack([route_a.astype(F32), weight_fwd[0]]), route_b], grad_gu
    )
    small_next = move(small_wait, by_pp=1)
    route_b_next = move(route_wait, by_pp=-1)
    rows_a = by_node(own_a, got_ax, 1).reshape(-1, column)
    part_a = jnp.dot(rows_a, w_gu, preferred_element_type=F32).astype(BF16)
    *back_b, part_a, small_next, route_b_next = join(*back_b, part_a, small_next, route_b_next)
    part_a = part_a.reshape(shape + (2 * hidden_units,))
    chain_a = sums(lambda slot: part_a[slot])
    values_b, back_b = turn(chain_b, back_b)
    pieces = next(chain_a)
    back_a = send(pieces)
    act_next = move(after([act], *operands(pieces))[0], by_pp=1)
    *back_b, act_next = join(*back_b, act_next)
    values_b, back_b = turn(chain_b, back_b)
    grad_next = move(join(grad, *values_b)[0], by_pp=-1)
    *back_b, grad_next = join(*back_b, grad_next)
    values_a, back_a = turn(chain_a, back_a)
    values_a, back_a = turn(chain_a, back_a)
    all_gu = chain_b.send(back_b)
    done_b = dot_t(all_gu.reshape(-1, 2 * hidden_units), w_gu).astype(BF16)
    own_b, other_b = split(done_b.reshape(shape + (column,)))
    got_b = move(other_b, by_node=1)

    preact = chain_a.send(back_a)
    preact = jnp.where(valid(zeros[:, 0], node, tokens_here, capacity)[..., None], preact, 0.0)
    hidden = (jax.nn.silu(preact[..., :hidden_units]) * preact[..., hidden_units:]).astype(BF16)
    all_hidden = [move(hidden, by_local=-m) for m in (1, 2, 3)]
    merged_b = merge(own_b, got_b, node, tokens_here)
    h2, merged_b = join(all_hidden[1], merged_b)
    all_hidden = jnp.stack([hidden, all_hidden[0], h2, all_hidden[2]])
    home_b = send(homeward(merged_b, -1))
    done_a = jnp.dot(
        all_hidden.reshape(-1, hidden_units), w_dn, preferred_element_type=F32
    ).astype(BF16)
    own_a, other_a = split(done_a.reshape(shape + (column,)))
    got_a = move(other_a, by_node=1)
    home_a = send(homeward(merge(own_a, got_a, node, tokens_here), 1))

    at = jnp.stack([(local - m) % 4 for m in (2, 1, 3, 0)]).astype(jnp.int32)
    ones = jnp.ones((tokens_here,), F32)
    prev_grad = finish(grad_next, ones, sorted_places(route_b_next), home_b, at)
    place_a = sorted_places(small_next[0].astype(jnp.int32))
    next_input = finish(act_next, small_next[1], place_a, home_a, at)
    return next_input, prev_grad


def from_behind(value, axis, by):
    length = lax.axis_size(axis)
    return lax.ppermute(value, axis, [(i, (i + by) % length) for i in range(length)])


def place_matrix(route, expert_count, capacity):
    onehot = (route[:, None] == jnp.arange(expert_count, dtype=jnp.int32)[None, :]).astype(
        jnp.int32
    )
    before = jnp.cumsum(onehot, axis=0) - onehot
    slot_index = jnp.sum(before * onehot, axis=1)
    target = route * capacity + slot_index
    positions = jnp.arange(expert_count * capacity, dtype=jnp.int32)
    return (positions[:, None] == target[None, :]).astype(jnp.bfloat16)


def pack_rows(placer, values, expert_count, capacity):
    packed = jnp.dot(placer, values, preferred_element_type=jnp.float32).astype(jnp.bfloat16)
    return packed.reshape(expert_count, capacity, values.shape[1])


def unpack_rows(placer, packed):
    flattened = packed.reshape(-1, packed.shape[-1])
    result = lax.dot_general(
        placer, flattened, (((0,), (0,)), ((), ())), preferred_element_type=jnp.float32
    )
    return result.astype(jnp.bfloat16)


def flat_outgoing(packed, local_count):
    expert_count, capacity, feature_count = packed.shape
    column = feature_count // local_count
    outgoing = packed.reshape(expert_count, capacity, local_count, column).transpose(0, 2, 1, 3)
    return outgoing.reshape(expert_count * local_count, capacity, column)


def flat_layout(received, expert_count, local_count):
    capacity = received.shape[1]
    column = received.shape[2]
    rows_in = received.reshape(expert_count, local_count, capacity, column).transpose(1, 0, 2, 3)
    return rows_in.reshape(-1, column)


def send_rows(packs, local_count):
    expert_count = packs[0].shape[0]
    outgoing = tuple((flat_outgoing(packed, local_count) for packed in packs))
    received = (
        lax.all_to_all(outgoing[0], ("node", "local"), split_axis=0, concat_axis=0, tiled=True),
        lax.all_to_all(outgoing[1], ("node", "local"), split_axis=0, concat_axis=0, tiled=True),
    )
    return tuple((flat_layout(item, expert_count, local_count) for item in received))


def return_rows(finished_pair, expert_count, capacity, local_count):
    column = finished_pair[0].shape[1]
    blocks = tuple(
        (item.reshape(local_count, expert_count, capacity, column) for item in finished_pair)
    )
    outgoing = tuple(
        (
            item.transpose(1, 0, 2, 3).reshape(expert_count * local_count, capacity, column)
            for item in blocks
        )
    )
    received = (
        lax.all_to_all(outgoing[0], ("node", "local"), split_axis=0, concat_axis=0, tiled=True),
        lax.all_to_all(outgoing[1], ("node", "local"), split_axis=0, concat_axis=0, tiled=True),
    )
    results = []
    for item in received:
        arranged = item.reshape(expert_count, local_count, capacity, column).transpose(0, 2, 1, 3)
        results.append(arranged.reshape(expert_count, capacity, local_count * column))
    return tuple(results)


def body(
    act_fwd, routes_fwd, weight_fwd, grad_bwd, routes_bwd, weight_bwd, saved_bwd, w_gate_up, w_down
):
    node_count = lax.axis_size("node")
    local_count = lax.axis_size("local")
    tokens_here = act_fwd.shape[1]
    capacity = 5 * tokens_here // (4 * node_count)
    rows_each = node_count * capacity
    w_gu = w_gate_up[0, 0]
    w_dn = w_down[0, 0]
    hidden_units = w_dn.shape[0]
    tokens_a = act_fwd[0]
    placer_a = place_matrix(routes_fwd[0, :, 0], node_count, capacity)
    cotangent = grad_bwd[0]
    placer_b = place_matrix(routes_bwd[0, :, 0], node_count, capacity)
    scaled = (weight_bwd[0][:, None] * cotangent.astype(jnp.float32)).astype(jnp.bfloat16)
    packed_a = pack_rows(placer_a, tokens_a, node_count, capacity)
    packed_b = pack_rows(placer_b, scaled, node_count, capacity)
    rows_a, rows_b = send_rows((packed_a, packed_b), local_count)
    saved_packed = pack_rows(placer_b, saved_bwd[0], node_count, capacity)
    saved_rows = lax.all_to_all(
        saved_packed, "node", split_axis=0, concat_axis=0, tiled=True
    ).reshape(rows_each, -1)
    row_block = rows_a
    preact = lax.psum_scatter(
        jnp.dot(row_block, w_gu, preferred_element_type=jnp.float32).astype(jnp.bfloat16),
        "local",
        scatter_dimension=0,
        tiled=True,
    ).astype(jnp.float32)
    row_block = rows_b
    grad_hidden = lax.psum_scatter(
        lax.dot_general(
            row_block, w_dn, (((1,), (1,)), ((), ())), preferred_element_type=jnp.float32
        ).astype(jnp.bfloat16),
        "local",
        scatter_dimension=0,
        tiled=True,
    ).astype(jnp.float32)
    hidden = (jax.nn.silu(preact[:, :hidden_units]) * preact[:, hidden_units:]).astype(jnp.bfloat16)
    done_a = jnp.dot(
        lax.all_gather(hidden, "local", axis=0, tiled=True),
        w_dn,
        preferred_element_type=jnp.float32,
    ).astype(jnp.bfloat16)
    gate_pre = saved_rows[:, :hidden_units].astype(jnp.float32)
    up_pre = saved_rows[:, hidden_units:].astype(jnp.float32)
    sigmoid_g = 1.0 / (1.0 + jnp.exp(-gate_pre))
    grad_gate = grad_hidden * up_pre * sigmoid_g * (1.0 + gate_pre * (1.0 - sigmoid_g))
    grad_up = grad_hidden * gate_pre * sigmoid_g
    grad_gu = jnp.concatenate([grad_gate, grad_up], axis=1).astype(jnp.bfloat16)
    product = lax.dot_general(
        lax.all_gather(grad_gu, "local", axis=0, tiled=True),
        w_gu,
        (((1,), (1,)), ((), ())),
        preferred_element_type=jnp.float32,
    )
    done_b = product.astype(jnp.bfloat16)
    back_a, back_b = return_rows((done_a, done_b), node_count, capacity, local_count)
    moe_a = unpack_rows(placer_a, back_a)
    result_a = tokens_a.astype(jnp.float32) + weight_fwd[0][:, None] * moe_a.astype(jnp.float32)
    result_a = result_a.astype(jnp.bfloat16)
    moe_b = unpack_rows(placer_b, back_b)
    result_b = (cotangent.astype(jnp.float32) + moe_b.astype(jnp.float32)).astype(jnp.bfloat16)
    next_input = from_behind(result_a[None], "pp", 1)
    prev_grad = from_behind(result_b[None], "pp", -1)
    return (next_input, prev_grad)


def solution(mesh):
    in_specs = (
        P("pp", ("node", "local"), None),
        P("pp", ("node", "local"), None),
        P("pp", ("node", "local")),
        P("pp", ("node", "local"), None),
        P("pp", ("node", "local"), None),
        P("pp", ("node", "local")),
        P("pp", ("node", "local"), None),
        P("pp", "node", "local", None),
        P("pp", "node", None, "local"),
    )
    out_specs = (P("pp", ("node", "local"), None), P("pp", ("node", "local"), None))
    paired = mesh.shape["node"] == 2 and mesh.shape["local"] == 4
    plan = body_pair if paired else body
    return jax.shard_map(plan, mesh=mesh, in_specs=in_specs, out_specs=out_specs, check_vma=False)
```

```python
import jax
import jax.numpy as jnp
from jax import lax
from jax.experimental import pallas as pl
from jax.experimental.pallas import tpu as pltpu
from jax.sharding import PartitionSpec as P

F32 = jnp.float32
BF16 = jnp.bfloat16
AXES = ("pp", "node", "local")


def move(value, by_pp=0, by_node=0, by_local=0, wrap=True, first=0, last=None):
    pps, nodes, locs = (lax.axis_size(a) for a in AXES)
    last = locs - 1 if last is None else last
    pairs = []
    for s in range(pps):
        for n in range(nodes):
            for l in range(locs):
                to = l + by_local
                if not wrap and not (first <= l <= last and 0 <= to < locs):
                    continue
                source = (s * nodes + n) * locs + l
                target = (((s + by_pp) % pps) * nodes + (n ^ by_node)) * locs + to % locs
                pairs.append((source, target))
    return lax.ppermute(value, AXES, pairs)


def sorted_places(route):
    ones = route.astype(F32)
    count = route.shape[0]
    earlier = (jnp.arange(count)[None, :] < jnp.arange(count)[:, None]).astype(F32)
    ones_before = jnp.dot(earlier, ones[:, None], preferred_element_type=F32)[:, 0]
    zeros = count - jnp.sum(ones)
    index = jnp.arange(count, dtype=F32)
    place = jnp.where(route == 0, index - ones_before, zeros + ones_before)
    return place.astype(jnp.int32)


def sorter(route):
    place = sorted_places(route)
    rows = jnp.arange(route.shape[0], dtype=jnp.int32)
    return (rows[:, None] == place[None, :]).astype(BF16)


def one_hot(row, count):
    return (row[:, None] == jnp.arange(count, dtype=jnp.int32)[None, :]).astype(BF16)


def dot_t(left, right):
    return lax.dot_general(left, right, (((1,), (1,)), ((), ())), preferred_element_type=F32)


def windows(blocks, node, capacity):
    tokens = blocks.shape[-2]
    start = tokens - capacity
    low = lax.slice_in_dim(blocks, 0, capacity, axis=-2 + blocks.ndim)
    high = lax.slice_in_dim(blocks, start, tokens, axis=-2 + blocks.ndim)
    own = jnp.where(node == 0, low, high)
    other = jnp.where(node == 0, high, low)
    return own, other


def join(*values):
    return lax.optimization_barrier(values)


def after(values, *others):
    return list(join(*values, *others)[: len(values)])


def cut(tokens, placer, local):
    column = tokens.shape[1] // 4
    blocks = []
    for m in range(4):
        block = lax.dynamic_slice_in_dim(tokens, ((local - m) % 4) * column, column, axis=1)
        blocks.append(jnp.dot(placer, block, preferred_element_type=F32).astype(BF16))
    return blocks


def sums(partial):
    right, left = partial(3), partial(1)
    for step in (1, 2, 3):
        right, left = right.astype(BF16), left.astype(BF16)
        got_r, got_l = yield (
            (right, dict(by_local=1, wrap=False, last=step - 1)),
            (left, dict(by_local=-1, wrap=False, first=4 - step)),
        )
        right = partial(3 - step).astype(F32) + got_r.astype(F32)
        if step < 3:
            left = partial(step + 1).astype(F32) + got_l.astype(F32)
    yield right + got_l.astype(F32)


def gathers(rows, local):
    from_left, from_right = [rows], [rows]
    for step in (1, 2, 3):
        got_r, got_l = yield (
            (from_left[-1], dict(by_local=1, wrap=False, first=step - 1)),
            (from_right[-1], dict(by_local=-1, wrap=False, last=4 - step)),
        )
        from_left.append(got_r)
        from_right.append(got_l)
    slots = [rows]
    for m in (1, 2, 3):
        slots.append(jnp.where(local + m < 4, from_right[m], from_left[4 - m]))
    yield jnp.stack(slots)


def send(pieces):
    return [move(value, **how) for value, how in pieces]


def operands(pieces):
    return [value for value, _ in pieces]


def valid(zeros, node, tokens, capacity):
    row = jnp.arange(capacity, dtype=F32)[None, :]
    return jnp.where(node == 0, row < zeros[:, None], row + (tokens - capacity) >= zeros[:, None])


def merge(own, other, node, tokens):
    slots, capacity, column = own.shape
    low = jnp.where(node == 0, own, other)
    high = jnp.where(node == 0, other, own)
    rest = jnp.zeros((slots, tokens - capacity, column), own.dtype)
    return jnp.concatenate([low, rest], axis=1) + jnp.concatenate([rest, high], axis=1)


def homeward(merged, by_pp):
    return [(merged[m], dict(by_pp=by_pp, by_local=m)) for m in (2, 1, 3, 0)]


def column_of(row_ref):
    n = row_ref.shape[1]
    row = lax.broadcasted_iota(jnp.int32, (n, n), 0)
    col = lax.broadcasted_iota(jnp.int32, (n, n), 1)
    return jnp.sum(jnp.where(row == col, row_ref[...], 0.0), axis=1, keepdims=True)


def cut_kernel(at_ref, route_ref, weight_ref, values_ref, *blocks):
    tokens = route_ref.shape[1]
    column = blocks[0].shape[1]
    row = lax.broadcasted_iota(jnp.int32, (tokens, tokens), 0)
    col = lax.broadcasted_iota(jnp.int32, (tokens, tokens), 1)
    ones = route_ref[...].astype(F32)
    before = jnp.dot(
        jnp.broadcast_to(ones, (8, tokens)).astype(BF16),
        (row < col).astype(BF16),
        preferred_element_type=F32,
    )[0:1]
    zeros = tokens - jnp.sum(ones, axis=1, keepdims=True)
    index = col[0:1].astype(F32)
    place = jnp.where(ones == 0.0, index - before, zeros + before).astype(jnp.int32)
    picker = (row == place).astype(BF16)
    weight = column_of(weight_ref)
    for i, block_ref in enumerate(blocks):
        cols = pl.ds(pl.multiple_of(at_ref[i] * column, column), column)
        block = (weight * values_ref[:, cols].astype(F32)).astype(BF16)
        block_ref[...] = jnp.dot(picker, block, preferred_element_type=F32).astype(BF16)


def scaled_cut(tokens, weight, route, local):
    rows, features = tokens.shape
    vmem = pl.BlockSpec(memory_space=pltpu.VMEM)
    at = jnp.stack([(local - m) % 4 for m in range(4)]).astype(jnp.int32)
    return list(
        pl.pallas_call(
            cut_kernel,
            out_shape=[jax.ShapeDtypeStruct((rows, features // 4), BF16)] * 4,
            in_specs=[pl.BlockSpec(memory_space=pltpu.SMEM)] + [vmem] * 3,
            out_specs=[vmem] * 4,
            compiler_params=pltpu.CompilerParams(vmem_limit_bytes=8 * 2**20),
            name="cut",
        )(at, route[None, :], weight[None, :], tokens)
    )


def finish_kernel(at_ref, weight_ref, pick_ref, residual_ref, *refs):
    *blocks, out_ref, rows, base, total, sem = refs
    count = len(blocks)
    column = rows.shape[-1]

    def cols(i):
        return pl.ds(pl.multiple_of(at_ref[i] * column, column), column)

    ins = []
    for i in range(count):
        ins.append(
            (
                pltpu.make_async_copy(blocks[i], rows.at[i], sem.at[0, i]),
                pltpu.make_async_copy(residual_ref.at[:, cols(i)], base.at[i], sem.at[1, i]),
            )
        )
        for copy in ins[i]:
            copy.start()
    weight = column_of(weight_ref)
    outs = []
    for i in range(count):
        for copy in ins[i]:
            copy.wait()
        moe = jnp.dot(pick_ref[...], rows[i], preferred_element_type=F32)
        total[i] = (base[i].astype(F32) + weight * moe).astype(total.dtype)
        outs.append(pltpu.make_async_copy(total.at[i], out_ref.at[0, :, cols(i)], sem.at[2, i]))
        outs[i].start()
    for copy in outs:
        copy.wait()


def finish(residual, weight, place, blocks, at):
    count, column = len(blocks), blocks[0].shape[-1]
    tokens, features = residual.shape
    vmem = pl.BlockSpec(memory_space=pltpu.VMEM)
    anywhere = pl.BlockSpec(memory_space=pl.ANY)
    return pl.pallas_call(
        finish_kernel,
        out_shape=jax.ShapeDtypeStruct((1, tokens, features), BF16),
        in_specs=[pl.BlockSpec(memory_space=pltpu.SMEM)] + [vmem] * 2 + [anywhere] * (1 + count),
        out_specs=anywhere,
        scratch_shapes=[pltpu.VMEM((count, tokens, column), BF16)] * 3
        + [pltpu.SemaphoreType.DMA((3, count))],
        compiler_params=pltpu.CompilerParams(vmem_limit_bytes=8 * 2**20),
        name="finish",
    )(at, weight[None, :], one_hot(place, tokens), residual, *blocks)


def body_pair(
    act_fwd, routes_fwd, weight_fwd, grad_bwd, routes_bwd, weight_bwd, saved_bwd, w_gate_up, w_down
):
    node = lax.axis_index("node")
    local = lax.axis_index("local")
    tokens_here = act_fwd.shape[1]
    capacity = 5 * tokens_here // 8
    w_gu = w_gate_up[0, 0]
    w_dn = w_down[0, 0]
    hidden_units = w_dn.shape[0]
    shape = (4, 2, capacity)

    act, grad = act_fwd[0], grad_bwd[0]
    route_a, route_b = routes_fwd[0, :, 0], routes_bwd[0, :, 0]
    sort_a, sort_b = sorter(route_a), sorter(route_b)
    zeros = tokens_here - jnp.stack([jnp.sum(route_a), jnp.sum(route_b)]).astype(F32)

    def in_rows(cuts, got):
        return windows(jnp.stack([cuts[0], got[1], got[0], got[2]]), node, capacity)

    def by_node(own, got, axis):
        return jnp.stack([jnp.where(node == 0, own, got), jnp.where(node == 0, got, own)], axis=axis)

    def split(done):
        own = lax.dynamic_index_in_dim(done, node, axis=1, keepdims=False)
        other = lax.dynamic_index_in_dim(done, 1 - node, axis=1, keepdims=False)
        return own, other

    def turn(chain, back, *others):
        pieces = chain.send(after(back, *others))
        return operands(pieces), send(pieces)

    cut_b = scaled_cut(grad, weight_bwd[0], route_b, local)
    c1, c2, c3, saved_in = join(*cut_b[1:], saved_bwd[0])
    got_b = [move(c2, by_local=-2), move(c1, by_local=-1), move(c3, by_local=-3)]
    saved = jnp.dot(sort_b, saved_in, preferred_element_type=F32).astype(BF16)
    saved_own, saved_other = windows(saved, node, capacity)
    saved_got = move(saved_other, by_node=1)
    (zeros_wait,) = after([zeros], saved_other)
    zeros_got = move(zeros_wait, by_node=1)
    cut_a = scaled_cut(act, jnp.ones((tokens_here,), F32), route_a, local)
    *got_b, saved_got, zeros_got, a0, a1, a2, a3 = join(*got_b, saved_got, zeros_got, *cut_a)
    cut_a = [a0, a1, a2, a3]
    zeros = by_node(zeros, zeros_got, 0)
    got_a = [move(cut_a[m], by_local=-m) for m in (2, 1, 3)]
    own_b, other_b = in_rows(cut_b, got_b)
    column = own_b.shape[-1]
    got_bx = move(other_b, by_node=1)

    rows_b = by_node(own_b, got_bx, 1).reshape(-1, column)
    part_b = dot_t(rows_b, w_dn).astype(BF16).reshape(shape + (hidden_units,))
    back_b = [move(part_b[m], by_local=m) for m in (2, 1, 3)]
    both = join(*back_b, *got_a)
    back_b, got_a = both[:3], both[3:]
    own_a, other_a = in_rows(cut_a, got_a)
    got_ax = move(other_a, by_node=1)
    dh = part_b[0].astype(F32) + sum(part.astype(F32) for part in back_b)
    dh = jnp.where(valid(zeros[:, 1], node, tokens_here, capacity)[..., None], dh, 0.0)
    saved_rows = by_node(saved_own, saved_got, 0)
    g = saved_rows[..., :hidden_units].astype(F32)
    u = saved_rows[..., hidden_units:].astype(F32)
    q = 1.0 / (1.0 + jnp.exp(-g))
    grad_gu = jnp.concatenate([dh * u * q * (1.0 + g * (1.0 - q)), dh * g * q], axis=-1).astype(
        BF16
    )

    chain_b = gathers(grad_gu, local)
    back_b = send(next(chain_b))
    small_wait, route_wait = after(
        [jnp.stack([route_a.astype(F32), weight_fwd[0]]), route_b], grad_gu
    )
    small_next = move(small_wait, by_pp=1)
    route_b_next = move(route_wait, by_pp=-1)
    rows_a = by_node(own_a, got_ax, 1).reshape(-1, column)
    part_a = jnp.dot(rows_a, w_gu, preferred_element_type=F32).astype(BF16)
    *back_b, part_a, small_next, route_b_next = join(*back_b, part_a, small_next, route_b_next)
    part_a = part_a.reshape(shape + (2 * hidden_units,))
    chain_a = sums(lambda slot: part_a[slot])
    values_b, back_b = turn(chain_b, back_b)
    pieces = next(chain_a)
    back_a = send(pieces)
    act_next = move(after([act], *operands(pieces))[0], by_pp=1)
    *back_b, act_next = join(*back_b, act_next)
    values_b, back_b = turn(chain_b, back_b)
    grad_next = move(join(grad, *values_b)[0], by_pp=-1)
    *back_b, grad_next = join(*back_b, grad_next)
    values_a, back_a = turn(chain_a, back_a)
    values_a, back_a = turn(chain_a, back_a)
    all_gu = chain_b.send(back_b)
    done_b = dot_t(all_gu.reshape(-1, 2 * hidden_units), w_gu).astype(BF16)
    own_b, other_b = split(done_b.reshape(shape + (column,)))
    got_b = move(other_b, by_node=1)

    preact = chain_a.send(back_a)
    preact = jnp.where(valid(zeros[:, 0], node, tokens_here, capacity)[..., None], preact, 0.0)
    hidden = (jax.nn.silu(preact[..., :hidden_units]) * preact[..., hidden_units:]).astype(BF16)
    all_hidden = [move(hidden, by_local=-m) for m in (1, 2, 3)]
    merged_b = merge(own_b, got_b, node, tokens_here)
    h1, merged_b = join(all_hidden[0], merged_b)
    all_hidden = jnp.stack([hidden, h1, *all_hidden[1:]])
    home_b = send(homeward(merged_b, -1))
    done_a = jnp.dot(
        all_hidden.reshape(-1, hidden_units), w_dn, preferred_element_type=F32
    ).astype(BF16)
    own_a, other_a = split(done_a.reshape(shape + (column,)))
    got_a = move(other_a, by_node=1)
    home_a = send(homeward(merge(own_a, got_a, node, tokens_here), 1))

    at = jnp.stack([(local - m) % 4 for m in (2, 1, 3, 0)]).astype(jnp.int32)
    ones = jnp.ones((tokens_here,), F32)
    prev_grad = finish(grad_next, ones, sorted_places(route_b_next), home_b, at)
    place_a = sorted_places(small_next[0].astype(jnp.int32))
    next_input = finish(act_next, small_next[1], place_a, home_a, at)
    return next_input, prev_grad


def from_behind(value, axis, by):
    length = lax.axis_size(axis)
    return lax.ppermute(value, axis, [(i, (i + by) % length) for i in range(length)])


def place_matrix(route, expert_count, capacity):
    onehot = (route[:, None] == jnp.arange(expert_count, dtype=jnp.int32)[None, :]).astype(
        jnp.int32
    )
    before = jnp.cumsum(onehot, axis=0) - onehot
    slot_index = jnp.sum(before * onehot, axis=1)
    target = route * capacity + slot_index
    positions = jnp.arange(expert_count * capacity, dtype=jnp.int32)
    return (positions[:, None] == target[None, :]).astype(jnp.bfloat16)


def pack_rows(placer, values, expert_count, capacity):
    packed = jnp.dot(placer, values, preferred_element_type=jnp.float32).astype(jnp.bfloat16)
    return packed.reshape(expert_count, capacity, values.shape[1])


def unpack_rows(placer, packed):
    flattened = packed.reshape(-1, packed.shape[-1])
    result = lax.dot_general(
        placer, flattened, (((0,), (0,)), ((), ())), preferred_element_type=jnp.float32
    )
    return result.astype(jnp.bfloat16)


def flat_outgoing(packed, local_count):
    expert_count, capacity, feature_count = packed.shape
    column = feature_count // local_count
    outgoing = packed.reshape(expert_count, capacity, local_count, column).transpose(0, 2, 1, 3)
    return outgoing.reshape(expert_count * local_count, capacity, column)


def flat_layout(received, expert_count, local_count):
    capacity = received.shape[1]
    column = received.shape[2]
    rows_in = received.reshape(expert_count, local_count, capacity, column).transpose(1, 0, 2, 3)
    return rows_in.reshape(-1, column)


def send_rows(packs, local_count):
    expert_count = packs[0].shape[0]
    outgoing = tuple((flat_outgoing(packed, local_count) for packed in packs))
    received = (
        lax.all_to_all(outgoing[0], ("node", "local"), split_axis=0, concat_axis=0, tiled=True),
        lax.all_to_all(outgoing[1], ("node", "local"), split_axis=0, concat_axis=0, tiled=True),
    )
    return tuple((flat_layout(item, expert_count, local_count) for item in received))


def return_rows(finished_pair, expert_count, capacity, local_count):
    column = finished_pair[0].shape[1]
    blocks = tuple(
        (item.reshape(local_count, expert_count, capacity, column) for item in finished_pair)
    )
    outgoing = tuple(
        (
            item.transpose(1, 0, 2, 3).reshape(expert_count * local_count, capacity, column)
            for item in blocks
        )
    )
    received = (
        lax.all_to_all(outgoing[0], ("node", "local"), split_axis=0, concat_axis=0, tiled=True),
        lax.all_to_all(outgoing[1], ("node", "local"), split_axis=0, concat_axis=0, tiled=True),
    )
    results = []
    for item in received:
        arranged = item.reshape(expert_count, local_count, capacity, column).transpose(0, 2, 1, 3)
        results.append(arranged.reshape(expert_count, capacity, local_count * column))
    return tuple(results)


def body(
    act_fwd, routes_fwd, weight_fwd, grad_bwd, routes_bwd, weight_bwd, saved_bwd, w_gate_up, w_down
):
    node_count = lax.axis_size("node")
    local_count = lax.axis_size("local")
    tokens_here = act_fwd.shape[1]
    capacity = 5 * tokens_here // (4 * node_count)
    rows_each = node_count * capacity
    w_gu = w_gate_up[0, 0]
    w_dn = w_down[0, 0]
    hidden_units = w_dn.shape[0]
    tokens_a = act_fwd[0]
    placer_a = place_matrix(routes_fwd[0, :, 0], node_count, capacity)
    cotangent = grad_bwd[0]
    placer_b = place_matrix(routes_bwd[0, :, 0], node_count, capacity)
    scaled = (weight_bwd[0][:, None] * cotangent.astype(jnp.float32)).astype(jnp.bfloat16)
    packed_a = pack_rows(placer_a, tokens_a, node_count, capacity)
    packed_b = pack_rows(placer_b, scaled, node_count, capacity)
    rows_a, rows_b = send_rows((packed_a, packed_b), local_count)
    saved_packed = pack_rows(placer_b, saved_bwd[0], node_count, capacity)
    saved_rows = lax.all_to_all(
        saved_packed, "node", split_axis=0, concat_axis=0, tiled=True
    ).reshape(rows_each, -1)
    row_block = rows_a
    preact = lax.psum_scatter(
        jnp.dot(row_block, w_gu, preferred_element_type=jnp.float32).astype(jnp.bfloat16),
        "local",
        scatter_dimension=0,
        tiled=True,
    ).astype(jnp.float32)
    row_block = rows_b
    grad_hidden = lax.psum_scatter(
        lax.dot_general(
            row_block, w_dn, (((1,), (1,)), ((), ())), preferred_element_type=jnp.float32
        ).astype(jnp.bfloat16),
        "local",
        scatter_dimension=0,
        tiled=True,
    ).astype(jnp.float32)
    hidden = (jax.nn.silu(preact[:, :hidden_units]) * preact[:, hidden_units:]).astype(jnp.bfloat16)
    done_a = jnp.dot(
        lax.all_gather(hidden, "local", axis=0, tiled=True),
        w_dn,
        preferred_element_type=jnp.float32,
    ).astype(jnp.bfloat16)
    gate_pre = saved_rows[:, :hidden_units].astype(jnp.float32)
    up_pre = saved_rows[:, hidden_units:].astype(jnp.float32)
    sigmoid_g = 1.0 / (1.0 + jnp.exp(-gate_pre))
    grad_gate = grad_hidden * up_pre * sigmoid_g * (1.0 + gate_pre * (1.0 - sigmoid_g))
    grad_up = grad_hidden * gate_pre * sigmoid_g
    grad_gu = jnp.concatenate([grad_gate, grad_up], axis=1).astype(jnp.bfloat16)
    product = lax.dot_general(
        lax.all_gather(grad_gu, "local", axis=0, tiled=True),
        w_gu,
        (((1,), (1,)), ((), ())),
        preferred_element_type=jnp.float32,
    )
    done_b = product.astype(jnp.bfloat16)
    back_a, back_b = return_rows((done_a, done_b), node_count, capacity, local_count)
    moe_a = unpack_rows(placer_a, back_a)
    result_a = tokens_a.astype(jnp.float32) + weight_fwd[0][:, None] * moe_a.astype(jnp.float32)
    result_a = result_a.astype(jnp.bfloat16)
    moe_b = unpack_rows(placer_b, back_b)
    result_b = (cotangent.astype(jnp.float32) + moe_b.astype(jnp.float32)).astype(jnp.bfloat16)
    next_input = from_behind(result_a[None], "pp", 1)
    prev_grad = from_behind(result_b[None], "pp", -1)
    return (next_input, prev_grad)


def solution(mesh):
    in_specs = (
        P("pp", ("node", "local"), None),
        P("pp", ("node", "local"), None),
        P("pp", ("node", "local")),
        P("pp", ("node", "local"), None),
        P("pp", ("node", "local"), None),
        P("pp", ("node", "local")),
        P("pp", ("node", "local"), None),
        P("pp", "node", "local", None),
        P("pp", "node", None, "local"),
    )
    out_specs = (P("pp", ("node", "local"), None), P("pp", ("node", "local"), None))
    paired = mesh.shape["node"] == 2 and mesh.shape["local"] == 4
    plan = body_pair if paired else body
    return jax.shard_map(plan, mesh=mesh, in_specs=in_specs, out_specs=out_specs, check_vma=False)
```
